32 devices in a mesh: grp: 2 (over x), head: 16 (over z, y, core).
Axes of the slice: x: 2, y: 2, z: 4, core: 2. Of those that a mesh axis runs over, the one named last changes fastest.
Arguments:
- queries: bfloat16 [2048, 2, 16, 256], P('head', 'grp'), parts along dimension 1, may hold values from -12 to 12
- new_kv: bfloat16 [2048, 2, 2, 512], P('head', 'grp'), parts along dimension 1, may hold values from -4 to 4
- cache: bfloat16 [32, 256, 512], P(('grp', 'head')), parts along dimension 0, may hold values from -12 to 12
- resid: bfloat16 [2048, 2, 2048], P('head', 'grp'), parts along dimension 1, may hold values from -6 to 6
- w_out: bfloat16 [16, 256, 2048], P(None, 'head'), may hold values from -0.375 to 0.375
- norm_gain: float32 [2048], replicated, may hold values from 0.1 to 1.9
- expert_ids: int32 [2048, 2, 2], P('head', 'grp'), parts along dimension 1, may hold values from 0 to 15, all different within a row; in each aligned block of 128 rows (0 to 127, 128 to 255, ..., all dimensions but the last counted through in order) at most 32 rows name the same one
- expert_gates: float32 [2048, 2, 2], P('head', 'grp'), parts along dimension 1, may hold values from 0.2 to 1
- w_in: bfloat16 [16, 2048, 1024], P('head'), may hold values from -0.125 to 0.125
- w_down: bfloat16 [16, 512, 2048], P('head'), may hold values from -0.25 to 0.25
Outputs:
- layer_out: bfloat16 [2048, 2, 2048], P('head', 'grp'), parts along dimension 1
The draws below stay inside these ranges and needn't reach their ends.
There are 2 independent parts, one for each index of `grp`. The reference program is written for one: setup_inputs(seed, part) draws one part's arguments, and reference() takes and returns one part's arrays. A program takes and returns all parts, laid end to end along the dimension named above; an argument that names none is the same for every part. Nothing has to cross between parts.
Inputs may be any that keep to these rules, and one draw needn't show every extreme that they name: `expert_ids`: rows are taken in order over positions and then sequences; in each aligned block of 128 such rows (the rows of one device) no expert is named by more than 32 rows, a bound that some block reaches. A row names 2 different experts.
All inputs are finite; a program needn't handle non-finite values.
Results may differ from the reference program's by a relative error of at most 0.009.
Values may be sent and summed in bfloat16 or wider, within the bound.
No kernel may reach another device: no remote copies, remote signals or barrier semaphores. Data moves between devices by JAX's collectives and lax.ppermute only.
A program may use at most 128 MiB of HBM per device.

```python
import math
import jax
import jax.numpy as jnp
import numpy as np
from jax import lax

D = 2048
HEADS = 16
KV_HEADS = 2
HD = 256
FF_E = 512
TOP = 2
SPAN = 2048
CACHE = 2048
SEQS = 1
ROWS = 128
EXPERTS = 16
CAP = 32
N_HEAD = 16


def draw_queries(key, part):
    full_shape = (SPAN, SEQS, HEADS, HD)
    values = 2.0 * jnp.clip(jax.random.normal(jax.random.fold_in(key, 1), full_shape, jnp.float32), -4.0, 4.0)
    return values.astype(jnp.bfloat16)


def draw_cache(key, part):
    full_shape = (SEQS * KV_HEADS, CACHE, 2 * HD)
    values = jnp.clip(jax.random.normal(jax.random.fold_in(key, 2), full_shape, jnp.float32), -4.0, 4.0)
    paged = values.reshape(SEQS * HEADS, CACHE // (HEADS // KV_HEADS), 2 * HD)
    return paged.astype(jnp.bfloat16)


def level_of(own_key, extent, pieces, least, high):
    loudness, own = 1.0, jax.random.fold_in(own_key, 6)
    for dim, blocks in pieces:
        steps = jnp.exp(jax.random.uniform(jax.random.fold_in(own, dim), (blocks,), jnp.float32, least / len(pieces), high / len(pieces)))
        loudness = loudness * jnp.repeat(steps, extent[dim] // blocks).reshape([-1 if axis == dim else 1 for axis in range(len(extent))])
    return loudness


def routed_block(own_key, own, number, rows, number_of, top, bound, skew):
    order = jax.random.permutation(own_key, number_of)
    packed, ordinary = shares(number_of, rows * top, bound, skew, True), shares(number_of, rows * top, bound, skew, False)
    places = jnp.arange(number_of)

    def named(lengths, rotation):
        used = int((lengths > 0).sum())
        fixed = max(1, used // 4)
        passed = fixed + (places - fixed + rotation * (used - fixed)) % max(1, number_of - fixed)
        return jnp.zeros((number_of,), jnp.int32).at[order[jnp.where(places < fixed, places, passed)]].set(jnp.asarray(lengths, jnp.int32))

    lengths = jnp.where(number % 4 == 0, named(packed, number // 4), named(ordinary, number - number // 4 - 1))
    mixed = jax.random.permutation(jax.random.fold_in(own, 3), number_of)
    source_of, taker = mixed[0:number_of // 2 * 2:2], mixed[1:number_of // 2 * 2:2]
    slack = jnp.minimum(lengths[source_of] - 1, bound - lengths[taker]) // 2
    slack = jnp.where((source_of == order[0]) | (taker == order[0]) | (lengths[taker] == 0), 0, jnp.maximum(slack, 0))
    passed = jax.random.randint(jax.random.fold_in(own, 4), (number_of // 2,), 0, 1 << 20) % (slack + 1)
    lengths = lengths.at[source_of].add(-passed).at[taker].add(passed)
    members = jnp.searchsorted(jnp.cumsum(lengths), jnp.arange(rows * top), side="right").astype(jnp.int32)
    table = members.reshape(top, rows).T
    table = table[jax.random.permutation(jax.random.fold_in(own, 1), rows)]
    rotation = jax.random.randint(jax.random.fold_in(own, 2), (rows, 1), 0, top)
    return jnp.take_along_axis(table, (jnp.arange(top)[None, :] + rotation) % top, axis=1)


def shares(amount, total, reach, slope, full):
    weights = [(1 << 20) // math.isqrt(rank ** slope) + 1 for rank in range(1, amount + 1)]
    largest = reach if full else min(reach, max(-(-total // amount), total * weights[0] // sum(weights)))
    least = 1 if total - largest >= amount - 1 else 0
    counts, rest = [largest] + [least] * (amount - 1), total - largest - least * (amount - 1)
    while rest > 0:
        free = [i for i in range(1, amount) if counts[i] < largest] or [i for i in range(1, amount) if counts[i] < reach]
        pool, remaining = sum([weights[i] for i in free]), rest
        for i in free:
            extra = min(reach - counts[i], max(1, remaining * weights[i] // pool), rest)
            counts[i] = counts[i] + extra
            rest = rest - extra
    return np.array(counts)


def noise(stream_key, shape, deviation, reach, shards=(), kind=jnp.bfloat16):
    result = deviation * jax.random.normal(stream_key, shape, jnp.float32)
    if shards:
        result = result * level_of(stream_key, shape, shards, -0.22, 0.18)
    return jnp.clip(result, -reach, reach).astype(kind)


def setup_inputs(seed: int = 0, part: int = 0) -> dict:
    streams_of = jax.random.split(jax.random.key(seed), 11)
    own_keys = jax.random.split(jax.random.fold_in(streams_of[10], part), 11)
    queries = draw_queries(jax.random.fold_in(jax.random.fold_in(streams_of[10], part), 71), part)
    new_kv = noise(own_keys[1], (SPAN, SEQS, KV_HEADS, 2 * HD), 1.0, 4.0, ((0, 16),))
    cache = draw_cache(jax.random.fold_in(jax.random.fold_in(streams_of[10], part), 71), part)
    resid = noise(own_keys[3], (SPAN, SEQS, D), 1.0, 6.0, ((0, 16),))
    w_out = noise(streams_of[4], (HEADS, HD, D), HD ** -0.5, 0.375, ((1, 16),))
    norm_gain = jnp.clip(1.0 + 0.18 * jax.random.normal(streams_of[5], (D,), jnp.float32), 0.1, 1.9)
    expert_ids_keys = jax.random.split(jax.random.fold_in(own_keys[6], 1), SPAN * SEQS // ROWS)
    expert_ids_turns = jax.random.permutation(jax.random.fold_in(own_keys[6], 3), SPAN * SEQS // ROWS)
    expert_ids = jax.vmap(lambda own, number: routed_block(jax.random.fold_in(own_keys[6], 2), own, number, ROWS, EXPERTS, TOP, CAP, 0))(expert_ids_keys, expert_ids_turns).reshape((SPAN, SEQS, TOP))
    expert_gates = jnp.clip(0.2 + 0.8 * jax.random.uniform(own_keys[7], (SPAN, SEQS, TOP), jnp.float32) ** level_of(own_keys[7], (SPAN, SEQS, TOP), ((0, 16),), -0.2, 0.2), 0.2, 1.0)
    w_in = noise(streams_of[8], (EXPERTS, D, 2 * FF_E), D ** -0.5, 0.125, ((0, 16),))
    w_down = noise(streams_of[9], (EXPERTS, FF_E, D), FF_E ** -0.5, 0.25, ((0, 16),))
    return dict(queries=queries, new_kv=new_kv, cache=cache, resid=resid, w_out=w_out, norm_gain=norm_gain, expert_ids=expert_ids, expert_gates=expert_gates, w_in=w_in, w_down=w_down)


def attend_slot(query_rows_all, new_keys, new_values, cached):
    length = query_rows_all.shape[0]
    block_rows = min(512, length)
    score_scale = HD ** (-0.5)
    old_keys = cached[:, :HD]
    old_values = cached[:, HD:]
    key_positions = jnp.arange(length, dtype=jnp.int32)

    def one_block(first_row):
        query_rows = lax.dynamic_slice_in_dim(query_rows_all, first_row, block_rows, 0)
        old_scores = jnp.dot(query_rows, old_keys.T, preferred_element_type=jnp.float32) * score_scale
        new_scores = jnp.dot(query_rows, new_keys.T, preferred_element_type=jnp.float32) * score_scale
        row_positions = first_row + jnp.arange(block_rows, dtype=jnp.int32)
        allowed = key_positions[None, :] <= row_positions[:, None]
        new_scores = jnp.where(allowed, new_scores, -jnp.inf)
        row_max = jnp.maximum(lax.optimization_barrier(jnp.max(old_scores, 1)), lax.optimization_barrier(jnp.max(new_scores, 1)))[:, None]
        old_exp = jnp.exp(old_scores - row_max)
        new_exp = jnp.exp(new_scores - row_max)
        denominator = lax.optimization_barrier(jnp.sum(old_exp, 1)) + lax.optimization_barrier(jnp.sum(new_exp, 1))
        weighted_sum = jnp.dot(old_exp.astype(jnp.bfloat16), old_values, preferred_element_type=jnp.float32)
        weighted_sum = weighted_sum + jnp.dot(new_exp.astype(jnp.bfloat16), new_values, preferred_element_type=jnp.float32)
        return (weighted_sum / denominator[:, None]).astype(jnp.bfloat16)
    starts = (jnp.arange(length // block_rows) * block_rows).astype(jnp.int32)
    return lax.map(one_block, starts).reshape(length, HD)

def reference(queries, new_kv, cache, resid, w_out, norm_gain, expert_ids, expert_gates, w_in, w_down):
    group_size = HEADS // KV_HEADS
    slot_count = SEQS * HEADS
    query_slots = queries.reshape(SPAN, slot_count, HD).transpose(1, 0, 2)
    pair_slots = new_kv.reshape(SPAN, SEQS * KV_HEADS, 2 * HD).transpose(1, 0, 2)
    cached_slots = cache.reshape(SEQS * KV_HEADS, CACHE, 2 * HD)

    def per_slot(slot_index):
        pair_index = (slot_index // group_size).astype(jnp.int32)
        slot_queries = lax.dynamic_index_in_dim(query_slots, slot_index, 0, keepdims=False)
        slot_pairs = lax.dynamic_index_in_dim(pair_slots, pair_index, 0, keepdims=False)
        slot_cache = lax.dynamic_index_in_dim(cached_slots, pair_index, 0, keepdims=False)
        return attend_slot(slot_queries, slot_pairs[:, :HD], slot_pairs[:, HD:], slot_cache)
    outputs = lax.map(per_slot, jnp.arange(slot_count, dtype=jnp.int32))
    attended = outputs.transpose(1, 0, 2).reshape(SPAN * SEQS, HEADS * HD)
    stream = resid.reshape(SPAN * SEQS, D).astype(jnp.float32)
    stream = stream + jnp.dot(attended, w_out.reshape(HEADS * HD, D), preferred_element_type=jnp.float32)
    normed = stream * lax.rsqrt(lax.optimization_barrier(jnp.mean(stream * stream, 1, keepdims=True)) + 1e-06) * norm_gain
    normed = normed.astype(jnp.bfloat16)
    flat_ids = expert_ids.reshape(-1).astype(jnp.int32)
    assignments = flat_ids.shape[0]
    onehot = (flat_ids[:, None] == jnp.arange(EXPERTS, dtype=jnp.int32)[None, :]).astype(jnp.int32)
    earlier = jnp.cumsum(onehot, 0).astype(jnp.int32) - onehot
    slot_rank = lax.optimization_barrier(jnp.sum(earlier * onehot, 1)).astype(jnp.int32)
    limit = N_HEAD * CAP
    target = (flat_ids * limit + slot_rank).astype(jnp.int32)
    table = jnp.full((EXPERTS * limit,), assignments, jnp.int32)
    table = table.at[target].set(jnp.arange(assignments).astype(jnp.int32))
    repeated = jnp.concatenate([jnp.repeat(normed, TOP, axis=0), jnp.zeros((1, D), jnp.bfloat16)], 0)

    def per_expert(inputs):
        row_index, gate_up, down_weight = inputs
        expert_rows = repeated[row_index]
        inner_act = jnp.dot(expert_rows, gate_up, preferred_element_type=jnp.float32)
        hidden = (jax.nn.silu(inner_act[:, :FF_E]) * inner_act[:, FF_E:]).astype(jnp.bfloat16)
        return jnp.dot(hidden, down_weight, preferred_element_type=jnp.float32).astype(jnp.bfloat16)
    results = lax.map(per_expert, (table.reshape(EXPERTS, limit), w_in, w_down))
    picked = results.reshape(EXPERTS * limit, D)[target].astype(jnp.float32)
    weighted = picked * expert_gates.reshape(-1)[:, None]
    expert_sum = weighted.reshape(SPAN * SEQS, TOP, D).sum(1)
    return (stream + expert_sum).astype(jnp.bfloat16).reshape(SPAN, SEQS, D)
```

```python
import functools

import jax
import jax.numpy as jnp
from jax import lax
from jax.experimental import pallas as pl
from jax.experimental.pallas import tpu as pltpu
from jax.sharding import PartitionSpec as P

eps_norm = 1e-06
F32 = jnp.float32
BF16 = jnp.bfloat16
HIGH_VMEM = 48 * 2**20


def anywhere():
    return pl.BlockSpec(memory_space=pl.ANY)


def in_vmem():
    return pl.BlockSpec(memory_space=pltpu.VMEM)


def attend_kernel(
    block, chunk, width, q_hbm, cache_hbm, kv_hbm, o_ref, q_ref, cache_ref, kv_ref, s0, s1, sems
):
    members, groups, piece, _ = kv_hbm.shape
    length = members * groups * piece
    old = cache_hbm.shape[0]
    scale = width**-0.5
    in_q = pltpu.make_async_copy(q_hbm, q_ref, sems.at[0])
    in_cache = pltpu.make_async_copy(cache_hbm, cache_ref, sems.at[1])
    in_q.start()
    in_cache.start()
    in_kv = []
    for group in range(groups):
        for member in range(members):
            place = (group * members + member) * piece
            copy = pltpu.make_async_copy(
                kv_hbm.at[member, group], kv_ref.at[pl.ds(place, piece)], sems.at[2]
            )
            copy.start()
            in_kv.append(copy)
    in_q.wait()
    in_cache.wait()
    for copy in in_kv:
        copy.wait()
    scores = [s0, s1]

    def pieces(b):
        out = [(True, k, chunk, k) for k in range(0, old, chunk)]
        last = b * block
        for k in range(0, last, chunk):
            out.append((False, k, min(chunk, last - k), old + k))
        out.append((False, last, block, old + last))
        return out

    def make_scores(b, part, running):
        of_cache, first, count, column = part
        keys = (cache_ref if of_cache else kv_ref)[pl.ds(first, count), :width]
        s = lax.dot_general(
            q_ref[pl.ds(b * block, block), :],
            keys,
            (((1,), (1,)), ((), ())),
            preferred_element_type=F32,
        )
        if not of_cache and first == b * block:
            row = lax.broadcasted_iota(jnp.int32, s.shape, 0)
            col = lax.broadcasted_iota(jnp.int32, s.shape, 1)
            s = jnp.where(col <= row, s, -jnp.inf)
        scores[b % 2][:, pl.ds(column, count)] = s
        for k in range(0, count, 128):
            piece_max = s[:, k : k + 128]
            running = piece_max if running is None else jnp.maximum(running, piece_max)
        return running

    def use_scores(b, part, top, total, acc):
        of_cache, first, count, column = part
        values = (cache_ref if of_cache else kv_ref)[pl.ds(first, count), width:]
        e = jnp.exp((scores[b % 2][:, pl.ds(column, count)] - top) * scale)
        for k in range(0, count, 128):
            total = e[:, k : k + 128] if total is None else total + e[:, k : k + 128]
        product = jnp.dot(e.astype(BF16), values, preferred_element_type=F32)
        return total, product if acc is None else acc + product

    blocks = length // block
    running = None
    for part in pieces(0):
        running = make_scores(0, part, running)
    for b in range(blocks):
        top = jnp.max(running, 1, keepdims=True)
        now, later = pieces(b), pieces(b + 1) if b + 1 < blocks else []
        running, total, acc = None, None, None
        for k in range(max(len(now), len(later))):
            if k < len(now):
                total, acc = use_scores(b, now[k], top, total, acc)
            if k < len(later):
                running = make_scores(b + 1, later[k], running)
        o_ref[pl.ds(b * block, block), :] = (acc / jnp.sum(total, 1, keepdims=True)).astype(BF16)


def attend(q, cache, kv):
    length, width = q.shape
    old = cache.shape[0]
    block = min(256, length)
    chunk = min(512, old)
    return pl.pallas_call(
        functools.partial(attend_kernel, block, chunk, width),
        out_shape=jax.ShapeDtypeStruct((length, width), BF16),
        in_specs=[anywhere()] * 3,
        out_specs=in_vmem(),
        scratch_shapes=[
            pltpu.VMEM((length, width), BF16),
            pltpu.VMEM((old, 2 * width), BF16),
            pltpu.VMEM((length, 2 * width), BF16),
            pltpu.VMEM((block, old + length), F32),
            pltpu.VMEM((block, old + length), F32),
            pltpu.SemaphoreType.DMA((3,)),
        ],
        compiler_params=pltpu.CompilerParams(vmem_limit_bytes=HIGH_VMEM),
        cost_estimate=pl.CostEstimate(
            flops=4 * length * (old + length // 2) * width,
            bytes_accessed=4 * (2 * length + 2 * old) * width,
            transcendentals=length * (old + length // 2),
        ),
        name="attend",
    )(q, cache, kv)


def project_kernel(a_ref, w_ref, o_ref):
    members = a_ref.shape[0]
    planes, share = w_ref.shape[1], w_ref.shape[3]
    acc = None
    for head in range(members):
        w = jnp.concatenate(
            [w_ref[m, p, head] for p in range(planes) for m in range(members)], 0
        )
        part = jnp.dot(a_ref[head], w, preferred_element_type=F32)
        acc = part if acc is None else acc + part
    o_ref[...] = acc.astype(BF16)


def project(a, w):
    members, rows, width = a.shape
    planes, share, model = w.shape[1], w.shape[3], w.shape[4]
    tile = min(512, model)
    return pl.pallas_call(
        project_kernel,
        grid=(model // tile,),
        out_shape=jax.ShapeDtypeStruct((rows, model), BF16),
        in_specs=[
            pl.BlockSpec((members, rows, width), lambda t: (0, 0, 0)),
            pl.BlockSpec((members, planes, members, share, tile), lambda t: (0, 0, 0, 0, t)),
        ],
        out_specs=pl.BlockSpec((rows, tile), lambda t: (0, t)),
        compiler_params=pltpu.CompilerParams(vmem_limit_bytes=HIGH_VMEM),
        cost_estimate=pl.CostEstimate(
            flops=2 * members * rows * width * model,
            bytes_accessed=2 * (members * width * model + members * rows * width + rows * model),
            transcendentals=0,
        ),
        name="project",
    )(a, w)


def route_kernel(parts_ref, resid_ref, gain_ref, slots_ref, stream_ref, out_ref):
    seqs, planes = parts_ref.shape[0], parts_ref.shape[1]
    streams = []
    for seq in range(seqs):
        stream = resid_ref[seq].astype(F32)
        projected = parts_ref[seq, 0].astype(F32)
        for p in range(1, planes):
            projected = projected + parts_ref[seq, p].astype(F32)
        streams.append(stream + projected)
    stream = jnp.concatenate(streams, 0) if seqs > 1 else streams[0]
    stream_ref[...] = stream
    normed = stream * lax.rsqrt(jnp.mean(stream * stream, 1, keepdims=True) + eps_norm)
    normed = (normed * gain_ref[...]).astype(BF16)
    slots, rows = out_ref.shape[0], stream.shape[0]
    place = lax.broadcasted_iota(jnp.int32, (slots, rows), 0)
    hit = place == slots_ref[0:1, :]
    for k in range(1, slots_ref.shape[0]):
        hit = hit | (place == slots_ref[k : k + 1, :])
    out_ref[...] = jnp.dot(hit.astype(BF16), normed, preferred_element_type=F32).astype(BF16)


def route(parts, resid, gain, slots_of, slots):
    seqs, planes, local_rows, model = parts.shape
    rows = seqs * local_rows
    return pl.pallas_call(
        route_kernel,
        out_shape=(
            jax.ShapeDtypeStruct((rows, model), F32),
            jax.ShapeDtypeStruct((slots, model), BF16),
        ),
        in_specs=[in_vmem()] * 4,
        out_specs=(in_vmem(), in_vmem()),
        compiler_params=pltpu.CompilerParams(vmem_limit_bytes=HIGH_VMEM),
        cost_estimate=pl.CostEstimate(
            flops=2 * slots * rows * model,
            bytes_accessed=2 * (planes + 3 + slots // rows) * rows * model,
            transcendentals=0,
        ),
        name="route",
    )(parts, resid, gain, slots_of)


def expert_kernel(x_ref, w_in_ref, w_down_ref, o_ref):
    hidden_width = w_down_ref.shape[0]
    inner = jnp.dot(x_ref[...], w_in_ref[...], preferred_element_type=F32)
    gate = inner[:, :hidden_width]
    hidden = (gate / (1.0 + jnp.exp(-gate)) * inner[:, hidden_width:]).astype(BF16)
    o_ref[...] = jnp.dot(hidden, w_down_ref[...], preferred_element_type=F32).astype(BF16)


def expert(x, w_in, w_down):
    rows, model = x.shape
    hidden_width = w_down.shape[0]
    return pl.pallas_call(
        expert_kernel,
        out_shape=jax.ShapeDtypeStruct((rows, model), BF16),
        in_specs=[in_vmem()] * 3,
        out_specs=in_vmem(),
        compiler_params=pltpu.CompilerParams(vmem_limit_bytes=HIGH_VMEM),
        cost_estimate=pl.CostEstimate(
            flops=6 * rows * model * hidden_width,
            bytes_accessed=2 * (2 * rows * model + 3 * model * hidden_width),
            transcendentals=rows * hidden_width,
        ),
        name="expert",
    )(x, w_in, w_down)


def combine_kernel(seqs, back_ref, stream_ref, slots_ref, gates_ref, o_ref):
    slots = back_ref.shape[0]
    rows = stream_ref.shape[0]
    place = lax.broadcasted_iota(jnp.int32, (rows, slots), 1)
    total = stream_ref[...]
    gathered = None
    for k in range(slots_ref.shape[1]):
        pick = (place == slots_ref[:, k : k + 1]).astype(BF16)
        picked = jnp.dot(pick, back_ref[...], preferred_element_type=F32)
        part = picked * gates_ref[:, k : k + 1]
        gathered = part if gathered is None else gathered + part
    out = (total + gathered).astype(BF16)
    local_rows = rows // seqs
    for seq in range(seqs):
        o_ref[seq] = out[seq * local_rows : (seq + 1) * local_rows]


def combine(back, stream, slots_of, gates, seqs):
    slots, model = back.shape
    rows = stream.shape[0]
    top = slots_of.shape[1]
    return pl.pallas_call(
        functools.partial(combine_kernel, seqs),
        out_shape=jax.ShapeDtypeStruct((seqs, rows // seqs, model), BF16),
        in_specs=[in_vmem()] * 4,
        out_specs=in_vmem(),
        compiler_params=pltpu.CompilerParams(vmem_limit_bytes=HIGH_VMEM),
        cost_estimate=pl.CostEstimate(
            flops=2 * top * slots * rows * model,
            bytes_accessed=2 * slots * model + 6 * rows * model,
            transcendentals=0,
        ),
        name="combine",
    )(back, stream, slots_of, gates)


def local(queries, new_kv, cache, resid, w_out, norm_gain, expert_ids, expert_gates, w_in, w_down):
    n = lax.axis_size("head")
    local_rows, seqs, heads, width = queries.shape
    pair_heads = new_kv.shape[2]
    members = heads // pair_heads
    groups = n // members
    model = resid.shape[2]
    rows = local_rows * seqs
    side = 1 << ((n.bit_length() - 1) // 2)
    side = min(side, heads)
    planes = n // side
    planes_of_seq = heads // side
    pair_groups = [[g * members + m for m in range(members)] for g in range(groups)]
    cross_groups = [[g * members + m for g in range(groups)] for m in range(members)]
    plane_groups = [[p * side + m for m in range(side)] for p in range(planes)]
    column_groups = [[p * side + m for p in range(planes)] for m in range(side)]

    query_slots = queries.reshape(local_rows, n, width).transpose(1, 0, 2)
    q = lax.all_to_all(query_slots, "head", split_axis=0, concat_axis=0, tiled=True)
    q = q.reshape(n * local_rows, width)

    kv_slots = new_kv.reshape(local_rows, groups, 2 * width).transpose(1, 0, 2)
    kv = lax.all_to_all(
        kv_slots, "head", split_axis=0, concat_axis=0, tiled=True, axis_index_groups=cross_groups
    )
    kv = lax.all_gather(kv, "head", axis=0, axis_index_groups=pair_groups)
    pages = lax.all_gather(cache, "head", axis=0, tiled=True, axis_index_groups=pair_groups)

    share = w_out.shape[1]
    w_planes = w_out.reshape(planes_of_seq, side, share, model)
    if planes > planes_of_seq:
        w_planes = jnp.tile(w_planes, (planes // planes_of_seq, 1, 1, 1))
    w = lax.all_to_all(
        w_planes, "head", split_axis=0, concat_axis=0, tiled=True, axis_index_groups=column_groups
    )
    w = lax.all_gather(w, "head", axis=0, axis_index_groups=plane_groups)
    if share % 16:
        w = w.transpose(2, 1, 0, 3, 4).reshape(1, 1, side, width, model)
        w = w.reshape(side, width, model)

    top = expert_ids.shape[2]
    experts = w_in.shape[0] * n
    capacity = max(2, 2 * rows * top // experts)
    ids = expert_ids.transpose(1, 0, 2).reshape(rows, top)
    gates = expert_gates.transpose(1, 0, 2).reshape(rows, top)
    onehot = (ids[:, :, None] == jnp.arange(experts, dtype=jnp.int32)).astype(jnp.int32)
    named = onehot.sum(1)
    before = jnp.cumsum(named, 0) - named
    slots_of = ids * capacity + jnp.sum(onehot * before[:, None, :], 2)
    slots = experts * capacity

    attended = attend(q, pages.reshape(-1, 2 * width), kv)
    a = attended.reshape(planes, side, local_rows, width).transpose(1, 0, 2, 3)
    a = a.reshape(side, planes * local_rows, width)
    a = lax.all_to_all(
        a, "head", split_axis=0, concat_axis=0, tiled=True, axis_index_groups=plane_groups
    )
    if share % 16:
        partial = jnp.einsum("hri,hid->rd", a, w, preferred_element_type=F32).astype(BF16)
    else:
        partial = project(a, w)
    parts = lax.all_to_all(
        partial.reshape(planes, local_rows, model),
        "head",
        split_axis=0,
        concat_axis=0,
        tiled=True,
        axis_index_groups=column_groups,
    )
    parts = parts.reshape(seqs, planes_of_seq, local_rows, model)
    stream, outgoing = route(
        parts, resid.transpose(1, 0, 2), norm_gain[None, :], slots_of.T, slots
    )
    arrived = lax.all_to_all(
        outgoing.reshape(n, slots // n, model), "head", split_axis=0, concat_axis=0, tiled=True
    )
    local_experts = w_in.shape[0]
    if local_experts == 1:
        answered = expert(arrived.reshape(slots, model), w_in[0], w_down[0])
        answered = answered.reshape(n, slots // n, model)
    else:
        arrived = arrived.reshape(n, local_experts, capacity, model).transpose(1, 0, 2, 3)
        arrived = arrived.reshape(local_experts, n * capacity, model)
        answered = jnp.stack([expert(arrived[e], w_in[e], w_down[e]) for e in range(local_experts)])
        answered = answered.reshape(local_experts, n, capacity, model).transpose(1, 0, 2, 3)
        answered = answered.reshape(n, slots // n, model)
    back = lax.all_to_all(answered, "head", split_axis=0, concat_axis=0, tiled=True)
    out = combine(back.reshape(slots, model), stream, slots_of, gates, seqs)
    return out.transpose(1, 0, 2)


def solution(mesh):
    return jax.shard_map(
        local,
        mesh=mesh,
        in_specs=(
            P("head", "grp", None, None),
            P("head", "grp", None, None),
            P(("grp", "head"), None, None),
            P("head", "grp", None),
            P(None, "head", None),
            P(),
            P("head", "grp", None),
            P("head", "grp", None),
            P("head", None, None),
            P("head", None, None),
        ),
        out_specs=P("head", "grp", None),
        check_vma=False,
    )
```

```python
import functools

import jax
import jax.numpy as jnp
from jax import lax
from jax.experimental import pallas as pl
from jax.experimental.pallas import tpu as pltpu
from jax.sharding import PartitionSpec as P

eps_norm = 1e-06
F32 = jnp.float32
BF16 = jnp.bfloat16
HIGH_VMEM = 48 * 2**20


def anywhere():
    return pl.BlockSpec(memory_space=pl.ANY)


def in_vmem():
    return pl.BlockSpec(memory_space=pltpu.VMEM)


def attend_kernel(
    block, chunk, width, q_hbm, cache_hbm, kv_hbm, o_ref, q_ref, cache_ref, kv_ref, s0, s1, sems
):
    members, groups, piece, _ = kv_hbm.shape
    length = members * groups * piece
    old = cache_hbm.shape[0]
    scale = width**-0.5
    in_q = pltpu.make_async_copy(q_hbm, q_ref, sems.at[0])
    in_cache = pltpu.make_async_copy(cache_hbm, cache_ref, sems.at[1])
    in_q.start()
    in_cache.start()
    in_kv = []
    for group in range(groups):
        for member in range(members):
            place = (group * members + member) * piece
            copy = pltpu.make_async_copy(
                kv_hbm.at[member, group], kv_ref.at[pl.ds(place, piece)], sems.at[2]
            )
            copy.start()
            in_kv.append(copy)
    in_q.wait()
    in_cache.wait()
    for copy in in_kv:
        copy.wait()
    scores = [s0, s1]

    def pieces(b):
        out = [(True, k, chunk, k) for k in range(0, old, chunk)]
        last = b * block
        for k in range(0, last, chunk):
            out.append((False, k, min(chunk, last - k), old + k))
        out.append((False, last, block, old + last))
        return out

    def make_scores(b, part, running):
        of_cache, first, count, column = part
        keys = (cache_ref if of_cache else kv_ref)[pl.ds(first, count), :width]
        s = lax.dot_general(
            q_ref[pl.ds(b * block, block), :],
            keys,
            (((1,), (1,)), ((), ())),
            preferred_element_type=F32,
        )
        if not of_cache and first == b * block:
            row = lax.broadcasted_iota(jnp.int32, s.shape, 0)
            col = lax.broadcasted_iota(jnp.int32, s.shape, 1)
            s = jnp.where(col <= row, s, -jnp.inf)
        scores[b % 2][:, pl.ds(column, count)] = s
        for k in range(0, count, 128):
            piece_max = s[:, k : k + 128]
            running = piece_max if running is None else jnp.maximum(running, piece_max)
        return running

    def use_scores(b, part, top, total, acc):
        of_cache, first, count, column = part
        values = (cache_ref if of_cache else kv_ref)[pl.ds(first, count), width:]
        e = jnp.exp((scores[b % 2][:, pl.ds(column, count)] - top) * scale)
        for k in range(0, count, 128):
            total = e[:, k : k + 128] if total is None else total + e[:, k : k + 128]
        product = jnp.dot(e.astype(BF16), values, preferred_element_type=F32)
        return total, product if acc is None else acc + product

    blocks = length // block
    running = None
    for part in pieces(0):
        running = make_scores(0, part, running)
    for b in range(blocks):
        top = jnp.max(running, 1, keepdims=True)
        now, later = pieces(b), pieces(b + 1) if b + 1 < blocks else []
        running, total, acc = None, None, None
        for k in range(max(len(now), len(later))):
            if k < len(now):
                total, acc = use_scores(b, now[k], top, total, acc)
            if k < len(later):
                running = make_scores(b + 1, later[k], running)
        o_ref[pl.ds(b * block, block), :] = (acc / jnp.sum(total, 1, keepdims=True)).astype(BF16)


def attend(q, cache, kv):
    length, width = q.shape
    old = cache.shape[0]
    block = min(256, length)
    chunk = min(512, old)
    return pl.pallas_call(
        functools.partial(attend_kernel, block, chunk, width),
        out_shape=jax.ShapeDtypeStruct((length, width), BF16),
        in_specs=[anywhere()] * 3,
        out_specs=in_vmem(),
        scratch_shapes=[
            pltpu.VMEM((length, width), BF16),
            pltpu.VMEM((old, 2 * width), BF16),
            pltpu.VMEM((length, 2 * width), BF16),
            pltpu.VMEM((block, old + length), F32),
            pltpu.VMEM((block, old + length), F32),
            pltpu.SemaphoreType.DMA((3,)),
        ],
        compiler_params=pltpu.CompilerParams(vmem_limit_bytes=HIGH_VMEM),
        cost_estimate=pl.CostEstimate(
            flops=4 * length * (old + length // 2) * width,
            bytes_accessed=4 * (2 * length + 2 * old) * width,
            transcendentals=length * (old + length // 2),
        ),
        name="attend",
    )(q, cache, kv)


def attend_pair_kernel(
    block,
    chunk,
    width,
    q_hbm,
    page_a,
    page_b,
    page_y,
    page_c,
    page_cy,
    kv_own,
    kv_y,
    kv_c,
    kv_cy,
    o_ref,
    q_ref,
    old_ref,
    kv_ref,
    s0,
    s1,
    sems,
):
    me = lax.axis_index("head")
    members, heads, piece, _ = q_hbm.shape
    length = members * piece
    planes = kv_own.shape[0]
    old = old_ref.shape[0]
    earlier_group = me // members > 0
    core = lax.rem(me, 2)
    copies = []

    def bring(source, target, sem):
        copy = pltpu.make_async_copy(source, target, sems.at[sem])
        copy.start()
        copies.append(copy)

    for member in range(members):
        for head in range(heads):
            bring(q_hbm.at[member, head], q_ref.at[head, pl.ds(member * piece, piece)], 0)
    place = 0
    for page in (page_a, page_b, page_y, page_c, page_cy):
        count = page.shape[0]
        bring(page, old_ref.at[pl.ds(place, count)], 1)
        place += count
    for flip, pieces_of in ((0, kv_own), (2, kv_y), (1, kv_c), (3, kv_cy)):
        for t in range(planes):
            number = jnp.bitwise_and(
                jnp.bitwise_xor(me, flip ^ (t * (members // 2))), members - 1
            )
            start = pl.multiple_of(number * piece, piece)
            area = 0 if t * (members // 2) >= members else length
            bring(pieces_of.at[t], kv_ref.at[pl.ds(area + start, piece)], 2)
    for copy in copies:
        copy.wait()
    scale = width**-0.5
    scores = [s0, s1]
    blocks = length // block
    units = [(head, b) for head in range(heads) for b in range(blocks)]

    def pieces(unit):
        _, b = units[unit]
        out = [("old", k, chunk, k) for k in range(0, old, chunk)]
        out += [("past", k, chunk, old + k) for k in range(0, length, chunk)]
        last = b * block
        for k in range(0, last, chunk):
            out.append(("new", length + k, min(chunk, last - k), old + length + k))
        out.append(("edge", length + last, block, old + length + last))
        return out

    def make_scores(unit, part, running):
        kind, first, count, column = part
        head, b = units[unit]
        keys = (old_ref if kind == "old" else kv_ref)[pl.ds(first, count), :width]
        s = lax.dot_general(
            q_ref[head, pl.ds(b * block, block), :],
            keys,
            (((1,), (1,)), ((), ())),
            preferred_element_type=F32,
        )
        if kind == "past":
            s = jnp.where(earlier_group, s, -jnp.inf)
        if kind == "edge":
            row = lax.broadcasted_iota(jnp.int32, s.shape, 0)
            col = lax.broadcasted_iota(jnp.int32, s.shape, 1)
            s = jnp.where(col <= row, s, -jnp.inf)
        scores[unit % 2][:, pl.ds(column, count)] = s
        for k in range(0, count, 128):
            piece_max = s[:, k : k + 128]
            running = piece_max if running is None else jnp.maximum(running, piece_max)
        return running

    def use_scores(unit, part, top, total, acc):
        kind, first, count, column = part
        values = (old_ref if kind == "old" else kv_ref)[pl.ds(first, count), width:]
        e = jnp.exp((scores[unit % 2][:, pl.ds(column, count)] - top) * scale)
        for k in range(0, count, 128):
            total = e[:, k : k + 128] if total is None else total + e[:, k : k + 128]
        product = jnp.dot(e.astype(BF16), values, preferred_element_type=F32)
        return total, product if acc is None else acc + product

    running = None
    for part in pieces(0):
        running = make_scores(0, part, running)
    for unit, (head, b) in enumerate(units):
        top = jnp.max(running, 1, keepdims=True)
        now = pieces(unit)
        later = pieces(unit + 1) if unit + 1 < len(units) else []
        running, total, acc = None, None, None
        for k in range(max(len(now), len(later))):
            if k < len(now):
                total, acc = use_scores(unit, now[k], top, total, acc)
            if k < len(later):
                running = make_scores(unit + 1, later[k], running)
        done = (acc / jnp.sum(total, 1, keepdims=True)).astype(BF16)
        for k in range(0, block, piece):
            member = (b * block + k) // piece
            side = jnp.bitwise_xor(core, member % 2)
            o_ref[side, pl.ds((member // 2) * piece, piece), pl.ds(head * width, width)] = done[
                k : k + piece
            ]


def attend_pair(q, pages, kvs):
    members, heads, piece, width = q.shape
    length = members * piece
    old = sum(page.shape[0] for page in pages)
    block = 2 * piece
    chunk = min(512, old, length)
    keys = old + 2 * length
    return pl.pallas_call(
        functools.partial(attend_pair_kernel, block, chunk, width),
        out_shape=jax.ShapeDtypeStruct((2, length // 2, heads * width), BF16),
        in_specs=[anywhere()] * (1 + len(pages) + len(kvs)),
        out_specs=in_vmem(),
        scratch_shapes=[
            pltpu.VMEM((heads, length, width), BF16),
            pltpu.VMEM((old, 2 * width), BF16),
            pltpu.VMEM((2 * length, 2 * width), BF16),
            pltpu.VMEM((block, keys), F32),
            pltpu.VMEM((block, keys), F32),
            pltpu.SemaphoreType.DMA((3,)),
        ],
        compiler_params=pltpu.CompilerParams(vmem_limit_bytes=HIGH_VMEM),
        cost_estimate=pl.CostEstimate(
            flops=4 * heads * length * (keys - length // 2) * width,
            bytes_accessed=4 * (heads * length + keys) * width,
            transcendentals=heads * length * (keys - length // 2),
        ),
        name="attend",
    )(q, *pages, *kvs)


def project_pair_kernel(a_ref, got_ref, w_own, w_c, w_x, w_cx, o_ref, w_ref, sems):
    me = lax.axis_index("head")
    half = lax.axis_index("grp")
    core = lax.rem(me, 2)
    planes, sides, heads, share, columns = w_own.shape
    width = w_ref.shape[1]
    copies = []
    for flip, x, pieces_of in ((0, 0, w_own), (1, 0, w_c), (0, 1, w_x), (1, 1, w_cx)):
        column = pl.multiple_of(jnp.bitwise_xor(half, x) * columns, columns)
        for t in range(planes):
            for u in range(sides):
                number = jnp.bitwise_xor(me, flip ^ (2 * u) ^ (4 * t))
                row = pl.multiple_of(number * share, share)
                copy = pltpu.make_async_copy(
                    pieces_of.at[t, u],
                    w_ref.at[:, pl.ds(row, share), pl.ds(column, columns)],
                    sems.at[0],
                )
                copy.start()
                copies.append(copy)
    for copy in copies:
        copy.wait()
    acc = None
    for k in range(heads):
        mine = k < heads // 2
        column = (k % (heads // 2)) * width
        a = a_ref[0, :, pl.ds(column, width)] if mine else got_ref[:, pl.ds(column, width)]
        head = jnp.bitwise_xor(core, 0 if mine else 1) * (heads // 2) + k % (heads // 2)
        part = jnp.dot(a, w_ref[head], preferred_element_type=F32)
        acc = part if acc is None else acc + part
    o_ref[...] = acc.astype(BF16)


def project_pair(a, got, w_own, w_c, w_x, w_cx):
    planes, sides, heads, share, columns = w_own.shape
    rows = got.shape[0]
    width = 2 * got.shape[1] // heads
    model = 2 * columns
    return pl.pallas_call(
        project_pair_kernel,
        out_shape=jax.ShapeDtypeStruct((rows, model), BF16),
        in_specs=[in_vmem(), in_vmem()] + [anywhere()] * 4,
        out_specs=in_vmem(),
        scratch_shapes=[
            pltpu.VMEM((heads, width, model), BF16),
            pltpu.SemaphoreType.DMA((1,)),
        ],
        compiler_params=pltpu.CompilerParams(vmem_limit_bytes=HIGH_VMEM),
        cost_estimate=pl.CostEstimate(
            flops=2 * heads * rows * width * model,
            bytes_accessed=2 * (heads * width * model + heads * rows * width + rows * model),
            transcendentals=0,
        ),
        name="project",
    )(a, got, w_own, w_c, w_x, w_cx)


def project_kernel(a_ref, w_ref, o_ref):
    members = a_ref.shape[0]
    planes, share = w_ref.shape[1], w_ref.shape[3]
    acc = None
    for head in range(members):
        w = jnp.concatenate(
            [w_ref[m, p, head] for p in range(planes) for m in range(members)], 0
        )
        part = jnp.dot(a_ref[head], w, preferred_element_type=F32)
        acc = part if acc is None else acc + part
    o_ref[...] = acc.astype(BF16)


def project(a, w):
    members, rows, width = a.shape
    planes, share, model = w.shape[1], w.shape[3], w.shape[4]
    tile = min(512, model)
    return pl.pallas_call(
        project_kernel,
        grid=(model // tile,),
        out_shape=jax.ShapeDtypeStruct((rows, model), BF16),
        in_specs=[
            pl.BlockSpec((members, rows, width), lambda t: (0, 0, 0)),
            pl.BlockSpec((members, planes, members, share, tile), lambda t: (0, 0, 0, 0, t)),
        ],
        out_specs=pl.BlockSpec((rows, tile), lambda t: (0, t)),
        compiler_params=pltpu.CompilerParams(vmem_limit_bytes=HIGH_VMEM),
        cost_estimate=pl.CostEstimate(
            flops=2 * members * rows * width * model,
            bytes_accessed=2 * (members * width * model + members * rows * width + rows * model),
            transcendentals=0,
        ),
        name="project",
    )(a, w)


def route_kernel(parts_ref, resid_ref, gain_ref, slots_ref, stream_ref, out_ref):
    seqs, planes = parts_ref.shape[0], parts_ref.shape[1]
    streams = []
    for seq in range(seqs):
        stream = resid_ref[seq].astype(F32)
        projected = parts_ref[seq, 0].astype(F32)
        for p in range(1, planes):
            projected = projected + parts_ref[seq, p].astype(F32)
        streams.append(stream + projected)
    stream = jnp.concatenate(streams, 0) if seqs > 1 else streams[0]
    stream_ref[...] = stream
    normed = stream * lax.rsqrt(jnp.mean(stream * stream, 1, keepdims=True) + eps_norm)
    normed = (normed * gain_ref[...]).astype(BF16)
    slots, rows = out_ref.shape[0], stream.shape[0]
    place = lax.broadcasted_iota(jnp.int32, (slots, rows), 0)
    hit = place == slots_ref[0:1, :]
    for k in range(1, slots_ref.shape[0]):
        hit = hit | (place == slots_ref[k : k + 1, :])
    out_ref[...] = jnp.dot(hit.astype(BF16), normed, preferred_element_type=F32).astype(BF16)


def route(parts, resid, gain, slots_of, slots):
    seqs, planes, local_rows, model = parts.shape
    rows = seqs * local_rows
    return pl.pallas_call(
        route_kernel,
        out_shape=(
            jax.ShapeDtypeStruct((rows, model), F32),
            jax.ShapeDtypeStruct((slots, model), BF16),
        ),
        in_specs=[in_vmem()] * 4,
        out_specs=(in_vmem(), in_vmem()),
        compiler_params=pltpu.CompilerParams(vmem_limit_bytes=HIGH_VMEM),
        cost_estimate=pl.CostEstimate(
            flops=2 * slots * rows * model,
            bytes_accessed=2 * (planes + 3 + slots // rows) * rows * model,
            transcendentals=0,
        ),
        name="route",
    )(parts, resid, gain, slots_of)


def expert_kernel(x_ref, w_in_ref, w_down_ref, o_ref):
    hidden_width = w_down_ref.shape[0]
    inner = jnp.dot(x_ref[...], w_in_ref[...], preferred_element_type=F32)
    gate = inner[:, :hidden_width]
    hidden = (gate / (1.0 + jnp.exp(-gate)) * inner[:, hidden_width:]).astype(BF16)
    o_ref[...] = jnp.dot(hidden, w_down_ref[...], preferred_element_type=F32).astype(BF16)


def expert(x, w_in, w_down):
    rows, model = x.shape
    hidden_width = w_down.shape[0]
    return pl.pallas_call(
        expert_kernel,
        out_shape=jax.ShapeDtypeStruct((rows, model), BF16),
        in_specs=[in_vmem()] * 3,
        out_specs=in_vmem(),
        compiler_params=pltpu.CompilerParams(vmem_limit_bytes=HIGH_VMEM),
        cost_estimate=pl.CostEstimate(
            flops=6 * rows * model * hidden_width,
            bytes_accessed=2 * (2 * rows * model + 3 * model * hidden_width),
            transcendentals=rows * hidden_width,
        ),
        name="expert",
    )(x, w_in, w_down)


def combine_kernel(seqs, back_ref, stream_ref, slots_ref, gates_ref, o_ref):
    slots = back_ref.shape[0]
    rows = stream_ref.shape[0]
    place = lax.broadcasted_iota(jnp.int32, (rows, slots), 1)
    total = stream_ref[...]
    gathered = None
    for k in range(slots_ref.shape[1]):
        pick = (place == slots_ref[:, k : k + 1]).astype(BF16)
        picked = jnp.dot(pick, back_ref[...], preferred_element_type=F32)
        part = picked * gates_ref[:, k : k + 1]
        gathered = part if gathered is None else gathered + part
    out = (total + gathered).astype(BF16)
    local_rows = rows // seqs
    for seq in range(seqs):
        o_ref[seq] = out[seq * local_rows : (seq + 1) * local_rows]


def combine(back, stream, slots_of, gates, seqs):
    slots, model = back.shape
    rows = stream.shape[0]
    top = slots_of.shape[1]
    return pl.pallas_call(
        functools.partial(combine_kernel, seqs),
        out_shape=jax.ShapeDtypeStruct((seqs, rows // seqs, model), BF16),
        in_specs=[in_vmem()] * 4,
        out_specs=in_vmem(),
        compiler_params=pltpu.CompilerParams(vmem_limit_bytes=HIGH_VMEM),
        cost_estimate=pl.CostEstimate(
            flops=2 * top * slots * rows * model,
            bytes_accessed=2 * slots * model + 6 * rows * model,
            transcendentals=0,
        ),
        name="combine",
    )(back, stream, slots_of, gates)


def flipped(value, axis, mask):
    pairs = [(source, source ^ mask) for source in range(lax.axis_size(axis))]
    return lax.ppermute(value, axis, pairs)


def parts_in_pairs(queries, new_kv, cache, w_out):
    n = lax.axis_size("head")
    local_rows, _, heads, width = queries.shape
    pair_heads = new_kv.shape[2]
    members = heads // pair_heads
    model = w_out.shape[2]
    share = w_out.shape[1]
    me = lax.axis_index("head")
    plane_bit = members // 2
    planes = n // plane_bit
    b = (me // plane_bit) % 2
    y = (me // 2) % 2
    group_sets = [[g * members + m for m in range(members)] for g in range(n // members)]

    query_slots = queries.reshape(local_rows, heads, width).transpose(1, 0, 2)
    query_slots = query_slots.reshape(members, heads // members, local_rows, width)
    q = lax.all_to_all(
        query_slots, "head", split_axis=0, concat_axis=0, tiled=True, axis_index_groups=group_sets
    )

    def page_target(source, other):
        p, plane, rest = source // members, (source // plane_bit) % 2, source % plane_bit
        return (plane ^ other) * members + p * plane_bit + rest

    page_a, page_b = (
        lax.ppermute(cache[0], "head", [(d, page_target(d, other)) for d in range(n)])
        for other in range(2)
    )
    own_pages = jnp.concatenate([page_a, page_b], 0)
    pages_y = flipped(own_pages, "head", 2)
    pages_c = flipped(own_pages, "head", 1)
    pages_cy = flipped(pages_y, "head", 1)

    kv_heads = new_kv.reshape(local_rows, pair_heads, 2 * width).transpose(1, 0, 2)
    kv_same = lax.dynamic_index_in_dim(kv_heads, b, 0, keepdims=False)
    kv_other = lax.dynamic_index_in_dim(kv_heads, 1 - b, 0, keepdims=False)
    kv_own = [kv_same]
    for t in range(1, planes):
        kv_own.append(flipped(kv_other if t % 2 else kv_same, "head", t * plane_bit))
    kv_own = jnp.stack(kv_own, 0)
    kv_y = flipped(kv_own, "head", 2)
    kv_c = flipped(kv_own, "head", 1)
    kv_cy = flipped(kv_y, "head", 1)

    columns = model // 2
    w = lax.dynamic_slice_in_dim(w_out, lax.axis_index("grp") * columns, columns, 2)
    w = w.reshape(2, 2, heads // 4, share, columns)
    w_keep = lax.dynamic_index_in_dim(w, y, 1, keepdims=False)
    w_give = lax.dynamic_index_in_dim(w, 1 - y, 1, keepdims=False)
    w_both = jnp.stack([w_keep, flipped(w_give, "head", 2)], 1)
    w_same = lax.dynamic_index_in_dim(w_both, b, 0, keepdims=False)
    w_other = lax.dynamic_index_in_dim(w_both, 1 - b, 0, keepdims=False)
    w_own = [w_same]
    for t in range(1, planes):
        w_own.append(flipped(w_other if t % 2 else w_same, "head", t * plane_bit))
    w_own = jnp.stack(w_own, 0)
    w_x = flipped(w_own, "grp", 1)
    w_c = flipped(w_own, "head", 1)
    w_cx = flipped(w_x, "head", 1)

    a = attend_pair(
        q, (page_a, page_b, pages_y, pages_c, pages_cy), (kv_own, kv_y, kv_c, kv_cy)
    )
    got = flipped(a[1], "head", 1)
    partial = project_pair(a, got, w_own, w_c, w_x, w_cx)
    quads = [
        [g * members + 2 * k + core for k in range(members // 2)]
        for g in range(n // members)
        for core in range(2)
    ]
    parts = lax.all_to_all(
        partial.reshape(members // 2, local_rows, model),
        "head",
        split_axis=0,
        concat_axis=0,
        tiled=True,
        axis_index_groups=quads,
    )
    return parts[None]


def parts_in_planes(queries, new_kv, cache, w_out):
    n = lax.axis_size("head")
    local_rows, seqs, heads, width = queries.shape
    pair_heads = new_kv.shape[2]
    members = heads // pair_heads
    groups = n // members
    model = w_out.shape[2]
    side = 1 << ((n.bit_length() - 1) // 2)
    side = min(side, heads)
    planes = n // side
    planes_of_seq = heads // side
    pair_groups = [[g * members + m for m in range(members)] for g in range(groups)]
    cross_groups = [[g * members + m for g in range(groups)] for m in range(members)]
    plane_groups = [[p * side + m for m in range(side)] for p in range(planes)]
    column_groups = [[p * side + m for p in range(planes)] for m in range(side)]

    query_slots = queries.reshape(local_rows, n, width).transpose(1, 0, 2)
    q = lax.all_to_all(query_slots, "head", split_axis=0, concat_axis=0, tiled=True)
    q = q.reshape(n * local_rows, width)

    kv_slots = new_kv.reshape(local_rows, groups, 2 * width).transpose(1, 0, 2)
    kv = lax.all_to_all(
        kv_slots, "head", split_axis=0, concat_axis=0, tiled=True, axis_index_groups=cross_groups
    )
    kv = lax.all_gather(kv, "head", axis=0, axis_index_groups=pair_groups)
    pages = lax.all_gather(cache, "head", axis=0, tiled=True, axis_index_groups=pair_groups)

    share = w_out.shape[1]
    w_planes = w_out.reshape(planes_of_seq, side, share, model)
    if planes > planes_of_seq:
        w_planes = jnp.tile(w_planes, (planes // planes_of_seq, 1, 1, 1))
    w = lax.all_to_all(
        w_planes, "head", split_axis=0, concat_axis=0, tiled=True, axis_index_groups=column_groups
    )
    w = lax.all_gather(w, "head", axis=0, axis_index_groups=plane_groups)
    if share % 16:
        w = w.transpose(2, 1, 0, 3, 4).reshape(1, 1, side, width, model)
        w = w.reshape(side, width, model)

    attended = attend(q, pages.reshape(-1, 2 * width), kv)
    a = attended.reshape(planes, side, local_rows, width).transpose(1, 0, 2, 3)
    a = a.reshape(side, planes * local_rows, width)
    a = lax.all_to_all(
        a, "head", split_axis=0, concat_axis=0, tiled=True, axis_index_groups=plane_groups
    )
    if share % 16:
        partial = jnp.einsum("hri,hid->rd", a, w, preferred_element_type=F32).astype(BF16)
    else:
        partial = project(a, w)
    parts = lax.all_to_all(
        partial.reshape(planes, local_rows, model),
        "head",
        split_axis=0,
        concat_axis=0,
        tiled=True,
        axis_index_groups=column_groups,
    )
    return parts.reshape(seqs, planes_of_seq, local_rows, model)


def local(queries, new_kv, cache, resid, w_out, norm_gain, expert_ids, expert_gates, w_in, w_down):
    n = lax.axis_size("head")
    local_rows, seqs, heads, width = queries.shape
    model = resid.shape[2]
    rows = local_rows * seqs
    members = heads // new_kv.shape[2]
    in_pairs = (
        lax.axis_size("grp") == 2
        and seqs == 1
        and new_kv.shape[2] == 2
        and n == heads == 2 * members
        and members == 8
        and cache.shape[0] == 1
        and w_out.shape[1] % 16 == 0
    )
    plan = parts_in_pairs if in_pairs else parts_in_planes
    parts = plan(queries, new_kv, cache, w_out)

    top = expert_ids.shape[2]
    experts = w_in.shape[0] * n
    capacity = max(2, 2 * rows * top // experts)
    ids = expert_ids.transpose(1, 0, 2).reshape(rows, top)
    gates = expert_gates.transpose(1, 0, 2).reshape(rows, top)
    onehot = (ids[:, :, None] == jnp.arange(experts, dtype=jnp.int32)).astype(jnp.int32)
    named = onehot.sum(1)
    before = jnp.cumsum(named, 0) - named
    slots_of = ids * capacity + jnp.sum(onehot * before[:, None, :], 2)
    slots = experts * capacity

    stream, outgoing = route(
        parts, resid.transpose(1, 0, 2), norm_gain[None, :], slots_of.T, slots
    )
    arrived = lax.all_to_all(
        outgoing.reshape(n, slots // n, model), "head", split_axis=0, concat_axis=0, tiled=True
    )
    local_experts = w_in.shape[0]
    if local_experts == 1:
        answered = expert(arrived.reshape(slots, model), w_in[0], w_down[0])
        answered = answered.reshape(n, slots // n, model)
    else:
        arrived = arrived.reshape(n, local_experts, capacity, model).transpose(1, 0, 2, 3)
        arrived = arrived.reshape(local_experts, n * capacity, model)
        answered = jnp.stack([expert(arrived[e], w_in[e], w_down[e]) for e in range(local_experts)])
        answered = answered.reshape(local_experts, n, capacity, model).transpose(1, 0, 2, 3)
        answered = answered.reshape(n, slots // n, model)
    back = lax.all_to_all(answered, "head", split_axis=0, concat_axis=0, tiled=True)
    out = combine(back.reshape(slots, model), stream, slots_of, gates, seqs)
    return out.transpose(1, 0, 2)


def solution(mesh):
    return jax.shard_map(
        local,
        mesh=mesh,
        in_specs=(
            P("head", "grp", None, None),
            P("head", "grp", None, None),
            P(("grp", "head"), None, None),
            P("head", "grp", None),
            P(None, "head", None),
            P(),
            P("head", "grp", None),
            P("head", "grp", None),
            P("head", None, None),
            P("head", None, None),
        ),
        out_specs=P("head", "grp", None),
        check_vma=False,
    )
```

```python
import functools

import jax
import jax.numpy as jnp
from jax import lax
from jax.experimental import pallas as pl
from jax.experimental.pallas import tpu as pltpu
from jax.sharding import PartitionSpec as P

eps_norm = 1e-06
F32 = jnp.float32
BF16 = jnp.bfloat16
HIGH_VMEM = 48 * 2**20


def in_hbm():
    return pl.BlockSpec(memory_space=pltpu.HBM)


def in_vmem():
    return pl.BlockSpec(memory_space=pltpu.VMEM)


def attend_kernel(
    block, chunk, width, q_hbm, cache_hbm, kv_hbm, o_ref, q_ref, cache_ref, kv_ref, s0, s1, sems
):
    members, groups, piece, _ = kv_hbm.shape
    length = members * groups * piece
    old = cache_hbm.shape[0]
    scale = width**-0.5
    in_q = pltpu.make_async_copy(q_hbm, q_ref, sems.at[0])
    in_cache = pltpu.make_async_copy(cache_hbm, cache_ref, sems.at[1])
    in_q.start()
    in_cache.start()
    in_kv = []
    for group in range(groups):
        for member in range(members):
            place = (group * members + member) * piece
            copy = pltpu.make_async_copy(
                kv_hbm.at[member, group], kv_ref.at[pl.ds(place, piece)], sems.at[2]
            )
            copy.start()
            in_kv.append(copy)
    in_q.wait()
    in_cache.wait()
    for copy in in_kv:
        copy.wait()
    scores = [s0, s1]

    def pieces(b):
        out = [(True, k, chunk, k) for k in range(0, old, chunk)]
        last = b * block
        for k in range(0, last, chunk):
            out.append((False, k, min(chunk, last - k), old + k))
        out.append((False, last, block, old + last))
        return out

    def make_scores(b, part, running):
        of_cache, first, count, column = part
        keys = (cache_ref if of_cache else kv_ref)[pl.ds(first, count), :width]
        s = lax.dot_general(
            q_ref[pl.ds(b * block, block), :],
            keys,
            (((1,), (1,)), ((), ())),
            preferred_element_type=F32,
        )
        if not of_cache and first == b * block:
            row = lax.broadcasted_iota(jnp.int32, s.shape, 0)
            col = lax.broadcasted_iota(jnp.int32, s.shape, 1)
            s = jnp.where(col <= row, s, -jnp.inf)
        scores[b % 2][:, pl.ds(column, count)] = s
        for k in range(0, count, 128):
            piece_max = s[:, k : k + 128]
            running = piece_max if running is None else jnp.maximum(running, piece_max)
        return running

    def use_scores(b, part, top, total, acc):
        of_cache, first, count, column = part
        values = (cache_ref if of_cache else kv_ref)[pl.ds(first, count), width:]
        e = jnp.exp((scores[b % 2][:, pl.ds(column, count)] - top) * scale)
        for k in range(0, count, 128):
            total = e[:, k : k + 128] if total is None else total + e[:, k : k + 128]
        product = jnp.dot(e.astype(BF16), values, preferred_element_type=F32)
        return total, product if acc is None else acc + product

    blocks = length // block
    running = None
    for part in pieces(0):
        running = make_scores(0, part, running)
    for b in range(blocks):
        top = jnp.max(running, 1, keepdims=True)
        now, later = pieces(b), pieces(b + 1) if b + 1 < blocks else []
        running, total, acc = None, None, None
        for k in range(max(len(now), len(later))):
            if k < len(now):
                total, acc = use_scores(b, now[k], top, total, acc)
            if k < len(later):
                running = make_scores(b + 1, later[k], running)
        o_ref[pl.ds(b * block, block), :] = (acc / jnp.sum(total, 1, keepdims=True)).astype(BF16)


def attend(q, cache, kv):
    length, width = q.shape
    old = cache.shape[0]
    block = min(256, length)
    chunk = min(512, old)
    return pl.pallas_call(
        functools.partial(attend_kernel, block, chunk, width),
        out_shape=jax.ShapeDtypeStruct((length, width), BF16),
        in_specs=[in_hbm()] * 3,
        out_specs=in_vmem(),
        scratch_shapes=[
            pltpu.VMEM((length, width), BF16),
            pltpu.VMEM((old, 2 * width), BF16),
            pltpu.VMEM((length, 2 * width), BF16),
            pltpu.VMEM((block, old + length), F32),
            pltpu.VMEM((block, old + length), F32),
            pltpu.SemaphoreType.DMA((3,)),
        ],
        compiler_params=pltpu.CompilerParams(vmem_limit_bytes=HIGH_VMEM),
        cost_estimate=pl.CostEstimate(
            flops=4 * length * (old + length // 2) * width,
            bytes_accessed=4 * (2 * length + 2 * old) * width,
            transcendentals=length * (old + length // 2),
        ),
        name="attend",
    )(q, cache, kv)


def attend_pair_kernel(
    block,
    chunk,
    width,
    q_hbm,
    page_a,
    page_b,
    page_y,
    page_c,
    page_cy,
    kv_own,
    kv_y,
    kv_c,
    kv_cy,
    o_ref,
    q_ref,
    old_ref,
    kv_ref,
    s0,
    s1,
    sems,
):
    me = lax.axis_index("head")
    members, heads, piece, _ = q_hbm.shape
    length = members * piece
    planes = kv_own.shape[0]
    old = old_ref.shape[0]
    earlier_group = me // members > 0
    core = lax.rem(me, 2)
    copies = []

    def bring(source, target, sem):
        copy = pltpu.make_async_copy(source, target, sems.at[sem])
        copy.start()
        copies.append(copy)

    for member in range(members):
        for head in range(heads):
            bring(q_hbm.at[member, head], q_ref.at[head, pl.ds(member * piece, piece)], 0)
    place = 0
    for page in (page_a, page_b, page_y, page_c, page_cy):
        count = page.shape[0]
        bring(page, old_ref.at[pl.ds(place, count)], 1)
        place += count
    for flip, pieces_of in ((0, kv_own), (2, kv_y), (1, kv_c), (3, kv_cy)):
        for t in range(planes):
            number = jnp.bitwise_and(
                jnp.bitwise_xor(me, flip ^ (t * (members // 2))), members - 1
            )
            start = pl.multiple_of(number * piece, piece)
            area = 0 if t * (members // 2) >= members else length
            bring(pieces_of.at[t], kv_ref.at[pl.ds(area + start, piece)], 2)
    for copy in copies:
        copy.wait()
    scale = width**-0.5
    scores = [s0, s1]
    blocks = length // block
    units = [(head, b) for head in range(heads) for b in range(blocks)]

    def pieces(unit):
        _, b = units[unit]
        out = [("old", k, chunk, k) for k in range(0, old, chunk)]
        out += [("past", k, chunk, old + k) for k in range(0, length, chunk)]
        last = b * block
        for k in range(0, last, chunk):
            out.append(("new", length + k, min(chunk, last - k), old + length + k))
        out.append(("edge", length + last, block, old + length + last))
        return out

    def make_scores(unit, part, running):
        kind, first, count, column = part
        head, b = units[unit]
        keys = (old_ref if kind == "old" else kv_ref)[pl.ds(first, count), :width]
        s = lax.dot_general(
            q_ref[head, pl.ds(b * block, block), :],
            keys,
            (((1,), (1,)), ((), ())),
            preferred_element_type=F32,
        )
        if kind == "past":
            s = jnp.where(earlier_group, s, -jnp.inf)
        if kind == "edge":
            row = lax.broadcasted_iota(jnp.int32, s.shape, 0)
            col = lax.broadcasted_iota(jnp.int32, s.shape, 1)
            s = jnp.where(col <= row, s, -jnp.inf)
        scores[unit % 2][:, pl.ds(column, count)] = s
        for k in range(0, count, 128):
            piece_max = s[:, k : k + 128]
            running = piece_max if running is None else jnp.maximum(running, piece_max)
        return running

    def use_scores(unit, part, top, total, acc):
        kind, first, count, column = part
        values = (old_ref if kind == "old" else kv_ref)[pl.ds(first, count), width:]
        e = jnp.exp((scores[unit % 2][:, pl.ds(column, count)] - top) * scale)
        for k in range(0, count, 128):
            total = e[:, k : k + 128] if total is None else total + e[:, k : k + 128]
        product = jnp.dot(e.astype(BF16), values, preferred_element_type=F32)
        return total, product if acc is None else acc + product

    running = None
    for part in pieces(0):
        running = make_scores(0, part, running)
    for unit, (head, b) in enumerate(units):
        top = jnp.max(running, 1, keepdims=True)
        now = pieces(unit)
        later = pieces(unit + 1) if unit + 1 < len(units) else []
        running, total, acc = None, None, None
        for k in range(max(len(now), len(later))):
            if k < len(now):
                total, acc = use_scores(unit, now[k], top, total, acc)
            if k < len(later):
                running = make_scores(unit + 1, later[k], running)
        done = (acc / jnp.sum(total, 1, keepdims=True)).astype(BF16)
        for k in range(0, block, piece):
            member = (b * block + k) // piece
            side = jnp.bitwise_xor(core, member % 2)
            o_ref[side, pl.ds((member // 2) * piece, piece), pl.ds(head * width, width)] = done[
                k : k + piece
            ]


def attend_pair(q, pages, kvs):
    members, heads, piece, width = q.shape
    length = members * piece
    old = sum(page.shape[0] for page in pages)
    block = 2 * piece
    chunk = min(512, old, length)
    keys = old + 2 * length
    return pl.pallas_call(
        functools.partial(attend_pair_kernel, block, chunk, width),
        out_shape=jax.ShapeDtypeStruct((2, length // 2, heads * width), BF16),
        in_specs=[in_hbm()] * (1 + len(pages) + len(kvs)),
        out_specs=in_vmem(),
        scratch_shapes=[
            pltpu.VMEM((heads, length, width), BF16),
            pltpu.VMEM((old, 2 * width), BF16),
            pltpu.VMEM((2 * length, 2 * width), BF16),
            pltpu.VMEM((block, keys), F32),
            pltpu.VMEM((block, keys), F32),
            pltpu.SemaphoreType.DMA((3,)),
        ],
        compiler_params=pltpu.CompilerParams(vmem_limit_bytes=HIGH_VMEM),
        cost_estimate=pl.CostEstimate(
            flops=4 * heads * length * (keys - length // 2) * width,
            bytes_accessed=4 * (heads * length + keys) * width,
            transcendentals=heads * length * (keys - length // 2),
        ),
        name="attend",
    )(q, *pages, *kvs)


def project_pair_kernel(a_ref, got_ref, w_own, w_c, w_x, w_cx, o_ref, w_ref, sems):
    me = lax.axis_index("head")
    half = lax.axis_index("grp")
    core = lax.rem(me, 2)
    planes, sides, heads, share, columns = w_own.shape
    width = w_ref.shape[1]
    copies = []
    for flip, x, pieces_of in ((0, 0, w_own), (1, 0, w_c), (0, 1, w_x), (1, 1, w_cx)):
        column = pl.multiple_of(jnp.bitwise_xor(half, x) * columns, columns)
        for t in range(planes):
            for u in range(sides):
                number = jnp.bitwise_xor(me, flip ^ (2 * u) ^ (4 * t))
                row = pl.multiple_of(number * share, share)
                copy = pltpu.make_async_copy(
                    pieces_of.at[t, u],
                    w_ref.at[:, pl.ds(row, share), pl.ds(column, columns)],
                    sems.at[0],
                )
                copy.start()
                copies.append(copy)
    for copy in copies:
        copy.wait()
    acc = None
    for k in range(heads):
        mine = k < heads // 2
        column = (k % (heads // 2)) * width
        a = a_ref[0, :, pl.ds(column, width)] if mine else got_ref[:, pl.ds(column, width)]
        head = jnp.bitwise_xor(core, 0 if mine else 1) * (heads // 2) + k % (heads // 2)
        part = jnp.dot(a, w_ref[head], preferred_element_type=F32)
        acc = part if acc is None else acc + part
    o_ref[...] = acc.astype(BF16)


def project_pair(a, got, w_own, w_c, w_x, w_cx):
    planes, sides, heads, share, columns = w_own.shape
    rows = got.shape[0]
    width = 2 * got.shape[1] // heads
    model = 2 * columns
    return pl.pallas_call(
        project_pair_kernel,
        out_shape=jax.ShapeDtypeStruct((rows, model), BF16),
        in_specs=[in_vmem(), in_vmem()] + [in_hbm()] * 4,
        out_specs=in_vmem(),
        scratch_shapes=[
            pltpu.VMEM((heads, width, model), BF16),
            pltpu.SemaphoreType.DMA((1,)),
        ],
        compiler_params=pltpu.CompilerParams(vmem_limit_bytes=HIGH_VMEM),
        cost_estimate=pl.CostEstimate(
            flops=2 * heads * rows * width * model,
            bytes_accessed=2 * (heads * width * model + heads * rows * width + rows * model),
            transcendentals=0,
        ),
        name="project",
    )(a, got, w_own, w_c, w_x, w_cx)


def project_kernel(a_ref, w_ref, o_ref):
    members = a_ref.shape[0]
    planes, share = w_ref.shape[1], w_ref.shape[3]
    acc = None
    for head in range(members):
        w = jnp.concatenate(
            [w_ref[m, p, head] for p in range(planes) for m in range(members)], 0
        )
        part = jnp.dot(a_ref[head], w, preferred_element_type=F32)
        acc = part if acc is None else acc + part
    o_ref[...] = acc.astype(BF16)


def project(a, w):
    members, rows, width = a.shape
    planes, share, model = w.shape[1], w.shape[3], w.shape[4]
    tile = min(512, model)
    return pl.pallas_call(
        project_kernel,
        grid=(model // tile,),
        out_shape=jax.ShapeDtypeStruct((rows, model), BF16),
        in_specs=[
            pl.BlockSpec((members, rows, width), lambda t: (0, 0, 0)),
            pl.BlockSpec((members, planes, members, share, tile), lambda t: (0, 0, 0, 0, t)),
        ],
        out_specs=pl.BlockSpec((rows, tile), lambda t: (0, t)),
        compiler_params=pltpu.CompilerParams(vmem_limit_bytes=HIGH_VMEM),
        cost_estimate=pl.CostEstimate(
            flops=2 * members * rows * width * model,
            bytes_accessed=2 * (members * width * model + members * rows * width + rows * model),
            transcendentals=0,
        ),
        name="project",
    )(a, w)


def route_kernel(parts_ref, resid_ref, gain_ref, slots_ref, stream_ref, out_ref):
    seqs, planes = parts_ref.shape[0], parts_ref.shape[1]
    streams = []
    for seq in range(seqs):
        stream = resid_ref[seq].astype(F32)
        projected = parts_ref[seq, 0].astype(F32)
        for p in range(1, planes):
            projected = projected + parts_ref[seq, p].astype(F32)
        streams.append(stream + projected)
    stream = jnp.concatenate(streams, 0) if seqs > 1 else streams[0]
    stream_ref[...] = stream
    normed = stream * lax.rsqrt(jnp.mean(stream * stream, 1, keepdims=True) + eps_norm)
    normed = (normed * gain_ref[...]).astype(BF16)
    slots, rows = out_ref.shape[0], stream.shape[0]
    place = lax.broadcasted_iota(jnp.int32, (slots, rows), 0)
    hit = place == slots_ref[0:1, :]
    for k in range(1, slots_ref.shape[0]):
        hit = hit | (place == slots_ref[k : k + 1, :])
    out_ref[...] = jnp.dot(hit.astype(BF16), normed, preferred_element_type=F32).astype(BF16)


def route(parts, resid, gain, slots_of, slots):
    seqs, planes, local_rows, model = parts.shape
    rows = seqs * local_rows
    return pl.pallas_call(
        route_kernel,
        out_shape=(
            jax.ShapeDtypeStruct((rows, model), F32),
            jax.ShapeDtypeStruct((slots, model), BF16),
        ),
        in_specs=[in_vmem()] * 4,
        out_specs=(in_vmem(), in_vmem()),
        compiler_params=pltpu.CompilerParams(vmem_limit_bytes=HIGH_VMEM),
        cost_estimate=pl.CostEstimate(
            flops=2 * slots * rows * model,
            bytes_accessed=2 * (planes + 3 + slots // rows) * rows * model,
            transcendentals=0,
        ),
        name="route",
    )(parts, resid, gain, slots_of)


def expert_kernel(x_ref, w_in_ref, w_down_ref, o_ref):
    hidden_width = w_down_ref.shape[0]
    inner = jnp.dot(x_ref[...], w_in_ref[...], preferred_element_type=F32)
    gate = inner[:, :hidden_width]
    hidden = (gate / (1.0 + jnp.exp(-gate)) * inner[:, hidden_width:]).astype(BF16)
    o_ref[...] = jnp.dot(hidden, w_down_ref[...], preferred_element_type=F32).astype(BF16)


def expert(x, w_in, w_down):
    rows, model = x.shape
    hidden_width = w_down.shape[0]
    return pl.pallas_call(
        expert_kernel,
        out_shape=jax.ShapeDtypeStruct((rows, model), BF16),
        in_specs=[in_vmem()] * 3,
        out_specs=in_vmem(),
        compiler_params=pltpu.CompilerParams(vmem_limit_bytes=HIGH_VMEM),
        cost_estimate=pl.CostEstimate(
            flops=6 * rows * model * hidden_width,
            bytes_accessed=2 * (2 * rows * model + 3 * model * hidden_width),
            transcendentals=rows * hidden_width,
        ),
        name="expert",
    )(x, w_in, w_down)


def combine_kernel(seqs, back_ref, stream_ref, slots_ref, gates_ref, o_ref):
    slots = back_ref.shape[0]
    rows = stream_ref.shape[0]
    place = lax.broadcasted_iota(jnp.int32, (rows, slots), 1)
    total = stream_ref[...]
    gathered = None
    for k in range(slots_ref.shape[1]):
        pick = (place == slots_ref[:, k : k + 1]).astype(BF16)
        picked = jnp.dot(pick, back_ref[...], preferred_element_type=F32)
        part = picked * gates_ref[:, k : k + 1]
        gathered = part if gathered is None else gathered + part
    out = (total + gathered).astype(BF16)
    local_rows = rows // seqs
    for seq in range(seqs):
        o_ref[seq] = out[seq * local_rows : (seq + 1) * local_rows]


def combine(back, stream, slots_of, gates, seqs):
    slots, model = back.shape
    rows = stream.shape[0]
    top = slots_of.shape[1]
    return pl.pallas_call(
        functools.partial(combine_kernel, seqs),
        out_shape=jax.ShapeDtypeStruct((seqs, rows // seqs, model), BF16),
        in_specs=[in_vmem()] * 4,
        out_specs=in_vmem(),
        compiler_params=pltpu.CompilerParams(vmem_limit_bytes=HIGH_VMEM),
        cost_estimate=pl.CostEstimate(
            flops=2 * top * slots * rows * model,
            bytes_accessed=2 * slots * model + 6 * rows * model,
            transcendentals=0,
        ),
        name="combine",
    )(back, stream, slots_of, gates)


def flipped(value, axis, mask):
    pairs = [(source, source ^ mask) for source in range(lax.axis_size(axis))]
    return lax.ppermute(value, axis, pairs)


def parts_in_pairs(queries, new_kv, cache, w_out):
    n = lax.axis_size("head")
    local_rows, _, heads, width = queries.shape
    pair_heads = new_kv.shape[2]
    members = heads // pair_heads
    model = w_out.shape[2]
    share = w_out.shape[1]
    me = lax.axis_index("head")
    plane_bit = members // 2
    planes = n // plane_bit
    b = (me // plane_bit) % 2
    y = (me // 2) % 2
    group_sets = [[g * members + m for m in range(members)] for g in range(n // members)]

    query_slots = queries.reshape(local_rows, heads, width).transpose(1, 0, 2)
    query_slots = query_slots.reshape(members, heads // members, local_rows, width)
    q = lax.all_to_all(
        query_slots, "head", split_axis=0, concat_axis=0, tiled=True, axis_index_groups=group_sets
    )

    def page_target(source, other):
        p, plane, rest = source // members, (source // plane_bit) % 2, source % plane_bit
        return (plane ^ other) * members + p * plane_bit + rest

    page_a, page_b = (
        lax.ppermute(cache[0], "head", [(d, page_target(d, other)) for d in range(n)])
        for other in range(2)
    )
    kv_heads = new_kv.reshape(local_rows, pair_heads, 2 * width).transpose(1, 0, 2)
    kv_same = lax.dynamic_index_in_dim(kv_heads, b, 0, keepdims=False)
    kv_other = lax.dynamic_index_in_dim(kv_heads, 1 - b, 0, keepdims=False)
    kv_own = [kv_same]
    for t in range(1, planes):
        kv_own.append(flipped(kv_other if t % 2 else kv_same, "head", t * plane_bit))

    columns = model // 2
    w = lax.dynamic_slice_in_dim(w_out, lax.axis_index("grp") * columns, columns, 2)
    w = w.reshape(2, 2, heads // 4, share, columns)
    w_keep = lax.dynamic_index_in_dim(w, y, 1, keepdims=False)
    w_give = lax.dynamic_index_in_dim(w, 1 - y, 1, keepdims=False)
    w_got = flipped(w_give, "head", 2)

    (page_a, page_b, kv_own, q), w_got = lax.optimization_barrier(
        ((page_a, page_b, kv_own, q), w_got)
    )
    own_pages = jnp.concatenate([page_a, page_b], 0)
    kv_own = jnp.stack(kv_own, 0)
    pages_y = flipped(own_pages, "head", 2)
    kv_y = flipped(kv_own, "head", 2)
    w_both = jnp.stack([w_keep, w_got], 1)
    w_same = lax.dynamic_index_in_dim(w_both, b, 0, keepdims=False)
    w_other = lax.dynamic_index_in_dim(w_both, 1 - b, 0, keepdims=False)
    w_own = [w_same]
    for t in range(1, planes):
        w_own.append(flipped(w_other if t % 2 else w_same, "head", t * plane_bit))
    pages_c = flipped(own_pages, "head", 1)
    kv_c = flipped(kv_own, "head", 1)
    (pages_y, kv_y), w_own = lax.optimization_barrier(((pages_y, kv_y), w_own))
    pages_cy = flipped(pages_y, "head", 1)
    kv_cy = flipped(kv_y, "head", 1)
    w_own = jnp.stack(w_own, 0)
    q, w_own = lax.optimization_barrier((q, w_own))
    w_x = flipped(w_own, "grp", 1)
    w_c = flipped(w_own, "head", 1)
    a = attend_pair(
        q, (page_a, page_b, pages_y, pages_c, pages_cy), (kv_own, kv_y, kv_c, kv_cy)
    )
    a, w_x, w_c = lax.optimization_barrier((a, w_x, w_c))
    w_cx = flipped(w_x, "head", 1)
    got = flipped(a[1], "head", 1)
    partial = project_pair(a, got, w_own, w_c, w_x, w_cx)
    quads = [
        [g * members + 2 * k + core for k in range(members // 2)]
        for g in range(n // members)
        for core in range(2)
    ]
    parts = lax.all_to_all(
        partial.reshape(members // 2, local_rows, model),
        "head",
        split_axis=0,
        concat_axis=0,
        tiled=True,
        axis_index_groups=quads,
    )
    return parts[None]


def parts_in_planes(queries, new_kv, cache, w_out):
    n = lax.axis_size("head")
    local_rows, seqs, heads, width = queries.shape
    pair_heads = new_kv.shape[2]
    members = heads // pair_heads
    groups = n // members
    model = w_out.shape[2]
    side = 1 << ((n.bit_length() - 1) // 2)
    side = min(side, heads)
    planes = n // side
    planes_of_seq = heads // side
    pair_groups = [[g * members + m for m in range(members)] for g in range(groups)]
    cross_groups = [[g * members + m for g in range(groups)] for m in range(members)]
    plane_groups = [[p * side + m for m in range(side)] for p in range(planes)]
    column_groups = [[p * side + m for p in range(planes)] for m in range(side)]

    query_slots = queries.reshape(local_rows, n, width).transpose(1, 0, 2)
    q = lax.all_to_all(query_slots, "head", split_axis=0, concat_axis=0, tiled=True)
    q = q.reshape(n * local_rows, width)

    kv_slots = new_kv.reshape(local_rows, groups, 2 * width).transpose(1, 0, 2)
    kv = lax.all_to_all(
        kv_slots, "head", split_axis=0, concat_axis=0, tiled=True, axis_index_groups=cross_groups
    )
    kv = lax.all_gather(kv, "head", axis=0, axis_index_groups=pair_groups)
    pages = lax.all_gather(cache, "head", axis=0, tiled=True, axis_index_groups=pair_groups)

    share = w_out.shape[1]
    w_planes = w_out.reshape(planes_of_seq, side, share, model)
    if planes > planes_of_seq:
        w_planes = jnp.tile(w_planes, (planes // planes_of_seq, 1, 1, 1))
    w = lax.all_to_all(
        w_planes, "head", split_axis=0, concat_axis=0, tiled=True, axis_index_groups=column_groups
    )
    w = lax.all_gather(w, "head", axis=0, axis_index_groups=plane_groups)
    if share % 16:
        w = w.transpose(2, 1, 0, 3, 4).reshape(1, 1, side, width, model)
        w = w.reshape(side, width, model)

    attended = attend(q, pages.reshape(-1, 2 * width), kv)
    a = attended.reshape(planes, side, local_rows, width).transpose(1, 0, 2, 3)
    a = a.reshape(side, planes * local_rows, width)
    a = lax.all_to_all(
        a, "head", split_axis=0, concat_axis=0, tiled=True, axis_index_groups=plane_groups
    )
    if share % 16:
        partial = jnp.einsum("hri,hid->rd", a, w, preferred_element_type=F32).astype(BF16)
    else:
        partial = project(a, w)
    parts = lax.all_to_all(
        partial.reshape(planes, local_rows, model),
        "head",
        split_axis=0,
        concat_axis=0,
        tiled=True,
        axis_index_groups=column_groups,
    )
    return parts.reshape(seqs, planes_of_seq, local_rows, model)


def local(queries, new_kv, cache, resid, w_out, norm_gain, expert_ids, expert_gates, w_in, w_down):
    n = lax.axis_size("head")
    local_rows, seqs, heads, width = queries.shape
    model = resid.shape[2]
    rows = local_rows * seqs
    members = heads // new_kv.shape[2]
    in_pairs = (
        lax.axis_size("grp") == 2
        and seqs == 1
        and new_kv.shape[2] == 2
        and n == heads == 2 * members
        and members == 8
        and cache.shape[0] == 1
        and w_out.shape[1] % 16 == 0
    )
    plan = parts_in_pairs if in_pairs else parts_in_planes
    parts = plan(queries, new_kv, cache, w_out)

    top = expert_ids.shape[2]
    experts = w_in.shape[0] * n
    capacity = max(2, 2 * rows * top // experts)
    ids = expert_ids.transpose(1, 0, 2).reshape(rows, top)
    gates = expert_gates.transpose(1, 0, 2).reshape(rows, top)
    onehot = (ids[:, :, None] == jnp.arange(experts, dtype=jnp.int32)).astype(jnp.int32)
    named = onehot.sum(1)
    before = jnp.cumsum(named, 0) - named
    slots_of = ids * capacity + jnp.sum(onehot * before[:, None, :], 2)
    slots = experts * capacity

    stream, outgoing = route(
        parts, resid.transpose(1, 0, 2), norm_gain[None, :], slots_of.T, slots
    )
    arrived = lax.all_to_all(
        outgoing.reshape(n, slots // n, model), "head", split_axis=0, concat_axis=0, tiled=True
    )
    local_experts = w_in.shape[0]
    if local_experts == 1:
        answered = expert(arrived.reshape(slots, model), w_in[0], w_down[0])
        answered = answered.reshape(n, slots // n, model)
    else:
        arrived = arrived.reshape(n, local_experts, capacity, model).transpose(1, 0, 2, 3)
        arrived = arrived.reshape(local_experts, n * capacity, model)
        answered = jnp.stack([expert(arrived[e], w_in[e], w_down[e]) for e in range(local_experts)])
        answered = answered.reshape(local_experts, n, capacity, model).transpose(1, 0, 2, 3)
        answered = answered.reshape(n, slots // n, model)
    back = lax.all_to_all(answered, "head", split_axis=0, concat_axis=0, tiled=True)
    out = combine(back.reshape(slots, model), stream, slots_of, gates, seqs)
    return out.transpose(1, 0, 2)


def solution(mesh):
    return jax.shard_map(
        local,
        mesh=mesh,
        in_specs=(
            P("head", "grp", None, None),
            P("head", "grp", None, None),
            P(("grp", "head"), None, None),
            P("head", "grp", None),
            P(None, "head", None),
            P(),
            P("head", "grp", None),
            P("head", "grp", None),
            P("head", None, None),
            P("head", None, None),
        ),
        out_specs=P("head", "grp", None),
        check_vma=False,
    )
```

```python
import functools

import jax
import jax.numpy as jnp
from jax import lax
from jax.experimental import pallas as pl
from jax.experimental.pallas import tpu as pltpu
from jax.sharding import PartitionSpec as P

eps_norm = 1e-06
F32 = jnp.float32
BF16 = jnp.bfloat16
HIGH_VMEM = 48 * 2**20


def in_hbm():
    return pl.BlockSpec(memory_space=pltpu.HBM)


def in_vmem():
    return pl.BlockSpec(memory_space=pltpu.VMEM)


def attend_kernel(
    block, chunk, width, q_hbm, cache_hbm, kv_hbm, o_ref, q_ref, cache_ref, kv_ref, s0, s1, sems
):
    members, groups, piece, _ = kv_hbm.shape
    length = members * groups * piece
    old = cache_hbm.shape[0]
    scale = width**-0.5
    in_q = pltpu.make_async_copy(q_hbm, q_ref, sems.at[0])
    in_cache = pltpu.make_async_copy(cache_hbm, cache_ref, sems.at[1])
    in_q.start()
    in_cache.start()
    in_kv = []
    for group in range(groups):
        for member in range(members):
            place = (group * members + member) * piece
            copy = pltpu.make_async_copy(
                kv_hbm.at[member, group], kv_ref.at[pl.ds(place, piece)], sems.at[2]
            )
            copy.start()
            in_kv.append(copy)
    in_q.wait()
    in_cache.wait()
    for copy in in_kv:
        copy.wait()
    scores = [s0, s1]

    def pieces(b):
        out = [(True, k, chunk, k) for k in range(0, old, chunk)]
        last = b * block
        for k in range(0, last, chunk):
            out.append((False, k, min(chunk, last - k), old + k))
        out.append((False, last, block, old + last))
        return out

    def make_scores(b, part, running):
        of_cache, first, count, column = part
        keys = (cache_ref if of_cache else kv_ref)[pl.ds(first, count), :width]
        s = lax.dot_general(
            q_ref[pl.ds(b * block, block), :],
            keys,
            (((1,), (1,)), ((), ())),
            preferred_element_type=F32,
        )
        if not of_cache and first == b * block:
            row = lax.broadcasted_iota(jnp.int32, s.shape, 0)
            col = lax.broadcasted_iota(jnp.int32, s.shape, 1)
            s = jnp.where(col <= row, s, -jnp.inf)
        scores[b % 2][:, pl.ds(column, count)] = s
        for k in range(0, count, 128):
            piece_max = s[:, k : k + 128]
            running = piece_max if running is None else jnp.maximum(running, piece_max)
        return running

    def use_scores(b, part, top, total, acc):
        of_cache, first, count, column = part
        values = (cache_ref if of_cache else kv_ref)[pl.ds(first, count), width:]
        e = jnp.exp((scores[b % 2][:, pl.ds(column, count)] - top) * scale)
        for k in range(0, count, 128):
            total = e[:, k : k + 128] if total is None else total + e[:, k : k + 128]
        product = jnp.dot(e.astype(BF16), values, preferred_element_type=F32)
        return total, product if acc is None else acc + product

    blocks = length // block
    running = None
    for part in pieces(0):
        running = make_scores(0, part, running)
    for b in range(blocks):
        top = jnp.max(running, 1, keepdims=True)
        now, later = pieces(b), pieces(b + 1) if b + 1 < blocks else []
        running, total, acc = None, None, None
        for k in range(max(len(now), len(later))):
            if k < len(now):
                total, acc = use_scores(b, now[k], top, total, acc)
            if k < len(later):
                running = make_scores(b + 1, later[k], running)
        o_ref[pl.ds(b * block, block), :] = (acc / jnp.sum(total, 1, keepdims=True)).astype(BF16)


def attend(q, cache, kv):
    length, width = q.shape
    old = cache.shape[0]
    block = min(256, length)
    chunk = min(512, old)
    return pl.pallas_call(
        functools.partial(attend_kernel, block, chunk, width),
        out_shape=jax.ShapeDtypeStruct((length, width), BF16),
        in_specs=[in_hbm()] * 3,
        out_specs=in_vmem(),
        scratch_shapes=[
            pltpu.VMEM((length, width), BF16),
            pltpu.VMEM((old, 2 * width), BF16),
            pltpu.VMEM((length, 2 * width), BF16),
            pltpu.VMEM((block, old + length), F32),
            pltpu.VMEM((block, old + length), F32),
            pltpu.SemaphoreType.DMA((3,)),
        ],
        compiler_params=pltpu.CompilerParams(vmem_limit_bytes=HIGH_VMEM),
        cost_estimate=pl.CostEstimate(
            flops=4 * length * (old + length // 2) * width,
            bytes_accessed=4 * (2 * length + 2 * old) * width,
            transcendentals=length * (old + length // 2),
        ),
        name="attend",
    )(q, cache, kv)


def attend_pair_kernel(
    block,
    chunk,
    width,
    q_hbm,
    page_a,
    page_b,
    page_y,
    page_c,
    page_cy,
    kv_own,
    kv_y,
    kv_c,
    kv_cy,
    o_ref,
    q_ref,
    old_ref,
    kv_ref,
    s0,
    s1,
    sems,
):
    me = lax.axis_index("head")
    members, heads, piece, _ = q_hbm.shape
    length = members * piece
    planes = kv_own.shape[0]
    old = old_ref.shape[0]
    earlier_group = me // members > 0
    core = lax.rem(me, 2)
    copies = []

    def bring(source, target, sem):
        copy = pltpu.make_async_copy(source, target, sems.at[sem])
        copy.start()
        copies.append(copy)

    for member in range(members):
        for head in range(heads):
            bring(q_hbm.at[member, head], q_ref.at[head, pl.ds(member * piece, piece)], 0)
    place = 0
    for page in (page_a, page_b, page_y, page_c, page_cy):
        count = page.shape[0]
        bring(page, old_ref.at[pl.ds(place, count)], 1)
        place += count
    for flip, pieces_of in ((0, kv_own), (2, kv_y), (1, kv_c), (3, kv_cy)):
        for t in range(planes):
            number = jnp.bitwise_and(
                jnp.bitwise_xor(me, flip ^ (t * (members // 2))), members - 1
            )
            start = pl.multiple_of(number * piece, piece)
            area = 0 if t * (members // 2) >= members else length
            bring(pieces_of.at[t], kv_ref.at[pl.ds(area + start, piece)], 2)
    for copy in copies:
        copy.wait()
    scale = width**-0.5
    scores = [s0, s1]
    blocks = length // block
    units = [(head, b) for head in range(heads) for b in range(blocks)]

    def pieces(unit):
        _, b = units[unit]
        out = [("old", k, chunk, k) for k in range(0, old, chunk)]
        out += [("past", k, chunk, old + k) for k in range(0, length, chunk)]
        last = b * block
        for k in range(0, last, chunk):
            out.append(("new", length + k, min(chunk, last - k), old + length + k))
        out.append(("edge", length + last, block, old + length + last))
        return out

    def make_scores(unit, part, running):
        kind, first, count, column = part
        head, b = units[unit]
        keys = (old_ref if kind == "old" else kv_ref)[pl.ds(first, count), :width]
        s = lax.dot_general(
            q_ref[head, pl.ds(b * block, block), :],
            keys,
            (((1,), (1,)), ((), ())),
            preferred_element_type=F32,
        )
        if kind == "past":
            s = jnp.where(earlier_group, s, -jnp.inf)
        if kind == "edge":
            row = lax.broadcasted_iota(jnp.int32, s.shape, 0)
            col = lax.broadcasted_iota(jnp.int32, s.shape, 1)
            s = jnp.where(col <= row, s, -jnp.inf)
        scores[unit % 2][:, pl.ds(column, count)] = s
        for k in range(0, count, 128):
            piece_max = s[:, k : k + 128]
            running = piece_max if running is None else jnp.maximum(running, piece_max)
        return running

    def use_scores(unit, part, top, total, acc):
        kind, first, count, column = part
        values = (old_ref if kind == "old" else kv_ref)[pl.ds(first, count), width:]
        e = jnp.exp((scores[unit % 2][:, pl.ds(column, count)] - top) * scale)
        for k in range(0, count, 128):
            total = e[:, k : k + 128] if total is None else total + e[:, k : k + 128]
        product = jnp.dot(e.astype(BF16), values, preferred_element_type=F32)
        return total, product if acc is None else acc + product

    running = None
    for part in pieces(0):
        running = make_scores(0, part, running)
    for unit, (head, b) in enumerate(units):
        top = jnp.max(running, 1, keepdims=True)
        now = pieces(unit)
        later = pieces(unit + 1) if unit + 1 < len(units) else []
        running, total, acc = None, None, None
        for k in range(max(len(now), len(later))):
            if k < len(now):
                total, acc = use_scores(unit, now[k], top, total, acc)
            if k < len(later):
                running = make_scores(unit + 1, later[k], running)
        done = (acc / jnp.sum(total, 1, keepdims=True)).astype(BF16)
        for k in range(0, block, piece):
            member = (b * block + k) // piece
            side = jnp.bitwise_xor(core, member % 2)
            o_ref[side, pl.ds((member // 2) * piece, piece), pl.ds(head * width, width)] = done[
                k : k + piece
            ]


def attend_pair(q, pages, kvs):
    members, heads, piece, width = q.shape
    length = members * piece
    old = sum(page.shape[0] for page in pages)
    block = 2 * piece
    chunk = min(512, old, length)
    keys = old + 2 * length
    return pl.pallas_call(
        functools.partial(attend_pair_kernel, block, chunk, width),
        out_shape=jax.ShapeDtypeStruct((2, length // 2, heads * width), BF16),
        in_specs=[in_hbm()] * (1 + len(pages) + len(kvs)),
        out_specs=in_vmem(),
        scratch_shapes=[
            pltpu.VMEM((heads, length, width), BF16),
            pltpu.VMEM((old, 2 * width), BF16),
            pltpu.VMEM((2 * length, 2 * width), BF16),
            pltpu.VMEM((block, keys), F32),
            pltpu.VMEM((block, keys), F32),
            pltpu.SemaphoreType.DMA((3,)),
        ],
        compiler_params=pltpu.CompilerParams(vmem_limit_bytes=HIGH_VMEM),
        cost_estimate=pl.CostEstimate(
            flops=4 * heads * length * (keys - length // 2) * width,
            bytes_accessed=4 * (heads * length + keys) * width,
            transcendentals=heads * length * (keys - length // 2),
        ),
        name="attend",
    )(q, *pages, *kvs)


def project_pair_kernel(a_ref, got_ref, *refs):
    near, far, (o_ref, w_ref, sems) = refs[:4], refs[4:8], refs[8:]
    me = lax.axis_index("head")
    half = lax.axis_index("grp")
    core = lax.rem(me, 2)
    steps, sides, heads, share, columns = near[0].shape
    width = w_ref.shape[1]
    copies = []
    for first, given in ((0, near), (steps, far)):
        for flip, x, pieces_of in zip((0, 1, 0, 1), (0, 0, 1, 1), given):
            column = pl.multiple_of(jnp.bitwise_xor(half, x) * columns, columns)
            for t in range(steps):
                for u in range(sides):
                    number = jnp.bitwise_xor(me, flip ^ (2 * u) ^ (4 * (first + t)))
                    row = pl.multiple_of(number * share, share)
                    copy = pltpu.make_async_copy(
                        pieces_of.at[t, u],
                        w_ref.at[:, pl.ds(row, share), pl.ds(column, columns)],
                        sems.at[0],
                    )
                    copy.start()
                    copies.append(copy)
    for copy in copies:
        copy.wait()
    acc = None
    for k in range(heads):
        mine = k < heads // 2
        column = (k % (heads // 2)) * width
        a = a_ref[0, :, pl.ds(column, width)] if mine else got_ref[:, pl.ds(column, width)]
        head = jnp.bitwise_xor(core, 0 if mine else 1) * (heads // 2) + k % (heads // 2)
        part = jnp.dot(a, w_ref[head], preferred_element_type=F32)
        acc = part if acc is None else acc + part
    o_ref[...] = acc.astype(BF16)


def project_pair(a, got, near, far):
    _, _, heads, share, columns = near[0].shape
    rows = got.shape[0]
    width = 2 * got.shape[1] // heads
    model = 2 * columns
    return pl.pallas_call(
        project_pair_kernel,
        out_shape=jax.ShapeDtypeStruct((rows, model), BF16),
        in_specs=[in_vmem(), in_vmem()] + [in_hbm()] * 8,
        out_specs=in_vmem(),
        scratch_shapes=[
            pltpu.VMEM((heads, width, model), BF16),
            pltpu.SemaphoreType.DMA((1,)),
        ],
        compiler_params=pltpu.CompilerParams(vmem_limit_bytes=HIGH_VMEM),
        cost_estimate=pl.CostEstimate(
            flops=2 * heads * rows * width * model,
            bytes_accessed=2 * (heads * width * model + heads * rows * width + rows * model),
            transcendentals=0,
        ),
        name="project",
    )(a, got, *near, *far)


def project_kernel(a_ref, w_ref, o_ref):
    members = a_ref.shape[0]
    planes, share = w_ref.shape[1], w_ref.shape[3]
    acc = None
    for head in range(members):
        w = jnp.concatenate(
            [w_ref[m, p, head] for p in range(planes) for m in range(members)], 0
        )
        part = jnp.dot(a_ref[head], w, preferred_element_type=F32)
        acc = part if acc is None else acc + part
    o_ref[...] = acc.astype(BF16)


def project(a, w):
    members, rows, width = a.shape
    planes, share, model = w.shape[1], w.shape[3], w.shape[4]
    tile = min(512, model)
    return pl.pallas_call(
        project_kernel,
        grid=(model // tile,),
        out_shape=jax.ShapeDtypeStruct((rows, model), BF16),
        in_specs=[
            pl.BlockSpec((members, rows, width), lambda t: (0, 0, 0)),
            pl.BlockSpec((members, planes, members, share, tile), lambda t: (0, 0, 0, 0, t)),
        ],
        out_specs=pl.BlockSpec((rows, tile), lambda t: (0, t)),
        compiler_params=pltpu.CompilerParams(vmem_limit_bytes=HIGH_VMEM),
        cost_estimate=pl.CostEstimate(
            flops=2 * members * rows * width * model,
            bytes_accessed=2 * (members * width * model + members * rows * width + rows * model),
            transcendentals=0,
        ),
        name="project",
    )(a, w)


def route_kernel(parts_ref, resid_ref, gain_ref, slots_ref, stream_ref, out_ref):
    seqs, planes = parts_ref.shape[0], parts_ref.shape[1]
    streams = []
    for seq in range(seqs):
        stream = resid_ref[seq].astype(F32)
        projected = parts_ref[seq, 0].astype(F32)
        for p in range(1, planes):
            projected = projected + parts_ref[seq, p].astype(F32)
        streams.append(stream + projected)
    stream = jnp.concatenate(streams, 0) if seqs > 1 else streams[0]
    stream_ref[...] = stream
    normed = stream * lax.rsqrt(jnp.mean(stream * stream, 1, keepdims=True) + eps_norm)
    normed = (normed * gain_ref[...]).astype(BF16)
    slots, rows = out_ref.shape[0], stream.shape[0]
    place = lax.broadcasted_iota(jnp.int32, (slots, rows), 0)
    hit = place == slots_ref[0:1, :]
    for k in range(1, slots_ref.shape[0]):
        hit = hit | (place == slots_ref[k : k + 1, :])
    out_ref[...] = jnp.dot(hit.astype(BF16), normed, preferred_element_type=F32).astype(BF16)


def route(parts, resid, gain, slots_of, slots):
    seqs, planes, local_rows, model = parts.shape
    rows = seqs * local_rows
    return pl.pallas_call(
        route_kernel,
        out_shape=(
            jax.ShapeDtypeStruct((rows, model), F32),
            jax.ShapeDtypeStruct((slots, model), BF16),
        ),
        in_specs=[in_vmem()] * 4,
        out_specs=(in_vmem(), in_vmem()),
        compiler_params=pltpu.CompilerParams(vmem_limit_bytes=HIGH_VMEM),
        cost_estimate=pl.CostEstimate(
            flops=2 * slots * rows * model,
            bytes_accessed=2 * (planes + 3 + slots // rows) * rows * model,
            transcendentals=0,
        ),
        name="route",
    )(parts, resid, gain, slots_of)


def expert_kernel(x_ref, w_in_ref, w_down_ref, o_ref):
    hidden_width = w_down_ref.shape[0]
    inner = jnp.dot(x_ref[...], w_in_ref[...], preferred_element_type=F32)
    gate = inner[:, :hidden_width]
    hidden = (gate / (1.0 + jnp.exp(-gate)) * inner[:, hidden_width:]).astype(BF16)
    o_ref[...] = jnp.dot(hidden, w_down_ref[...], preferred_element_type=F32).astype(BF16)


def expert(x, w_in, w_down):
    rows, model = x.shape
    hidden_width = w_down.shape[0]
    return pl.pallas_call(
        expert_kernel,
        out_shape=jax.ShapeDtypeStruct((rows, model), BF16),
        in_specs=[in_vmem()] * 3,
        out_specs=in_vmem(),
        compiler_params=pltpu.CompilerParams(vmem_limit_bytes=HIGH_VMEM),
        cost_estimate=pl.CostEstimate(
            flops=6 * rows * model * hidden_width,
            bytes_accessed=2 * (2 * rows * model + 3 * model * hidden_width),
            transcendentals=rows * hidden_width,
        ),
        name="expert",
    )(x, w_in, w_down)


def combine_kernel(seqs, back_ref, stream_ref, slots_ref, gates_ref, o_ref):
    slots = back_ref.shape[0]
    rows = stream_ref.shape[0]
    place = lax.broadcasted_iota(jnp.int32, (rows, slots), 1)
    total = stream_ref[...]
    gathered = None
    for k in range(slots_ref.shape[1]):
        pick = (place == slots_ref[:, k : k + 1]).astype(BF16)
        picked = jnp.dot(pick, back_ref[...], preferred_element_type=F32)
        part = picked * gates_ref[:, k : k + 1]
        gathered = part if gathered is None else gathered + part
    out = (total + gathered).astype(BF16)
    local_rows = rows // seqs
    for seq in range(seqs):
        o_ref[seq] = out[seq * local_rows : (seq + 1) * local_rows]


def combine(back, stream, slots_of, gates, seqs):
    slots, model = back.shape
    rows = stream.shape[0]
    top = slots_of.shape[1]
    return pl.pallas_call(
        functools.partial(combine_kernel, seqs),
        out_shape=jax.ShapeDtypeStruct((seqs, rows // seqs, model), BF16),
        in_specs=[in_vmem()] * 4,
        out_specs=in_vmem(),
        compiler_params=pltpu.CompilerParams(vmem_limit_bytes=HIGH_VMEM),
        cost_estimate=pl.CostEstimate(
            flops=2 * top * slots * rows * model,
            bytes_accessed=2 * slots * model + 6 * rows * model,
            transcendentals=0,
        ),
        name="combine",
    )(back, stream, slots_of, gates)


def slot_matrix(slots_ref, slots, rows):
    place = lax.broadcasted_iota(jnp.int32, (slots, rows), 0).astype(F32)
    hit = place == slots_ref[0:1, :]
    for k in range(1, slots_ref.shape[0]):
        hit = hit | (place == slots_ref[k : k + 1, :])
    return hit.astype(BF16)


def route_pair_kernel(parts_ref, resid_ref, gain_ref, slots_ref, stream_ref, normed_ref, out_ref):
    projected = parts_ref[0].astype(F32)
    for p in range(1, parts_ref.shape[0]):
        projected = projected + parts_ref[p].astype(F32)
    stream = resid_ref[...].astype(F32) + projected
    stream_ref[...] = stream
    normed = stream * lax.rsqrt(jnp.mean(stream * stream, 1, keepdims=True) + eps_norm)
    normed = (normed * gain_ref[...]).astype(BF16)
    normed_ref[...] = normed
    matrix = slot_matrix(slots_ref, out_ref.shape[0], stream.shape[0])
    out_ref[...] = jnp.dot(matrix, normed, preferred_element_type=F32).astype(BF16)


def route_pair(parts, resid, gain, slots_of, slots):
    planes, rows, model = parts.shape
    return pl.pallas_call(
        route_pair_kernel,
        out_shape=(
            jax.ShapeDtypeStruct((rows, model), F32),
            jax.ShapeDtypeStruct((rows, model), BF16),
            jax.ShapeDtypeStruct((slots, model), BF16),
        ),
        in_specs=[in_vmem()] * 4,
        out_specs=(in_vmem(), in_vmem(), in_vmem()),
        compiler_params=pltpu.CompilerParams(vmem_limit_bytes=HIGH_VMEM),
        cost_estimate=pl.CostEstimate(
            flops=2 * slots * rows * model,
            bytes_accessed=2 * ((planes + 4) * rows + slots) * model,
            transcendentals=0,
        ),
        name="route",
    )(parts, resid, gain, slots_of)


def spread_kernel(rows_ref, slots_ref, out_ref):
    matrix = slot_matrix(slots_ref, out_ref.shape[0], rows_ref.shape[0])
    out_ref[...] = jnp.dot(matrix, rows_ref[...], preferred_element_type=F32).astype(BF16)


def spread(rows, slots_of, slots):
    count, model = rows.shape
    return pl.pallas_call(
        spread_kernel,
        out_shape=jax.ShapeDtypeStruct((slots, model), BF16),
        in_specs=[in_vmem()] * 2,
        out_specs=in_vmem(),
        compiler_params=pltpu.CompilerParams(vmem_limit_bytes=HIGH_VMEM),
        cost_estimate=pl.CostEstimate(
            flops=2 * slots * count * model,
            bytes_accessed=2 * (count + slots) * model,
            transcendentals=0,
        ),
        name="spread",
    )(rows, slots_of)


def gather_kernel(back_ref, slots_ref, gates_ref, *refs):
    o_ref = refs[-1]
    shape = (slots_ref.shape[0], back_ref.shape[0])
    place = lax.broadcasted_iota(jnp.int32, shape, 1).astype(F32)
    total = None
    for k in range(slots_ref.shape[1]):
        pick = (place == slots_ref[:, k : k + 1]).astype(BF16)
        picked = jnp.dot(pick, back_ref[...], preferred_element_type=F32)
        part = picked * gates_ref[:, k : k + 1]
        total = part if total is None else total + part
    if len(refs) > 1:
        total = refs[0][...] + (total + refs[1][...].astype(F32))
    o_ref[...] = total.astype(BF16)


def gather(back, slots_of, gates, stream, partial):
    slots, model = back.shape
    rows, top = slots_of.shape
    more = [] if stream is None else [stream, partial]
    return pl.pallas_call(
        gather_kernel,
        out_shape=jax.ShapeDtypeStruct((rows, model), BF16),
        in_specs=[in_vmem()] * (3 + len(more)),
        out_specs=in_vmem(),
        compiler_params=pltpu.CompilerParams(vmem_limit_bytes=HIGH_VMEM),
        cost_estimate=pl.CostEstimate(
            flops=2 * top * slots * rows * model,
            bytes_accessed=2 * (slots + 4 * rows) * model,
            transcendentals=0,
        ),
        name="gather",
    )(back, slots_of, gates, *more)


def flipped(value, axis, mask):
    pairs = [(source, source ^ mask) for source in range(lax.axis_size(axis))]
    return lax.ppermute(value, axis, pairs)


def parts_in_pairs(queries, new_kv, cache, w_out):
    n = lax.axis_size("head")
    local_rows, _, heads, width = queries.shape
    pair_heads = new_kv.shape[2]
    members = heads // pair_heads
    model = w_out.shape[2]
    share = w_out.shape[1]
    me = lax.axis_index("head")
    plane_bit = members // 2
    planes = n // plane_bit
    b = (me // plane_bit) % 2
    y = (me // 2) % 2
    group_sets = [[g * members + m for m in range(members)] for g in range(n // members)]

    query_slots = queries.reshape(local_rows, heads, width).transpose(1, 0, 2)
    query_slots = query_slots.reshape(members, heads // members, local_rows, width)
    q = lax.all_to_all(
        query_slots, "head", split_axis=0, concat_axis=0, tiled=True, axis_index_groups=group_sets
    )

    def page_target(source, other):
        p, plane, rest = source // members, (source // plane_bit) % 2, source % plane_bit
        return (plane ^ other) * members + p * plane_bit + rest

    page_a, page_b = (
        lax.ppermute(cache[0], "head", [(d, page_target(d, other)) for d in range(n)])
        for other in range(2)
    )
    kv_heads = new_kv.reshape(local_rows, pair_heads, 2 * width).transpose(1, 0, 2)
    kv_same = lax.dynamic_index_in_dim(kv_heads, b, 0, keepdims=False)
    kv_other = lax.dynamic_index_in_dim(kv_heads, 1 - b, 0, keepdims=False)
    kv_own = [kv_same]
    for t in range(1, planes):
        kv_own.append(flipped(kv_other if t % 2 else kv_same, "head", t * plane_bit))

    columns = model // 2
    w = lax.dynamic_slice_in_dim(w_out, lax.axis_index("grp") * columns, columns, 2)
    w = w.reshape(2, 2, heads // 4, share, columns)
    w_keep = lax.dynamic_index_in_dim(w, y, 1, keepdims=False)
    w_give = lax.dynamic_index_in_dim(w, 1 - y, 1, keepdims=False)

    (page_a, page_b), w_give = lax.optimization_barrier(((page_a, page_b), w_give))
    own_pages = jnp.concatenate([page_a, page_b], 0)
    pages_y = flipped(own_pages, "head", 2)
    w_got = flipped(w_give, "head", 2)
    kv_own, w_got = lax.optimization_barrier((kv_own, w_got))
    kv_own = jnp.stack(kv_own, 0)
    kv_y = flipped(kv_own, "head", 2)
    w_both = jnp.stack([w_keep, w_got], 1)
    w_same = lax.dynamic_index_in_dim(w_both, b, 0, keepdims=False)
    w_other = lax.dynamic_index_in_dim(w_both, 1 - b, 0, keepdims=False)
    w_far = [
        flipped(w_other if t % 2 else w_same, "head", t * plane_bit) for t in range(1, planes)
    ]
    w_near = jnp.stack([w_same, w_far[0]], 0)
    w_near_x = flipped(w_near, "grp", 1)
    pages_y, kv_y, w_far = lax.optimization_barrier((pages_y, kv_y, w_far[1:]))
    pages_c = flipped(own_pages, "head", 1)
    kv_c = flipped(kv_own, "head", 1)
    pages_cy = flipped(pages_y, "head", 1)
    kv_cy = flipped(kv_y, "head", 1)
    w_far = jnp.stack(w_far, 0)
    q, w_far = lax.optimization_barrier((q, w_far))
    w_far_x = flipped(w_far, "grp", 1)
    w_near_c = flipped(w_near, "head", 1)
    w_far_c = flipped(w_far, "head", 1)
    a = attend_pair(
        q, (page_a, page_b, pages_y, pages_c, pages_cy), (kv_own, kv_y, kv_c, kv_cy)
    )
    a, w_near_x, w_far_x, w_near_c, w_far_c = lax.optimization_barrier(
        (a, w_near_x, w_far_x, w_near_c, w_far_c)
    )
    w_near_cx = flipped(w_near_x, "head", 1)
    w_far_cx = flipped(w_far_x, "head", 1)
    got = flipped(a[1], "head", 1)
    partial = project_pair(
        a,
        got,
        (w_near, w_near_c, w_near_x, w_near_cx),
        (w_far, w_far_c, w_far_x, w_far_cx),
    )
    quads = [
        [g * members + 2 * k + core for k in range(members // 2)]
        for g in range(n // members)
        for core in range(2)
    ]
    parts = lax.all_to_all(
        partial.reshape(members // 2, local_rows, model),
        "head",
        split_axis=0,
        concat_axis=0,
        tiled=True,
        axis_index_groups=quads,
    )
    return parts[None]


def parts_in_planes(queries, new_kv, cache, w_out):
    n = lax.axis_size("head")
    local_rows, seqs, heads, width = queries.shape
    pair_heads = new_kv.shape[2]
    members = heads // pair_heads
    groups = n // members
    model = w_out.shape[2]
    side = 1 << ((n.bit_length() - 1) // 2)
    side = min(side, heads)
    planes = n // side
    planes_of_seq = heads // side
    pair_groups = [[g * members + m for m in range(members)] for g in range(groups)]
    cross_groups = [[g * members + m for g in range(groups)] for m in range(members)]
    plane_groups = [[p * side + m for m in range(side)] for p in range(planes)]
    column_groups = [[p * side + m for p in range(planes)] for m in range(side)]

    query_slots = queries.reshape(local_rows, n, width).transpose(1, 0, 2)
    q = lax.all_to_all(query_slots, "head", split_axis=0, concat_axis=0, tiled=True)
    q = q.reshape(n * local_rows, width)

    kv_slots = new_kv.reshape(local_rows, groups, 2 * width).transpose(1, 0, 2)
    kv = lax.all_to_all(
        kv_slots, "head", split_axis=0, concat_axis=0, tiled=True, axis_index_groups=cross_groups
    )
    kv = lax.all_gather(kv, "head", axis=0, axis_index_groups=pair_groups)
    pages = lax.all_gather(cache, "head", axis=0, tiled=True, axis_index_groups=pair_groups)

    share = w_out.shape[1]
    w_planes = w_out.reshape(planes_of_seq, side, share, model)
    if planes > planes_of_seq:
        w_planes = jnp.tile(w_planes, (planes // planes_of_seq, 1, 1, 1))
    w = lax.all_to_all(
        w_planes, "head", split_axis=0, concat_axis=0, tiled=True, axis_index_groups=column_groups
    )
    w = lax.all_gather(w, "head", axis=0, axis_index_groups=plane_groups)
    if share % 16:
        w = w.transpose(2, 1, 0, 3, 4).reshape(1, 1, side, width, model)
        w = w.reshape(side, width, model)

    attended = attend(q, pages.reshape(-1, 2 * width), kv)
    a = attended.reshape(planes, side, local_rows, width).transpose(1, 0, 2, 3)
    a = a.reshape(side, planes * local_rows, width)
    a = lax.all_to_all(
        a, "head", split_axis=0, concat_axis=0, tiled=True, axis_index_groups=plane_groups
    )
    if share % 16:
        partial = jnp.einsum("hri,hid->rd", a, w, preferred_element_type=F32).astype(BF16)
    else:
        partial = project(a, w)
    parts = lax.all_to_all(
        partial.reshape(planes, local_rows, model),
        "head",
        split_axis=0,
        concat_axis=0,
        tiled=True,
        axis_index_groups=column_groups,
    )
    return parts.reshape(seqs, planes_of_seq, local_rows, model)


def route_in_pairs(parts, resid, norm_gain, slots_of, gates, w_in, w_down, capacity, members):
    n = lax.axis_size("head")
    local_rows, seqs, model = resid.shape
    top = slots_of.shape[1]
    me = lax.axis_index("head")
    group_sets = [[g * members + m for m in range(members)] for g in range(n // members)]
    group_slots = members * capacity

    def around(value):
        value = value.reshape(members, capacity, model)
        value = lax.all_to_all(
            value, "head", split_axis=0, concat_axis=0, tiled=True, axis_index_groups=group_sets
        )
        return value.reshape(group_slots, model)

    own = jnp.concatenate([slots_of.astype(F32), gates], 1)
    other = flipped(own, "head", members)
    first = ((me // members) * group_slots).astype(F32)
    slots_own, gates_own = own[:, :top] - first, own[:, top:]
    slots_other, gates_other = other[:, :top] - first, other[:, top:]

    stream, normed, out_own = route_pair(
        parts, resid.reshape(local_rows, model), norm_gain[None, :], slots_own.T, group_slots
    )
    normed_other = flipped(normed, "head", members)
    answer_own = expert(around(out_own), w_in, w_down)
    out_other = spread(normed_other, slots_other.T, group_slots)
    answer_other = expert(around(out_other), w_in, w_down)
    partial = gather(around(answer_other), slots_other, gates_other, None, None)
    partial, answer_own = lax.optimization_barrier((partial, answer_own))
    partial = flipped(partial, "head", members)
    out = gather(around(answer_own), slots_own, gates_own, stream, partial)
    return out.reshape(local_rows, seqs, model)


def local(queries, new_kv, cache, resid, w_out, norm_gain, expert_ids, expert_gates, w_in, w_down):
    n = lax.axis_size("head")
    local_rows, seqs, heads, width = queries.shape
    model = resid.shape[2]
    rows = local_rows * seqs
    members = heads // new_kv.shape[2]
    in_pairs = (
        lax.axis_size("grp") == 2
        and seqs == 1
        and new_kv.shape[2] == 2
        and n == heads == 2 * members
        and members == 8
        and cache.shape[0] == 1
        and w_out.shape[1] % 16 == 0
    )
    plan = parts_in_pairs if in_pairs else parts_in_planes
    parts = plan(queries, new_kv, cache, w_out)

    top = expert_ids.shape[2]
    experts = w_in.shape[0] * n
    capacity = max(2, 2 * rows * top // experts)
    ids = expert_ids.transpose(1, 0, 2).reshape(rows, top)
    gates = expert_gates.transpose(1, 0, 2).reshape(rows, top)
    onehot = (ids[:, :, None] == jnp.arange(experts, dtype=jnp.int32)).astype(jnp.int32)
    named = onehot.sum(1)
    before = jnp.cumsum(named, 0) - named
    slots_of = ids * capacity + jnp.sum(onehot * before[:, None, :], 2)
    slots = experts * capacity
    if in_pairs and w_in.shape[0] == 1:
        return route_in_pairs(
            parts[0], resid, norm_gain, slots_of, gates, w_in[0], w_down[0], capacity, members
        )
    stream, outgoing = route(
        parts, resid.transpose(1, 0, 2), norm_gain[None, :], slots_of.T, slots
    )
    arrived = lax.all_to_all(
        outgoing.reshape(n, slots // n, model), "head", split_axis=0, concat_axis=0, tiled=True
    )
    local_experts = w_in.shape[0]
    if local_experts == 1:
        answered = expert(arrived.reshape(slots, model), w_in[0], w_down[0])
        answered = answered.reshape(n, slots // n, model)
    else:
        arrived = arrived.reshape(n, local_experts, capacity, model).transpose(1, 0, 2, 3)
        arrived = arrived.reshape(local_experts, n * capacity, model)
        answered = jnp.stack([expert(arrived[e], w_in[e], w_down[e]) for e in range(local_experts)])
        answered = answered.reshape(local_experts, n, capacity, model).transpose(1, 0, 2, 3)
        answered = answered.reshape(n, slots // n, model)
    back = lax.all_to_all(answered, "head", split_axis=0, concat_axis=0, tiled=True)
    out = combine(back.reshape(slots, model), stream, slots_of, gates, seqs)
    return out.transpose(1, 0, 2)


def solution(mesh):
    return jax.shard_map(
        local,
        mesh=mesh,
        in_specs=(
            P("head", "grp", None, None),
            P("head", "grp", None, None),
            P(("grp", "head"), None, None),
            P("head", "grp", None),
            P(None, "head", None),
            P(),
            P("head", "grp", None),
            P("head", "grp", None),
            P("head", None, None),
            P("head", None, None),
        ),
        out_specs=P("head", "grp", None),
        check_vma=False,
    )
```

```python
import functools

import jax
import jax.numpy as jnp
from jax import lax
from jax.experimental import pallas as pl
from jax.experimental.pallas import tpu as pltpu
from jax.sharding import PartitionSpec as P

eps_norm = 1e-06
F32 = jnp.float32
BF16 = jnp.bfloat16
HIGH_VMEM = 48 * 2**20
ATTEND_VMEM = 32 * 2**20


def in_hbm():
    return pl.BlockSpec(memory_space=pltpu.HBM)


def in_vmem():
    return pl.BlockSpec(memory_space=pltpu.VMEM)


def attend_kernel(
    block, chunk, width, q_hbm, cache_hbm, kv_hbm, o_ref, q_ref, cache_ref, kv_ref, s0, s1, sems
):
    members, groups, piece, _ = kv_hbm.shape
    length = members * groups * piece
    old = cache_hbm.shape[0]
    scale = width**-0.5
    in_q = pltpu.make_async_copy(q_hbm, q_ref, sems.at[0])
    in_cache = pltpu.make_async_copy(cache_hbm, cache_ref, sems.at[1])
    in_q.start()
    in_cache.start()
    in_kv = []
    for group in range(groups):
        for member in range(members):
            place = (group * members + member) * piece
            copy = pltpu.make_async_copy(
                kv_hbm.at[member, group], kv_ref.at[pl.ds(place, piece)], sems.at[2]
            )
            copy.start()
            in_kv.append(copy)
    in_q.wait()
    in_cache.wait()
    for copy in in_kv:
        copy.wait()
    scores = [s0, s1]

    def pieces(b):
        out = [(True, k, chunk, k) for k in range(0, old, chunk)]
        last = b * block
        for k in range(0, last, chunk):
            out.append((False, k, min(chunk, last - k), old + k))
        out.append((False, last, block, old + last))
        return out

    def make_scores(b, part, running):
        of_cache, first, count, column = part
        keys = (cache_ref if of_cache else kv_ref)[pl.ds(first, count), :width]
        s = lax.dot_general(
            q_ref[pl.ds(b * block, block), :],
            keys,
            (((1,), (1,)), ((), ())),
            preferred_element_type=F32,
        )
        if not of_cache and first == b * block:
            row = lax.broadcasted_iota(jnp.int32, s.shape, 0)
            col = lax.broadcasted_iota(jnp.int32, s.shape, 1)
            s = jnp.where(col <= row, s, -jnp.inf)
        scores[b % 2][:, pl.ds(column, count)] = s
        for k in range(0, count, 128):
            piece_max = s[:, k : k + 128]
            running = piece_max if running is None else jnp.maximum(running, piece_max)
        return running

    def use_scores(b, part, top, total, acc):
        of_cache, first, count, column = part
        values = (cache_ref if of_cache else kv_ref)[pl.ds(first, count), width:]
        e = jnp.exp((scores[b % 2][:, pl.ds(column, count)] - top) * scale)
        for k in range(0, count, 128):
            total = e[:, k : k + 128] if total is None else total + e[:, k : k + 128]
        product = jnp.dot(e.astype(BF16), values, preferred_element_type=F32)
        return total, product if acc is None else acc + product

    blocks = length // block
    running = None
    for part in pieces(0):
        running = make_scores(0, part, running)
    for b in range(blocks):
        top = jnp.max(running, 1, keepdims=True)
        now, later = pieces(b), pieces(b + 1) if b + 1 < blocks else []
        running, total, acc = None, None, None
        for k in range(max(len(now), len(later))):
            if k < len(now):
                total, acc = use_scores(b, now[k], top, total, acc)
            if k < len(later):
                running = make_scores(b + 1, later[k], running)
        o_ref[pl.ds(b * block, block), :] = (acc / jnp.sum(total, 1, keepdims=True)).astype(BF16)


def attend(q, cache, kv):
    length, width = q.shape
    old = cache.shape[0]
    block = min(256, length)
    chunk = min(512, old)
    return pl.pallas_call(
        functools.partial(attend_kernel, block, chunk, width),
        out_shape=jax.ShapeDtypeStruct((length, width), BF16),
        in_specs=[in_hbm()] * 3,
        out_specs=in_vmem(),
        scratch_shapes=[
            pltpu.VMEM((length, width), BF16),
            pltpu.VMEM((old, 2 * width), BF16),
            pltpu.VMEM((length, 2 * width), BF16),
            pltpu.VMEM((block, old + length), F32),
            pltpu.VMEM((block, old + length), F32),
            pltpu.SemaphoreType.DMA((3,)),
        ],
        compiler_params=pltpu.CompilerParams(vmem_limit_bytes=HIGH_VMEM),
        cost_estimate=pl.CostEstimate(
            flops=4 * length * (old + length // 2) * width,
            bytes_accessed=4 * (2 * length + 2 * old) * width,
            transcendentals=length * (old + length // 2),
        ),
        name="attend",
    )(q, cache, kv)


def attend_units(q_ref, units, pieces, arrays, scores, width, prior, finish):
    scale = width**-0.5

    def make_scores(unit, part, running):
        name, first, count, column, mask = part
        head, row, rows = units[unit]
        s = lax.dot_general(
            q_ref[head, pl.ds(row, rows), :],
            arrays[name][pl.ds(first, count), :width],
            (((1,), (1,)), ((), ())),
            preferred_element_type=F32,
        )
        if mask is not None:
            s = jnp.where(mask(s.shape), s, -jnp.inf)
        scores[unit % 2][:, pl.ds(column, count)] = s
        for k in range(0, count, 128):
            piece_max = s[:, k : k + 128]
            running = piece_max if running is None else jnp.maximum(running, piece_max)
        return running

    def use_scores(unit, part, top, total, acc):
        name, first, count, column, _ = part
        e = jnp.exp((scores[unit % 2][:, pl.ds(column, count)] - top) * scale)
        for k in range(0, count, 128):
            total = e[:, k : k + 128] if total is None else total + e[:, k : k + 128]
        values = arrays[name][pl.ds(first, count), width:]
        product = jnp.dot(e.astype(BF16), values, preferred_element_type=F32)
        return total, product if acc is None else acc + product

    running = None
    for part in pieces(0):
        running = make_scores(0, part, running)
    for unit in range(len(units)):
        top = jnp.max(running, 1, keepdims=True)
        before = prior(unit)
        if before is not None:
            top = jnp.maximum(top, before[0])
        now = pieces(unit)
        later = pieces(unit + 1) if unit + 1 < len(units) else []
        running, total, acc = None, None, None
        for k in range(max(len(now), len(later))):
            if k < len(now):
                total, acc = use_scores(unit, now[k], top, total, acc)
            if k < len(later):
                running = make_scores(unit + 1, later[k], running)
        if before is not None:
            shrink = jnp.exp((before[0] - top) * scale)
            total = total + before[1] * shrink
            acc = acc + before[2] * shrink
        finish(unit, top, total, acc)


def bring_queries(q_hbm, q_ref, sem):
    members, heads, piece, _ = q_hbm.shape
    copies = []
    for member in range(members):
        for head in range(heads):
            copies.append(
                pltpu.make_async_copy(
                    q_hbm.at[member, head], q_ref.at[head, pl.ds(member * piece, piece)], sem
                )
            )
    return copies


def attend_old_kernel(block, chunk, width, count, q_hbm, *refs):
    pages, (top_ref, total_ref, acc_ref, q_ref, old_ref, s0, s1, sems) = refs[:count], refs[count:]
    copies = bring_queries(q_hbm, q_ref, sems.at[0])
    place = 0
    for page in pages:
        copies.append(
            pltpu.make_async_copy(page, old_ref.at[pl.ds(place, page.shape[0])], sems.at[1])
        )
        place += page.shape[0]
    for copy in copies:
        copy.start()
    for copy in copies:
        copy.wait()
    heads, length, _ = q_ref.shape
    units = [(head, row, block) for head in range(heads) for row in range(0, length, block)]

    def pieces(unit):
        return [("old", k, chunk, k, None) for k in range(0, old_ref.shape[0], chunk)]

    def finish(unit, top, total, acc):
        head, row, rows = units[unit]
        top_ref[head, pl.ds(row, rows), :] = jnp.broadcast_to(top, total.shape)
        total_ref[head, pl.ds(row, rows), :] = total
        acc_ref[head, pl.ds(row, rows), :] = acc

    attend_units(
        q_ref, units, pieces, {"old": old_ref}, [s0, s1], width, lambda unit: None, finish
    )


def attend_old(q, pages):
    members, heads, piece, width = q.shape
    length = members * piece
    old = sum(page.shape[0] for page in pages)
    block = 2 * piece
    chunk = min(512, old)
    lanes = jax.ShapeDtypeStruct((heads, length, 128), F32)
    return pl.pallas_call(
        functools.partial(attend_old_kernel, block, chunk, width, len(pages)),
        out_shape=(lanes, lanes, jax.ShapeDtypeStruct((heads, length, width), F32)),
        in_specs=[in_hbm()] * (1 + len(pages)),
        out_specs=(in_vmem(),) * 3,
        scratch_shapes=[
            pltpu.VMEM((heads, length, width), BF16),
            pltpu.VMEM((old, 2 * width), BF16),
            pltpu.VMEM((block, old), F32),
            pltpu.VMEM((block, old), F32),
            pltpu.SemaphoreType.DMA((2,)),
        ],
        compiler_params=pltpu.CompilerParams(vmem_limit_bytes=ATTEND_VMEM),
        cost_estimate=pl.CostEstimate(
            flops=4 * heads * length * old * width,
            bytes_accessed=4 * (heads * length + old) * width,
            transcendentals=heads * length * old,
        ),
        name="attend_old",
    )(q, *pages)


def attend_new_kernel(
    block,
    chunk,
    width,
    q_hbm,
    kv_own,
    kv_y,
    kv_c,
    kv_cy,
    top_ref,
    total_ref,
    acc_ref,
    o_ref,
    q_ref,
    kv_ref,
    s0,
    s1,
    sems,
):
    me = lax.axis_index("head")
    members, heads, piece, _ = q_hbm.shape
    length = members * piece
    planes = kv_own.shape[0]
    earlier_group = me // members > 0
    core = lax.rem(me, 2)
    copies = bring_queries(q_hbm, q_ref, sems.at[0])
    for flip, pieces_of in ((0, kv_own), (2, kv_y), (1, kv_c), (3, kv_cy)):
        for t in range(planes):
            number = jnp.bitwise_and(
                jnp.bitwise_xor(me, flip ^ (t * (members // 2))), members - 1
            )
            start = pl.multiple_of(number * piece, piece)
            area = 0 if t * (members // 2) >= members else length
            copies.append(
                pltpu.make_async_copy(
                    pieces_of.at[t], kv_ref.at[pl.ds(area + start, piece)], sems.at[1]
                )
            )
    for copy in copies:
        copy.start()
    for copy in copies:
        copy.wait()
    units = [(head, row, block) for head in range(heads) for row in range(0, length, block)]

    def earlier(shape):
        return jnp.broadcast_to(earlier_group, shape)

    def causal(shape):
        row = lax.broadcasted_iota(jnp.int32, shape, 0)
        return lax.broadcasted_iota(jnp.int32, shape, 1) <= row

    def pieces(unit):
        _, row, rows = units[unit]
        out = [("new", k, chunk, k, earlier) for k in range(0, length, chunk)]
        for k in range(0, row, chunk):
            out.append(("new", length + k, min(chunk, row - k), length + k, None))
        return out + [("new", length + row, rows, length + row, causal)]

    def prior(unit):
        head, row, rows = units[unit]
        at = pl.ds(row, rows)
        return top_ref[head, at, :1], total_ref[head, at, :], acc_ref[head, at, :]

    def finish(unit, top, total, acc):
        head, row, rows = units[unit]
        done = (acc / jnp.sum(total, 1, keepdims=True)).astype(BF16)
        for k in range(0, rows, piece):
            member = (row + k) // piece
            side = jnp.bitwise_xor(core, member % 2)
            o_ref[side, pl.ds((member // 2) * piece, piece), pl.ds(head * width, width)] = done[
                k : k + piece
            ]

    attend_units(q_ref, units, pieces, {"new": kv_ref}, [s0, s1], width, prior, finish)


def attend_new(q, kvs, old):
    members, heads, piece, width = q.shape
    length = members * piece
    block = 2 * piece
    chunk = min(512, length)
    return pl.pallas_call(
        functools.partial(attend_new_kernel, block, chunk, width),
        out_shape=jax.ShapeDtypeStruct((2, length // 2, heads * width), BF16),
        in_specs=[in_hbm()] * (1 + len(kvs)) + [in_vmem()] * 3,
        out_specs=in_vmem(),
        scratch_shapes=[
            pltpu.VMEM((heads, length, width), BF16),
            pltpu.VMEM((2 * length, 2 * width), BF16),
            pltpu.VMEM((block, 2 * length), F32),
            pltpu.VMEM((block, 2 * length), F32),
            pltpu.SemaphoreType.DMA((2,)),
        ],
        compiler_params=pltpu.CompilerParams(vmem_limit_bytes=ATTEND_VMEM),
        cost_estimate=pl.CostEstimate(
            flops=6 * heads * length * length * width,
            bytes_accessed=4 * (2 * heads * length + 2 * length) * width,
            transcendentals=3 * heads * length * length // 2,
        ),
        name="attend_new",
    )(q, *kvs, *old)


def project_pair_kernel(a_ref, got_ref, *refs):
    near, far, (o_ref, w_ref, sems) = refs[:4], refs[4:8], refs[8:]
    me = lax.axis_index("head")
    half = lax.axis_index("grp")
    core = lax.rem(me, 2)
    steps, sides, heads, share, columns = near[0].shape
    width = w_ref.shape[1]
    copies = []
    for first, given in ((0, near), (steps, far)):
        for flip, x, pieces_of in zip((0, 1, 0, 1), (0, 0, 1, 1), given):
            column = pl.multiple_of(jnp.bitwise_xor(half, x) * columns, columns)
            for t in range(steps):
                for u in range(sides):
                    number = jnp.bitwise_xor(me, flip ^ (2 * u) ^ (4 * (first + t)))
                    row = pl.multiple_of(number * share, share)
                    copy = pltpu.make_async_copy(
                        pieces_of.at[t, u],
                        w_ref.at[:, pl.ds(row, share), pl.ds(column, columns)],
                        sems.at[0],
                    )
                    copy.start()
                    copies.append(copy)
    for copy in copies:
        copy.wait()
    acc = None
    for k in range(heads):
        mine = k < heads // 2
        column = (k % (heads // 2)) * width
        a = a_ref[0, :, pl.ds(column, width)] if mine else got_ref[:, pl.ds(column, width)]
        head = jnp.bitwise_xor(core, 0 if mine else 1) * (heads // 2) + k % (heads // 2)
        part = jnp.dot(a, w_ref[head], preferred_element_type=F32)
        acc = part if acc is None else acc + part
    o_ref[...] = acc.astype(BF16)


def project_pair(a, got, near, far):
    _, _, heads, share, columns = near[0].shape
    rows = got.shape[0]
    width = 2 * got.shape[1] // heads
    model = 2 * columns
    return pl.pallas_call(
        project_pair_kernel,
        out_shape=jax.ShapeDtypeStruct((rows, model), BF16),
        in_specs=[in_vmem(), in_vmem()] + [in_hbm()] * 8,
        out_specs=in_vmem(),
        scratch_shapes=[
            pltpu.VMEM((heads, width, model), BF16),
            pltpu.SemaphoreType.DMA((1,)),
        ],
        compiler_params=pltpu.CompilerParams(vmem_limit_bytes=HIGH_VMEM),
        cost_estimate=pl.CostEstimate(
            flops=2 * heads * rows * width * model,
            bytes_accessed=2 * (heads * width * model + heads * rows * width + rows * model),
            transcendentals=0,
        ),
        name="project",
    )(a, got, *near, *far)


def project_kernel(a_ref, w_ref, o_ref):
    members = a_ref.shape[0]
    planes, share = w_ref.shape[1], w_ref.shape[3]
    acc = None
    for head in range(members):
        w = jnp.concatenate(
            [w_ref[m, p, head] for p in range(planes) for m in range(members)], 0
        )
        part = jnp.dot(a_ref[head], w, preferred_element_type=F32)
        acc = part if acc is None else acc + part
    o_ref[...] = acc.astype(BF16)


def project(a, w):
    members, rows, width = a.shape
    planes, share, model = w.shape[1], w.shape[3], w.shape[4]
    tile = min(512, model)
    return pl.pallas_call(
        project_kernel,
        grid=(model // tile,),
        out_shape=jax.ShapeDtypeStruct((rows, model), BF16),
        in_specs=[
            pl.BlockSpec((members, rows, width), lambda t: (0, 0, 0)),
            pl.BlockSpec((members, planes, members, share, tile), lambda t: (0, 0, 0, 0, t)),
        ],
        out_specs=pl.BlockSpec((rows, tile), lambda t: (0, t)),
        compiler_params=pltpu.CompilerParams(vmem_limit_bytes=HIGH_VMEM),
        cost_estimate=pl.CostEstimate(
            flops=2 * members * rows * width * model,
            bytes_accessed=2 * (members * width * model + members * rows * width + rows * model),
            transcendentals=0,
        ),
        name="project",
    )(a, w)


def route_kernel(parts_ref, resid_ref, gain_ref, slots_ref, stream_ref, out_ref):
    seqs, planes = parts_ref.shape[0], parts_ref.shape[1]
    streams = []
    for seq in range(seqs):
        stream = resid_ref[seq].astype(F32)
        projected = parts_ref[seq, 0].astype(F32)
        for p in range(1, planes):
            projected = projected + parts_ref[seq, p].astype(F32)
        streams.append(stream + projected)
    stream = jnp.concatenate(streams, 0) if seqs > 1 else streams[0]
    stream_ref[...] = stream
    normed = stream * lax.rsqrt(jnp.mean(stream * stream, 1, keepdims=True) + eps_norm)
    normed = (normed * gain_ref[...]).astype(BF16)
    slots, rows = out_ref.shape[0], stream.shape[0]
    place = lax.broadcasted_iota(jnp.int32, (slots, rows), 0)
    hit = place == slots_ref[0:1, :]
    for k in range(1, slots_ref.shape[0]):
        hit = hit | (place == slots_ref[k : k + 1, :])
    out_ref[...] = jnp.dot(hit.astype(BF16), normed, preferred_element_type=F32).astype(BF16)


def route(parts, resid, gain, slots_of, slots):
    seqs, planes, local_rows, model = parts.shape
    rows = seqs * local_rows
    return pl.pallas_call(
        route_kernel,
        out_shape=(
            jax.ShapeDtypeStruct((rows, model), F32),
            jax.ShapeDtypeStruct((slots, model), BF16),
        ),
        in_specs=[in_vmem()] * 4,
        out_specs=(in_vmem(), in_vmem()),
        compiler_params=pltpu.CompilerParams(vmem_limit_bytes=HIGH_VMEM),
        cost_estimate=pl.CostEstimate(
            flops=2 * slots * rows * model,
            bytes_accessed=2 * (planes + 3 + slots // rows) * rows * model,
            transcendentals=0,
        ),
        name="route",
    )(parts, resid, gain, slots_of)


def expert_kernel(x_ref, w_in_ref, w_down_ref, o_ref):
    hidden_width = w_down_ref.shape[0]
    inner = jnp.dot(x_ref[...], w_in_ref[...], preferred_element_type=F32)
    gate = inner[:, :hidden_width]
    hidden = (gate / (1.0 + jnp.exp(-gate)) * inner[:, hidden_width:]).astype(BF16)
    o_ref[...] = jnp.dot(hidden, w_down_ref[...], preferred_element_type=F32).astype(BF16)


def expert(x, w_in, w_down):
    rows, model = x.shape
    hidden_width = w_down.shape[0]
    return pl.pallas_call(
        expert_kernel,
        out_shape=jax.ShapeDtypeStruct((rows, model), BF16),
        in_specs=[in_vmem()] * 3,
        out_specs=in_vmem(),
        compiler_params=pltpu.CompilerParams(vmem_limit_bytes=HIGH_VMEM),
        cost_estimate=pl.CostEstimate(
            flops=6 * rows * model * hidden_width,
            bytes_accessed=2 * (2 * rows * model + 3 * model * hidden_width),
            transcendentals=rows * hidden_width,
        ),
        name="expert",
    )(x, w_in, w_down)


def combine_kernel(seqs, back_ref, stream_ref, slots_ref, gates_ref, o_ref):
    slots = back_ref.shape[0]
    rows = stream_ref.shape[0]
    place = lax.broadcasted_iota(jnp.int32, (rows, slots), 1)
    total = stream_ref[...]
    gathered = None
    for k in range(slots_ref.shape[1]):
        pick = (place == slots_ref[:, k : k + 1]).astype(BF16)
        picked = jnp.dot(pick, back_ref[...], preferred_element_type=F32)
        part = picked * gates_ref[:, k : k + 1]
        gathered = part if gathered is None else gathered + part
    out = (total + gathered).astype(BF16)
    local_rows = rows // seqs
    for seq in range(seqs):
        o_ref[seq] = out[seq * local_rows : (seq + 1) * local_rows]


def combine(back, stream, slots_of, gates, seqs):
    slots, model = back.shape
    rows = stream.shape[0]
    top = slots_of.shape[1]
    return pl.pallas_call(
        functools.partial(combine_kernel, seqs),
        out_shape=jax.ShapeDtypeStruct((seqs, rows // seqs, model), BF16),
        in_specs=[in_vmem()] * 4,
        out_specs=in_vmem(),
        compiler_params=pltpu.CompilerParams(vmem_limit_bytes=HIGH_VMEM),
        cost_estimate=pl.CostEstimate(
            flops=2 * top * slots * rows * model,
            bytes_accessed=2 * slots * model + 6 * rows * model,
            transcendentals=0,
        ),
        name="combine",
    )(back, stream, slots_of, gates)


def slot_matrix(slots_ref, slots, rows):
    place = lax.broadcasted_iota(jnp.int32, (slots, rows), 0).astype(F32)
    hit = place == slots_ref[0:1, :]
    for k in range(1, slots_ref.shape[0]):
        hit = hit | (place == slots_ref[k : k + 1, :])
    return hit.astype(BF16)


def route_pair_kernel(parts_ref, resid_ref, gain_ref, slots_ref, stream_ref, normed_ref, out_ref):
    projected = parts_ref[0].astype(F32)
    for p in range(1, parts_ref.shape[0]):
        projected = projected + parts_ref[p].astype(F32)
    stream = resid_ref[...].astype(F32) + projected
    stream_ref[...] = stream
    normed = stream * lax.rsqrt(jnp.mean(stream * stream, 1, keepdims=True) + eps_norm)
    normed = (normed * gain_ref[...]).astype(BF16)
    normed_ref[...] = normed
    matrix = slot_matrix(slots_ref, out_ref.shape[0], stream.shape[0])
    out_ref[...] = jnp.dot(matrix, normed, preferred_element_type=F32).astype(BF16)


def route_pair(parts, resid, gain, slots_of, slots):
    planes, rows, model = parts.shape
    return pl.pallas_call(
        route_pair_kernel,
        out_shape=(
            jax.ShapeDtypeStruct((rows, model), F32),
            jax.ShapeDtypeStruct((rows, model), BF16),
            jax.ShapeDtypeStruct((slots, model), BF16),
        ),
        in_specs=[in_vmem()] * 4,
        out_specs=(in_vmem(), in_vmem(), in_vmem()),
        compiler_params=pltpu.CompilerParams(vmem_limit_bytes=HIGH_VMEM),
        cost_estimate=pl.CostEstimate(
            flops=2 * slots * rows * model,
            bytes_accessed=2 * ((planes + 4) * rows + slots) * model,
            transcendentals=0,
        ),
        name="route",
    )(parts, resid, gain, slots_of)


def spread_kernel(rows_ref, slots_ref, out_ref):
    matrix = slot_matrix(slots_ref, out_ref.shape[0], rows_ref.shape[0])
    out_ref[...] = jnp.dot(matrix, rows_ref[...], preferred_element_type=F32).astype(BF16)


def spread(rows, slots_of, slots):
    count, model = rows.shape
    return pl.pallas_call(
        spread_kernel,
        out_shape=jax.ShapeDtypeStruct((slots, model), BF16),
        in_specs=[in_vmem()] * 2,
        out_specs=in_vmem(),
        compiler_params=pltpu.CompilerParams(vmem_limit_bytes=HIGH_VMEM),
        cost_estimate=pl.CostEstimate(
            flops=2 * slots * count * model,
            bytes_accessed=2 * (count + slots) * model,
            transcendentals=0,
        ),
        name="spread",
    )(rows, slots_of)


def gather_kernel(back_ref, slots_ref, gates_ref, *refs):
    o_ref = refs[-1]
    shape = (slots_ref.shape[0], back_ref.shape[0])
    place = lax.broadcasted_iota(jnp.int32, shape, 1).astype(F32)
    total = None
    for k in range(slots_ref.shape[1]):
        pick = (place == slots_ref[:, k : k + 1]).astype(BF16)
        picked = jnp.dot(pick, back_ref[...], preferred_element_type=F32)
        part = picked * gates_ref[:, k : k + 1]
        total = part if total is None else total + part
    if len(refs) > 1:
        total = refs[0][...] + (total + refs[1][...].astype(F32))
    o_ref[...] = total.astype(BF16)


def gather(back, slots_of, gates, stream, partial):
    slots, model = back.shape
    rows, top = slots_of.shape
    more = [] if stream is None else [stream, partial]
    return pl.pallas_call(
        gather_kernel,
        out_shape=jax.ShapeDtypeStruct((rows, model), BF16),
        in_specs=[in_vmem()] * (3 + len(more)),
        out_specs=in_vmem(),
        compiler_params=pltpu.CompilerParams(vmem_limit_bytes=HIGH_VMEM),
        cost_estimate=pl.CostEstimate(
            flops=2 * top * slots * rows * model,
            bytes_accessed=2 * (slots + 4 * rows) * model,
            transcendentals=0,
        ),
        name="gather",
    )(back, slots_of, gates, *more)


def flipped(value, axis, mask):
    pairs = [(source, source ^ mask) for source in range(lax.axis_size(axis))]
    return lax.ppermute(value, axis, pairs)


def parts_in_pairs(queries, new_kv, cache, w_out):
    n = lax.axis_size("head")
    local_rows, _, heads, width = queries.shape
    pair_heads = new_kv.shape[2]
    members = heads // pair_heads
    model = w_out.shape[2]
    share = w_out.shape[1]
    me = lax.axis_index("head")
    plane_bit = members // 2
    planes = n // plane_bit
    b = (me // plane_bit) % 2
    y = (me // 2) % 2
    group_sets = [[g * members + m for m in range(members)] for g in range(n // members)]

    def page_target(source, other):
        p, plane, rest = source // members, (source // plane_bit) % 2, source % plane_bit
        return (plane ^ other) * members + p * plane_bit + rest

    page_a, page_b = (
        lax.ppermute(cache[0], "head", [(d, page_target(d, other)) for d in range(n)])
        for other in range(2)
    )

    columns = model // 2
    w = lax.dynamic_slice_in_dim(w_out, lax.axis_index("grp") * columns, columns, 2)
    w = w.reshape(2, 2, heads // 4, share, columns)
    w_keep = lax.dynamic_index_in_dim(w, y, 1, keepdims=False)
    w_give = lax.dynamic_index_in_dim(w, 1 - y, 1, keepdims=False)
    w_got = flipped(w_give, "head", 2)

    query_slots = queries.reshape(local_rows, heads, width).transpose(1, 0, 2)
    query_slots = query_slots.reshape(members, heads // members, local_rows, width)
    kv_heads = new_kv.reshape(local_rows, pair_heads, 2 * width).transpose(1, 0, 2)
    kv_same = lax.dynamic_index_in_dim(kv_heads, b, 0, keepdims=False)
    kv_other = lax.dynamic_index_in_dim(kv_heads, 1 - b, 0, keepdims=False)
    (page_a, page_b), kv_same, kv_other, query_slots = lax.optimization_barrier(
        ((page_a, page_b), kv_same, kv_other, query_slots)
    )
    page_ya = flipped(page_a, "head", 2)
    page_yb = flipped(page_b, "head", 2)
    kv_own = [kv_same]
    for t in range(1, planes):
        kv_own.append(flipped(kv_other if t % 2 else kv_same, "head", t * plane_bit))
    q = lax.all_to_all(
        query_slots, "head", split_axis=0, concat_axis=0, tiled=True, axis_index_groups=group_sets
    )

    page_c = flipped(jnp.concatenate([page_a, page_b], 0), "head", 1)
    kv_own, w_got = lax.optimization_barrier((kv_own, w_got))
    kv_own = jnp.stack(kv_own, 0)
    kv_y = flipped(kv_own, "head", 2)
    kv_c = flipped(kv_own, "head", 1)
    w_both = jnp.stack([w_keep, w_got], 1)
    w_same = lax.dynamic_index_in_dim(w_both, b, 0, keepdims=False)
    w_other = lax.dynamic_index_in_dim(w_both, 1 - b, 0, keepdims=False)
    w_far = [
        flipped(w_other if t % 2 else w_same, "head", t * plane_bit) for t in range(1, planes)
    ]
    w_near = jnp.stack([w_same, w_far[0]], 0)
    page_cya = flipped(page_ya, "head", 1)
    page_cyb = flipped(page_yb, "head", 1)
    q, w_near = lax.optimization_barrier((q, w_near))
    w_near_x = flipped(w_near, "grp", 1)
    old = attend_old(q, (page_a, page_b, page_ya, page_yb, page_c, page_cya, page_cyb))
    old, kv_y, kv_c, w_far = lax.optimization_barrier((old, kv_y, kv_c, w_far[1:]))
    kv_cy = flipped(kv_y, "head", 1)
    w_far = jnp.stack(w_far, 0)
    q, w_far = lax.optimization_barrier((q, w_far))
    w_far_x = flipped(w_far, "grp", 1)
    w_near_c = flipped(w_near, "head", 1)
    w_far_c = flipped(w_far, "head", 1)
    a = attend_new(q, (kv_own, kv_y, kv_c, kv_cy), old)
    a, w_near_x, w_far_x, w_near_c, w_far_c = lax.optimization_barrier(
        (a, w_near_x, w_far_x, w_near_c, w_far_c)
    )
    w_near_cx = flipped(w_near_x, "head", 1)
    w_far_cx = flipped(w_far_x, "head", 1)
    got = flipped(a[1], "head", 1)
    partial = project_pair(
        a,
        got,
        (w_near, w_near_c, w_near_x, w_near_cx),
        (w_far, w_far_c, w_far_x, w_far_cx),
    )
    quads = [
        [g * members + 2 * k + core for k in range(members // 2)]
        for g in range(n // members)
        for core in range(2)
    ]
    parts = lax.all_to_all(
        partial.reshape(members // 2, local_rows, model),
        "head",
        split_axis=0,
        concat_axis=0,
        tiled=True,
        axis_index_groups=quads,
    )
    return parts[None]


def parts_in_planes(queries, new_kv, cache, w_out):
    n = lax.axis_size("head")
    local_rows, seqs, heads, width = queries.shape
    pair_heads = new_kv.shape[2]
    members = heads // pair_heads
    groups = n // members
    model = w_out.shape[2]
    side = 1 << ((n.bit_length() - 1) // 2)
    side = min(side, heads)
    planes = n // side
    planes_of_seq = heads // side
    pair_groups = [[g * members + m for m in range(members)] for g in range(groups)]
    cross_groups = [[g * members + m for g in range(groups)] for m in range(members)]
    plane_groups = [[p * side + m for m in range(side)] for p in range(planes)]
    column_groups = [[p * side + m for p in range(planes)] for m in range(side)]

    query_slots = queries.reshape(local_rows, n, width).transpose(1, 0, 2)
    q = lax.all_to_all(query_slots, "head", split_axis=0, concat_axis=0, tiled=True)
    q = q.reshape(n * local_rows, width)

    kv_slots = new_kv.reshape(local_rows, groups, 2 * width).transpose(1, 0, 2)
    kv = lax.all_to_all(
        kv_slots, "head", split_axis=0, concat_axis=0, tiled=True, axis_index_groups=cross_groups
    )
    kv = lax.all_gather(kv, "head", axis=0, axis_index_groups=pair_groups)
    pages = lax.all_gather(cache, "head", axis=0, tiled=True, axis_index_groups=pair_groups)

    share = w_out.shape[1]
    w_planes = w_out.reshape(planes_of_seq, side, share, model)
    if planes > planes_of_seq:
        w_planes = jnp.tile(w_planes, (planes // planes_of_seq, 1, 1, 1))
    w = lax.all_to_all(
        w_planes, "head", split_axis=0, concat_axis=0, tiled=True, axis_index_groups=column_groups
    )
    w = lax.all_gather(w, "head", axis=0, axis_index_groups=plane_groups)
    if share % 16:
        w = w.transpose(2, 1, 0, 3, 4).reshape(1, 1, side, width, model)
        w = w.reshape(side, width, model)

    attended = attend(q, pages.reshape(-1, 2 * width), kv)
    a = attended.reshape(planes, side, local_rows, width).transpose(1, 0, 2, 3)
    a = a.reshape(side, planes * local_rows, width)
    a = lax.all_to_all(
        a, "head", split_axis=0, concat_axis=0, tiled=True, axis_index_groups=plane_groups
    )
    if share % 16:
        partial = jnp.einsum("hri,hid->rd", a, w, preferred_element_type=F32).astype(BF16)
    else:
        partial = project(a, w)
    parts = lax.all_to_all(
        partial.reshape(planes, local_rows, model),
        "head",
        split_axis=0,
        concat_axis=0,
        tiled=True,
        axis_index_groups=column_groups,
    )
    return parts.reshape(seqs, planes_of_seq, local_rows, model)


def route_in_pairs(parts, resid, norm_gain, slots_of, gates, w_in, w_down, capacity, members):
    n = lax.axis_size("head")
    local_rows, seqs, model = resid.shape
    top = slots_of.shape[1]
    me = lax.axis_index("head")
    group_sets = [[g * members + m for m in range(members)] for g in range(n // members)]
    group_slots = members * capacity

    def around(value):
        value = value.reshape(members, capacity, model)
        value = lax.all_to_all(
            value, "head", split_axis=0, concat_axis=0, tiled=True, axis_index_groups=group_sets
        )
        return value.reshape(group_slots, model)

    own = jnp.concatenate([slots_of.astype(F32), gates], 1)
    other = flipped(own, "head", members)
    first = ((me // members) * group_slots).astype(F32)
    slots_own, gates_own = own[:, :top] - first, own[:, top:]
    slots_other, gates_other = other[:, :top] - first, other[:, top:]

    stream, normed, out_own = route_pair(
        parts, resid.reshape(local_rows, model), norm_gain[None, :], slots_own.T, group_slots
    )
    normed_other = flipped(normed, "head", members)
    answer_own = expert(around(out_own), w_in, w_down)
    normed_other, answer_own = lax.optimization_barrier((normed_other, answer_own))
    out_other = spread(normed_other, slots_other.T, group_slots)
    answer_other = expert(around(out_other), w_in, w_down)
    partial = gather(around(answer_other), slots_other, gates_other, None, None)
    partial, answer_own = lax.optimization_barrier((partial, answer_own))
    partial = flipped(partial, "head", members)
    out = gather(around(answer_own), slots_own, gates_own, stream, partial)
    return out.reshape(local_rows, seqs, model)


def local(queries, new_kv, cache, resid, w_out, norm_gain, expert_ids, expert_gates, w_in, w_down):
    n = lax.axis_size("head")
    local_rows, seqs, heads, width = queries.shape
    model = resid.shape[2]
    rows = local_rows * seqs
    members = heads // new_kv.shape[2]
    in_pairs = (
        lax.axis_size("grp") == 2
        and seqs == 1
        and new_kv.shape[2] == 2
        and n == heads == 2 * members
        and members == 8
        and cache.shape[0] == 1
        and w_out.shape[1] % 16 == 0
    )
    plan = parts_in_pairs if in_pairs else parts_in_planes
    parts = plan(queries, new_kv, cache, w_out)

    top = expert_ids.shape[2]
    experts = w_in.shape[0] * n
    capacity = max(2, 2 * rows * top // experts)
    ids = expert_ids.transpose(1, 0, 2).reshape(rows, top)
    gates = expert_gates.transpose(1, 0, 2).reshape(rows, top)
    onehot = (ids[:, :, None] == jnp.arange(experts, dtype=jnp.int32)).astype(jnp.int32)
    named = onehot.sum(1)
    before = jnp.cumsum(named, 0) - named
    slots_of = ids * capacity + jnp.sum(onehot * before[:, None, :], 2)
    slots = experts * capacity
    if in_pairs and w_in.shape[0] == 1:
        return route_in_pairs(
            parts[0], resid, norm_gain, slots_of, gates, w_in[0], w_down[0], capacity, members
        )
    stream, outgoing = route(
        parts, resid.transpose(1, 0, 2), norm_gain[None, :], slots_of.T, slots
    )
    arrived = lax.all_to_all(
        outgoing.reshape(n, slots // n, model), "head", split_axis=0, concat_axis=0, tiled=True
    )
    local_experts = w_in.shape[0]
    if local_experts == 1:
        answered = expert(arrived.reshape(slots, model), w_in[0], w_down[0])
        answered = answered.reshape(n, slots // n, model)
    else:
        arrived = arrived.reshape(n, local_experts, capacity, model).transpose(1, 0, 2, 3)
        arrived = arrived.reshape(local_experts, n * capacity, model)
        answered = jnp.stack([expert(arrived[e], w_in[e], w_down[e]) for e in range(local_experts)])
        answered = answered.reshape(local_experts, n, capacity, model).transpose(1, 0, 2, 3)
        answered = answered.reshape(n, slots // n, model)
    back = lax.all_to_all(answered, "head", split_axis=0, concat_axis=0, tiled=True)
    out = combine(back.reshape(slots, model), stream, slots_of, gates, seqs)
    return out.transpose(1, 0, 2)


def solution(mesh):
    return jax.shard_map(
        local,
        mesh=mesh,
        in_specs=(
            P("head", "grp", None, None),
            P("head", "grp", None, None),
            P(("grp", "head"), None, None),
            P("head", "grp", None),
            P(None, "head", None),
            P(),
            P("head", "grp", None),
            P("head", "grp", None),
            P("head", None, None),
            P("head", None, None),
        ),
        out_specs=P("head", "grp", None),
        check_vma=False,
    )
```

```python
import functools

import jax
import jax.numpy as jnp
from jax import lax
from jax.experimental import pallas as pl
from jax.experimental.pallas import tpu as pltpu
from jax.sharding import PartitionSpec as P

eps_norm = 1e-06
F32 = jnp.float32
BF16 = jnp.bfloat16
HIGH_VMEM = 48 * 2**20
ATTEND_VMEM = 32 * 2**20


def in_hbm():
    return pl.BlockSpec(memory_space=pltpu.HBM)


def in_vmem():
    return pl.BlockSpec(memory_space=pltpu.VMEM)


def attend_kernel(
    block, chunk, width, q_hbm, cache_hbm, kv_hbm, o_ref, q_ref, cache_ref, kv_ref, s0, s1, sems
):
    members, groups, piece, _ = kv_hbm.shape
    length = members * groups * piece
    old = cache_hbm.shape[0]
    scale = width**-0.5
    in_q = pltpu.make_async_copy(q_hbm, q_ref, sems.at[0])
    in_cache = pltpu.make_async_copy(cache_hbm, cache_ref, sems.at[1])
    in_q.start()
    in_cache.start()
    in_kv = []
    for group in range(groups):
        for member in range(members):
            place = (group * members + member) * piece
            copy = pltpu.make_async_copy(
                kv_hbm.at[member, group], kv_ref.at[pl.ds(place, piece)], sems.at[2]
            )
            copy.start()
            in_kv.append(copy)
    in_q.wait()
    in_cache.wait()
    for copy in in_kv:
        copy.wait()
    scores = [s0, s1]

    def pieces(b):
        out = [(True, k, chunk, k) for k in range(0, old, chunk)]
        last = b * block
        for k in range(0, last, chunk):
            out.append((False, k, min(chunk, last - k), old + k))
        out.append((False, last, block, old + last))
        return out

    def make_scores(b, part, running):
        of_cache, first, count, column = part
        keys = (cache_ref if of_cache else kv_ref)[pl.ds(first, count), :width]
        s = lax.dot_general(
            q_ref[pl.ds(b * block, block), :],
            keys,
            (((1,), (1,)), ((), ())),
            preferred_element_type=F32,
        )
        if not of_cache and first == b * block:
            row = lax.broadcasted_iota(jnp.int32, s.shape, 0)
            col = lax.broadcasted_iota(jnp.int32, s.shape, 1)
            s = jnp.where(col <= row, s, -jnp.inf)
        scores[b % 2][:, pl.ds(column, count)] = s
        for k in range(0, count, 128):
            piece_max = s[:, k : k + 128]
            running = piece_max if running is None else jnp.maximum(running, piece_max)
        return running

    def use_scores(b, part, top, total, acc):
        of_cache, first, count, column = part
        values = (cache_ref if of_cache else kv_ref)[pl.ds(first, count), width:]
        e = jnp.exp((scores[b % 2][:, pl.ds(column, count)] - top) * scale)
        for k in range(0, count, 128):
            total = e[:, k : k + 128] if total is None else total + e[:, k : k + 128]
        product = jnp.dot(e.astype(BF16), values, preferred_element_type=F32)
        return total, product if acc is None else acc + product

    blocks = length // block
    running = None
    for part in pieces(0):
        running = make_scores(0, part, running)
    for b in range(blocks):
        top = jnp.max(running, 1, keepdims=True)
        now, later = pieces(b), pieces(b + 1) if b + 1 < blocks else []
        running, total, acc = None, None, None
        for k in range(max(len(now), len(later))):
            if k < len(now):
                total, acc = use_scores(b, now[k], top, total, acc)
            if k < len(later):
                running = make_scores(b + 1, later[k], running)
        o_ref[pl.ds(b * block, block), :] = (acc / jnp.sum(total, 1, keepdims=True)).astype(BF16)


def attend(q, cache, kv):
    length, width = q.shape
    old = cache.shape[0]
    block = min(256, length)
    chunk = min(512, old)
    return pl.pallas_call(
        functools.partial(attend_kernel, block, chunk, width),
        out_shape=jax.ShapeDtypeStruct((length, width), BF16),
        in_specs=[in_hbm()] * 3,
        out_specs=in_vmem(),
        scratch_shapes=[
            pltpu.VMEM((length, width), BF16),
            pltpu.VMEM((old, 2 * width), BF16),
            pltpu.VMEM((length, 2 * width), BF16),
            pltpu.VMEM((block, old + length), F32),
            pltpu.VMEM((block, old + length), F32),
            pltpu.SemaphoreType.DMA((3,)),
        ],
        compiler_params=pltpu.CompilerParams(vmem_limit_bytes=HIGH_VMEM),
        cost_estimate=pl.CostEstimate(
            flops=4 * length * (old + length // 2) * width,
            bytes_accessed=4 * (2 * length + 2 * old) * width,
            transcendentals=length * (old + length // 2),
        ),
        name="attend",
    )(q, cache, kv)


def attend_pair_kernel(
    block,
    chunk,
    width,
    q_hbm,
    own_pages,
    y_pages,
    c_pages,
    cy_pages,
    near,
    far,
    near_y,
    far_y,
    near_c,
    far_c,
    near_cy,
    far_cy,
    o_ref,
    q_ref,
    old_ref,
    kv_ref,
    s0,
    s1,
    sems,
):
    me = lax.axis_index("head")
    members, heads, piece, _ = q_hbm.shape
    length = members * piece
    steps = near.shape[0]
    old = old_ref.shape[0]
    earlier_group = me // members > 0
    core = lax.rem(me, 2)
    copies = []

    def bring(source, target, sem):
        copy = pltpu.make_async_copy(source, target, sems.at[sem])
        copy.start()
        copies.append(copy)

    for member in range(members):
        for head in range(heads):
            bring(q_hbm.at[member, head], q_ref.at[head, pl.ds(member * piece, piece)], 0)
    place = 0
    for page in (own_pages, y_pages, c_pages, cy_pages):
        count = page.shape[0]
        bring(page, old_ref.at[pl.ds(place, count)], 1)
        place += count
    for flip, group in (
        (0, (near, far)),
        (2, (near_y, far_y)),
        (1, (near_c, far_c)),
        (3, (near_cy, far_cy)),
    ):
        for other, pieces_of in enumerate(group):
            for t in range(steps):
                number = jnp.bitwise_and(
                    jnp.bitwise_xor(me, flip ^ (t * (members // 2))), members - 1
                )
                start = pl.multiple_of(number * piece, piece)
                area = 0 if other else length
                bring(pieces_of.at[t], kv_ref.at[pl.ds(area + start, piece)], 2)
    for copy in copies:
        copy.wait()
    scale = width**-0.5
    scores = [s0, s1]
    blocks = length // block
    units = [(head, b) for head in range(heads) for b in range(blocks)]

    def pieces(unit):
        _, b = units[unit]
        out = [("old", k, chunk, k) for k in range(0, old, chunk)]
        out += [("past", k, chunk, old + k) for k in range(0, length, chunk)]
        last = b * block
        for k in range(0, last, chunk):
            out.append(("new", length + k, min(chunk, last - k), old + length + k))
        out.append(("edge", length + last, block, old + length + last))
        return out

    def make_scores(unit, part, running):
        kind, first, count, column = part
        head, b = units[unit]
        keys = (old_ref if kind == "old" else kv_ref)[pl.ds(first, count), :width]
        s = lax.dot_general(
            q_ref[head, pl.ds(b * block, block), :],
            keys,
            (((1,), (1,)), ((), ())),
            preferred_element_type=F32,
        )
        if kind == "past":
            s = jnp.where(earlier_group, s, -jnp.inf)
        if kind == "edge":
            row = lax.broadcasted_iota(jnp.int32, s.shape, 0)
            col = lax.broadcasted_iota(jnp.int32, s.shape, 1)
            s = jnp.where(col <= row, s, -jnp.inf)
        scores[unit % 2][:, pl.ds(column, count)] = s
        for k in range(0, count, 128):
            piece_max = s[:, k : k + 128]
            running = piece_max if running is None else jnp.maximum(running, piece_max)
        return running

    def use_scores(unit, part, top, total, acc):
        kind, first, count, column = part
        values = (old_ref if kind == "old" else kv_ref)[pl.ds(first, count), width:]
        e = jnp.exp((scores[unit % 2][:, pl.ds(column, count)] - top) * scale)
        for k in range(0, count, 128):
            total = e[:, k : k + 128] if total is None else total + e[:, k : k + 128]
        product = jnp.dot(e.astype(BF16), values, preferred_element_type=F32)
        return total, product if acc is None else acc + product

    running = None
    for part in pieces(0):
        running = make_scores(0, part, running)
    for unit, (head, b) in enumerate(units):
        top = jnp.max(running, 1, keepdims=True)
        now = pieces(unit)
        later = pieces(unit + 1) if unit + 1 < len(units) else []
        running, total, acc = None, None, None
        for k in range(max(len(now), len(later))):
            if k < len(now):
                total, acc = use_scores(unit, now[k], top, total, acc)
            if k < len(later):
                running = make_scores(unit + 1, later[k], running)
        done = (acc / jnp.sum(total, 1, keepdims=True)).astype(BF16)
        for k in range(0, block, piece):
            member = (b * block + k) // piece
            side = jnp.bitwise_xor(core, member % 2)
            o_ref[side, pl.ds((member // 2) * piece, piece), pl.ds(head * width, width)] = done[
                k : k + piece
            ]


def attend_pair(q, pages, kvs):
    members, heads, piece, width = q.shape
    length = members * piece
    old = sum(page.shape[0] for page in pages)
    block = 2 * piece
    chunk = min(512, old, length)
    keys = old + 2 * length
    return pl.pallas_call(
        functools.partial(attend_pair_kernel, block, chunk, width),
        out_shape=jax.ShapeDtypeStruct((2, length // 2, heads * width), BF16),
        in_specs=[in_hbm()] * (1 + len(pages) + len(kvs)),
        out_specs=in_vmem(),
        scratch_shapes=[
            pltpu.VMEM((heads, length, width), BF16),
            pltpu.VMEM((old, 2 * width), BF16),
            pltpu.VMEM((2 * length, 2 * width), BF16),
            pltpu.VMEM((block, keys), F32),
            pltpu.VMEM((block, keys), F32),
            pltpu.SemaphoreType.DMA((3,)),
        ],
        compiler_params=pltpu.CompilerParams(vmem_limit_bytes=ATTEND_VMEM),
        cost_estimate=pl.CostEstimate(
            flops=4 * heads * length * (keys - length // 2) * width,
            bytes_accessed=4 * (heads * length + keys) * width,
            transcendentals=heads * length * (keys - length // 2),
        ),
        name="attend",
    )(q, *pages, *kvs)


def project_pair_kernel(a_ref, got_ref, *refs):
    near, far, (o_ref, w_ref, sems) = refs[:4], refs[4:8], refs[8:]
    me = lax.axis_index("head")
    half = lax.axis_index("grp")
    core = lax.rem(me, 2)
    steps, sides, heads, share, columns = near[0].shape
    width = w_ref.shape[1]
    copies = []
    for first, given in ((0, near), (steps, far)):
        for flip, x, pieces_of in zip((0, 1, 0, 1), (0, 0, 1, 1), given):
            column = pl.multiple_of(jnp.bitwise_xor(half, x) * columns, columns)
            for t in range(steps):
                for u in range(sides):
                    number = jnp.bitwise_xor(me, flip ^ (2 * u) ^ (4 * (first + t)))
                    row = pl.multiple_of(number * share, share)
                    copy = pltpu.make_async_copy(
                        pieces_of.at[t, u],
                        w_ref.at[:, pl.ds(row, share), pl.ds(column, columns)],
                        sems.at[0],
                    )
                    copy.start()
                    copies.append(copy)
    for copy in copies:
        copy.wait()
    acc = None
    for k in range(heads):
        mine = k < heads // 2
        column = (k % (heads // 2)) * width
        a = a_ref[0, :, pl.ds(column, width)] if mine else got_ref[:, pl.ds(column, width)]
        head = jnp.bitwise_xor(core, 0 if mine else 1) * (heads // 2) + k % (heads // 2)
        part = jnp.dot(a, w_ref[head], preferred_element_type=F32)
        acc = part if acc is None else acc + part
    o_ref[...] = acc.astype(BF16)


def project_pair(a, got, near, far):
    _, _, heads, share, columns = near[0].shape
    rows = got.shape[0]
    width = 2 * got.shape[1] // heads
    model = 2 * columns
    return pl.pallas_call(
        project_pair_kernel,
        out_shape=jax.ShapeDtypeStruct((rows, model), BF16),
        in_specs=[in_vmem(), in_vmem()] + [in_hbm()] * 8,
        out_specs=in_vmem(),
        scratch_shapes=[
            pltpu.VMEM((heads, width, model), BF16),
            pltpu.SemaphoreType.DMA((1,)),
        ],
        compiler_params=pltpu.CompilerParams(vmem_limit_bytes=HIGH_VMEM),
        cost_estimate=pl.CostEstimate(
            flops=2 * heads * rows * width * model,
            bytes_accessed=2 * (heads * width * model + heads * rows * width + rows * model),
            transcendentals=0,
        ),
        name="project",
    )(a, got, *near, *far)


def project_kernel(a_ref, w_ref, o_ref):
    members = a_ref.shape[0]
    planes, share = w_ref.shape[1], w_ref.shape[3]
    acc = None
    for head in range(members):
        w = jnp.concatenate(
            [w_ref[m, p, head] for p in range(planes) for m in range(members)], 0
        )
        part = jnp.dot(a_ref[head], w, preferred_element_type=F32)
        acc = part if acc is None else acc + part
    o_ref[...] = acc.astype(BF16)


def project(a, w):
    members, rows, width = a.shape
    planes, share, model = w.shape[1], w.shape[3], w.shape[4]
    tile = min(512, model)
    return pl.pallas_call(
        project_kernel,
        grid=(model // tile,),
        out_shape=jax.ShapeDtypeStruct((rows, model), BF16),
        in_specs=[
            pl.BlockSpec((members, rows, width), lambda t: (0, 0, 0)),
            pl.BlockSpec((members, planes, members, share, tile), lambda t: (0, 0, 0, 0, t)),
        ],
        out_specs=pl.BlockSpec((rows, tile), lambda t: (0, t)),
        compiler_params=pltpu.CompilerParams(vmem_limit_bytes=HIGH_VMEM),
        cost_estimate=pl.CostEstimate(
            flops=2 * members * rows * width * model,
            bytes_accessed=2 * (members * width * model + members * rows * width + rows * model),
            transcendentals=0,
        ),
        name="project",
    )(a, w)


def route_kernel(parts_ref, resid_ref, gain_ref, slots_ref, stream_ref, out_ref):
    seqs, planes = parts_ref.shape[0], parts_ref.shape[1]
    streams = []
    for seq in range(seqs):
        stream = resid_ref[seq].astype(F32)
        projected = parts_ref[seq, 0].astype(F32)
        for p in range(1, planes):
            projected = projected + parts_ref[seq, p].astype(F32)
        streams.append(stream + projected)
    stream = jnp.concatenate(streams, 0) if seqs > 1 else streams[0]
    stream_ref[...] = stream
    normed = stream * lax.rsqrt(jnp.mean(stream * stream, 1, keepdims=True) + eps_norm)
    normed = (normed * gain_ref[...]).astype(BF16)
    slots, rows = out_ref.shape[0], stream.shape[0]
    place = lax.broadcasted_iota(jnp.int32, (slots, rows), 0)
    hit = place == slots_ref[0:1, :]
    for k in range(1, slots_ref.shape[0]):
        hit = hit | (place == slots_ref[k : k + 1, :])
    out_ref[...] = jnp.dot(hit.astype(BF16), normed, preferred_element_type=F32).astype(BF16)


def route(parts, resid, gain, slots_of, slots):
    seqs, planes, local_rows, model = parts.shape
    rows = seqs * local_rows
    return pl.pallas_call(
        route_kernel,
        out_shape=(
            jax.ShapeDtypeStruct((rows, model), F32),
            jax.ShapeDtypeStruct((slots, model), BF16),
        ),
        in_specs=[in_vmem()] * 4,
        out_specs=(in_vmem(), in_vmem()),
        compiler_params=pltpu.CompilerParams(vmem_limit_bytes=HIGH_VMEM),
        cost_estimate=pl.CostEstimate(
            flops=2 * slots * rows * model,
            bytes_accessed=2 * (planes + 3 + slots // rows) * rows * model,
            transcendentals=0,
        ),
        name="route",
    )(parts, resid, gain, slots_of)


def expert_kernel(x_ref, w_in_ref, w_down_ref, o_ref):
    hidden_width = w_down_ref.shape[0]
    inner = jnp.dot(x_ref[...], w_in_ref[...], preferred_element_type=F32)
    gate = inner[:, :hidden_width]
    hidden = (gate / (1.0 + jnp.exp(-gate)) * inner[:, hidden_width:]).astype(BF16)
    o_ref[...] = jnp.dot(hidden, w_down_ref[...], preferred_element_type=F32).astype(BF16)


def expert(x, w_in, w_down):
    rows, model = x.shape
    hidden_width = w_down.shape[0]
    return pl.pallas_call(
        expert_kernel,
        out_shape=jax.ShapeDtypeStruct((rows, model), BF16),
        in_specs=[in_vmem()] * 3,
        out_specs=in_vmem(),
        compiler_params=pltpu.CompilerParams(vmem_limit_bytes=HIGH_VMEM),
        cost_estimate=pl.CostEstimate(
            flops=6 * rows * model * hidden_width,
            bytes_accessed=2 * (2 * rows * model + 3 * model * hidden_width),
            transcendentals=rows * hidden_width,
        ),
        name="expert",
    )(x, w_in, w_down)


def combine_kernel(seqs, back_ref, stream_ref, slots_ref, gates_ref, o_ref):
    slots = back_ref.shape[0]
    rows = stream_ref.shape[0]
    place = lax.broadcasted_iota(jnp.int32, (rows, slots), 1)
    total = stream_ref[...]
    gathered = None
    for k in range(slots_ref.shape[1]):
        pick = (place == slots_ref[:, k : k + 1]).astype(BF16)
        picked = jnp.dot(pick, back_ref[...], preferred_element_type=F32)
        part = picked * gates_ref[:, k : k + 1]
        gathered = part if gathered is None else gathered + part
    out = (total + gathered).astype(BF16)
    local_rows = rows // seqs
    for seq in range(seqs):
        o_ref[seq] = out[seq * local_rows : (seq + 1) * local_rows]


def combine(back, stream, slots_of, gates, seqs):
    slots, model = back.shape
    rows = stream.shape[0]
    top = slots_of.shape[1]
    return pl.pallas_call(
        functools.partial(combine_kernel, seqs),
        out_shape=jax.ShapeDtypeStruct((seqs, rows // seqs, model), BF16),
        in_specs=[in_vmem()] * 4,
        out_specs=in_vmem(),
        compiler_params=pltpu.CompilerParams(vmem_limit_bytes=HIGH_VMEM),
        cost_estimate=pl.CostEstimate(
            flops=2 * top * slots * rows * model,
            bytes_accessed=2 * slots * model + 6 * rows * model,
            transcendentals=0,
        ),
        name="combine",
    )(back, stream, slots_of, gates)


def slot_matrix(slots_ref, slots, rows):
    place = lax.broadcasted_iota(jnp.int32, (slots, rows), 0).astype(F32)
    hit = place == slots_ref[0:1, :]
    for k in range(1, slots_ref.shape[0]):
        hit = hit | (place == slots_ref[k : k + 1, :])
    return hit.astype(BF16)


def by_copies(body, name, inputs, outputs, flops, bytes_accessed, transcendentals=0):
    count = len(inputs)

    def kernel(*refs):
        ins, outs = refs[:count], refs[count : count + len(outputs)]
        rest = refs[count + len(outputs) :]
        in_vm, out_vm, sems = rest[:count], rest[count:-1], rest[-1]
        copies = [
            pltpu.make_async_copy(ins[k], in_vm[k], sems.at[k]) for k in range(count)
        ]
        for copy in copies:
            copy.start()
        body(lambda k: copies[k].wait(), in_vm, out_vm)
        back = [
            pltpu.make_async_copy(out_vm[k], outs[k], sems.at[count + k])
            for k in range(len(outputs))
        ]
        for copy in back:
            copy.start()
        for copy in back:
            copy.wait()

    shapes = [jax.ShapeDtypeStruct(shape, dtype) for shape, dtype in outputs]
    return pl.pallas_call(
        kernel,
        out_shape=shapes,
        in_specs=[in_hbm()] * count,
        out_specs=[in_hbm()] * len(outputs),
        scratch_shapes=[pltpu.VMEM(x.shape, x.dtype) for x in inputs]
        + [pltpu.VMEM(shape, dtype) for shape, dtype in outputs]
        + [pltpu.SemaphoreType.DMA((count + len(outputs),))],
        compiler_params=pltpu.CompilerParams(vmem_limit_bytes=HIGH_VMEM),
        cost_estimate=pl.CostEstimate(
            flops=flops, bytes_accessed=bytes_accessed, transcendentals=transcendentals
        ),
        name=name,
    )(*inputs)


def route_pair(parts, resid, gain, slots_of, slots):
    planes, rows, model = parts.shape

    def body(wait, ins, outs):
        parts_ref, resid_ref, gain_ref, slots_ref = ins
        stream_ref, normed_ref, out_ref = outs
        wait(0)
        projected = parts_ref[0].astype(F32)
        for p in range(1, planes):
            projected = projected + parts_ref[p].astype(F32)
        wait(1)
        stream = resid_ref[...].astype(F32) + projected
        stream_ref[...] = stream
        normed = stream * lax.rsqrt(jnp.mean(stream * stream, 1, keepdims=True) + eps_norm)
        wait(2)
        normed = (normed * gain_ref[...]).astype(BF16)
        normed_ref[...] = normed
        wait(3)
        matrix = slot_matrix(slots_ref, slots, rows)
        out_ref[...] = jnp.dot(matrix, normed, preferred_element_type=F32).astype(BF16)

    return by_copies(
        body,
        "route",
        [parts, resid, gain, slots_of],
        [((rows, model), F32), ((rows, model), BF16), ((slots, model), BF16)],
        2 * slots * rows * model,
        2 * ((planes + 4) * rows + slots) * model,
    )


def spread(given, slots_of, slots):
    rows, model = given.shape

    def body(wait, ins, outs):
        wait(1)
        matrix = slot_matrix(ins[1], slots, rows)
        wait(0)
        product = jnp.dot(matrix, ins[0][...], preferred_element_type=F32)
        outs[0][...] = product.astype(BF16)

    return by_copies(
        body,
        "spread",
        [given, slots_of],
        [((slots, model), BF16)],
        2 * slots * rows * model,
        2 * (rows + slots) * model,
    )[0]


def expert_pair(x, w_in, w_down):
    rows, model = x.shape
    hidden_width = w_down.shape[0]
    parts = 4
    depth = model // parts

    def kernel(x_hbm, in_hbm_ref, down_hbm, o_hbm, x_ref, in_ref, down_ref, o_ref, sems):
        bring_x = pltpu.make_async_copy(x_hbm, x_ref, sems.at[parts])
        bring_x.start()
        bring_in = []
        for k in range(parts):
            at = pl.ds(k * depth, depth)
            bring_in.append(pltpu.make_async_copy(in_hbm_ref.at[at], in_ref.at[at], sems.at[k]))
            bring_in[k].start()
        bring_down = pltpu.make_async_copy(down_hbm, down_ref, sems.at[parts + 1])
        bring_down.start()
        bring_x.wait()
        inner = None
        for k in range(parts):
            bring_in[k].wait()
            at = pl.ds(k * depth, depth)
            part = jnp.dot(x_ref[:, at], in_ref[at, :], preferred_element_type=F32)
            inner = part if inner is None else inner + part
        gate = inner[:, :hidden_width]
        hidden = (gate / (1.0 + jnp.exp(-gate)) * inner[:, hidden_width:]).astype(BF16)
        bring_down.wait()
        o_ref[...] = jnp.dot(hidden, down_ref[...], preferred_element_type=F32).astype(BF16)
        back = pltpu.make_async_copy(o_ref, o_hbm, sems.at[parts + 2])
        back.start()
        back.wait()

    return pl.pallas_call(
        kernel,
        out_shape=jax.ShapeDtypeStruct((rows, model), BF16),
        in_specs=[in_hbm()] * 3,
        out_specs=in_hbm(),
        scratch_shapes=[
            pltpu.VMEM((rows, model), BF16),
            pltpu.VMEM(w_in.shape, BF16),
            pltpu.VMEM(w_down.shape, BF16),
            pltpu.VMEM((rows, model), BF16),
            pltpu.SemaphoreType.DMA((parts + 3,)),
        ],
        compiler_params=pltpu.CompilerParams(vmem_limit_bytes=HIGH_VMEM),
        cost_estimate=pl.CostEstimate(
            flops=6 * rows * model * hidden_width,
            bytes_accessed=2 * (2 * rows * model + 3 * model * hidden_width),
            transcendentals=rows * hidden_width,
        ),
        name="expert",
    )(x, w_in, w_down)


def gather(back, slots_of, gates, stream, partial):
    slots, model = back.shape
    rows, top = slots_of.shape
    more = [] if stream is None else [stream, partial]

    def body(wait, ins, outs):
        back_ref, slots_ref, gates_ref = ins[:3]
        for k in (1, 2, 0):
            wait(k)
        place = lax.broadcasted_iota(jnp.int32, (rows, slots), 1).astype(F32)
        total = None
        for k in range(top):
            pick = (place == slots_ref[:, k : k + 1]).astype(BF16)
            picked = jnp.dot(pick, back_ref[...], preferred_element_type=F32)
            part = picked * gates_ref[:, k : k + 1]
            total = part if total is None else total + part
        if more:
            wait(3)
            wait(4)
            total = ins[3][...] + (total + ins[4][...].astype(F32))
        outs[0][...] = total.astype(BF16)

    return by_copies(
        body,
        "gather",
        [back, slots_of, gates] + more,
        [((rows, model), BF16)],
        2 * top * slots * rows * model,
        2 * (slots + 4 * rows) * model,
    )[0]


def flipped(value, axis, mask):
    pairs = [(source, source ^ mask) for source in range(lax.axis_size(axis))]
    return lax.ppermute(value, axis, pairs)


def parts_in_pairs(queries, new_kv, cache, w_out, other):
    n = lax.axis_size("head")
    local_rows, _, heads, width = queries.shape
    pair_heads = new_kv.shape[2]
    members = heads // pair_heads
    model = w_out.shape[2]
    share = w_out.shape[1]
    me = lax.axis_index("head")
    plane_bit = members // 2
    planes = n // plane_bit
    b = (me // plane_bit) % 2
    y = (me // 2) % 2
    group_sets = [[g * members + m for m in range(members)] for g in range(n // members)]

    kv_heads = new_kv.reshape(local_rows, pair_heads, 2 * width).transpose(1, 0, 2)
    kv_same = lax.dynamic_index_in_dim(kv_heads, b, 0, keepdims=False)
    kv_other = lax.dynamic_index_in_dim(kv_heads, 1 - b, 0, keepdims=False)
    page = cache[0]
    first = flipped(jnp.concatenate([kv_other, page], 0), "head", plane_bit)

    columns = model // 2
    w = lax.dynamic_slice_in_dim(w_out, lax.axis_index("grp") * columns, columns, 2)
    w = w.reshape(2, 2, heads // 4, share, columns)
    w_keep = lax.dynamic_index_in_dim(w, y, 1, keepdims=False)
    w_give = lax.dynamic_index_in_dim(w, 1 - y, 1, keepdims=False)
    query_slots = queries.reshape(local_rows, heads, width).transpose(1, 0, 2)
    query_slots = query_slots.reshape(members, heads // members, local_rows, width)
    first, query_slots, w_give = lax.optimization_barrier((first, query_slots, w_give))

    near = jnp.stack([kv_same, first[:local_rows]], 0)
    near_pages = jnp.concatenate([page, first[local_rows:]], 0)
    far = flipped(near, "head", members)
    has_pages = [d for d in range(n) if d // members == (d // plane_bit) % 2]
    far_pages = lax.ppermute(near_pages, "head", [(d, d ^ members) for d in has_pages])
    near_y = flipped(near, "head", 2)
    w_got = flipped(w_give, "head", 2)
    q = lax.all_to_all(
        query_slots, "head", split_axis=0, concat_axis=0, tiled=True, axis_index_groups=group_sets
    )
    far, far_pages, w_got = lax.optimization_barrier((far, far_pages, w_got))
    own_pages = jnp.where(me // members == b, near_pages, far_pages)
    y_pages = flipped(own_pages, "head", 2)
    far_y = flipped(far, "head", 2)
    w_both = jnp.stack([w_keep, w_got], 1)
    w_same = lax.dynamic_index_in_dim(w_both, b, 0, keepdims=False)
    w_other = lax.dynamic_index_in_dim(w_both, 1 - b, 0, keepdims=False)
    w_near = jnp.stack([w_same, flipped(w_other, "head", plane_bit)], 0)
    w_far = flipped(w_near, "head", members)
    near_c = flipped(near, "head", 1)
    far_c = flipped(far, "head", 1)
    c_pages = flipped(own_pages, "head", 1)
    y_pages, far_y, w_near = lax.optimization_barrier((y_pages, far_y, w_near))
    near_cy = flipped(near_y, "head", 1)
    far_cy = flipped(far_y, "head", 1)
    cy_pages = flipped(y_pages, "head", 1)
    w_near_x = flipped(w_near, "grp", 1)
    q, w_far = lax.optimization_barrier((q, w_far))
    w_far_x = flipped(w_far, "grp", 1)
    w_near_c = flipped(w_near, "head", 1)
    w_far_c = flipped(w_far, "head", 1)
    a = attend_pair(
        q,
        (own_pages, y_pages, c_pages, cy_pages),
        (near, far, near_y, far_y, near_c, far_c, near_cy, far_cy),
    )
    a, w_near_x, w_far_x, w_near_c, w_far_c, other = lax.optimization_barrier(
        (a, w_near_x, w_far_x, w_near_c, w_far_c, other)
    )
    w_near_cx = flipped(w_near_x, "head", 1)
    w_far_cx = flipped(w_far_x, "head", 1)
    got = flipped(a[1], "head", 1)
    partial = project_pair(
        a,
        got,
        (w_near, w_near_c, w_near_x, w_near_cx),
        (w_far, w_far_c, w_far_x, w_far_cx),
    )
    quads = [
        [g * members + 2 * k + core for k in range(members // 2)]
        for g in range(n // members)
        for core in range(2)
    ]
    parts = lax.all_to_all(
        partial.reshape(members // 2, local_rows, model),
        "head",
        split_axis=0,
        concat_axis=0,
        tiled=True,
        axis_index_groups=quads,
    )
    return parts, other


def parts_in_planes(queries, new_kv, cache, w_out):
    n = lax.axis_size("head")
    local_rows, seqs, heads, width = queries.shape
    pair_heads = new_kv.shape[2]
    members = heads // pair_heads
    groups = n // members
    model = w_out.shape[2]
    side = 1 << ((n.bit_length() - 1) // 2)
    side = min(side, heads)
    planes = n // side
    planes_of_seq = heads // side
    pair_groups = [[g * members + m for m in range(members)] for g in range(groups)]
    cross_groups = [[g * members + m for g in range(groups)] for m in range(members)]
    plane_groups = [[p * side + m for m in range(side)] for p in range(planes)]
    column_groups = [[p * side + m for p in range(planes)] for m in range(side)]

    query_slots = queries.reshape(local_rows, n, width).transpose(1, 0, 2)
    q = lax.all_to_all(query_slots, "head", split_axis=0, concat_axis=0, tiled=True)
    q = q.reshape(n * local_rows, width)

    kv_slots = new_kv.reshape(local_rows, groups, 2 * width).transpose(1, 0, 2)
    kv = lax.all_to_all(
        kv_slots, "head", split_axis=0, concat_axis=0, tiled=True, axis_index_groups=cross_groups
    )
    kv = lax.all_gather(kv, "head", axis=0, axis_index_groups=pair_groups)
    pages = lax.all_gather(cache, "head", axis=0, tiled=True, axis_index_groups=pair_groups)

    share = w_out.shape[1]
    w_planes = w_out.reshape(planes_of_seq, side, share, model)
    if planes > planes_of_seq:
        w_planes = jnp.tile(w_planes, (planes // planes_of_seq, 1, 1, 1))
    w = lax.all_to_all(
        w_planes, "head", split_axis=0, concat_axis=0, tiled=True, axis_index_groups=column_groups
    )
    w = lax.all_gather(w, "head", axis=0, axis_index_groups=plane_groups)
    if share % 16:
        w = w.transpose(2, 1, 0, 3, 4).reshape(1, 1, side, width, model)
        w = w.reshape(side, width, model)

    attended = attend(q, pages.reshape(-1, 2 * width), kv)
    a = attended.reshape(planes, side, local_rows, width).transpose(1, 0, 2, 3)
    a = a.reshape(side, planes * local_rows, width)
    a = lax.all_to_all(
        a, "head", split_axis=0, concat_axis=0, tiled=True, axis_index_groups=plane_groups
    )
    if share % 16:
        partial = jnp.einsum("hri,hid->rd", a, w, preferred_element_type=F32).astype(BF16)
    else:
        partial = project(a, w)
    parts = lax.all_to_all(
        partial.reshape(planes, local_rows, model),
        "head",
        split_axis=0,
        concat_axis=0,
        tiled=True,
        axis_index_groups=column_groups,
    )
    return parts.reshape(seqs, planes_of_seq, local_rows, model)


def route_in_pairs(parts, resid, norm_gain, own, other, top, w_in, w_down, capacity, members):
    n = lax.axis_size("head")
    local_rows, seqs, model = resid.shape
    me = lax.axis_index("head")
    group_sets = [[g * members + m for m in range(members)] for g in range(n // members)]
    group_slots = members * capacity

    def around(value):
        value = value.reshape(members, capacity, model)
        value = lax.all_to_all(
            value, "head", split_axis=0, concat_axis=0, tiled=True, axis_index_groups=group_sets
        )
        return value.reshape(group_slots, model)

    first = ((me // members) * group_slots).astype(F32)
    slots_own, gates_own = own[:, :top] - first, own[:, top:]
    slots_other, gates_other = other[:, :top] - first, other[:, top:]

    stream, normed, out_own = route_pair(
        parts, resid.reshape(local_rows, model), norm_gain[None, :], slots_own.T, group_slots
    )
    normed_other = flipped(normed, "head", members)
    arrived_own = around(out_own)
    normed_other, arrived_own = lax.optimization_barrier((normed_other, arrived_own))
    answer_own = expert_pair(arrived_own, w_in, w_down)
    out_other = spread(normed_other, slots_other.T, group_slots)
    answer_other = expert_pair(around(out_other), w_in, w_down)
    partial = gather(around(answer_other), slots_other, gates_other, None, None)
    partial, answer_own = lax.optimization_barrier((partial, answer_own))
    partial = flipped(partial, "head", members)
    out = gather(around(answer_own), slots_own, gates_own, stream, partial)
    return out.reshape(local_rows, seqs, model)


def local(queries, new_kv, cache, resid, w_out, norm_gain, expert_ids, expert_gates, w_in, w_down):
    n = lax.axis_size("head")
    local_rows, seqs, heads, width = queries.shape
    model = resid.shape[2]
    rows = local_rows * seqs
    members = heads // new_kv.shape[2]
    in_pairs = (
        lax.axis_size("grp") == 2
        and seqs == 1
        and new_kv.shape[2] == 2
        and n == heads == 2 * members
        and members == 8
        and cache.shape[0] == 1
        and w_in.shape[0] == 1
        and w_out.shape[1] % 16 == 0
    )

    top = expert_ids.shape[2]
    experts = w_in.shape[0] * n
    capacity = max(2, 2 * rows * top // experts)
    ids = expert_ids.transpose(1, 0, 2).reshape(rows, top)
    gates = expert_gates.transpose(1, 0, 2).reshape(rows, top)
    onehot = (ids[:, :, None] == jnp.arange(experts, dtype=jnp.int32)).astype(jnp.int32)
    named = onehot.sum(1)
    before = jnp.cumsum(named, 0) - named
    slots_of = ids * capacity + jnp.sum(onehot * before[:, None, :], 2)
    slots = experts * capacity
    if in_pairs:
        own = jnp.concatenate([slots_of.astype(F32), gates], 1)
        other = flipped(own, "head", members)
        parts, other = parts_in_pairs(queries, new_kv, cache, w_out, other)
        return route_in_pairs(
            parts, resid, norm_gain, own, other, top, w_in[0], w_down[0], capacity, members
        )
    parts = parts_in_planes(queries, new_kv, cache, w_out)
    stream, outgoing = route(
        parts, resid.transpose(1, 0, 2), norm_gain[None, :], slots_of.T, slots
    )
    arrived = lax.all_to_all(
        outgoing.reshape(n, slots // n, model), "head", split_axis=0, concat_axis=0, tiled=True
    )
    local_experts = w_in.shape[0]
    if local_experts == 1:
        answered = expert(arrived.reshape(slots, model), w_in[0], w_down[0])
        answered = answered.reshape(n, slots // n, model)
    else:
        arrived = arrived.reshape(n, local_experts, capacity, model).transpose(1, 0, 2, 3)
        arrived = arrived.reshape(local_experts, n * capacity, model)
        answered = jnp.stack([expert(arrived[e], w_in[e], w_down[e]) for e in range(local_experts)])
        answered = answered.reshape(local_experts, n, capacity, model).transpose(1, 0, 2, 3)
        answered = answered.reshape(n, slots // n, model)
    back = lax.all_to_all(answered, "head", split_axis=0, concat_axis=0, tiled=True)
    out = combine(back.reshape(slots, model), stream, slots_of, gates, seqs)
    return out.transpose(1, 0, 2)


def solution(mesh):
    return jax.shard_map(
        local,
        mesh=mesh,
        in_specs=(
            P("head", "grp", None, None),
            P("head", "grp", None, None),
            P(("grp", "head"), None, None),
            P("head", "grp", None),
            P(None, "head", None),
            P(),
            P("head", "grp", None),
            P("head", "grp", None),
            P("head", None, None),
            P("head", None, None),
        ),
        out_specs=P("head", "grp", None),
        check_vma=False,
    )
```

```python
import functools

import jax
import jax.numpy as jnp
from jax import lax
from jax.experimental import pallas as pl
from jax.experimental.pallas import tpu as pltpu
from jax.sharding import PartitionSpec as P

eps_norm = 1e-06
F32 = jnp.float32
BF16 = jnp.bfloat16
HIGH_VMEM = 48 * 2**20
LOG2_E = 1.4426950408889634


def in_hbm():
    return pl.BlockSpec(memory_space=pltpu.HBM)


def in_vmem():
    return pl.BlockSpec(memory_space=pltpu.VMEM)


def attend_kernel(
    block, chunk, width, q_hbm, cache_hbm, kv_hbm, o_ref, q_ref, cache_ref, kv_ref, s0, s1, sems
):
    members, groups, piece, _ = kv_hbm.shape
    length = members * groups * piece
    old = cache_hbm.shape[0]
    scale = width**-0.5
    in_q = pltpu.make_async_copy(q_hbm, q_ref, sems.at[0])
    in_cache = pltpu.make_async_copy(cache_hbm, cache_ref, sems.at[1])
    in_q.start()
    in_cache.start()
    in_kv = []
    for group in range(groups):
        for member in range(members):
            place = (group * members + member) * piece
            copy = pltpu.make_async_copy(
                kv_hbm.at[member, group], kv_ref.at[pl.ds(place, piece)], sems.at[2]
            )
            copy.start()
            in_kv.append(copy)
    in_q.wait()
    in_cache.wait()
    for copy in in_kv:
        copy.wait()
    scores = [s0, s1]

    def pieces(b):
        out = [(True, k, chunk, k) for k in range(0, old, chunk)]
        last = b * block
        for k in range(0, last, chunk):
            out.append((False, k, min(chunk, last - k), old + k))
        out.append((False, last, block, old + last))
        return out

    def make_scores(b, part, running):
        of_cache, first, count, column = part
        keys = (cache_ref if of_cache else kv_ref)[pl.ds(first, count), :width]
        s = lax.dot_general(
            q_ref[pl.ds(b * block, block), :],
            keys,
            (((1,), (1,)), ((), ())),
            preferred_element_type=F32,
        )
        if not of_cache and first == b * block:
            row = lax.broadcasted_iota(jnp.int32, s.shape, 0)
            col = lax.broadcasted_iota(jnp.int32, s.shape, 1)
            s = jnp.where(col <= row, s, -jnp.inf)
        scores[b % 2][:, pl.ds(column, count)] = s
        for k in range(0, count, 128):
            piece_max = s[:, k : k + 128]
            running = piece_max if running is None else jnp.maximum(running, piece_max)
        return running

    def use_scores(b, part, top, total, acc):
        of_cache, first, count, column = part
        values = (cache_ref if of_cache else kv_ref)[pl.ds(first, count), width:]
        e = jnp.exp((scores[b % 2][:, pl.ds(column, count)] - top) * scale)
        for k in range(0, count, 128):
            total = e[:, k : k + 128] if total is None else total + e[:, k : k + 128]
        product = jnp.dot(e.astype(BF16), values, preferred_element_type=F32)
        return total, product if acc is None else acc + product

    blocks = length // block
    running = None
    for part in pieces(0):
        running = make_scores(0, part, running)
    for b in range(blocks):
        top = jnp.max(running, 1, keepdims=True)
        now, later = pieces(b), pieces(b + 1) if b + 1 < blocks else []
        running, total, acc = None, None, None
        for k in range(max(len(now), len(later))):
            if k < len(now):
                total, acc = use_scores(b, now[k], top, total, acc)
            if k < len(later):
                running = make_scores(b + 1, later[k], running)
        o_ref[pl.ds(b * block, block), :] = (acc / jnp.sum(total, 1, keepdims=True)).astype(BF16)


def attend(q, cache, kv):
    length, width = q.shape
    old = cache.shape[0]
    block = min(256, length)
    chunk = min(512, old)
    return pl.pallas_call(
        functools.partial(attend_kernel, block, chunk, width),
        out_shape=jax.ShapeDtypeStruct((length, width), BF16),
        in_specs=[in_hbm()] * 3,
        out_specs=in_vmem(),
        scratch_shapes=[
            pltpu.VMEM((length, width), BF16),
            pltpu.VMEM((old, 2 * width), BF16),
            pltpu.VMEM((length, 2 * width), BF16),
            pltpu.VMEM((block, old + length), F32),
            pltpu.VMEM((block, old + length), F32),
            pltpu.SemaphoreType.DMA((3,)),
        ],
        compiler_params=pltpu.CompilerParams(vmem_limit_bytes=HIGH_VMEM),
        cost_estimate=pl.CostEstimate(
            flops=4 * length * (old + length // 2) * width,
            bytes_accessed=4 * (2 * length + 2 * old) * width,
            transcendentals=length * (old + length // 2),
        ),
        name="attend",
    )(q, cache, kv)


def attend_pair_kernel(
    block,
    chunk,
    width,
    q_hbm,
    page_a,
    page_b,
    page_y,
    page_c,
    page_cy,
    kv_own,
    kv_y,
    kv_c,
    kv_cy,
    o_ref,
    q_ref,
    old_ref,
    kv_ref,
    s0,
    s1,
    sems,
):
    me = lax.axis_index("head")
    members, heads, piece, _ = q_hbm.shape
    length = members * piece
    planes = kv_own.shape[0]
    old = old_ref.shape[0]
    earlier_group = me // members > 0
    core = lax.rem(me, 2)
    copies = []

    def bring(source, target, sem):
        copy = pltpu.make_async_copy(source, target, sems.at[sem])
        copy.start()
        copies.append(copy)

    for member in range(members):
        for head in range(heads):
            bring(q_hbm.at[member, head], q_ref.at[head, pl.ds(member * piece, piece)], 0)
    place = 0
    for page in (page_a, page_b, page_y, page_c, page_cy):
        count = page.shape[0]
        bring(page, old_ref.at[pl.ds(place, count)], 1)
        place += count
    for flip, pieces_of in ((0, kv_own), (2, kv_y), (1, kv_c), (3, kv_cy)):
        for t in range(planes):
            number = jnp.bitwise_and(
                jnp.bitwise_xor(me, flip ^ (t * (members // 2))), members - 1
            )
            start = pl.multiple_of(number * piece, piece)
            area = 0 if t * (members // 2) >= members else length
            bring(pieces_of.at[t], kv_ref.at[pl.ds(area + start, piece)], 2)
    for copy in copies:
        copy.wait()
    scale = width**-0.5 * LOG2_E
    scores = [s0, s1]
    blocks = length // block
    units = [(head, b) for head in range(heads) for b in range(blocks)]

    def pieces(unit):
        _, b = units[unit]
        out = [("old", k, chunk, k) for k in range(0, old, chunk)]
        out += [("past", k, chunk, old + k) for k in range(0, length, chunk)]
        last = b * block
        for k in range(0, last, chunk):
            out.append(("new", length + k, min(chunk, last - k), old + length + k))
        out.append(("edge", length + last, block, old + length + last))
        return out

    def make_scores(unit, part, running):
        kind, first, count, column = part
        head, b = units[unit]
        keys = (old_ref if kind == "old" else kv_ref)[pl.ds(first, count), :width]
        s = lax.dot_general(
            q_ref[head, pl.ds(b * block, block), :],
            keys,
            (((1,), (1,)), ((), ())),
            preferred_element_type=F32,
        )
        if kind == "past":
            s = jnp.where(earlier_group, s, -jnp.inf)
        if kind == "edge":
            row = lax.broadcasted_iota(jnp.int32, s.shape, 0)
            col = lax.broadcasted_iota(jnp.int32, s.shape, 1)
            s = jnp.where(col <= row, s, -jnp.inf)
        scores[unit % 2][:, pl.ds(column, count)] = s
        for k in range(0, count, 128):
            piece_max = s[:, k : k + 128]
            running = piece_max if running is None else jnp.maximum(running, piece_max)
        return running

    def use_scores(unit, part, top, total, acc):
        kind, first, count, column = part
        values = (old_ref if kind == "old" else kv_ref)[pl.ds(first, count), width:]
        e = jnp.exp2((scores[unit % 2][:, pl.ds(column, count)] - top) * scale)
        for k in range(0, count, 128):
            total = e[:, k : k + 128] if total is None else total + e[:, k : k + 128]
        product = jnp.dot(e.astype(BF16), values, preferred_element_type=F32)
        return total, product if acc is None else acc + product

    running = None
    for part in pieces(0):
        running = make_scores(0, part, running)
    for unit, (head, b) in enumerate(units):
        top = jnp.max(running, 1, keepdims=True)
        now = pieces(unit)
        later = pieces(unit + 1) if unit + 1 < len(units) else []
        running, total, acc = None, None, None
        for k in range(max(len(now), len(later))):
            if k < len(now):
                total, acc = use_scores(unit, now[k], top, total, acc)
            if k < len(later):
                running = make_scores(unit + 1, later[k], running)
        done = (acc / jnp.sum(total, 1, keepdims=True)).astype(BF16)
        for k in range(0, block, piece):
            member = (b * block + k) // piece
            side = jnp.bitwise_xor(core, member % 2)
            o_ref[side, pl.ds((member // 2) * piece, piece), pl.ds(head * width, width)] = done[
                k : k + piece
            ]


def attend_pair(q, pages, kvs):
    members, heads, piece, width = q.shape
    length = members * piece
    old = sum(page.shape[0] for page in pages)
    block = min(4 * piece, length)
    chunk = min(512, old, length)
    keys = old + 2 * length
    return pl.pallas_call(
        functools.partial(attend_pair_kernel, block, chunk, width),
        out_shape=jax.ShapeDtypeStruct((2, length // 2, heads * width), BF16),
        in_specs=[in_hbm()] * (1 + len(pages) + len(kvs)),
        out_specs=in_vmem(),
        scratch_shapes=[
            pltpu.VMEM((heads, length, width), BF16),
            pltpu.VMEM((old, 2 * width), BF16),
            pltpu.VMEM((2 * length, 2 * width), BF16),
            pltpu.VMEM((block, keys), F32),
            pltpu.VMEM((block, keys), F32),
            pltpu.SemaphoreType.DMA((3,)),
        ],
        compiler_params=pltpu.CompilerParams(vmem_limit_bytes=HIGH_VMEM),
        cost_estimate=pl.CostEstimate(
            flops=4 * heads * length * (keys - length // 2) * width,
            bytes_accessed=4 * (heads * length + keys) * width,
            transcendentals=heads * length * (keys - length // 2),
        ),
        name="attend",
    )(q, *pages, *kvs)


def project_pair_kernel(a_ref, got_ref, *refs):
    near, far, outs, (w_ref, sems) = refs[:4], refs[4:8], refs[8:-2], refs[-2:]
    me = lax.axis_index("head")
    half = lax.axis_index("grp")
    core = lax.rem(me, 2)
    chip = jnp.bitwise_and(me // 2, len(outs) - 1)
    steps, sides, heads, share, columns = near[0].shape
    width = w_ref.shape[1]
    copies = []
    for first, given in ((0, near), (steps, far)):
        for flip, x, pieces_of in zip((0, 1, 0, 1), (0, 0, 1, 1), given):
            column = pl.multiple_of(jnp.bitwise_xor(half, x) * columns, columns)
            for t in range(steps):
                for u in range(sides):
                    number = jnp.bitwise_xor(me, flip ^ (2 * u) ^ (4 * (first + t)))
                    row = pl.multiple_of(number * share, share)
                    copy = pltpu.make_async_copy(
                        pieces_of.at[t, u],
                        w_ref.at[:, pl.ds(row, share), pl.ds(column, columns)],
                        sems.at[0],
                    )
                    copy.start()
                    copies.append(copy)
    rows = outs[0].shape[0]
    starts = [
        pl.multiple_of(jnp.bitwise_xor(chip, k) * rows, rows) for k in range(len(outs))
    ]
    blocks = []
    for k in range(heads):
        mine = k < heads // 2
        column = (k % (heads // 2)) * width
        at = pl.ds(column, width)
        blocks.append(
            jnp.concatenate(
                [
                    a_ref[0, pl.ds(start, rows), at] if mine else got_ref[pl.ds(start, rows), at]
                    for start in starts
                ],
                0,
            )
        )
    for copy in copies:
        copy.wait()
    acc = None
    for k in range(heads):
        head = jnp.bitwise_xor(core, 0 if k < heads // 2 else 1) * (heads // 2) + k % (heads // 2)
        part = jnp.dot(blocks[k], w_ref[head], preferred_element_type=F32)
        acc = part if acc is None else acc + part
    for k, out in enumerate(outs):
        out[...] = acc[k * rows : (k + 1) * rows].astype(BF16)


def project_pair(a, got, near, far, parts):
    _, _, heads, share, columns = near[0].shape
    rows = got.shape[0]
    width = 2 * got.shape[1] // heads
    model = 2 * columns
    return pl.pallas_call(
        project_pair_kernel,
        out_shape=[jax.ShapeDtypeStruct((rows // parts, model), BF16)] * parts,
        in_specs=[in_vmem(), in_vmem()] + [in_hbm()] * 8,
        out_specs=[in_vmem()] * parts,
        scratch_shapes=[
            pltpu.VMEM((heads, width, model), BF16),
            pltpu.SemaphoreType.DMA((1,)),
        ],
        compiler_params=pltpu.CompilerParams(vmem_limit_bytes=HIGH_VMEM),
        cost_estimate=pl.CostEstimate(
            flops=2 * heads * rows * width * model,
            bytes_accessed=2 * (heads * width * model + heads * rows * width + rows * model),
            transcendentals=0,
        ),
        name="project",
    )(a, got, *near, *far)


def project_kernel(a_ref, w_ref, o_ref):
    members = a_ref.shape[0]
    planes, share = w_ref.shape[1], w_ref.shape[3]
    acc = None
    for head in range(members):
        w = jnp.concatenate(
            [w_ref[m, p, head] for p in range(planes) for m in range(members)], 0
        )
        part = jnp.dot(a_ref[head], w, preferred_element_type=F32)
        acc = part if acc is None else acc + part
    o_ref[...] = acc.astype(BF16)


def project(a, w):
    members, rows, width = a.shape
    planes, share, model = w.shape[1], w.shape[3], w.shape[4]
    tile = min(512, model)
    return pl.pallas_call(
        project_kernel,
        grid=(model // tile,),
        out_shape=jax.ShapeDtypeStruct((rows, model), BF16),
        in_specs=[
            pl.BlockSpec((members, rows, width), lambda t: (0, 0, 0)),
            pl.BlockSpec((members, planes, members, share, tile), lambda t: (0, 0, 0, 0, t)),
        ],
        out_specs=pl.BlockSpec((rows, tile), lambda t: (0, t)),
        compiler_params=pltpu.CompilerParams(vmem_limit_bytes=HIGH_VMEM),
        cost_estimate=pl.CostEstimate(
            flops=2 * members * rows * width * model,
            bytes_accessed=2 * (members * width * model + members * rows * width + rows * model),
            transcendentals=0,
        ),
        name="project",
    )(a, w)


def route_kernel(resid_ref, gain_ref, slots_ref, *refs):
    parts_refs, (stream_ref, out_ref) = refs[:-2], refs[-2:]
    seqs = resid_ref.shape[0]
    streams = []
    for seq in range(seqs):
        stream = resid_ref[seq].astype(F32)
        projected = parts_refs[0][seq].astype(F32)
        for part in parts_refs[1:]:
            projected = projected + part[seq].astype(F32)
        streams.append(stream + projected)
    stream = jnp.concatenate(streams, 0) if seqs > 1 else streams[0]
    stream_ref[...] = stream
    normed = stream * lax.rsqrt(jnp.mean(stream * stream, 1, keepdims=True) + eps_norm)
    normed = (normed * gain_ref[...]).astype(BF16)
    slots, rows = out_ref.shape[0], stream.shape[0]
    place = lax.broadcasted_iota(jnp.int32, (slots, rows), 0)
    hit = place == slots_ref[0:1, :]
    for k in range(1, slots_ref.shape[0]):
        hit = hit | (place == slots_ref[k : k + 1, :])
    out_ref[...] = jnp.dot(hit.astype(BF16), normed, preferred_element_type=F32).astype(BF16)


def route(parts, resid, gain, slots_of, slots):
    seqs, local_rows, model = resid.shape
    rows = seqs * local_rows
    return pl.pallas_call(
        route_kernel,
        out_shape=(
            jax.ShapeDtypeStruct((rows, model), F32),
            jax.ShapeDtypeStruct((slots, model), BF16),
        ),
        in_specs=[in_vmem()] * (3 + len(parts)),
        out_specs=(in_vmem(), in_vmem()),
        compiler_params=pltpu.CompilerParams(vmem_limit_bytes=HIGH_VMEM),
        cost_estimate=pl.CostEstimate(
            flops=2 * slots * rows * model,
            bytes_accessed=2 * (len(parts) + 3 + slots // rows) * rows * model,
            transcendentals=0,
        ),
        name="route",
    )(resid, gain, slots_of, *parts)


def expert_kernel(x_ref, w_in_ref, w_down_ref, o_ref):
    hidden_width = w_down_ref.shape[0]
    inner = jnp.dot(x_ref[...], w_in_ref[...], preferred_element_type=F32)
    gate = inner[:, :hidden_width]
    hidden = (gate / (1.0 + jnp.exp(-gate)) * inner[:, hidden_width:]).astype(BF16)
    o_ref[...] = jnp.dot(hidden, w_down_ref[...], preferred_element_type=F32).astype(BF16)


def expert(x, w_in, w_down):
    rows, model = x.shape
    hidden_width = w_down.shape[0]
    return pl.pallas_call(
        expert_kernel,
        out_shape=jax.ShapeDtypeStruct((rows, model), BF16),
        in_specs=[in_vmem()] * 3,
        out_specs=in_vmem(),
        compiler_params=pltpu.CompilerParams(vmem_limit_bytes=HIGH_VMEM),
        cost_estimate=pl.CostEstimate(
            flops=6 * rows * model * hidden_width,
            bytes_accessed=2 * (2 * rows * model + 3 * model * hidden_width),
            transcendentals=rows * hidden_width,
        ),
        name="expert",
    )(x, w_in, w_down)


def expert_pair(x, w_in, w_down):
    rows, model = x.shape
    hidden_width = w_down.shape[0]
    parts = 4
    depth = model // parts

    def kernel(x_hbm, in_hbm_ref, down_hbm, o_hbm, x_ref, in_ref, down_ref, o_ref, sems):
        bring_x = pltpu.make_async_copy(x_hbm, x_ref, sems.at[parts])
        bring_x.start()
        bring_in = []
        for k in range(parts):
            at = pl.ds(k * depth, depth)
            bring_in.append(pltpu.make_async_copy(in_hbm_ref.at[at], in_ref.at[at], sems.at[k]))
            bring_in[k].start()
        bring_down = pltpu.make_async_copy(down_hbm, down_ref, sems.at[parts + 1])
        bring_down.start()
        bring_x.wait()
        inner = None
        for k in range(parts):
            bring_in[k].wait()
            at = pl.ds(k * depth, depth)
            part = jnp.dot(x_ref[:, at], in_ref[at, :], preferred_element_type=F32)
            inner = part if inner is None else inner + part
        gate = inner[:, :hidden_width]
        hidden = (gate / (1.0 + jnp.exp(-gate)) * inner[:, hidden_width:]).astype(BF16)
        bring_down.wait()
        o_ref[...] = jnp.dot(hidden, down_ref[...], preferred_element_type=F32).astype(BF16)
        back = pltpu.make_async_copy(o_ref, o_hbm, sems.at[parts + 2])
        back.start()
        back.wait()

    return pl.pallas_call(
        kernel,
        out_shape=jax.ShapeDtypeStruct((rows, model), BF16),
        in_specs=[in_hbm()] * 3,
        out_specs=in_hbm(),
        scratch_shapes=[
            pltpu.VMEM((rows, model), BF16),
            pltpu.VMEM(w_in.shape, BF16),
            pltpu.VMEM(w_down.shape, BF16),
            pltpu.VMEM((rows, model), BF16),
            pltpu.SemaphoreType.DMA((parts + 3,)),
        ],
        compiler_params=pltpu.CompilerParams(vmem_limit_bytes=HIGH_VMEM),
        cost_estimate=pl.CostEstimate(
            flops=6 * rows * model * hidden_width,
            bytes_accessed=2 * (2 * rows * model + 3 * model * hidden_width),
            transcendentals=rows * hidden_width,
        ),
        name="expert",
    )(x, w_in, w_down)


def combine_kernel(seqs, back_ref, stream_ref, slots_ref, gates_ref, o_ref):
    slots = back_ref.shape[0]
    rows = stream_ref.shape[0]
    place = lax.broadcasted_iota(jnp.int32, (rows, slots), 1)
    total = stream_ref[...]
    gathered = None
    for k in range(slots_ref.shape[1]):
        pick = (place == slots_ref[:, k : k + 1]).astype(BF16)
        picked = jnp.dot(pick, back_ref[...], preferred_element_type=F32)
        part = picked * gates_ref[:, k : k + 1]
        gathered = part if gathered is None else gathered + part
    out = (total + gathered).astype(BF16)
    local_rows = rows // seqs
    for seq in range(seqs):
        o_ref[seq] = out[seq * local_rows : (seq + 1) * local_rows]


def combine(back, stream, slots_of, gates, seqs):
    slots, model = back.shape
    rows = stream.shape[0]
    top = slots_of.shape[1]
    return pl.pallas_call(
        functools.partial(combine_kernel, seqs),
        out_shape=jax.ShapeDtypeStruct((seqs, rows // seqs, model), BF16),
        in_specs=[in_vmem()] * 4,
        out_specs=in_vmem(),
        compiler_params=pltpu.CompilerParams(vmem_limit_bytes=HIGH_VMEM),
        cost_estimate=pl.CostEstimate(
            flops=2 * top * slots * rows * model,
            bytes_accessed=2 * slots * model + 6 * rows * model,
            transcendentals=0,
        ),
        name="combine",
    )(back, stream, slots_of, gates)


def flipped(value, axis, mask):
    pairs = [(source, source ^ mask) for source in range(lax.axis_size(axis))]
    return lax.ppermute(value, axis, pairs)


def parts_in_pairs(queries, new_kv, cache, w_out):
    n = lax.axis_size("head")
    local_rows, _, heads, width = queries.shape
    pair_heads = new_kv.shape[2]
    members = heads // pair_heads
    model = w_out.shape[2]
    share = w_out.shape[1]
    me = lax.axis_index("head")
    plane_bit = members // 2
    planes = n // plane_bit
    b = (me // plane_bit) % 2
    y = (me // 2) % 2
    group_sets = [[g * members + m for m in range(members)] for g in range(n // members)]

    query_slots = queries.reshape(local_rows, heads, width).transpose(1, 0, 2)
    query_slots = query_slots.reshape(members, heads // members, local_rows, width)
    q = lax.all_to_all(
        query_slots, "head", split_axis=0, concat_axis=0, tiled=True, axis_index_groups=group_sets
    )

    def page_target(source, other):
        p, plane, rest = source // members, (source // plane_bit) % 2, source % plane_bit
        return (plane ^ other) * members + p * plane_bit + rest

    page_a, page_b = (
        lax.ppermute(cache[0], "head", [(d, page_target(d, other)) for d in range(n)])
        for other in range(2)
    )
    kv_heads = new_kv.reshape(local_rows, pair_heads, 2 * width).transpose(1, 0, 2)
    kv_same = lax.dynamic_index_in_dim(kv_heads, b, 0, keepdims=False)
    kv_other = lax.dynamic_index_in_dim(kv_heads, 1 - b, 0, keepdims=False)
    columns = model // 2
    w = lax.dynamic_slice_in_dim(w_out, lax.axis_index("grp") * columns, columns, 2)
    w = w.reshape(2, 2, heads // 4, share, columns)
    w_keep = lax.dynamic_index_in_dim(w, y, 1, keepdims=False)
    w_give = lax.dynamic_index_in_dim(w, 1 - y, 1, keepdims=False)
    w_got = flipped(w_give, "head", 2)
    kv_last, w_got = lax.optimization_barrier((kv_other, w_got))
    kv_own = [
        kv_same,
        flipped(kv_other, "head", plane_bit),
        flipped(kv_same, "head", 2 * plane_bit),
        flipped(kv_last, "head", 3 * plane_bit),
    ]

    (page_a, page_b, kv_own, q), w_got = lax.optimization_barrier(
        ((page_a, page_b, kv_own, q), w_got)
    )
    own_pages = jnp.concatenate([page_a, page_b], 0)
    kv_own = jnp.stack(kv_own, 0)
    pages_y = flipped(own_pages, "head", 2)
    kv_y = flipped(kv_own, "head", 2)
    w_both = jnp.stack([w_keep, w_got], 1)
    w_same = lax.dynamic_index_in_dim(w_both, b, 0, keepdims=False)
    w_other = lax.dynamic_index_in_dim(w_both, 1 - b, 0, keepdims=False)
    w_near = jnp.stack([w_same, flipped(w_other, "head", plane_bit)], 0)
    w_near_x = flipped(w_near, "grp", 1)
    w_far = [flipped(w_same, "head", 2 * plane_bit), flipped(w_other, "head", 3 * plane_bit)]
    pages_c = flipped(own_pages, "head", 1)
    kv_c = flipped(kv_own, "head", 1)
    (pages_y, kv_y), w_far = lax.optimization_barrier(((pages_y, kv_y), w_far))
    pages_cy = flipped(pages_y, "head", 1)
    kv_cy = flipped(kv_y, "head", 1)
    w_far = jnp.stack(w_far, 0)
    q, w_far = lax.optimization_barrier((q, w_far))
    w_far_x = flipped(w_far, "grp", 1)
    w_near_c = flipped(w_near, "head", 1)
    a = attend_pair(
        q, (page_a, page_b, pages_y, pages_c, pages_cy), (kv_own, kv_y, kv_c, kv_cy)
    )
    got = flipped(a[1], "head", 1)
    a, w_near_x, w_far_x, w_near_c = lax.optimization_barrier((a, w_near_x, w_far_x, w_near_c))
    w_far_c = flipped(w_far, "head", 1)
    w_near_cx = flipped(w_near_x, "head", 1)
    w_far_cx = flipped(w_far_x, "head", 1)
    partial = project_pair(
        a,
        got,
        (w_near, w_near_c, w_near_x, w_near_cx),
        (w_far, w_far_c, w_far_x, w_far_cx),
        members // 2,
    )
    parts = [partial[0]] + [flipped(partial[k], "head", 2 * k) for k in (3, 2, 1)]
    return [part[None] for part in parts]


def parts_in_planes(queries, new_kv, cache, w_out):
    n = lax.axis_size("head")
    local_rows, seqs, heads, width = queries.shape
    pair_heads = new_kv.shape[2]
    members = heads // pair_heads
    groups = n // members
    model = w_out.shape[2]
    side = 1 << ((n.bit_length() - 1) // 2)
    side = min(side, heads)
    planes = n // side
    planes_of_seq = heads // side
    pair_groups = [[g * members + m for m in range(members)] for g in range(groups)]
    cross_groups = [[g * members + m for g in range(groups)] for m in range(members)]
    plane_groups = [[p * side + m for m in range(side)] for p in range(planes)]
    column_groups = [[p * side + m for p in range(planes)] for m in range(side)]

    query_slots = queries.reshape(local_rows, n, width).transpose(1, 0, 2)
    q = lax.all_to_all(query_slots, "head", split_axis=0, concat_axis=0, tiled=True)
    q = q.reshape(n * local_rows, width)

    kv_slots = new_kv.reshape(local_rows, groups, 2 * width).transpose(1, 0, 2)
    kv = lax.all_to_all(
        kv_slots, "head", split_axis=0, concat_axis=0, tiled=True, axis_index_groups=cross_groups
    )
    kv = lax.all_gather(kv, "head", axis=0, axis_index_groups=pair_groups)
    pages = lax.all_gather(cache, "head", axis=0, tiled=True, axis_index_groups=pair_groups)

    share = w_out.shape[1]
    w_planes = w_out.reshape(planes_of_seq, side, share, model)
    if planes > planes_of_seq:
        w_planes = jnp.tile(w_planes, (planes // planes_of_seq, 1, 1, 1))
    w = lax.all_to_all(
        w_planes, "head", split_axis=0, concat_axis=0, tiled=True, axis_index_groups=column_groups
    )
    w = lax.all_gather(w, "head", axis=0, axis_index_groups=plane_groups)
    if share % 16:
        w = w.transpose(2, 1, 0, 3, 4).reshape(1, 1, side, width, model)
        w = w.reshape(side, width, model)

    attended = attend(q, pages.reshape(-1, 2 * width), kv)
    a = attended.reshape(planes, side, local_rows, width).transpose(1, 0, 2, 3)
    a = a.reshape(side, planes * local_rows, width)
    a = lax.all_to_all(
        a, "head", split_axis=0, concat_axis=0, tiled=True, axis_index_groups=plane_groups
    )
    if share % 16:
        partial = jnp.einsum("hri,hid->rd", a, w, preferred_element_type=F32).astype(BF16)
    else:
        partial = project(a, w)
    parts = lax.all_to_all(
        partial.reshape(planes, local_rows, model),
        "head",
        split_axis=0,
        concat_axis=0,
        tiled=True,
        axis_index_groups=column_groups,
    )
    parts = parts.reshape(seqs, planes_of_seq, local_rows, model)
    return [parts[:, k] for k in range(planes_of_seq)]


def local(queries, new_kv, cache, resid, w_out, norm_gain, expert_ids, expert_gates, w_in, w_down):
    n = lax.axis_size("head")
    local_rows, seqs, heads, width = queries.shape
    model = resid.shape[2]
    rows = local_rows * seqs
    members = heads // new_kv.shape[2]
    in_pairs = (
        lax.axis_size("grp") == 2
        and seqs == 1
        and new_kv.shape[2] == 2
        and n == heads == 2 * members
        and members == 8
        and cache.shape[0] == 1
        and w_in.shape[0] == 1
        and w_out.shape[1] % 16 == 0
    )
    plan = parts_in_pairs if in_pairs else parts_in_planes
    parts = plan(queries, new_kv, cache, w_out)

    top = expert_ids.shape[2]
    experts = w_in.shape[0] * n
    capacity = max(2, 2 * rows * top // experts)
    ids = expert_ids.transpose(1, 0, 2).reshape(rows, top)
    gates = expert_gates.transpose(1, 0, 2).reshape(rows, top)
    onehot = (ids[:, :, None] == jnp.arange(experts, dtype=jnp.int32)).astype(jnp.int32)
    named = onehot.sum(1)
    before = jnp.cumsum(named, 0) - named
    slots_of = ids * capacity + jnp.sum(onehot * before[:, None, :], 2)
    slots = experts * capacity

    stream, outgoing = route(
        parts, resid.transpose(1, 0, 2), norm_gain[None, :], slots_of.T, slots
    )
    arrived = lax.all_to_all(
        outgoing.reshape(n, slots // n, model), "head", split_axis=0, concat_axis=0, tiled=True
    )
    local_experts = w_in.shape[0]
    if local_experts == 1:
        answered = expert_pair(arrived.reshape(slots, model), w_in[0], w_down[0])
        answered = answered.reshape(n, slots // n, model)
    else:
        arrived = arrived.reshape(n, local_experts, capacity, model).transpose(1, 0, 2, 3)
        arrived = arrived.reshape(local_experts, n * capacity, model)
        answered = jnp.stack([expert(arrived[e], w_in[e], w_down[e]) for e in range(local_experts)])
        answered = answered.reshape(local_experts, n, capacity, model).transpose(1, 0, 2, 3)
        answered = answered.reshape(n, slots // n, model)
    back = lax.all_to_all(answered, "head", split_axis=0, concat_axis=0, tiled=True)
    out = combine(back.reshape(slots, model), stream, slots_of, gates, seqs)
    return out.transpose(1, 0, 2)


def solution(mesh):
    return jax.shard_map(
        local,
        mesh=mesh,
        in_specs=(
            P("head", "grp", None, None),
            P("head", "grp", None, None),
            P(("grp", "head"), None, None),
            P("head", "grp", None),
            P(None, "head", None),
            P(),
            P("head", "grp", None),
            P("head", "grp", None),
            P("head", None, None),
            P("head", None, None),
        ),
        out_specs=P("head", "grp", None),
        check_vma=False,
    )
```

```python
import functools

import jax
import jax.numpy as jnp
from jax import lax
from jax.experimental import pallas as pl
from jax.experimental.pallas import tpu as pltpu
from jax.sharding import PartitionSpec as P

eps_norm = 1e-06
F32 = jnp.float32
BF16 = jnp.bfloat16
HIGH_VMEM = 48 * 2**20
LOG2_E = 1.4426950408889634


def in_hbm():
    return pl.BlockSpec(memory_space=pltpu.HBM)


def in_vmem():
    return pl.BlockSpec(memory_space=pltpu.VMEM)


def attend_kernel(
    block, chunk, width, q_hbm, cache_hbm, kv_hbm, o_ref, q_ref, cache_ref, kv_ref, s0, s1, sems
):
    members, groups, piece, _ = kv_hbm.shape
    length = members * groups * piece
    old = cache_hbm.shape[0]
    scale = width**-0.5
    in_q = pltpu.make_async_copy(q_hbm, q_ref, sems.at[0])
    in_cache = pltpu.make_async_copy(cache_hbm, cache_ref, sems.at[1])
    in_q.start()
    in_cache.start()
    in_kv = []
    for group in range(groups):
        for member in range(members):
            place = (group * members + member) * piece
            copy = pltpu.make_async_copy(
                kv_hbm.at[member, group], kv_ref.at[pl.ds(place, piece)], sems.at[2]
            )
            copy.start()
            in_kv.append(copy)
    in_q.wait()
    in_cache.wait()
    for copy in in_kv:
        copy.wait()
    scores = [s0, s1]

    def pieces(b):
        out = [(True, k, chunk, k) for k in range(0, old, chunk)]
        last = b * block
        for k in range(0, last, chunk):
            out.append((False, k, min(chunk, last - k), old + k))
        out.append((False, last, block, old + last))
        return out

    def make_scores(b, part, running):
        of_cache, first, count, column = part
        keys = (cache_ref if of_cache else kv_ref)[pl.ds(first, count), :width]
        s = lax.dot_general(
            q_ref[pl.ds(b * block, block), :],
            keys,
            (((1,), (1,)), ((), ())),
            preferred_element_type=F32,
        )
        if not of_cache and first == b * block:
            row = lax.broadcasted_iota(jnp.int32, s.shape, 0)
            col = lax.broadcasted_iota(jnp.int32, s.shape, 1)
            s = jnp.where(col <= row, s, -jnp.inf)
        scores[b % 2][:, pl.ds(column, count)] = s
        for k in range(0, count, 128):
            piece_max = s[:, k : k + 128]
            running = piece_max if running is None else jnp.maximum(running, piece_max)
        return running

    def use_scores(b, part, top, total, acc):
        of_cache, first, count, column = part
        values = (cache_ref if of_cache else kv_ref)[pl.ds(first, count), width:]
        e = jnp.exp((scores[b % 2][:, pl.ds(column, count)] - top) * scale)
        for k in range(0, count, 128):
            total = e[:, k : k + 128] if total is None else total + e[:, k : k + 128]
        product = jnp.dot(e.astype(BF16), values, preferred_element_type=F32)
        return total, product if acc is None else acc + product

    blocks = length // block
    running = None
    for part in pieces(0):
        running = make_scores(0, part, running)
    for b in range(blocks):
        top = jnp.max(running, 1, keepdims=True)
        now, later = pieces(b), pieces(b + 1) if b + 1 < blocks else []
        running, total, acc = None, None, None
        for k in range(max(len(now), len(later))):
            if k < len(now):
                total, acc = use_scores(b, now[k], top, total, acc)
            if k < len(later):
                running = make_scores(b + 1, later[k], running)
        o_ref[pl.ds(b * block, block), :] = (acc / jnp.sum(total, 1, keepdims=True)).astype(BF16)


def attend(q, cache, kv):
    length, width = q.shape
    old = cache.shape[0]
    block = min(256, length)
    chunk = min(512, old)
    return pl.pallas_call(
        functools.partial(attend_kernel, block, chunk, width),
        out_shape=jax.ShapeDtypeStruct((length, width), BF16),
        in_specs=[in_hbm()] * 3,
        out_specs=in_vmem(),
        scratch_shapes=[
            pltpu.VMEM((length, width), BF16),
            pltpu.VMEM((old, 2 * width), BF16),
            pltpu.VMEM((length, 2 * width), BF16),
            pltpu.VMEM((block, old + length), F32),
            pltpu.VMEM((block, old + length), F32),
            pltpu.SemaphoreType.DMA((3,)),
        ],
        compiler_params=pltpu.CompilerParams(vmem_limit_bytes=HIGH_VMEM),
        cost_estimate=pl.CostEstimate(
            flops=4 * length * (old + length // 2) * width,
            bytes_accessed=4 * (2 * length + 2 * old) * width,
            transcendentals=length * (old + length // 2),
        ),
        name="attend",
    )(q, cache, kv)


def attend_pair_kernel(
    block,
    chunk,
    width,
    q_hbm,
    page_a,
    page_b,
    page_y,
    page_c,
    page_cy,
    kv_own,
    kv_c,
    o_ref,
    q_ref,
    old_ref,
    kv_ref,
    s0,
    s1,
    sems,
):
    me = lax.axis_index("head")
    members, heads, piece, _ = q_hbm.shape
    length = members * piece
    planes, sides = kv_own.shape[:2]
    old = old_ref.shape[0]
    earlier_group = me // members > 0
    core = lax.rem(me, 2)
    copies = []

    def bring(source, target, sem):
        copy = pltpu.make_async_copy(source, target, sems.at[sem])
        copy.start()
        copies.append(copy)

    for member in range(members):
        for head in range(heads):
            bring(q_hbm.at[member, head], q_ref.at[head, pl.ds(member * piece, piece)], 0)
    place = 0
    for page in (page_a, page_b, page_y, page_c, page_cy):
        count = page.shape[0]
        bring(page, old_ref.at[pl.ds(place, count)], 1)
        place += count
    for flip, pieces_of in ((0, kv_own), (1, kv_c)):
        for t in range(planes):
            for u in range(sides):
                number = jnp.bitwise_and(
                    jnp.bitwise_xor(me, flip ^ (2 * u) ^ (t * (members // 2))), members - 1
                )
                start = pl.multiple_of(number * piece, piece)
                area = 0 if t * (members // 2) >= members else length
                bring(pieces_of.at[t, u], kv_ref.at[pl.ds(area + start, piece)], 2)
    for copy in copies:
        copy.wait()
    scale = width**-0.5 * LOG2_E
    scores = [s0, s1]
    blocks = length // block
    units = [(head, b) for head in range(heads) for b in range(blocks)]

    def pieces(unit):
        _, b = units[unit]
        out = [("old", k, chunk, k) for k in range(0, old, chunk)]
        out += [("past", k, chunk, old + k) for k in range(0, length, chunk)]
        last = b * block
        for k in range(0, last, chunk):
            out.append(("new", length + k, min(chunk, last - k), old + length + k))
        out.append(("edge", length + last, block, old + length + last))
        return out

    def make_scores(unit, part, running):
        kind, first, count, column = part
        head, b = units[unit]
        keys = (old_ref if kind == "old" else kv_ref)[pl.ds(first, count), :width]
        s = lax.dot_general(
            q_ref[head, pl.ds(b * block, block), :],
            keys,
            (((1,), (1,)), ((), ())),
            preferred_element_type=F32,
        )
        if kind == "past":
            s = jnp.where(earlier_group, s, -jnp.inf)
        if kind == "edge":
            row = lax.broadcasted_iota(jnp.int32, s.shape, 0)
            col = lax.broadcasted_iota(jnp.int32, s.shape, 1)
            s = jnp.where(col <= row, s, -jnp.inf)
        scores[unit % 2][:, pl.ds(column, count)] = s
        for k in range(0, count, 128):
            piece_max = s[:, k : k + 128]
            running = piece_max if running is None else jnp.maximum(running, piece_max)
        return running

    def use_scores(unit, part, top, total, acc):
        kind, first, count, column = part
        values = (old_ref if kind == "old" else kv_ref)[pl.ds(first, count), width:]
        e = jnp.exp2((scores[unit % 2][:, pl.ds(column, count)] - top) * scale)
        for k in range(0, count, 128):
            total = e[:, k : k + 128] if total is None else total + e[:, k : k + 128]
        product = jnp.dot(e.astype(BF16), values, preferred_element_type=F32)
        return total, product if acc is None else acc + product

    running = None
    for part in pieces(0):
        running = make_scores(0, part, running)
    for unit, (head, b) in enumerate(units):
        top = jnp.max(running, 1, keepdims=True)
        now = pieces(unit)
        later = pieces(unit + 1) if unit + 1 < len(units) else []
        running, total, acc = None, None, None
        for k in range(max(len(now), len(later))):
            if k < len(now):
                total, acc = use_scores(unit, now[k], top, total, acc)
            if k < len(later):
                running = make_scores(unit + 1, later[k], running)
        done = (acc / jnp.sum(total, 1, keepdims=True)).astype(BF16)
        for k in range(0, block, piece):
            member = (b * block + k) // piece
            side = jnp.bitwise_xor(core, member % 2)
            o_ref[side, pl.ds((member // 2) * piece, piece), pl.ds(head * width, width)] = done[
                k : k + piece
            ]


def attend_pair(q, pages, kvs):
    members, heads, piece, width = q.shape
    length = members * piece
    old = sum(page.shape[0] for page in pages)
    block = 2 * piece
    chunk = min(512, old, length)
    keys = old + 2 * length
    return pl.pallas_call(
        functools.partial(attend_pair_kernel, block, chunk, width),
        out_shape=jax.ShapeDtypeStruct((2, length // 2, heads * width), BF16),
        in_specs=[in_hbm()] * (1 + len(pages) + len(kvs)),
        out_specs=in_vmem(),
        scratch_shapes=[
            pltpu.VMEM((heads, length, width), BF16),
            pltpu.VMEM((old, 2 * width), BF16),
            pltpu.VMEM((2 * length, 2 * width), BF16),
            pltpu.VMEM((block, keys), F32),
            pltpu.VMEM((block, keys), F32),
            pltpu.SemaphoreType.DMA((3,)),
        ],
        compiler_params=pltpu.CompilerParams(vmem_limit_bytes=HIGH_VMEM),
        cost_estimate=pl.CostEstimate(
            flops=4 * heads * length * (keys - length // 2) * width,
            bytes_accessed=4 * (heads * length + keys) * width,
            transcendentals=heads * length * (keys - length // 2),
        ),
        name="attend",
    )(q, *pages, *kvs)


def project_pair_kernel(a_ref, got_ref, *refs):
    near, far, outs, (w_ref, all_ref, sems) = refs[:4], refs[4:8], refs[8:-3], refs[-3:]
    me = lax.axis_index("head")
    half = lax.axis_index("grp")
    core = lax.rem(me, 2)
    chip = jnp.bitwise_and(me // 2, len(outs) - 1)
    steps, sides, heads, share, columns = near[0].shape
    width = w_ref.shape[1]
    copies = []
    for first, given in ((0, near), (steps, far)):
        for flip, x, pieces_of in zip((0, 1, 0, 1), (0, 0, 1, 1), given):
            column = pl.multiple_of(jnp.bitwise_xor(half, x) * columns, columns)
            for t in range(steps):
                for u in range(sides):
                    number = jnp.bitwise_xor(me, flip ^ (2 * u) ^ (4 * (first + t)))
                    row = pl.multiple_of(number * share, share)
                    copy = pltpu.make_async_copy(
                        pieces_of.at[t, u],
                        w_ref.at[:, pl.ds(row, share), pl.ds(column, columns)],
                        sems.at[0],
                    )
                    copy.start()
                    copies.append(copy)
    for copy in copies:
        copy.wait()
    acc = None
    for k in range(heads):
        mine = k < heads // 2
        at = pl.ds((k % (heads // 2)) * width, width)
        rows_of = a_ref[0, :, at] if mine else got_ref[:, at]
        head = jnp.bitwise_xor(core, 0 if mine else 1) * (heads // 2) + k % (heads // 2)
        part = jnp.dot(rows_of, w_ref[head], preferred_element_type=F32)
        acc = part if acc is None else acc + part
    all_ref[...] = acc.astype(BF16)
    rows = outs[0].shape[0]
    for k, out in enumerate(outs):
        start = pl.multiple_of(jnp.bitwise_xor(chip, k) * rows, rows)
        out[...] = all_ref[pl.ds(start, rows), :]


def project_pair(a, got, near, far, parts):
    _, _, heads, share, columns = near[0].shape
    rows = got.shape[0]
    width = 2 * got.shape[1] // heads
    model = 2 * columns
    return pl.pallas_call(
        project_pair_kernel,
        out_shape=[jax.ShapeDtypeStruct((rows // parts, model), BF16)] * parts,
        in_specs=[in_vmem(), in_vmem()] + [in_hbm()] * 8,
        out_specs=[in_vmem()] * parts,
        scratch_shapes=[
            pltpu.VMEM((heads, width, model), BF16),
            pltpu.VMEM((rows, model), BF16),
            pltpu.SemaphoreType.DMA((1,)),
        ],
        compiler_params=pltpu.CompilerParams(vmem_limit_bytes=HIGH_VMEM),
        cost_estimate=pl.CostEstimate(
            flops=2 * heads * rows * width * model,
            bytes_accessed=2 * (heads * width * model + heads * rows * width + rows * model),
            transcendentals=0,
        ),
        name="project",
    )(a, got, *near, *far)


def project_kernel(a_ref, w_ref, o_ref):
    members = a_ref.shape[0]
    planes, share = w_ref.shape[1], w_ref.shape[3]
    acc = None
    for head in range(members):
        w = jnp.concatenate(
            [w_ref[m, p, head] for p in range(planes) for m in range(members)], 0
        )
        part = jnp.dot(a_ref[head], w, preferred_element_type=F32)
        acc = part if acc is None else acc + part
    o_ref[...] = acc.astype(BF16)


def project(a, w):
    members, rows, width = a.shape
    planes, share, model = w.shape[1], w.shape[3], w.shape[4]
    tile = min(512, model)
    return pl.pallas_call(
        project_kernel,
        grid=(model // tile,),
        out_shape=jax.ShapeDtypeStruct((rows, model), BF16),
        in_specs=[
            pl.BlockSpec((members, rows, width), lambda t: (0, 0, 0)),
            pl.BlockSpec((members, planes, members, share, tile), lambda t: (0, 0, 0, 0, t)),
        ],
        out_specs=pl.BlockSpec((rows, tile), lambda t: (0, t)),
        compiler_params=pltpu.CompilerParams(vmem_limit_bytes=HIGH_VMEM),
        cost_estimate=pl.CostEstimate(
            flops=2 * members * rows * width * model,
            bytes_accessed=2 * (members * width * model + members * rows * width + rows * model),
            transcendentals=0,
        ),
        name="project",
    )(a, w)


def route_kernel(resid_ref, gain_ref, slots_ref, *refs):
    parts_refs, (stream_ref, out_ref) = refs[:-2], refs[-2:]
    seqs = resid_ref.shape[0]
    streams = []
    for seq in range(seqs):
        stream = resid_ref[seq].astype(F32)
        projected = parts_refs[0][seq].astype(F32)
        for part in parts_refs[1:]:
            projected = projected + part[seq].astype(F32)
        streams.append(stream + projected)
    stream = jnp.concatenate(streams, 0) if seqs > 1 else streams[0]
    stream_ref[...] = stream
    normed = stream * lax.rsqrt(jnp.mean(stream * stream, 1, keepdims=True) + eps_norm)
    normed = (normed * gain_ref[...]).astype(BF16)
    slots, rows = out_ref.shape[0], stream.shape[0]
    place = lax.broadcasted_iota(jnp.int32, (slots, rows), 0)
    hit = place == slots_ref[0:1, :]
    for k in range(1, slots_ref.shape[0]):
        hit = hit | (place == slots_ref[k : k + 1, :])
    out_ref[...] = jnp.dot(hit.astype(BF16), normed, preferred_element_type=F32).astype(BF16)


def route(parts, resid, gain, slots_of, slots):
    seqs, local_rows, model = resid.shape
    rows = seqs * local_rows
    return pl.pallas_call(
        route_kernel,
        out_shape=(
            jax.ShapeDtypeStruct((rows, model), F32),
            jax.ShapeDtypeStruct((slots, model), BF16),
        ),
        in_specs=[in_vmem()] * (3 + len(parts)),
        out_specs=(in_vmem(), in_vmem()),
        compiler_params=pltpu.CompilerParams(vmem_limit_bytes=HIGH_VMEM),
        cost_estimate=pl.CostEstimate(
            flops=2 * slots * rows * model,
            bytes_accessed=2 * (len(parts) + 3 + slots // rows) * rows * model,
            transcendentals=0,
        ),
        name="route",
    )(resid, gain, slots_of, *parts)


def expert_kernel(x_ref, w_in_ref, w_down_ref, o_ref):
    hidden_width = w_down_ref.shape[0]
    inner = jnp.dot(x_ref[...], w_in_ref[...], preferred_element_type=F32)
    gate = inner[:, :hidden_width]
    hidden = (gate / (1.0 + jnp.exp(-gate)) * inner[:, hidden_width:]).astype(BF16)
    o_ref[...] = jnp.dot(hidden, w_down_ref[...], preferred_element_type=F32).astype(BF16)


def expert(x, w_in, w_down):
    rows, model = x.shape
    hidden_width = w_down.shape[0]
    return pl.pallas_call(
        expert_kernel,
        out_shape=jax.ShapeDtypeStruct((rows, model), BF16),
        in_specs=[in_vmem()] * 3,
        out_specs=in_vmem(),
        compiler_params=pltpu.CompilerParams(vmem_limit_bytes=HIGH_VMEM),
        cost_estimate=pl.CostEstimate(
            flops=6 * rows * model * hidden_width,
            bytes_accessed=2 * (2 * rows * model + 3 * model * hidden_width),
            transcendentals=rows * hidden_width,
        ),
        name="expert",
    )(x, w_in, w_down)


def expert_pair(x, w_in, w_down):
    rows, model = x.shape
    hidden_width = w_down.shape[0]
    parts = 4
    depth = model // parts

    def kernel(x_hbm, in_hbm_ref, down_hbm, o_hbm, x_ref, in_ref, down_ref, o_ref, sems):
        bring_x = pltpu.make_async_copy(x_hbm, x_ref, sems.at[parts])
        bring_x.start()
        bring_in = []
        for k in range(parts):
            at = pl.ds(k * depth, depth)
            bring_in.append(pltpu.make_async_copy(in_hbm_ref.at[at], in_ref.at[at], sems.at[k]))
            bring_in[k].start()
        bring_down = pltpu.make_async_copy(down_hbm, down_ref, sems.at[parts + 1])
        bring_down.start()
        bring_x.wait()
        inner = None
        for k in range(parts):
            bring_in[k].wait()
            at = pl.ds(k * depth, depth)
            part = jnp.dot(x_ref[:, at], in_ref[at, :], preferred_element_type=F32)
            inner = part if inner is None else inner + part
        gate = inner[:, :hidden_width]
        hidden = (gate / (1.0 + jnp.exp(-gate)) * inner[:, hidden_width:]).astype(BF16)
        bring_down.wait()
        o_ref[...] = jnp.dot(hidden, down_ref[...], preferred_element_type=F32).astype(BF16)
        back = pltpu.make_async_copy(o_ref, o_hbm, sems.at[parts + 2])
        back.start()
        back.wait()

    return pl.pallas_call(
        kernel,
        out_shape=jax.ShapeDtypeStruct((rows, model), BF16),
        in_specs=[in_hbm()] * 3,
        out_specs=in_hbm(),
        scratch_shapes=[
            pltpu.VMEM((rows, model), BF16),
            pltpu.VMEM(w_in.shape, BF16),
            pltpu.VMEM(w_down.shape, BF16),
            pltpu.VMEM((rows, model), BF16),
            pltpu.SemaphoreType.DMA((parts + 3,)),
        ],
        compiler_params=pltpu.CompilerParams(vmem_limit_bytes=HIGH_VMEM),
        cost_estimate=pl.CostEstimate(
            flops=6 * rows * model * hidden_width,
            bytes_accessed=2 * (2 * rows * model + 3 * model * hidden_width),
            transcendentals=rows * hidden_width,
        ),
        name="expert",
    )(x, w_in, w_down)


def combine_kernel(seqs, back_ref, stream_ref, slots_ref, gates_ref, o_ref):
    slots = back_ref.shape[0]
    rows = stream_ref.shape[0]
    place = lax.broadcasted_iota(jnp.int32, (rows, slots), 1)
    total = stream_ref[...]
    gathered = None
    for k in range(slots_ref.shape[1]):
        pick = (place == slots_ref[:, k : k + 1]).astype(BF16)
        picked = jnp.dot(pick, back_ref[...], preferred_element_type=F32)
        part = picked * gates_ref[:, k : k + 1]
        gathered = part if gathered is None else gathered + part
    out = (total + gathered).astype(BF16)
    local_rows = rows // seqs
    for seq in range(seqs):
        o_ref[seq] = out[seq * local_rows : (seq + 1) * local_rows]


def combine(back, stream, slots_of, gates, seqs):
    slots, model = back.shape
    rows = stream.shape[0]
    top = slots_of.shape[1]
    return pl.pallas_call(
        functools.partial(combine_kernel, seqs),
        out_shape=jax.ShapeDtypeStruct((seqs, rows // seqs, model), BF16),
        in_specs=[in_vmem()] * 4,
        out_specs=in_vmem(),
        compiler_params=pltpu.CompilerParams(vmem_limit_bytes=HIGH_VMEM),
        cost_estimate=pl.CostEstimate(
            flops=2 * top * slots * rows * model,
            bytes_accessed=2 * slots * model + 6 * rows * model,
            transcendentals=0,
        ),
        name="combine",
    )(back, stream, slots_of, gates)


def flipped(value, axis, mask):
    pairs = [(source, source ^ mask) for source in range(lax.axis_size(axis))]
    return lax.ppermute(value, axis, pairs)


def parts_in_pairs(queries, new_kv, cache, w_out):
    n = lax.axis_size("head")
    local_rows, _, heads, width = queries.shape
    pair_heads = new_kv.shape[2]
    members = heads // pair_heads
    model = w_out.shape[2]
    share = w_out.shape[1]
    me = lax.axis_index("head")
    plane_bit = members // 2
    planes = n // plane_bit
    b = (me // plane_bit) % 2
    y = (me // 2) % 2
    group_sets = [[g * members + m for m in range(members)] for g in range(n // members)]

    query_slots = queries.reshape(local_rows, heads, width).transpose(1, 0, 2)
    query_slots = query_slots.reshape(members, heads // members, local_rows, width)
    q = lax.all_to_all(
        query_slots, "head", split_axis=0, concat_axis=0, tiled=True, axis_index_groups=group_sets
    )

    def page_target(source, other):
        p, plane, rest = source // members, (source // plane_bit) % 2, source % plane_bit
        return (plane ^ other) * members + p * plane_bit + rest

    page_a, page_b = (
        lax.ppermute(cache[0], "head", [(d, page_target(d, other)) for d in range(n)])
        for other in range(2)
    )
    kv_heads = new_kv.reshape(local_rows, pair_heads, 2 * width).transpose(1, 0, 2)
    kv_beside = flipped(kv_heads, "head", 2)

    columns = model // 2
    w = lax.dynamic_slice_in_dim(w_out, lax.axis_index("grp") * columns, columns, 2)
    w = w.reshape(2, 2, heads // 4, share, columns)
    w_keep = lax.dynamic_index_in_dim(w, y, 1, keepdims=False)
    w_give = lax.dynamic_index_in_dim(w, 1 - y, 1, keepdims=False)
    w_got = flipped(w_give, "head", 2)

    page_a, page_b, kv_beside, w_got = lax.optimization_barrier(
        (page_a, page_b, kv_beside, w_got)
    )
    kv_both = jnp.stack([kv_heads, kv_beside], 1)
    kv_same = lax.dynamic_index_in_dim(kv_both, b, 0, keepdims=False)
    kv_other = lax.dynamic_index_in_dim(kv_both, 1 - b, 0, keepdims=False)
    kv_own = [kv_same]
    for t in range(1, planes):
        kv_own.append(flipped(kv_other if t % 2 else kv_same, "head", t * plane_bit))
    own_pages = jnp.concatenate([page_a, page_b], 0)
    pages_y = flipped(own_pages, "head", 2)
    w_both = jnp.stack([w_keep, w_got], 1)
    w_same = lax.dynamic_index_in_dim(w_both, b, 0, keepdims=False)
    w_other = lax.dynamic_index_in_dim(w_both, 1 - b, 0, keepdims=False)
    w_first = flipped(w_other, "head", plane_bit)
    pages_y, kv_own, w_first, q = lax.optimization_barrier((pages_y, kv_own, w_first, q))

    kv_own = jnp.stack(kv_own, 0)
    kv_c = flipped(kv_own, "head", 1)
    pages_c = flipped(own_pages, "head", 1)
    pages_cy = flipped(pages_y, "head", 1)
    w_near = jnp.stack([w_same, w_first], 0)
    w_far = flipped(w_near, "head", members)
    w_near_x = flipped(w_near, "grp", 1)
    a = attend_pair(q, (page_a, page_b, pages_y, pages_c, pages_cy), (kv_own, kv_c))
    got = flipped(a[1], "head", 1)
    a, w_far, w_near_x = lax.optimization_barrier((a, w_far, w_near_x))
    w_far_x = flipped(w_far, "grp", 1)
    w_near_c = flipped(w_near, "head", 1)
    w_far_c = flipped(w_far, "head", 1)
    w_near_cx = flipped(w_near_x, "head", 1)
    w_far_cx = flipped(w_far_x, "head", 1)
    partial = project_pair(
        a,
        got,
        (w_near, w_near_c, w_near_x, w_near_cx),
        (w_far, w_far_c, w_far_x, w_far_cx),
        members // 2,
    )
    parts = [partial[0]] + [flipped(partial[k], "head", 2 * k) for k in (3, 2, 1)]
    return [part[None] for part in parts]


def parts_in_planes(queries, new_kv, cache, w_out):
    n = lax.axis_size("head")
    local_rows, seqs, heads, width = queries.shape
    pair_heads = new_kv.shape[2]
    members = heads // pair_heads
    groups = n // members
    model = w_out.shape[2]
    side = 1 << ((n.bit_length() - 1) // 2)
    side = min(side, heads)
    planes = n // side
    planes_of_seq = heads // side
    pair_groups = [[g * members + m for m in range(members)] for g in range(groups)]
    cross_groups = [[g * members + m for g in range(groups)] for m in range(members)]
    plane_groups = [[p * side + m for m in range(side)] for p in range(planes)]
    column_groups = [[p * side + m for p in range(planes)] for m in range(side)]

    query_slots = queries.reshape(local_rows, n, width).transpose(1, 0, 2)
    q = lax.all_to_all(query_slots, "head", split_axis=0, concat_axis=0, tiled=True)
    q = q.reshape(n * local_rows, width)

    kv_slots = new_kv.reshape(local_rows, groups, 2 * width).transpose(1, 0, 2)
    kv = lax.all_to_all(
        kv_slots, "head", split_axis=0, concat_axis=0, tiled=True, axis_index_groups=cross_groups
    )
    kv = lax.all_gather(kv, "head", axis=0, axis_index_groups=pair_groups)
    pages = lax.all_gather(cache, "head", axis=0, tiled=True, axis_index_groups=pair_groups)

    share = w_out.shape[1]
    w_planes = w_out.reshape(planes_of_seq, side, share, model)
    if planes > planes_of_seq:
        w_planes = jnp.tile(w_planes, (planes // planes_of_seq, 1, 1, 1))
    w = lax.all_to_all(
        w_planes, "head", split_axis=0, concat_axis=0, tiled=True, axis_index_groups=column_groups
    )
    w = lax.all_gather(w, "head", axis=0, axis_index_groups=plane_groups)
    if share % 16:
        w = w.transpose(2, 1, 0, 3, 4).reshape(1, 1, side, width, model)
        w = w.reshape(side, width, model)

    attended = attend(q, pages.reshape(-1, 2 * width), kv)
    a = attended.reshape(planes, side, local_rows, width).transpose(1, 0, 2, 3)
    a = a.reshape(side, planes * local_rows, width)
    a = lax.all_to_all(
        a, "head", split_axis=0, concat_axis=0, tiled=True, axis_index_groups=plane_groups
    )
    if share % 16:
        partial = jnp.einsum("hri,hid->rd", a, w, preferred_element_type=F32).astype(BF16)
    else:
        partial = project(a, w)
    parts = lax.all_to_all(
        partial.reshape(planes, local_rows, model),
        "head",
        split_axis=0,
        concat_axis=0,
        tiled=True,
        axis_index_groups=column_groups,
    )
    parts = parts.reshape(seqs, planes_of_seq, local_rows, model)
    return [parts[:, k] for k in range(planes_of_seq)]


def local(queries, new_kv, cache, resid, w_out, norm_gain, expert_ids, expert_gates, w_in, w_down):
    n = lax.axis_size("head")
    local_rows, seqs, heads, width = queries.shape
    model = resid.shape[2]
    rows = local_rows * seqs
    members = heads // new_kv.shape[2]
    in_pairs = (
        lax.axis_size("grp") == 2
        and seqs == 1
        and new_kv.shape[2] == 2
        and n == heads == 2 * members
        and members == 8
        and cache.shape[0] == 1
        and w_in.shape[0] == 1
        and w_out.shape[1] % 16 == 0
    )
    plan = parts_in_pairs if in_pairs else parts_in_planes
    parts = plan(queries, new_kv, cache, w_out)

    top = expert_ids.shape[2]
    experts = w_in.shape[0] * n
    capacity = max(2, 2 * rows * top // experts)
    ids = expert_ids.transpose(1, 0, 2).reshape(rows, top)
    gates = expert_gates.transpose(1, 0, 2).reshape(rows, top)
    onehot = (ids[:, :, None] == jnp.arange(experts, dtype=jnp.int32)).astype(jnp.int32)
    named = onehot.sum(1)
    before = jnp.cumsum(named, 0) - named
    slots_of = ids * capacity + jnp.sum(onehot * before[:, None, :], 2)
    slots = experts * capacity

    stream, outgoing = route(
        parts, resid.transpose(1, 0, 2), norm_gain[None, :], slots_of.T, slots
    )
    arrived = lax.all_to_all(
        outgoing.reshape(n, slots // n, model), "head", split_axis=0, concat_axis=0, tiled=True
    )
    local_experts = w_in.shape[0]
    if local_experts == 1:
        answered = expert_pair(arrived.reshape(slots, model), w_in[0], w_down[0])
        answered = answered.reshape(n, slots // n, model)
    else:
        arrived = arrived.reshape(n, local_experts, capacity, model).transpose(1, 0, 2, 3)
        arrived = arrived.reshape(local_experts, n * capacity, model)
        answered = jnp.stack([expert(arrived[e], w_in[e], w_down[e]) for e in range(local_experts)])
        answered = answered.reshape(local_experts, n, capacity, model).transpose(1, 0, 2, 3)
        answered = answered.reshape(n, slots // n, model)
    back = lax.all_to_all(answered, "head", split_axis=0, concat_axis=0, tiled=True)
    out = combine(back.reshape(slots, model), stream, slots_of, gates, seqs)
    return out.transpose(1, 0, 2)


def solution(mesh):
    return jax.shard_map(
        local,
        mesh=mesh,
        in_specs=(
            P("head", "grp", None, None),
            P("head", "grp", None, None),
            P(("grp", "head"), None, None),
            P("head", "grp", None),
            P(None, "head", None),
            P(),
            P("head", "grp", None),
            P("head", "grp", None),
            P("head", None, None),
            P("head", None, None),
        ),
        out_specs=P("head", "grp", None),
        check_vma=False,
    )
```

```python
import functools

import jax
import jax.numpy as jnp
from jax import lax
from jax.experimental import pallas as pl
from jax.experimental.pallas import tpu as pltpu
from jax.sharding import PartitionSpec as P

eps_norm = 1e-06
F32 = jnp.float32
BF16 = jnp.bfloat16
HIGH_VMEM = 48 * 2**20
LOG2_E = 1.4426950408889634


def in_hbm():
    return pl.BlockSpec(memory_space=pltpu.HBM)


def in_vmem():
    return pl.BlockSpec(memory_space=pltpu.VMEM)


def attend_kernel(
    block, chunk, width, q_hbm, cache_hbm, kv_hbm, o_ref, q_ref, cache_ref, kv_ref, s0, s1, sems
):
    members, groups, piece, _ = kv_hbm.shape
    length = members * groups * piece
    old = cache_hbm.shape[0]
    scale = width**-0.5
    in_q = pltpu.make_async_copy(q_hbm, q_ref, sems.at[0])
    in_cache = pltpu.make_async_copy(cache_hbm, cache_ref, sems.at[1])
    in_q.start()
    in_cache.start()
    in_kv = []
    for group in range(groups):
        for member in range(members):
            place = (group * members + member) * piece
            copy = pltpu.make_async_copy(
                kv_hbm.at[member, group], kv_ref.at[pl.ds(place, piece)], sems.at[2]
            )
            copy.start()
            in_kv.append(copy)
    in_q.wait()
    in_cache.wait()
    for copy in in_kv:
        copy.wait()
    scores = [s0, s1]

    def pieces(b):
        out = [(True, k, chunk, k) for k in range(0, old, chunk)]
        last = b * block
        for k in range(0, last, chunk):
            out.append((False, k, min(chunk, last - k), old + k))
        out.append((False, last, block, old + last))
        return out

    def make_scores(b, part, running):
        of_cache, first, count, column = part
        keys = (cache_ref if of_cache else kv_ref)[pl.ds(first, count), :width]
        s = lax.dot_general(
            q_ref[pl.ds(b * block, block), :],
            keys,
            (((1,), (1,)), ((), ())),
            preferred_element_type=F32,
        )
        if not of_cache and first == b * block:
            row = lax.broadcasted_iota(jnp.int32, s.shape, 0)
            col = lax.broadcasted_iota(jnp.int32, s.shape, 1)
            s = jnp.where(col <= row, s, -jnp.inf)
        scores[b % 2][:, pl.ds(column, count)] = s
        for k in range(0, count, 128):
            piece_max = s[:, k : k + 128]
            running = piece_max if running is None else jnp.maximum(running, piece_max)
        return running

    def use_scores(b, part, top, total, acc):
        of_cache, first, count, column = part
        values = (cache_ref if of_cache else kv_ref)[pl.ds(first, count), width:]
        e = jnp.exp((scores[b % 2][:, pl.ds(column, count)] - top) * scale)
        for k in range(0, count, 128):
            total = e[:, k : k + 128] if total is None else total + e[:, k : k + 128]
        product = jnp.dot(e.astype(BF16), values, preferred_element_type=F32)
        return total, product if acc is None else acc + product

    blocks = length // block
    running = None
    for part in pieces(0):
        running = make_scores(0, part, running)
    for b in range(blocks):
        top = jnp.max(running, 1, keepdims=True)
        now, later = pieces(b), pieces(b + 1) if b + 1 < blocks else []
        running, total, acc = None, None, None
        for k in range(max(len(now), len(later))):
            if k < len(now):
                total, acc = use_scores(b, now[k], top, total, acc)
            if k < len(later):
                running = make_scores(b + 1, later[k], running)
        o_ref[pl.ds(b * block, block), :] = (acc / jnp.sum(total, 1, keepdims=True)).astype(BF16)


def attend(q, cache, kv):
    length, width = q.shape
    old = cache.shape[0]
    block = min(256, length)
    chunk = min(512, old)
    return pl.pallas_call(
        functools.partial(attend_kernel, block, chunk, width),
        out_shape=jax.ShapeDtypeStruct((length, width), BF16),
        in_specs=[in_hbm()] * 3,
        out_specs=in_vmem(),
        scratch_shapes=[
            pltpu.VMEM((length, width), BF16),
            pltpu.VMEM((old, 2 * width), BF16),
            pltpu.VMEM((length, 2 * width), BF16),
            pltpu.VMEM((block, old + length), F32),
            pltpu.VMEM((block, old + length), F32),
            pltpu.SemaphoreType.DMA((3,)),
        ],
        compiler_params=pltpu.CompilerParams(vmem_limit_bytes=HIGH_VMEM),
        cost_estimate=pl.CostEstimate(
            flops=4 * length * (old + length // 2) * width,
            bytes_accessed=4 * (2 * length + 2 * old) * width,
            transcendentals=length * (old + length // 2),
        ),
        name="attend",
    )(q, cache, kv)


def attend_pair_kernel(
    block,
    chunk,
    width,
    q_hbm,
    page_a,
    page_b,
    page_y,
    page_c,
    page_cy,
    kv_own,
    kv_c,
    o_ref,
    q_ref,
    old_ref,
    kv_ref,
    s0,
    s1,
    sems,
):
    me = lax.axis_index("head")
    members, heads, piece, _ = q_hbm.shape
    length = members * piece
    planes, sides = kv_own.shape[:2]
    old = old_ref.shape[0]
    earlier_group = me // members > 0
    core = lax.rem(me, 2)
    chip = jnp.bitwise_and(me // 2, members // 2 - 1)
    copies = []

    def bring(source, target, sem):
        copy = pltpu.make_async_copy(source, target, sems.at[sem])
        copy.start()
        copies.append(copy)

    for member in range(members):
        for head in range(heads):
            bring(q_hbm.at[member, head], q_ref.at[head, pl.ds(member * piece, piece)], 0)
    place = 0
    for page in (page_a, page_b, page_y, page_c, page_cy):
        count = page.shape[0]
        bring(page, old_ref.at[pl.ds(place, count)], 1)
        place += count
    for flip, pieces_of in ((0, kv_own), (1, kv_c)):
        for t in range(planes):
            for u in range(sides):
                number = jnp.bitwise_and(
                    jnp.bitwise_xor(me, flip ^ (2 * u) ^ (t * (members // 2))), members - 1
                )
                start = pl.multiple_of(number * piece, piece)
                area = 0 if t * (members // 2) >= members else length
                bring(pieces_of.at[t, u], kv_ref.at[pl.ds(area + start, piece)], 2)
    for copy in copies:
        copy.wait()
    scale = width**-0.5 * LOG2_E
    scores = [s0, s1]
    blocks = length // block
    units = [(head, b) for head in range(heads) for b in range(blocks)]

    def pieces(unit):
        _, b = units[unit]
        out = [("old", k, chunk, k) for k in range(0, old, chunk)]
        out += [("past", k, chunk, old + k) for k in range(0, length, chunk)]
        last = b * block
        for k in range(0, last, chunk):
            out.append(("new", length + k, min(chunk, last - k), old + length + k))
        out.append(("edge", length + last, block, old + length + last))
        return out

    def make_scores(unit, part, running):
        kind, first, count, column = part
        head, b = units[unit]
        keys = (old_ref if kind == "old" else kv_ref)[pl.ds(first, count), :width]
        s = lax.dot_general(
            q_ref[head, pl.ds(b * block, block), :],
            keys,
            (((1,), (1,)), ((), ())),
            preferred_element_type=F32,
        )
        if kind == "past":
            s = jnp.where(earlier_group, s, -jnp.inf)
        if kind == "edge":
            row = lax.broadcasted_iota(jnp.int32, s.shape, 0)
            col = lax.broadcasted_iota(jnp.int32, s.shape, 1)
            s = jnp.where(col <= row, s, -jnp.inf)
        scores[unit % 2][:, pl.ds(column, count)] = s
        for k in range(0, count, 128):
            piece_max = s[:, k : k + 128]
            running = piece_max if running is None else jnp.maximum(running, piece_max)
        return running

    def use_scores(unit, part, top, total, acc):
        kind, first, count, column = part
        values = (old_ref if kind == "old" else kv_ref)[pl.ds(first, count), width:]
        e = jnp.exp2((scores[unit % 2][:, pl.ds(column, count)] - top) * scale)
        for k in range(0, count, 128):
            total = e[:, k : k + 128] if total is None else total + e[:, k : k + 128]
        product = jnp.dot(e.astype(BF16), values, preferred_element_type=F32)
        return total, product if acc is None else acc + product

    running = None
    for part in pieces(0):
        running = make_scores(0, part, running)
    for unit, (head, b) in enumerate(units):
        top = jnp.max(running, 1, keepdims=True)
        now = pieces(unit)
        later = pieces(unit + 1) if unit + 1 < len(units) else []
        running, total, acc = None, None, None
        for k in range(max(len(now), len(later))):
            if k < len(now):
                total, acc = use_scores(unit, now[k], top, total, acc)
            if k < len(later):
                running = make_scores(unit + 1, later[k], running)
        done = (acc / jnp.sum(total, 1, keepdims=True)).astype(BF16)
        for k in range(0, block, piece):
            member = (b * block + k) // piece
            side = jnp.bitwise_xor(core, member % 2)
            start = pl.multiple_of(jnp.bitwise_xor(chip, member // 2) * piece, piece)
            o_ref[side, pl.ds(start, piece), pl.ds(head * width, width)] = done[k : k + piece]


def attend_pair(q, pages, kvs):
    members, heads, piece, width = q.shape
    length = members * piece
    old = sum(page.shape[0] for page in pages)
    block = 2 * piece
    chunk = min(512, old, length)
    keys = old + 2 * length
    return pl.pallas_call(
        functools.partial(attend_pair_kernel, block, chunk, width),
        out_shape=jax.ShapeDtypeStruct((2, length // 2, heads * width), BF16),
        in_specs=[in_hbm()] * (1 + len(pages) + len(kvs)),
        out_specs=in_vmem(),
        scratch_shapes=[
            pltpu.VMEM((heads, length, width), BF16),
            pltpu.VMEM((old, 2 * width), BF16),
            pltpu.VMEM((2 * length, 2 * width), BF16),
            pltpu.VMEM((block, keys), F32),
            pltpu.VMEM((block, keys), F32),
            pltpu.SemaphoreType.DMA((3,)),
        ],
        compiler_params=pltpu.CompilerParams(vmem_limit_bytes=HIGH_VMEM),
        cost_estimate=pl.CostEstimate(
            flops=4 * heads * length * (keys - length // 2) * width,
            bytes_accessed=4 * (heads * length + keys) * width,
            transcendentals=heads * length * (keys - length // 2),
        ),
        name="attend",
    )(q, *pages, *kvs)


def project_pair_kernel(a_ref, got_ref, *refs):
    near, far, outs, (w_ref, sems) = refs[:4], refs[4:8], refs[8:-2], refs[-2:]
    me = lax.axis_index("head")
    half = lax.axis_index("grp")
    core = lax.rem(me, 2)
    steps, sides, heads, share, columns = near[0].shape
    width = w_ref.shape[1]
    copies = []
    for first, given in ((0, near), (steps, far)):
        for flip, x, pieces_of in zip((0, 1, 0, 1), (0, 0, 1, 1), given):
            column = pl.multiple_of(jnp.bitwise_xor(half, x) * columns, columns)
            for t in range(steps):
                for u in range(sides):
                    number = jnp.bitwise_xor(me, flip ^ (2 * u) ^ (4 * (first + t)))
                    row = pl.multiple_of(number * share, share)
                    copy = pltpu.make_async_copy(
                        pieces_of.at[t, u],
                        w_ref.at[:, pl.ds(row, share), pl.ds(column, columns)],
                        sems.at[0],
                    )
                    copy.start()
                    copies.append(copy)
    for copy in copies:
        copy.wait()
    acc = None
    for k in range(heads):
        mine = k < heads // 2
        at = pl.ds((k % (heads // 2)) * width, width)
        rows_of = a_ref[0, :, at] if mine else got_ref[:, at]
        head = jnp.bitwise_xor(core, 0 if mine else 1) * (heads // 2) + k % (heads // 2)
        part = jnp.dot(rows_of, w_ref[head], preferred_element_type=F32)
        acc = part if acc is None else acc + part
    rows = outs[0].shape[0]
    for k, out in enumerate(outs):
        out[...] = acc[k * rows : (k + 1) * rows].astype(BF16)


def project_pair(a, got, near, far, parts):
    _, _, heads, share, columns = near[0].shape
    rows = got.shape[0]
    width = 2 * got.shape[1] // heads
    model = 2 * columns
    return pl.pallas_call(
        project_pair_kernel,
        out_shape=[jax.ShapeDtypeStruct((rows // parts, model), BF16)] * parts,
        in_specs=[in_vmem(), in_vmem()] + [in_hbm()] * 8,
        out_specs=[in_vmem()] * parts,
        scratch_shapes=[
            pltpu.VMEM((heads, width, model), BF16),
            pltpu.SemaphoreType.DMA((1,)),
        ],
        compiler_params=pltpu.CompilerParams(vmem_limit_bytes=HIGH_VMEM),
        cost_estimate=pl.CostEstimate(
            flops=2 * heads * rows * width * model,
            bytes_accessed=2 * (heads * width * model + heads * rows * width + rows * model),
            transcendentals=0,
        ),
        name="project",
    )(a, got, *near, *far)


def project_kernel(a_ref, w_ref, o_ref):
    members = a_ref.shape[0]
    planes, share = w_ref.shape[1], w_ref.shape[3]
    acc = None
    for head in range(members):
        w = jnp.concatenate(
            [w_ref[m, p, head] for p in range(planes) for m in range(members)], 0
        )
        part = jnp.dot(a_ref[head], w, preferred_element_type=F32)
        acc = part if acc is None else acc + part
    o_ref[...] = acc.astype(BF16)


def project(a, w):
    members, rows, width = a.shape
    planes, share, model = w.shape[1], w.shape[3], w.shape[4]
    tile = min(512, model)
    return pl.pallas_call(
        project_kernel,
        grid=(model // tile,),
        out_shape=jax.ShapeDtypeStruct((rows, model), BF16),
        in_specs=[
            pl.BlockSpec((members, rows, width), lambda t: (0, 0, 0)),
            pl.BlockSpec((members, planes, members, share, tile), lambda t: (0, 0, 0, 0, t)),
        ],
        out_specs=pl.BlockSpec((rows, tile), lambda t: (0, t)),
        compiler_params=pltpu.CompilerParams(vmem_limit_bytes=HIGH_VMEM),
        cost_estimate=pl.CostEstimate(
            flops=2 * members * rows * width * model,
            bytes_accessed=2 * (members * width * model + members * rows * width + rows * model),
            transcendentals=0,
        ),
        name="project",
    )(a, w)


def route_kernel(resid_ref, gain_ref, slots_ref, *refs):
    parts_refs, (stream_ref, out_ref) = refs[:-2], refs[-2:]
    seqs = resid_ref.shape[0]
    streams = []
    for seq in range(seqs):
        stream = resid_ref[seq].astype(F32)
        projected = parts_refs[0][seq].astype(F32)
        for part in parts_refs[1:]:
            projected = projected + part[seq].astype(F32)
        streams.append(stream + projected)
    stream = jnp.concatenate(streams, 0) if seqs > 1 else streams[0]
    stream_ref[...] = stream
    normed = stream * lax.rsqrt(jnp.mean(stream * stream, 1, keepdims=True) + eps_norm)
    normed = (normed * gain_ref[...]).astype(BF16)
    slots, rows = out_ref.shape[0], stream.shape[0]
    place = lax.broadcasted_iota(jnp.int32, (slots, rows), 0)
    hit = place == slots_ref[0:1, :]
    for k in range(1, slots_ref.shape[0]):
        hit = hit | (place == slots_ref[k : k + 1, :])
    out_ref[...] = jnp.dot(hit.astype(BF16), normed, preferred_element_type=F32).astype(BF16)


def route(parts, resid, gain, slots_of, slots):
    seqs, local_rows, model = resid.shape
    rows = seqs * local_rows
    return pl.pallas_call(
        route_kernel,
        out_shape=(
            jax.ShapeDtypeStruct((rows, model), F32),
            jax.ShapeDtypeStruct((slots, model), BF16),
        ),
        in_specs=[in_vmem()] * (3 + len(parts)),
        out_specs=(in_vmem(), in_vmem()),
        compiler_params=pltpu.CompilerParams(vmem_limit_bytes=HIGH_VMEM),
        cost_estimate=pl.CostEstimate(
            flops=2 * slots * rows * model,
            bytes_accessed=2 * (len(parts) + 3 + slots // rows) * rows * model,
            transcendentals=0,
        ),
        name="route",
    )(resid, gain, slots_of, *parts)


def expert_kernel(x_ref, w_in_ref, w_down_ref, o_ref):
    hidden_width = w_down_ref.shape[0]
    inner = jnp.dot(x_ref[...], w_in_ref[...], preferred_element_type=F32)
    gate = inner[:, :hidden_width]
    hidden = (gate / (1.0 + jnp.exp(-gate)) * inner[:, hidden_width:]).astype(BF16)
    o_ref[...] = jnp.dot(hidden, w_down_ref[...], preferred_element_type=F32).astype(BF16)


def expert(x, w_in, w_down):
    rows, model = x.shape
    hidden_width = w_down.shape[0]
    return pl.pallas_call(
        expert_kernel,
        out_shape=jax.ShapeDtypeStruct((rows, model), BF16),
        in_specs=[in_vmem()] * 3,
        out_specs=in_vmem(),
        compiler_params=pltpu.CompilerParams(vmem_limit_bytes=HIGH_VMEM),
        cost_estimate=pl.CostEstimate(
            flops=6 * rows * model * hidden_width,
            bytes_accessed=2 * (2 * rows * model + 3 * model * hidden_width),
            transcendentals=rows * hidden_width,
        ),
        name="expert",
    )(x, w_in, w_down)


def expert_pair(x, w_in, w_down):
    rows, model = x.shape
    hidden_width = w_down.shape[0]
    parts = 4
    depth = model // parts

    def kernel(x_hbm, in_hbm_ref, down_hbm, o_hbm, x_ref, in_ref, down_ref, o_ref, sems):
        bring_x = pltpu.make_async_copy(x_hbm, x_ref, sems.at[parts])
        bring_x.start()
        bring_in = []
        for k in range(parts):
            at = pl.ds(k * depth, depth)
            bring_in.append(pltpu.make_async_copy(in_hbm_ref.at[at], in_ref.at[at], sems.at[k]))
            bring_in[k].start()
        bring_down = pltpu.make_async_copy(down_hbm, down_ref, sems.at[parts + 1])
        bring_down.start()
        bring_x.wait()
        inner = None
        for k in range(parts):
            bring_in[k].wait()
            at = pl.ds(k * depth, depth)
            part = jnp.dot(x_ref[:, at], in_ref[at, :], preferred_element_type=F32)
            inner = part if inner is None else inner + part
        gate = inner[:, :hidden_width]
        hidden = (gate / (1.0 + jnp.exp(-gate)) * inner[:, hidden_width:]).astype(BF16)
        bring_down.wait()
        o_ref[...] = jnp.dot(hidden, down_ref[...], preferred_element_type=F32).astype(BF16)
        back = pltpu.make_async_copy(o_ref, o_hbm, sems.at[parts + 2])
        back.start()
        back.wait()

    return pl.pallas_call(
        kernel,
        out_shape=jax.ShapeDtypeStruct((rows, model), BF16),
        in_specs=[in_hbm()] * 3,
        out_specs=in_hbm(),
        scratch_shapes=[
            pltpu.VMEM((rows, model), BF16),
            pltpu.VMEM(w_in.shape, BF16),
            pltpu.VMEM(w_down.shape, BF16),
            pltpu.VMEM((rows, model), BF16),
            pltpu.SemaphoreType.DMA((parts + 3,)),
        ],
        compiler_params=pltpu.CompilerParams(vmem_limit_bytes=HIGH_VMEM),
        cost_estimate=pl.CostEstimate(
            flops=6 * rows * model * hidden_width,
            bytes_accessed=2 * (2 * rows * model + 3 * model * hidden_width),
            transcendentals=rows * hidden_width,
        ),
        name="expert",
    )(x, w_in, w_down)


def combine_kernel(seqs, back_ref, stream_ref, slots_ref, gates_ref, o_ref):
    slots = back_ref.shape[0]
    rows = stream_ref.shape[0]
    place = lax.broadcasted_iota(jnp.int32, (rows, slots), 1)
    total = stream_ref[...]
    gathered = None
    for k in range(slots_ref.shape[1]):
        pick = (place == slots_ref[:, k : k + 1]).astype(BF16)
        picked = jnp.dot(pick, back_ref[...], preferred_element_type=F32)
        part = picked * gates_ref[:, k : k + 1]
        gathered = part if gathered is None else gathered + part
    out = (total + gathered).astype(BF16)
    local_rows = rows // seqs
    for seq in range(seqs):
        o_ref[seq] = out[seq * local_rows : (seq + 1) * local_rows]


def combine(back, stream, slots_of, gates, seqs):
    slots, model = back.shape
    rows = stream.shape[0]
    top = slots_of.shape[1]
    return pl.pallas_call(
        functools.partial(combine_kernel, seqs),
        out_shape=jax.ShapeDtypeStruct((seqs, rows // seqs, model), BF16),
        in_specs=[in_vmem()] * 4,
        out_specs=in_vmem(),
        compiler_params=pltpu.CompilerParams(vmem_limit_bytes=HIGH_VMEM),
        cost_estimate=pl.CostEstimate(
            flops=2 * top * slots * rows * model,
            bytes_accessed=2 * slots * model + 6 * rows * model,
            transcendentals=0,
        ),
        name="combine",
    )(back, stream, slots_of, gates)


def flipped(value, axis, mask):
    pairs = [(source, source ^ mask) for source in range(lax.axis_size(axis))]
    return lax.ppermute(value, axis, pairs)


def parts_in_pairs(queries, new_kv, cache, w_out):
    n = lax.axis_size("head")
    local_rows, _, heads, width = queries.shape
    pair_heads = new_kv.shape[2]
    members = heads // pair_heads
    model = w_out.shape[2]
    share = w_out.shape[1]
    me = lax.axis_index("head")
    plane_bit = members // 2
    planes = n // plane_bit
    b = (me // plane_bit) % 2
    y = (me // 2) % 2
    group_sets = [[g * members + m for m in range(members)] for g in range(n // members)]

    query_slots = queries.reshape(local_rows, heads, width).transpose(1, 0, 2)
    query_slots = query_slots.reshape(members, heads // members, local_rows, width)

    def page_target(source, other):
        p, plane, rest = source // members, (source // plane_bit) % 2, source % plane_bit
        return (plane ^ other) * members + p * plane_bit + rest

    page_a, page_b = (
        lax.ppermute(cache[0], "head", [(d, page_target(d, other)) for d in range(n)])
        for other in range(2)
    )
    kv_heads = new_kv.reshape(local_rows, pair_heads, 2 * width).transpose(1, 0, 2)
    kv_beside = flipped(kv_heads, "head", 2)

    columns = model // 2
    w = lax.dynamic_slice_in_dim(w_out, lax.axis_index("grp") * columns, columns, 2)
    w = w.reshape(2, 2, heads // 4, share, columns)
    w_keep = lax.dynamic_index_in_dim(w, y, 1, keepdims=False)
    w_give = lax.dynamic_index_in_dim(w, 1 - y, 1, keepdims=False)
    w_got = flipped(w_give, "head", 2)

    page_a, page_b, kv_beside, query_slots = lax.optimization_barrier(
        (page_a, page_b, kv_beside, query_slots)
    )
    kv_both = jnp.stack([kv_heads, kv_beside], 1)
    kv_same = lax.dynamic_index_in_dim(kv_both, b, 0, keepdims=False)
    kv_other = lax.dynamic_index_in_dim(kv_both, 1 - b, 0, keepdims=False)
    kv_own = [kv_same]
    for t in range(1, planes):
        kv_own.append(flipped(kv_other if t % 2 else kv_same, "head", t * plane_bit))
    own_pages = jnp.concatenate([page_a, page_b], 0)
    pages_y = flipped(own_pages, "head", 2)
    q = lax.all_to_all(
        query_slots, "head", split_axis=0, concat_axis=0, tiled=True, axis_index_groups=group_sets
    )
    w_both = jnp.stack([w_keep, w_got], 1)
    w_same = lax.dynamic_index_in_dim(w_both, b, 0, keepdims=False)
    w_other = lax.dynamic_index_in_dim(w_both, 1 - b, 0, keepdims=False)
    w_first = flipped(w_other, "head", plane_bit)
    pages_y, kv_own, w_first, q = lax.optimization_barrier((pages_y, kv_own, w_first, q))

    kv_own = jnp.stack(kv_own, 0)
    kv_c = flipped(kv_own, "head", 1)
    pages_c = flipped(own_pages, "head", 1)
    pages_cy = flipped(pages_y, "head", 1)
    w_near = jnp.stack([w_same, w_first], 0)
    w_far = flipped(w_near, "head", members)
    w_near_x = flipped(w_near, "grp", 1)
    a = attend_pair(q, (page_a, page_b, pages_y, pages_c, pages_cy), (kv_own, kv_c))
    got = flipped(a[1], "head", 1)
    a, w_far, w_near_x = lax.optimization_barrier((a, w_far, w_near_x))
    w_far_x = flipped(w_far, "grp", 1)
    w_near_c = flipped(w_near, "head", 1)
    w_far_c = flipped(w_far, "head", 1)
    w_near_cx = flipped(w_near_x, "head", 1)
    w_far_cx = flipped(w_far_x, "head", 1)
    partial = project_pair(
        a,
        got,
        (w_near, w_near_c, w_near_x, w_near_cx),
        (w_far, w_far_c, w_far_x, w_far_cx),
        members // 2,
    )
    parts = [partial[0]] + [flipped(partial[k], "head", 2 * k) for k in (3, 2, 1)]
    return [part[None] for part in parts]


def parts_in_planes(queries, new_kv, cache, w_out):
    n = lax.axis_size("head")
    local_rows, seqs, heads, width = queries.shape
    pair_heads = new_kv.shape[2]
    members = heads // pair_heads
    groups = n // members
    model = w_out.shape[2]
    side = 1 << ((n.bit_length() - 1) // 2)
    side = min(side, heads)
    planes = n // side
    planes_of_seq = heads // side
    pair_groups = [[g * members + m for m in range(members)] for g in range(groups)]
    cross_groups = [[g * members + m for g in range(groups)] for m in range(members)]
    plane_groups = [[p * side + m for m in range(side)] for p in range(planes)]
    column_groups = [[p * side + m for p in range(planes)] for m in range(side)]

    query_slots = queries.reshape(local_rows, n, width).transpose(1, 0, 2)
    q = lax.all_to_all(query_slots, "head", split_axis=0, concat_axis=0, tiled=True)
    q = q.reshape(n * local_rows, width)

    kv_slots = new_kv.reshape(local_rows, groups, 2 * width).transpose(1, 0, 2)
    kv = lax.all_to_all(
        kv_slots, "head", split_axis=0, concat_axis=0, tiled=True, axis_index_groups=cross_groups
    )
    kv = lax.all_gather(kv, "head", axis=0, axis_index_groups=pair_groups)
    pages = lax.all_gather(cache, "head", axis=0, tiled=True, axis_index_groups=pair_groups)

    share = w_out.shape[1]
    w_planes = w_out.reshape(planes_of_seq, side, share, model)
    if planes > planes_of_seq:
        w_planes = jnp.tile(w_planes, (planes // planes_of_seq, 1, 1, 1))
    w = lax.all_to_all(
        w_planes, "head", split_axis=0, concat_axis=0, tiled=True, axis_index_groups=column_groups
    )
    w = lax.all_gather(w, "head", axis=0, axis_index_groups=plane_groups)
    if share % 16:
        w = w.transpose(2, 1, 0, 3, 4).reshape(1, 1, side, width, model)
        w = w.reshape(side, width, model)

    attended = attend(q, pages.reshape(-1, 2 * width), kv)
    a = attended.reshape(planes, side, local_rows, width).transpose(1, 0, 2, 3)
    a = a.reshape(side, planes * local_rows, width)
    a = lax.all_to_all(
        a, "head", split_axis=0, concat_axis=0, tiled=True, axis_index_groups=plane_groups
    )
    if share % 16:
        partial = jnp.einsum("hri,hid->rd", a, w, preferred_element_type=F32).astype(BF16)
    else:
        partial = project(a, w)
    parts = lax.all_to_all(
        partial.reshape(planes, local_rows, model),
        "head",
        split_axis=0,
        concat_axis=0,
        tiled=True,
        axis_index_groups=column_groups,
    )
    parts = parts.reshape(seqs, planes_of_seq, local_rows, model)
    return [parts[:, k] for k in range(planes_of_seq)]


def local(queries, new_kv, cache, resid, w_out, norm_gain, expert_ids, expert_gates, w_in, w_down):
    n = lax.axis_size("head")
    local_rows, seqs, heads, width = queries.shape
    model = resid.shape[2]
    rows = local_rows * seqs
    members = heads // new_kv.shape[2]
    in_pairs = (
        lax.axis_size("grp") == 2
        and seqs == 1
        and new_kv.shape[2] == 2
        and n == heads == 2 * members
        and members == 8
        and cache.shape[0] == 1
        and w_in.shape[0] == 1
        and w_out.shape[1] % 16 == 0
    )
    plan = parts_in_pairs if in_pairs else parts_in_planes
    parts = plan(queries, new_kv, cache, w_out)

    top = expert_ids.shape[2]
    experts = w_in.shape[0] * n
    capacity = max(2, 2 * rows * top // experts)
    ids = expert_ids.transpose(1, 0, 2).reshape(rows, top)
    gates = expert_gates.transpose(1, 0, 2).reshape(rows, top)
    onehot = (ids[:, :, None] == jnp.arange(experts, dtype=jnp.int32)).astype(jnp.int32)
    named = onehot.sum(1)
    before = jnp.cumsum(named, 0) - named
    slots_of = ids * capacity + jnp.sum(onehot * before[:, None, :], 2)
    slots = experts * capacity

    stream, outgoing = route(
        parts, resid.transpose(1, 0, 2), norm_gain[None, :], slots_of.T, slots
    )
    arrived = lax.all_to_all(
        outgoing.reshape(n, slots // n, model), "head", split_axis=0, concat_axis=0, tiled=True
    )
    local_experts = w_in.shape[0]
    if local_experts == 1:
        answered = expert_pair(arrived.reshape(slots, model), w_in[0], w_down[0])
        answered = answered.reshape(n, slots // n, model)
    else:
        arrived = arrived.reshape(n, local_experts, capacity, model).transpose(1, 0, 2, 3)
        arrived = arrived.reshape(local_experts, n * capacity, model)
        answered = jnp.stack([expert(arrived[e], w_in[e], w_down[e]) for e in range(local_experts)])
        answered = answered.reshape(local_experts, n, capacity, model).transpose(1, 0, 2, 3)
        answered = answered.reshape(n, slots // n, model)
    back = lax.all_to_all(answered, "head", split_axis=0, concat_axis=0, tiled=True)
    out = combine(back.reshape(slots, model), stream, slots_of, gates, seqs)
    return out.transpose(1, 0, 2)


def solution(mesh):
    return jax.shard_map(
        local,
        mesh=mesh,
        in_specs=(
            P("head", "grp", None, None),
            P("head", "grp", None, None),
            P(("grp", "head"), None, None),
            P("head", "grp", None),
            P(None, "head", None),
            P(),
            P("head", "grp", None),
            P("head", "grp", None),
            P("head", None, None),
            P("head", None, None),
        ),
        out_specs=P("head", "grp", None),
        check_vma=False,
    )
```

```python
import functools

import jax
import jax.numpy as jnp
from jax import lax
from jax.experimental import pallas as pl
from jax.experimental.pallas import tpu as pltpu
from jax.sharding import PartitionSpec as P

eps_norm = 1e-06
F32 = jnp.float32
BF16 = jnp.bfloat16
HIGH_VMEM = 48 * 2**20
LOG2_E = 1.4426950408889634


def in_hbm():
    return pl.BlockSpec(memory_space=pltpu.HBM)


def in_vmem():
    return pl.BlockSpec(memory_space=pltpu.VMEM)


def attend_kernel(
    block, chunk, width, q_hbm, cache_hbm, kv_hbm, o_ref, q_ref, cache_ref, kv_ref, s0, s1, sems
):
    members, groups, piece, _ = kv_hbm.shape
    length = members * groups * piece
    old = cache_hbm.shape[0]
    scale = width**-0.5
    in_q = pltpu.make_async_copy(q_hbm, q_ref, sems.at[0])
    in_cache = pltpu.make_async_copy(cache_hbm, cache_ref, sems.at[1])
    in_q.start()
    in_cache.start()
    in_kv = []
    for group in range(groups):
        for member in range(members):
            place = (group * members + member) * piece
            copy = pltpu.make_async_copy(
                kv_hbm.at[member, group], kv_ref.at[pl.ds(place, piece)], sems.at[2]
            )
            copy.start()
            in_kv.append(copy)
    in_q.wait()
    in_cache.wait()
    for copy in in_kv:
        copy.wait()
    scores = [s0, s1]

    def pieces(b):
        out = [(True, k, chunk, k) for k in range(0, old, chunk)]
        last = b * block
        for k in range(0, last, chunk):
            out.append((False, k, min(chunk, last - k), old + k))
        out.append((False, last, block, old + last))
        return out

    def make_scores(b, part, running):
        of_cache, first, count, column = part
        keys = (cache_ref if of_cache else kv_ref)[pl.ds(first, count), :width]
        s = lax.dot_general(
            q_ref[pl.ds(b * block, block), :],
            keys,
            (((1,), (1,)), ((), ())),
            preferred_element_type=F32,
        )
        if not of_cache and first == b * block:
            row = lax.broadcasted_iota(jnp.int32, s.shape, 0)
            col = lax.broadcasted_iota(jnp.int32, s.shape, 1)
            s = jnp.where(col <= row, s, -jnp.inf)
        scores[b % 2][:, pl.ds(column, count)] = s
        for k in range(0, count, 128):
            piece_max = s[:, k : k + 128]
            running = piece_max if running is None else jnp.maximum(running, piece_max)
        return running

    def use_scores(b, part, top, total, acc):
        of_cache, first, count, column = part
        values = (cache_ref if of_cache else kv_ref)[pl.ds(first, count), width:]
        e = jnp.exp((scores[b % 2][:, pl.ds(column, count)] - top) * scale)
        for k in range(0, count, 128):
            total = e[:, k : k + 128] if total is None else total + e[:, k : k + 128]
        product = jnp.dot(e.astype(BF16), values, preferred_element_type=F32)
        return total, product if acc is None else acc + product

    blocks = length // block
    running = None
    for part in pieces(0):
        running = make_scores(0, part, running)
    for b in range(blocks):
        top = jnp.max(running, 1, keepdims=True)
        now, later = pieces(b), pieces(b + 1) if b + 1 < blocks else []
        running, total, acc = None, None, None
        for k in range(max(len(now), len(later))):
            if k < len(now):
                total, acc = use_scores(b, now[k], top, total, acc)
            if k < len(later):
                running = make_scores(b + 1, later[k], running)
        o_ref[pl.ds(b * block, block), :] = (acc / jnp.sum(total, 1, keepdims=True)).astype(BF16)


def attend(q, cache, kv):
    length, width = q.shape
    old = cache.shape[0]
    block = min(256, length)
    chunk = min(512, old)
    return pl.pallas_call(
        functools.partial(attend_kernel, block, chunk, width),
        out_shape=jax.ShapeDtypeStruct((length, width), BF16),
        in_specs=[in_hbm()] * 3,
        out_specs=in_vmem(),
        scratch_shapes=[
            pltpu.VMEM((length, width), BF16),
            pltpu.VMEM((old, 2 * width), BF16),
            pltpu.VMEM((length, 2 * width), BF16),
            pltpu.VMEM((block, old + length), F32),
            pltpu.VMEM((block, old + length), F32),
            pltpu.SemaphoreType.DMA((3,)),
        ],
        compiler_params=pltpu.CompilerParams(vmem_limit_bytes=HIGH_VMEM),
        cost_estimate=pl.CostEstimate(
            flops=4 * length * (old + length // 2) * width,
            bytes_accessed=4 * (2 * length + 2 * old) * width,
            transcendentals=length * (old + length // 2),
        ),
        name="attend",
    )(q, cache, kv)


def attend_pair_kernel(
    block,
    chunk,
    width,
    q_hbm,
    page_a,
    page_b,
    page_y,
    page_c,
    page_cy,
    kv_own,
    kv_c,
    o_ref,
    q_ref,
    old_ref,
    kv_ref,
    s0,
    s1,
    sems,
):
    me = lax.axis_index("head")
    members, heads, piece, _ = q_hbm.shape
    length = members * piece
    planes, sides = kv_own.shape[:2]
    old = old_ref.shape[0]
    earlier_group = me // members > 0
    core = lax.rem(me, 2)
    chip = jnp.bitwise_and(me // 2, members // 2 - 1)
    copies = []

    def bring(source, target, sem):
        copy = pltpu.make_async_copy(source, target, sems.at[sem])
        copy.start()
        copies.append(copy)

    for member in range(members):
        for head in range(heads):
            bring(q_hbm.at[member, head], q_ref.at[head, pl.ds(member * piece, piece)], 0)
    place = 0
    for page in (page_a, page_b, page_y, page_c, page_cy):
        count = page.shape[0]
        bring(page, old_ref.at[pl.ds(place, count)], 1)
        place += count
    for flip, pieces_of in ((0, kv_own), (1, kv_c)):
        for t in range(planes):
            for u in range(sides):
                number = jnp.bitwise_and(
                    jnp.bitwise_xor(me, flip ^ (2 * u) ^ (t * (members // 2))), members - 1
                )
                start = pl.multiple_of(number * piece, piece)
                area = 0 if t * (members // 2) >= members else length
                bring(pieces_of.at[t, u], kv_ref.at[pl.ds(area + start, piece)], 2)
    for copy in copies:
        copy.wait()
    scale = width**-0.5 * LOG2_E
    scores = [s0, s1]
    blocks = length // block
    units = [(head, b) for head in range(heads) for b in range(blocks)]

    def pieces(unit):
        _, b = units[unit]
        out = [("old", k, chunk, k) for k in range(0, old, chunk)]
        out += [("past", k, chunk, old + k) for k in range(0, length, chunk)]
        last = b * block
        for k in range(0, last, chunk):
            out.append(("new", length + k, min(chunk, last - k), old + length + k))
        out.append(("edge", length + last, block, old + length + last))
        return out

    def make_scores(unit, part, running):
        kind, first, count, column = part
        head, b = units[unit]
        keys = (old_ref if kind == "old" else kv_ref)[pl.ds(first, count), :width]
        s = lax.dot_general(
            q_ref[head, pl.ds(b * block, block), :],
            keys,
            (((1,), (1,)), ((), ())),
            preferred_element_type=F32,
        )
        if kind == "past":
            s = jnp.where(earlier_group, s, -jnp.inf)
        if kind == "edge":
            row = lax.broadcasted_iota(jnp.int32, s.shape, 0)
            col = lax.broadcasted_iota(jnp.int32, s.shape, 1)
            s = jnp.where(col <= row, s, -jnp.inf)
        scores[unit % 2][:, pl.ds(column, count)] = s
        for k in range(0, count, 128):
            piece_max = s[:, k : k + 128]
            running = piece_max if running is None else jnp.maximum(running, piece_max)
        return running

    def use_scores(unit, part, top, total, acc):
        kind, first, count, column = part
        values = (old_ref if kind == "old" else kv_ref)[pl.ds(first, count), width:]
        e = jnp.exp2((scores[unit % 2][:, pl.ds(column, count)] - top) * scale)
        for k in range(0, count, 128):
            total = e[:, k : k + 128] if total is None else total + e[:, k : k + 128]
        product = jnp.dot(e.astype(BF16), values, preferred_element_type=F32)
        return total, product if acc is None else acc + product

    running = None
    for part in pieces(0):
        running = make_scores(0, part, running)
    for unit, (head, b) in enumerate(units):
        top = jnp.max(running, 1, keepdims=True)
        now = pieces(unit)
        later = pieces(unit + 1) if unit + 1 < len(units) else []
        running, total, acc = None, None, None
        for k in range(max(len(now), len(later))):
            if k < len(now):
                total, acc = use_scores(unit, now[k], top, total, acc)
            if k < len(later):
                running = make_scores(unit + 1, later[k], running)
        done = (acc / jnp.sum(total, 1, keepdims=True)).astype(BF16)
        for k in range(0, block, piece):
            member = (b * block + k) // piece
            side = jnp.bitwise_xor(core, member % 2)
            start = pl.multiple_of(jnp.bitwise_xor(chip, member // 2) * piece, piece)
            o_ref[side, pl.ds(start, piece), pl.ds(head * width, width)] = done[k : k + piece]


def attend_pair(q, pages, kvs):
    members, heads, piece, width = q.shape
    length = members * piece
    old = sum(page.shape[0] for page in pages)
    block = 2 * piece
    chunk = min(512, old, length)
    keys = old + 2 * length
    return pl.pallas_call(
        functools.partial(attend_pair_kernel, block, chunk, width),
        out_shape=jax.ShapeDtypeStruct((2, length // 2, heads * width), BF16),
        in_specs=[in_hbm()] * (1 + len(pages) + len(kvs)),
        out_specs=in_vmem(),
        scratch_shapes=[
            pltpu.VMEM((heads, length, width), BF16),
            pltpu.VMEM((old, 2 * width), BF16),
            pltpu.VMEM((2 * length, 2 * width), BF16),
            pltpu.VMEM((block, keys), F32),
            pltpu.VMEM((block, keys), F32),
            pltpu.SemaphoreType.DMA((3,)),
        ],
        compiler_params=pltpu.CompilerParams(vmem_limit_bytes=HIGH_VMEM),
        cost_estimate=pl.CostEstimate(
            flops=4 * heads * length * (keys - length // 2) * width,
            bytes_accessed=4 * (heads * length + keys) * width,
            transcendentals=heads * length * (keys - length // 2),
        ),
        name="attend",
    )(q, *pages, *kvs)


def project_pair_kernel(a_ref, got_ref, *refs):
    near, far, outs, (w_ref, sems) = refs[:4], refs[4:8], refs[8:-2], refs[-2:]
    me = lax.axis_index("head")
    half = lax.axis_index("grp")
    core = lax.rem(me, 2)
    steps, sides, heads, share, columns = near[0].shape
    width = w_ref.shape[1]
    copies = []
    for first, given in ((0, near), (steps, far)):
        for flip, x, pieces_of in zip((0, 1, 0, 1), (0, 0, 1, 1), given):
            column = pl.multiple_of(jnp.bitwise_xor(half, x) * columns, columns)
            for t in range(steps):
                for u in range(sides):
                    number = jnp.bitwise_xor(me, flip ^ (2 * u) ^ (4 * (first + t)))
                    row = pl.multiple_of(number * share, share)
                    copy = pltpu.make_async_copy(
                        pieces_of.at[t, u],
                        w_ref.at[:, pl.ds(row, share), pl.ds(column, columns)],
                        sems.at[0],
                    )
                    copy.start()
                    copies.append(copy)
    for copy in copies:
        copy.wait()
    acc = None
    for k in range(heads):
        mine = k < heads // 2
        at = pl.ds((k % (heads // 2)) * width, width)
        rows_of = a_ref[0, :, at] if mine else got_ref[:, at]
        head = jnp.bitwise_xor(core, 0 if mine else 1) * (heads // 2) + k % (heads // 2)
        part = jnp.dot(rows_of, w_ref[head], preferred_element_type=F32)
        acc = part if acc is None else acc + part
    rows = outs[0].shape[0]
    for k, out in enumerate(outs):
        out[...] = acc[k * rows : (k + 1) * rows].astype(BF16)


def project_pair(a, got, near, far, parts):
    _, _, heads, share, columns = near[0].shape
    rows = got.shape[0]
    width = 2 * got.shape[1] // heads
    model = 2 * columns
    return pl.pallas_call(
        project_pair_kernel,
        out_shape=[jax.ShapeDtypeStruct((rows // parts, model), BF16)] * parts,
        in_specs=[in_vmem(), in_vmem()] + [in_hbm()] * 8,
        out_specs=[in_vmem()] * parts,
        scratch_shapes=[
            pltpu.VMEM((heads, width, model), BF16),
            pltpu.SemaphoreType.DMA((1,)),
        ],
        compiler_params=pltpu.CompilerParams(vmem_limit_bytes=HIGH_VMEM),
        cost_estimate=pl.CostEstimate(
            flops=2 * heads * rows * width * model,
            bytes_accessed=2 * (heads * width * model + heads * rows * width + rows * model),
            transcendentals=0,
        ),
        name="project",
    )(a, got, *near, *far)


def project_kernel(a_ref, w_ref, o_ref):
    members = a_ref.shape[0]
    planes, share = w_ref.shape[1], w_ref.shape[3]
    acc = None
    for head in range(members):
        w = jnp.concatenate(
            [w_ref[m, p, head] for p in range(planes) for m in range(members)], 0
        )
        part = jnp.dot(a_ref[head], w, preferred_element_type=F32)
        acc = part if acc is None else acc + part
    o_ref[...] = acc.astype(BF16)


def project(a, w):
    members, rows, width = a.shape
    planes, share, model = w.shape[1], w.shape[3], w.shape[4]
    tile = min(512, model)
    return pl.pallas_call(
        project_kernel,
        grid=(model // tile,),
        out_shape=jax.ShapeDtypeStruct((rows, model), BF16),
        in_specs=[
            pl.BlockSpec((members, rows, width), lambda t: (0, 0, 0)),
            pl.BlockSpec((members, planes, members, share, tile), lambda t: (0, 0, 0, 0, t)),
        ],
        out_specs=pl.BlockSpec((rows, tile), lambda t: (0, t)),
        compiler_params=pltpu.CompilerParams(vmem_limit_bytes=HIGH_VMEM),
        cost_estimate=pl.CostEstimate(
            flops=2 * members * rows * width * model,
            bytes_accessed=2 * (members * width * model + members * rows * width + rows * model),
            transcendentals=0,
        ),
        name="project",
    )(a, w)


def route_kernel(resid_ref, gain_ref, slots_ref, *refs):
    parts_refs, (stream_ref, out_ref) = refs[:-2], refs[-2:]
    seqs = resid_ref.shape[0]
    streams = []
    for seq in range(seqs):
        stream = resid_ref[seq].astype(F32)
        projected = parts_refs[0][seq].astype(F32)
        for part in parts_refs[1:]:
            projected = projected + part[seq].astype(F32)
        streams.append(stream + projected)
    stream = jnp.concatenate(streams, 0) if seqs > 1 else streams[0]
    stream_ref[...] = stream
    normed = stream * lax.rsqrt(jnp.mean(stream * stream, 1, keepdims=True) + eps_norm)
    normed = (normed * gain_ref[...]).astype(BF16)
    slots, rows = out_ref.shape[0], stream.shape[0]
    place = lax.broadcasted_iota(jnp.int32, (slots, rows), 0)
    hit = place == slots_ref[0:1, :]
    for k in range(1, slots_ref.shape[0]):
        hit = hit | (place == slots_ref[k : k + 1, :])
    out_ref[...] = jnp.dot(hit.astype(BF16), normed, preferred_element_type=F32).astype(BF16)


def route(parts, resid, gain, slots_of, slots):
    seqs, local_rows, model = resid.shape
    rows = seqs * local_rows
    return pl.pallas_call(
        route_kernel,
        out_shape=(
            jax.ShapeDtypeStruct((rows, model), F32),
            jax.ShapeDtypeStruct((slots, model), BF16),
        ),
        in_specs=[in_vmem()] * (3 + len(parts)),
        out_specs=(in_vmem(), in_vmem()),
        compiler_params=pltpu.CompilerParams(vmem_limit_bytes=HIGH_VMEM),
        cost_estimate=pl.CostEstimate(
            flops=2 * slots * rows * model,
            bytes_accessed=2 * (len(parts) + 3 + slots // rows) * rows * model,
            transcendentals=0,
        ),
        name="route",
    )(resid, gain, slots_of, *parts)


def expert_kernel(x_ref, w_in_ref, w_down_ref, o_ref):
    hidden_width = w_down_ref.shape[0]
    inner = jnp.dot(x_ref[...], w_in_ref[...], preferred_element_type=F32)
    gate = inner[:, :hidden_width]
    hidden = (gate / (1.0 + jnp.exp(-gate)) * inner[:, hidden_width:]).astype(BF16)
    o_ref[...] = jnp.dot(hidden, w_down_ref[...], preferred_element_type=F32).astype(BF16)


def expert(x, w_in, w_down):
    rows, model = x.shape
    hidden_width = w_down.shape[0]
    return pl.pallas_call(
        expert_kernel,
        out_shape=jax.ShapeDtypeStruct((rows, model), BF16),
        in_specs=[in_vmem()] * 3,
        out_specs=in_vmem(),
        compiler_params=pltpu.CompilerParams(vmem_limit_bytes=HIGH_VMEM),
        cost_estimate=pl.CostEstimate(
            flops=6 * rows * model * hidden_width,
            bytes_accessed=2 * (2 * rows * model + 3 * model * hidden_width),
            transcendentals=rows * hidden_width,
        ),
        name="expert",
    )(x, w_in, w_down)


def expert_pair(x, w_in, w_down):
    rows, model = x.shape
    hidden_width = w_down.shape[0]
    parts = 4
    depth = model // parts

    def kernel(x_hbm, in_hbm_ref, down_hbm, o_hbm, x_ref, in_ref, down_ref, o_ref, sems):
        bring_x = pltpu.make_async_copy(x_hbm, x_ref, sems.at[parts])
        bring_x.start()
        bring_in = []
        for k in range(parts):
            at = pl.ds(k * depth, depth)
            bring_in.append(pltpu.make_async_copy(in_hbm_ref.at[at], in_ref.at[at], sems.at[k]))
            bring_in[k].start()
        bring_down = pltpu.make_async_copy(down_hbm, down_ref, sems.at[parts + 1])
        bring_down.start()
        bring_x.wait()
        inner = None
        for k in range(parts):
            bring_in[k].wait()
            at = pl.ds(k * depth, depth)
            part = jnp.dot(x_ref[:, at], in_ref[at, :], preferred_element_type=F32)
            inner = part if inner is None else inner + part
        gate = inner[:, :hidden_width]
        hidden = (gate / (1.0 + jnp.exp(-gate)) * inner[:, hidden_width:]).astype(BF16)
        bring_down.wait()
        o_ref[...] = jnp.dot(hidden, down_ref[...], preferred_element_type=F32).astype(BF16)
        back = pltpu.make_async_copy(o_ref, o_hbm, sems.at[parts + 2])
        back.start()
        back.wait()

    return pl.pallas_call(
        kernel,
        out_shape=jax.ShapeDtypeStruct((rows, model), BF16),
        in_specs=[in_hbm()] * 3,
        out_specs=in_hbm(),
        scratch_shapes=[
            pltpu.VMEM((rows, model), BF16),
            pltpu.VMEM(w_in.shape, BF16),
            pltpu.VMEM(w_down.shape, BF16),
            pltpu.VMEM((rows, model), BF16),
            pltpu.SemaphoreType.DMA((parts + 3,)),
        ],
        compiler_params=pltpu.CompilerParams(vmem_limit_bytes=HIGH_VMEM),
        cost_estimate=pl.CostEstimate(
            flops=6 * rows * model * hidden_width,
            bytes_accessed=2 * (2 * rows * model + 3 * model * hidden_width),
            transcendentals=rows * hidden_width,
        ),
        name="expert",
    )(x, w_in, w_down)


def combine_kernel(seqs, back_ref, stream_ref, slots_ref, gates_ref, o_ref):
    slots = back_ref.shape[0]
    rows = stream_ref.shape[0]
    place = lax.broadcasted_iota(jnp.int32, (rows, slots), 1)
    total = stream_ref[...]
    gathered = None
    for k in range(slots_ref.shape[1]):
        pick = (place == slots_ref[:, k : k + 1]).astype(BF16)
        picked = jnp.dot(pick, back_ref[...], preferred_element_type=F32)
        part = picked * gates_ref[:, k : k + 1]
        gathered = part if gathered is None else gathered + part
    out = (total + gathered).astype(BF16)
    local_rows = rows // seqs
    for seq in range(seqs):
        o_ref[seq] = out[seq * local_rows : (seq + 1) * local_rows]


def combine(back, stream, slots_of, gates, seqs):
    slots, model = back.shape
    rows = stream.shape[0]
    top = slots_of.shape[1]
    return pl.pallas_call(
        functools.partial(combine_kernel, seqs),
        out_shape=jax.ShapeDtypeStruct((seqs, rows // seqs, model), BF16),
        in_specs=[in_vmem()] * 4,
        out_specs=in_vmem(),
        compiler_params=pltpu.CompilerParams(vmem_limit_bytes=HIGH_VMEM),
        cost_estimate=pl.CostEstimate(
            flops=2 * top * slots * rows * model,
            bytes_accessed=2 * slots * model + 6 * rows * model,
            transcendentals=0,
        ),
        name="combine",
    )(back, stream, slots_of, gates)


def flipped(value, axis, mask):
    pairs = [(source, source ^ mask) for source in range(lax.axis_size(axis))]
    return lax.ppermute(value, axis, pairs)


def parts_in_pairs(queries, new_kv, cache, w_out):
    n = lax.axis_size("head")
    local_rows, _, heads, width = queries.shape
    pair_heads = new_kv.shape[2]
    members = heads // pair_heads
    model = w_out.shape[2]
    share = w_out.shape[1]
    me = lax.axis_index("head")
    plane_bit = members // 2
    planes = n // plane_bit
    b = (me // plane_bit) % 2
    y = (me // 2) % 2
    group_sets = [[g * members + m for m in range(members)] for g in range(n // members)]

    query_slots = queries.reshape(local_rows, heads, width).transpose(1, 0, 2)
    query_slots = query_slots.reshape(members, heads // members, local_rows, width)

    def page_target(source, other):
        p, plane, rest = source // members, (source // plane_bit) % 2, source % plane_bit
        return (plane ^ other) * members + p * plane_bit + rest

    page_a, page_b = (
        lax.ppermute(cache[0], "head", [(d, page_target(d, other)) for d in range(n)])
        for other in range(2)
    )
    kv_heads = new_kv.reshape(local_rows, pair_heads, 2 * width).transpose(1, 0, 2)
    kv_ordered = jnp.stack(
        [
            lax.dynamic_index_in_dim(kv_heads, b, 0, keepdims=False),
            lax.dynamic_index_in_dim(kv_heads, 1 - b, 0, keepdims=False),
        ],
        0,
    )
    kv_beside = flipped(kv_ordered, "head", 2)

    columns = model // 2
    w = lax.dynamic_slice_in_dim(w_out, lax.axis_index("grp") * columns, columns, 2)
    w = w.reshape(2, 2, heads // 4, share, columns)
    w = [lax.dynamic_index_in_dim(w, plane, 0, keepdims=False) for plane in (b, 1 - b)]
    w_keep = [lax.dynamic_index_in_dim(part, y, 0, keepdims=False) for part in w]
    w_give = [lax.dynamic_index_in_dim(part, 1 - y, 0, keepdims=False) for part in w]
    w_got = flipped(jnp.stack(w_give, 0), "head", 2)

    page_a, page_b, kv_beside, w_got, query_slots = lax.optimization_barrier(
        (page_a, page_b, kv_beside, w_got, query_slots)
    )
    kv_same, kv_other = (jnp.stack([kv_ordered[k], kv_beside[k]], 0) for k in range(2))
    kv_own = [kv_same]
    for t in range(1, planes):
        kv_own.append(flipped(kv_other if t % 2 else kv_same, "head", t * plane_bit))
    own_pages = jnp.concatenate([page_a, page_b], 0)
    pages_y = flipped(own_pages, "head", 2)
    w_same, w_other = (jnp.stack([w_keep[k], w_got[k]], 0) for k in range(2))
    w_first = flipped(w_other, "head", plane_bit)
    query_slots, w_first = lax.optimization_barrier((query_slots, w_first))
    q = lax.all_to_all(
        query_slots, "head", split_axis=0, concat_axis=0, tiled=True, axis_index_groups=group_sets
    )
    pages_y, kv_own, w_first, q = lax.optimization_barrier((pages_y, kv_own, w_first, q))

    kv_own = jnp.stack(kv_own, 0)
    kv_c = flipped(kv_own, "head", 1)
    pages_c = flipped(own_pages, "head", 1)
    pages_cy = flipped(pages_y, "head", 1)
    w_near = jnp.stack([w_same, w_first], 0)
    w_far = flipped(w_near, "head", members)
    w_near_x = flipped(w_near, "grp", 1)
    a = attend_pair(q, (page_a, page_b, pages_y, pages_c, pages_cy), (kv_own, kv_c))
    got = flipped(a[1], "head", 1)
    a, w_far, w_near_x = lax.optimization_barrier((a, w_far, w_near_x))
    w_far_x = flipped(w_far, "grp", 1)
    w_near_c = flipped(w_near, "head", 1)
    w_far_c = flipped(w_far, "head", 1)
    w_near_cx = flipped(w_near_x, "head", 1)
    w_far_cx = flipped(w_far_x, "head", 1)
    partial = project_pair(
        a,
        got,
        (w_near, w_near_c, w_near_x, w_near_cx),
        (w_far, w_far_c, w_far_x, w_far_cx),
        members // 2,
    )
    parts = [partial[0]] + [flipped(partial[k], "head", 2 * k) for k in (3, 2, 1)]
    return [part[None] for part in parts]


def parts_in_planes(queries, new_kv, cache, w_out):
    n = lax.axis_size("head")
    local_rows, seqs, heads, width = queries.shape
    pair_heads = new_kv.shape[2]
    members = heads // pair_heads
    groups = n // members
    model = w_out.shape[2]
    side = 1 << ((n.bit_length() - 1) // 2)
    side = min(side, heads)
    planes = n // side
    planes_of_seq = heads // side
    pair_groups = [[g * members + m for m in range(members)] for g in range(groups)]
    cross_groups = [[g * members + m for g in range(groups)] for m in range(members)]
    plane_groups = [[p * side + m for m in range(side)] for p in range(planes)]
    column_groups = [[p * side + m for p in range(planes)] for m in range(side)]

    query_slots = queries.reshape(local_rows, n, width).transpose(1, 0, 2)
    q = lax.all_to_all(query_slots, "head", split_axis=0, concat_axis=0, tiled=True)
    q = q.reshape(n * local_rows, width)

    kv_slots = new_kv.reshape(local_rows, groups, 2 * width).transpose(1, 0, 2)
    kv = lax.all_to_all(
        kv_slots, "head", split_axis=0, concat_axis=0, tiled=True, axis_index_groups=cross_groups
    )
    kv = lax.all_gather(kv, "head", axis=0, axis_index_groups=pair_groups)
    pages = lax.all_gather(cache, "head", axis=0, tiled=True, axis_index_groups=pair_groups)

    share = w_out.shape[1]
    w_planes = w_out.reshape(planes_of_seq, side, share, model)
    if planes > planes_of_seq:
        w_planes = jnp.tile(w_planes, (planes // planes_of_seq, 1, 1, 1))
    w = lax.all_to_all(
        w_planes, "head", split_axis=0, concat_axis=0, tiled=True, axis_index_groups=column_groups
    )
    w = lax.all_gather(w, "head", axis=0, axis_index_groups=plane_groups)
    if share % 16:
        w = w.transpose(2, 1, 0, 3, 4).reshape(1, 1, side, width, model)
        w = w.reshape(side, width, model)

    attended = attend(q, pages.reshape(-1, 2 * width), kv)
    a = attended.reshape(planes, side, local_rows, width).transpose(1, 0, 2, 3)
    a = a.reshape(side, planes * local_rows, width)
    a = lax.all_to_all(
        a, "head", split_axis=0, concat_axis=0, tiled=True, axis_index_groups=plane_groups
    )
    if share % 16:
        partial = jnp.einsum("hri,hid->rd", a, w, preferred_element_type=F32).astype(BF16)
    else:
        partial = project(a, w)
    parts = lax.all_to_all(
        partial.reshape(planes, local_rows, model),
        "head",
        split_axis=0,
        concat_axis=0,
        tiled=True,
        axis_index_groups=column_groups,
    )
    parts = parts.reshape(seqs, planes_of_seq, local_rows, model)
    return [parts[:, k] for k in range(planes_of_seq)]


def local(queries, new_kv, cache, resid, w_out, norm_gain, expert_ids, expert_gates, w_in, w_down):
    n = lax.axis_size("head")
    local_rows, seqs, heads, width = queries.shape
    model = resid.shape[2]
    rows = local_rows * seqs
    members = heads // new_kv.shape[2]
    in_pairs = (
        lax.axis_size("grp") == 2
        and seqs == 1
        and new_kv.shape[2] == 2
        and n == heads == 2 * members
        and members == 8
        and cache.shape[0] == 1
        and w_in.shape[0] == 1
        and w_out.shape[1] % 16 == 0
    )
    plan = parts_in_pairs if in_pairs else parts_in_planes
    parts = plan(queries, new_kv, cache, w_out)

    top = expert_ids.shape[2]
    experts = w_in.shape[0] * n
    capacity = max(2, 2 * rows * top // experts)
    ids = expert_ids.transpose(1, 0, 2).reshape(rows, top)
    gates = expert_gates.transpose(1, 0, 2).reshape(rows, top)
    onehot = (ids[:, :, None] == jnp.arange(experts, dtype=jnp.int32)).astype(jnp.int32)
    named = onehot.sum(1)
    before = jnp.cumsum(named, 0) - named
    slots_of = ids * capacity + jnp.sum(onehot * before[:, None, :], 2)
    slots = experts * capacity

    stream, outgoing = route(
        parts, resid.transpose(1, 0, 2), norm_gain[None, :], slots_of.T, slots
    )
    arrived = lax.all_to_all(
        outgoing.reshape(n, slots // n, model), "head", split_axis=0, concat_axis=0, tiled=True
    )
    local_experts = w_in.shape[0]
    if local_experts == 1:
        answered = expert_pair(arrived.reshape(slots, model), w_in[0], w_down[0])
        answered = answered.reshape(n, slots // n, model)
    else:
        arrived = arrived.reshape(n, local_experts, capacity, model).transpose(1, 0, 2, 3)
        arrived = arrived.reshape(local_experts, n * capacity, model)
        answered = jnp.stack([expert(arrived[e], w_in[e], w_down[e]) for e in range(local_experts)])
        answered = answered.reshape(local_experts, n, capacity, model).transpose(1, 0, 2, 3)
        answered = answered.reshape(n, slots // n, model)
    back = lax.all_to_all(answered, "head", split_axis=0, concat_axis=0, tiled=True)
    out = combine(back.reshape(slots, model), stream, slots_of, gates, seqs)
    return out.transpose(1, 0, 2)


def solution(mesh):
    return jax.shard_map(
        local,
        mesh=mesh,
        in_specs=(
            P("head", "grp", None, None),
            P("head", "grp", None, None),
            P(("grp", "head"), None, None),
            P("head", "grp", None),
            P(None, "head", None),
            P(),
            P("head", "grp", None),
            P("head", "grp", None),
            P("head", None, None),
            P("head", None, None),
        ),
        out_specs=P("head", "grp", None),
        check_vma=False,
    )
```

```python
import functools

import jax
import jax.numpy as jnp
from jax import lax
from jax.experimental import pallas as pl
from jax.experimental.pallas import tpu as pltpu
from jax.sharding import PartitionSpec as P

eps_norm = 1e-06
F32 = jnp.float32
BF16 = jnp.bfloat16
HIGH_VMEM = 48 * 2**20
LOG2_E = 1.4426950408889634


def in_hbm():
    return pl.BlockSpec(memory_space=pltpu.HBM)


def in_vmem():
    return pl.BlockSpec(memory_space=pltpu.VMEM)


def attend_kernel(
    block, chunk, width, q_hbm, cache_hbm, kv_hbm, o_ref, q_ref, cache_ref, kv_ref, s0, s1, sems
):
    members, groups, piece, _ = kv_hbm.shape
    length = members * groups * piece
    old = cache_hbm.shape[0]
    scale = width**-0.5
    in_q = pltpu.make_async_copy(q_hbm, q_ref, sems.at[0])
    in_cache = pltpu.make_async_copy(cache_hbm, cache_ref, sems.at[1])
    in_q.start()
    in_cache.start()
    in_kv = []
    for group in range(groups):
        for member in range(members):
            place = (group * members + member) * piece
            copy = pltpu.make_async_copy(
                kv_hbm.at[member, group], kv_ref.at[pl.ds(place, piece)], sems.at[2]
            )
            copy.start()
            in_kv.append(copy)
    in_q.wait()
    in_cache.wait()
    for copy in in_kv:
        copy.wait()
    scores = [s0, s1]

    def pieces(b):
        out = [(True, k, chunk, k) for k in range(0, old, chunk)]
        last = b * block
        for k in range(0, last, chunk):
            out.append((False, k, min(chunk, last - k), old + k))
        out.append((False, last, block, old + last))
        return out

    def make_scores(b, part, running):
        of_cache, first, count, column = part
        keys = (cache_ref if of_cache else kv_ref)[pl.ds(first, count), :width]
        s = lax.dot_general(
            q_ref[pl.ds(b * block, block), :],
            keys,
            (((1,), (1,)), ((), ())),
            preferred_element_type=F32,
        )
        if not of_cache and first == b * block:
            row = lax.broadcasted_iota(jnp.int32, s.shape, 0)
            col = lax.broadcasted_iota(jnp.int32, s.shape, 1)
            s = jnp.where(col <= row, s, -jnp.inf)
        scores[b % 2][:, pl.ds(column, count)] = s
        for k in range(0, count, 128):
            piece_max = s[:, k : k + 128]
            running = piece_max if running is None else jnp.maximum(running, piece_max)
        return running

    def use_scores(b, part, top, total, acc):
        of_cache, first, count, column = part
        values = (cache_ref if of_cache else kv_ref)[pl.ds(first, count), width:]
        e = jnp.exp((scores[b % 2][:, pl.ds(column, count)] - top) * scale)
        for k in range(0, count, 128):
            total = e[:, k : k + 128] if total is None else total + e[:, k : k + 128]
        product = jnp.dot(e.astype(BF16), values, preferred_element_type=F32)
        return total, product if acc is None else acc + product

    blocks = length // block
    running = None
    for part in pieces(0):
        running = make_scores(0, part, running)
    for b in range(blocks):
        top = jnp.max(running, 1, keepdims=True)
        now, later = pieces(b), pieces(b + 1) if b + 1 < blocks else []
        running, total, acc = None, None, None
        for k in range(max(len(now), len(later))):
            if k < len(now):
                total, acc = use_scores(b, now[k], top, total, acc)
            if k < len(later):
                running = make_scores(b + 1, later[k], running)
        o_ref[pl.ds(b * block, block), :] = (acc / jnp.sum(total, 1, keepdims=True)).astype(BF16)


def attend(q, cache, kv):
    length, width = q.shape
    old = cache.shape[0]
    block = min(256, length)
    chunk = min(512, old)
    return pl.pallas_call(
        functools.partial(attend_kernel, block, chunk, width),
        out_shape=jax.ShapeDtypeStruct((length, width), BF16),
        in_specs=[in_hbm()] * 3,
        out_specs=in_vmem(),
        scratch_shapes=[
            pltpu.VMEM((length, width), BF16),
            pltpu.VMEM((old, 2 * width), BF16),
            pltpu.VMEM((length, 2 * width), BF16),
            pltpu.VMEM((block, old + length), F32),
            pltpu.VMEM((block, old + length), F32),
            pltpu.SemaphoreType.DMA((3,)),
        ],
        compiler_params=pltpu.CompilerParams(vmem_limit_bytes=HIGH_VMEM),
        cost_estimate=pl.CostEstimate(
            flops=4 * length * (old + length // 2) * width,
            bytes_accessed=4 * (2 * length + 2 * old) * width,
            transcendentals=length * (old + length // 2),
        ),
        name="attend",
    )(q, cache, kv)


def attend_pair_kernel(
    block,
    chunk,
    width,
    q_hbm,
    page_own,
    page_y,
    page_c,
    page_cy,
    kv_own,
    kv_y,
    kv_c,
    kv_cy,
    o_ref,
    q_ref,
    old_ref,
    kv_ref,
    s0,
    s1,
    sems,
):
    me = lax.axis_index("head")
    members, heads, piece, _ = q_hbm.shape
    length = members * piece
    planes = kv_own.shape[0]
    old = old_ref.shape[0]
    earlier_group = me // members > 0
    core = lax.rem(me, 2)
    chip = jnp.bitwise_and(me // 2, members // 2 - 1)
    copies = []

    def bring(source, target, sem):
        copy = pltpu.make_async_copy(source, target, sems.at[sem])
        copy.start()
        copies.append(copy)

    for member in range(members):
        for head in range(heads):
            bring(q_hbm.at[member, head], q_ref.at[head, pl.ds(member * piece, piece)], 0)
    place = 0
    for page in (page_own, page_y, page_c, page_cy):
        count = page.shape[0]
        bring(page, old_ref.at[pl.ds(place, count)], 1)
        place += count
    for flip, pieces_of in ((0, kv_own), (2, kv_y), (1, kv_c), (3, kv_cy)):
        for t in range(planes):
            number = jnp.bitwise_and(
                jnp.bitwise_xor(me, flip ^ (t * (members // 2))), members - 1
            )
            start = pl.multiple_of(number * piece, piece)
            area = 0 if t * (members // 2) >= members else length
            bring(pieces_of.at[t], kv_ref.at[pl.ds(area + start, piece)], 2)
    for copy in copies:
        copy.wait()
    scale = width**-0.5 * LOG2_E
    scores = [s0, s1]
    blocks = length // block
    units = [(head, b) for head in range(heads) for b in range(blocks)]

    def pieces(unit):
        _, b = units[unit]
        out = [("old", k, chunk, k) for k in range(0, old, chunk)]
        out += [("past", k, chunk, old + k) for k in range(0, length, chunk)]
        last = b * block
        for k in range(0, last, chunk):
            out.append(("new", length + k, min(chunk, last - k), old + length + k))
        out.append(("edge", length + last, block, old + length + last))
        return out

    def make_scores(unit, part, running):
        kind, first, count, column = part
        head, b = units[unit]
        keys = (old_ref if kind == "old" else kv_ref)[pl.ds(first, count), :width]
        s = lax.dot_general(
            q_ref[head, pl.ds(b * block, block), :],
            keys,
            (((1,), (1,)), ((), ())),
            preferred_element_type=F32,
        )
        if kind == "past":
            s = jnp.where(earlier_group, s, -jnp.inf)
        if kind == "edge":
            row = lax.broadcasted_iota(jnp.int32, s.shape, 0)
            col = lax.broadcasted_iota(jnp.int32, s.shape, 1)
            s = jnp.where(col <= row, s, -jnp.inf)
        scores[unit % 2][:, pl.ds(column, count)] = s
        for k in range(0, count, 128):
            piece_max = s[:, k : k + 128]
            running = piece_max if running is None else jnp.maximum(running, piece_max)
        return running

    def use_scores(unit, part, top, total, acc):
        kind, first, count, column = part
        values = (old_ref if kind == "old" else kv_ref)[pl.ds(first, count), width:]
        e = jnp.exp2((scores[unit % 2][:, pl.ds(column, count)] - top) * scale)
        for k in range(0, count, 128):
            total = e[:, k : k + 128] if total is None else total + e[:, k : k + 128]
        product = jnp.dot(e.astype(BF16), values, preferred_element_type=F32)
        return total, product if acc is None else acc + product

    running = None
    for part in pieces(0):
        running = make_scores(0, part, running)
    for unit, (head, b) in enumerate(units):
        top = jnp.max(running, 1, keepdims=True)
        now = pieces(unit)
        later = pieces(unit + 1) if unit + 1 < len(units) else []
        running, total, acc = None, None, None
        for k in range(max(len(now), len(later))):
            if k < len(now):
                total, acc = use_scores(unit, now[k], top, total, acc)
            if k < len(later):
                running = make_scores(unit + 1, later[k], running)
        done = (acc / jnp.sum(total, 1, keepdims=True)).astype(BF16)
        for k in range(0, block, piece):
            member = (b * block + k) // piece
            side = jnp.bitwise_xor(core, member % 2)
            start = pl.multiple_of(jnp.bitwise_xor(chip, member // 2) * piece, piece)
            o_ref[side, pl.ds(start, piece), pl.ds(head * width, width)] = done[k : k + piece]


def attend_pair(q, pages, kvs):
    members, heads, piece, width = q.shape
    length = members * piece
    old = sum(page.shape[0] for page in pages)
    block = 2 * piece
    chunk = min(512, old, length)
    keys = old + 2 * length
    return pl.pallas_call(
        functools.partial(attend_pair_kernel, block, chunk, width),
        out_shape=jax.ShapeDtypeStruct((2, length // 2, heads * width), BF16),
        in_specs=[in_hbm()] * (1 + len(pages) + len(kvs)),
        out_specs=in_vmem(),
        scratch_shapes=[
            pltpu.VMEM((heads, length, width), BF16),
            pltpu.VMEM((old, 2 * width), BF16),
            pltpu.VMEM((2 * length, 2 * width), BF16),
            pltpu.VMEM((block, keys), F32),
            pltpu.VMEM((block, keys), F32),
            pltpu.SemaphoreType.DMA((3,)),
        ],
        compiler_params=pltpu.CompilerParams(vmem_limit_bytes=HIGH_VMEM),
        cost_estimate=pl.CostEstimate(
            flops=4 * heads * length * (keys - length // 2) * width,
            bytes_accessed=4 * (heads * length + keys) * width,
            transcendentals=heads * length * (keys - length // 2),
        ),
        name="attend",
    )(q, *pages, *kvs)


def project_pair_kernel(a_ref, got_ref, *refs):
    near, far, outs, (w_ref, sems) = refs[:4], refs[4:8], refs[8:-2], refs[-2:]
    me = lax.axis_index("head")
    half = lax.axis_index("grp")
    core = lax.rem(me, 2)
    steps, sides, heads, share, columns = near[0].shape
    width = w_ref.shape[1]
    copies = []
    for first, given in ((0, near), (steps, far)):
        for flip, x, pieces_of in zip((0, 1, 0, 1), (0, 0, 1, 1), given):
            column = pl.multiple_of(jnp.bitwise_xor(half, x) * columns, columns)
            for t in range(steps):
                for u in range(sides):
                    number = jnp.bitwise_xor(me, flip ^ (2 * u) ^ (4 * (first + t)))
                    row = pl.multiple_of(number * share, share)
                    copy = pltpu.make_async_copy(
                        pieces_of.at[t, u],
                        w_ref.at[:, pl.ds(row, share), pl.ds(column, columns)],
                        sems.at[0],
                    )
                    copy.start()
                    copies.append(copy)
    for copy in copies:
        copy.wait()
    acc = None
    for k in range(heads):
        mine = k < heads // 2
        at = pl.ds((k % (heads // 2)) * width, width)
        rows_of = a_ref[0, :, at] if mine else got_ref[:, at]
        head = jnp.bitwise_xor(core, 0 if mine else 1) * (heads // 2) + k % (heads // 2)
        part = jnp.dot(rows_of, w_ref[head], preferred_element_type=F32)
        acc = part if acc is None else acc + part
    rows = outs[0].shape[0]
    for k, out in enumerate(outs):
        out[...] = acc[k * rows : (k + 1) * rows].astype(BF16)


def project_pair(a, got, near, far, parts):
    _, _, heads, share, columns = near[0].shape
    rows = got.shape[0]
    width = 2 * got.shape[1] // heads
    model = 2 * columns
    return pl.pallas_call(
        project_pair_kernel,
        out_shape=[jax.ShapeDtypeStruct((rows // parts, model), BF16)] * parts,
        in_specs=[in_vmem(), in_vmem()] + [in_hbm()] * 8,
        out_specs=[in_vmem()] * parts,
        scratch_shapes=[
            pltpu.VMEM((heads, width, model), BF16),
            pltpu.SemaphoreType.DMA((1,)),
        ],
        compiler_params=pltpu.CompilerParams(vmem_limit_bytes=HIGH_VMEM),
        cost_estimate=pl.CostEstimate(
            flops=2 * heads * rows * width * model,
            bytes_accessed=2 * (heads * width * model + heads * rows * width + rows * model),
            transcendentals=0,
        ),
        name="project",
    )(a, got, *near, *far)


def project_kernel(a_ref, w_ref, o_ref):
    members = a_ref.shape[0]
    planes, share = w_ref.shape[1], w_ref.shape[3]
    acc = None
    for head in range(members):
        w = jnp.concatenate(
            [w_ref[m, p, head] for p in range(planes) for m in range(members)], 0
        )
        part = jnp.dot(a_ref[head], w, preferred_element_type=F32)
        acc = part if acc is None else acc + part
    o_ref[...] = acc.astype(BF16)


def project(a, w):
    members, rows, width = a.shape
    planes, share, model = w.shape[1], w.shape[3], w.shape[4]
    tile = min(512, model)
    return pl.pallas_call(
        project_kernel,
        grid=(model // tile,),
        out_shape=jax.ShapeDtypeStruct((rows, model), BF16),
        in_specs=[
            pl.BlockSpec((members, rows, width), lambda t: (0, 0, 0)),
            pl.BlockSpec((members, planes, members, share, tile), lambda t: (0, 0, 0, 0, t)),
        ],
        out_specs=pl.BlockSpec((rows, tile), lambda t: (0, t)),
        compiler_params=pltpu.CompilerParams(vmem_limit_bytes=HIGH_VMEM),
        cost_estimate=pl.CostEstimate(
            flops=2 * members * rows * width * model,
            bytes_accessed=2 * (members * width * model + members * rows * width + rows * model),
            transcendentals=0,
        ),
        name="project",
    )(a, w)


def route_kernel(resid_ref, gain_ref, slots_ref, *refs):
    parts_refs, (stream_ref, out_ref) = refs[:-2], refs[-2:]
    seqs = resid_ref.shape[0]
    streams = []
    for seq in range(seqs):
        stream = resid_ref[seq].astype(F32)
        projected = parts_refs[0][seq].astype(F32)
        for part in parts_refs[1:]:
            projected = projected + part[seq].astype(F32)
        streams.append(stream + projected)
    stream = jnp.concatenate(streams, 0) if seqs > 1 else streams[0]
    stream_ref[...] = stream
    normed = stream * lax.rsqrt(jnp.mean(stream * stream, 1, keepdims=True) + eps_norm)
    normed = (normed * gain_ref[...]).astype(BF16)
    slots, rows = out_ref.shape[0], stream.shape[0]
    place = lax.broadcasted_iota(jnp.int32, (slots, rows), 0)
    hit = place == slots_ref[0:1, :]
    for k in range(1, slots_ref.shape[0]):
        hit = hit | (place == slots_ref[k : k + 1, :])
    out_ref[...] = jnp.dot(hit.astype(BF16), normed, preferred_element_type=F32).astype(BF16)


def route(parts, resid, gain, slots_of, slots):
    seqs, local_rows, model = resid.shape
    rows = seqs * local_rows
    return pl.pallas_call(
        route_kernel,
        out_shape=(
            jax.ShapeDtypeStruct((rows, model), F32),
            jax.ShapeDtypeStruct((slots, model), BF16),
        ),
        in_specs=[in_vmem()] * (3 + len(parts)),
        out_specs=(in_vmem(), in_vmem()),
        compiler_params=pltpu.CompilerParams(vmem_limit_bytes=HIGH_VMEM),
        cost_estimate=pl.CostEstimate(
            flops=2 * slots * rows * model,
            bytes_accessed=2 * (len(parts) + 3 + slots // rows) * rows * model,
            transcendentals=0,
        ),
        name="route",
    )(resid, gain, slots_of, *parts)


def expert_kernel(x_ref, w_in_ref, w_down_ref, o_ref):
    hidden_width = w_down_ref.shape[0]
    inner = jnp.dot(x_ref[...], w_in_ref[...], preferred_element_type=F32)
    gate = inner[:, :hidden_width]
    hidden = (gate / (1.0 + jnp.exp(-gate)) * inner[:, hidden_width:]).astype(BF16)
    o_ref[...] = jnp.dot(hidden, w_down_ref[...], preferred_element_type=F32).astype(BF16)


def expert(x, w_in, w_down):
    rows, model = x.shape
    hidden_width = w_down.shape[0]
    return pl.pallas_call(
        expert_kernel,
        out_shape=jax.ShapeDtypeStruct((rows, model), BF16),
        in_specs=[in_vmem()] * 3,
        out_specs=in_vmem(),
        compiler_params=pltpu.CompilerParams(vmem_limit_bytes=HIGH_VMEM),
        cost_estimate=pl.CostEstimate(
            flops=6 * rows * model * hidden_width,
            bytes_accessed=2 * (2 * rows * model + 3 * model * hidden_width),
            transcendentals=rows * hidden_width,
        ),
        name="expert",
    )(x, w_in, w_down)


def expert_pair(x, w_in, w_down):
    rows, model = x.shape
    hidden_width = w_down.shape[0]
    parts = 4
    depth = model // parts

    def kernel(x_hbm, in_hbm_ref, down_hbm, o_hbm, x_ref, in_ref, down_ref, o_ref, sems):
        bring_x = pltpu.make_async_copy(x_hbm, x_ref, sems.at[parts])
        bring_x.start()
        bring_in = []
        for k in range(parts):
            at = pl.ds(k * depth, depth)
            bring_in.append(pltpu.make_async_copy(in_hbm_ref.at[at], in_ref.at[at], sems.at[k]))
            bring_in[k].start()
        bring_down = pltpu.make_async_copy(down_hbm, down_ref, sems.at[parts + 1])
        bring_down.start()
        bring_x.wait()
        inner = None
        for k in range(parts):
            bring_in[k].wait()
            at = pl.ds(k * depth, depth)
            part = jnp.dot(x_ref[:, at], in_ref[at, :], preferred_element_type=F32)
            inner = part if inner is None else inner + part
        gate = inner[:, :hidden_width]
        hidden = (gate / (1.0 + jnp.exp(-gate)) * inner[:, hidden_width:]).astype(BF16)
        bring_down.wait()
        o_ref[...] = jnp.dot(hidden, down_ref[...], preferred_element_type=F32).astype(BF16)
        back = pltpu.make_async_copy(o_ref, o_hbm, sems.at[parts + 2])
        back.start()
        back.wait()

    return pl.pallas_call(
        kernel,
        out_shape=jax.ShapeDtypeStruct((rows, model), BF16),
        in_specs=[in_hbm()] * 3,
        out_specs=in_hbm(),
        scratch_shapes=[
            pltpu.VMEM((rows, model), BF16),
            pltpu.VMEM(w_in.shape, BF16),
            pltpu.VMEM(w_down.shape, BF16),
            pltpu.VMEM((rows, model), BF16),
            pltpu.SemaphoreType.DMA((parts + 3,)),
        ],
        compiler_params=pltpu.CompilerParams(vmem_limit_bytes=HIGH_VMEM),
        cost_estimate=pl.CostEstimate(
            flops=6 * rows * model * hidden_width,
            bytes_accessed=2 * (2 * rows * model + 3 * model * hidden_width),
            transcendentals=rows * hidden_width,
        ),
        name="expert",
    )(x, w_in, w_down)


def combine_kernel(seqs, back_ref, stream_ref, slots_ref, gates_ref, o_ref):
    slots = back_ref.shape[0]
    rows = stream_ref.shape[0]
    place = lax.broadcasted_iota(jnp.int32, (rows, slots), 1)
    total = stream_ref[...]
    gathered = None
    for k in range(slots_ref.shape[1]):
        pick = (place == slots_ref[:, k : k + 1]).astype(BF16)
        picked = jnp.dot(pick, back_ref[...], preferred_element_type=F32)
        part = picked * gates_ref[:, k : k + 1]
        gathered = part if gathered is None else gathered + part
    out = (total + gathered).astype(BF16)
    local_rows = rows // seqs
    for seq in range(seqs):
        o_ref[seq] = out[seq * local_rows : (seq + 1) * local_rows]


def combine(back, stream, slots_of, gates, seqs):
    slots, model = back.shape
    rows = stream.shape[0]
    top = slots_of.shape[1]
    return pl.pallas_call(
        functools.partial(combine_kernel, seqs),
        out_shape=jax.ShapeDtypeStruct((seqs, rows // seqs, model), BF16),
        in_specs=[in_vmem()] * 4,
        out_specs=in_vmem(),
        compiler_params=pltpu.CompilerParams(vmem_limit_bytes=HIGH_VMEM),
        cost_estimate=pl.CostEstimate(
            flops=2 * top * slots * rows * model,
            bytes_accessed=2 * slots * model + 6 * rows * model,
            transcendentals=0,
        ),
        name="combine",
    )(back, stream, slots_of, gates)


def flipped(value, axis, mask):
    pairs = [(source, source ^ mask) for source in range(lax.axis_size(axis))]
    return lax.ppermute(value, axis, pairs)


def parts_in_pairs(queries, new_kv, cache, w_out):
    n = lax.axis_size("head")
    local_rows, _, heads, width = queries.shape
    pair_heads = new_kv.shape[2]
    members = heads // pair_heads
    model = w_out.shape[2]
    share = w_out.shape[1]
    me = lax.axis_index("head")
    plane_bit = members // 2
    planes = n // plane_bit
    b = (me // plane_bit) % 2
    y = (me // 2) % 2
    group_sets = [[g * members + m for m in range(members)] for g in range(n // members)]

    query_slots = queries.reshape(local_rows, heads, width).transpose(1, 0, 2)
    query_slots = query_slots.reshape(members, heads // members, local_rows, width)
    q = lax.all_to_all(
        query_slots, "head", split_axis=0, concat_axis=0, tiled=True, axis_index_groups=group_sets
    )

    def page_target(source, other):
        p, plane, rest = source // members, (source // plane_bit) % 2, source % plane_bit
        return (plane ^ other) * members + p * plane_bit + rest

    page_a, page_b = (
        lax.ppermute(cache[0], "head", [(d, page_target(d, other)) for d in range(n)])
        for other in range(2)
    )
    kv_heads = new_kv.reshape(local_rows, pair_heads, 2 * width).transpose(1, 0, 2)
    kv_same = lax.dynamic_index_in_dim(kv_heads, b, 0, keepdims=False)
    kv_other = lax.dynamic_index_in_dim(kv_heads, 1 - b, 0, keepdims=False)
    columns = model // 2
    w = lax.dynamic_slice_in_dim(w_out, lax.axis_index("grp") * columns, columns, 2)
    w = w.reshape(2, 2, heads // 4, share, columns)
    w_keep = lax.dynamic_index_in_dim(w, y, 1, keepdims=False)
    w_give = lax.dynamic_index_in_dim(w, 1 - y, 1, keepdims=False)
    kv_own = [kv_same]
    for t in range(1, planes):
        kv_own.append(flipped(kv_other if t % 2 else kv_same, "head", t * plane_bit))

    (page_a, page_b, kv_own), w_give = lax.optimization_barrier(
        ((page_a, page_b, kv_own), w_give)
    )
    own_pages = jnp.concatenate([page_a, page_b], 0)
    kv_own = jnp.stack(kv_own, 0)
    pages_y = flipped(own_pages, "head", 2)
    kv_y = flipped(kv_own, "head", 2)
    w_got = flipped(w_give, "head", 2)
    w_both = jnp.stack([w_keep, w_got], 1)
    w_same = lax.dynamic_index_in_dim(w_both, b, 0, keepdims=False)
    w_other = lax.dynamic_index_in_dim(w_both, 1 - b, 0, keepdims=False)
    w_first = flipped(w_other, "head", plane_bit)
    w_far = [flipped(w_same, "head", 2 * plane_bit), flipped(w_other, "head", 3 * plane_bit)]
    pages_y, kv_y, own_pages, kv_own, w_first = lax.optimization_barrier(
        (pages_y, kv_y, own_pages, kv_own, w_first)
    )
    kv_c = flipped(kv_own, "head", 1)
    kv_cy = flipped(kv_y, "head", 1)
    pages_c = flipped(own_pages, "head", 1)
    pages_cy = flipped(pages_y, "head", 1)
    w_near = jnp.stack([w_same, w_first], 0)
    w_near_x = flipped(w_near, "grp", 1)
    w_far = jnp.stack(w_far, 0)
    q, w_far = lax.optimization_barrier((q, w_far))
    w_far_x = flipped(w_far, "grp", 1)
    a = attend_pair(q, (own_pages, pages_y, pages_c, pages_cy), (kv_own, kv_y, kv_c, kv_cy))
    got = flipped(a[1], "head", 1)
    a, w_near_x, w_far_x = lax.optimization_barrier((a, w_near_x, w_far_x))
    w_near_c = flipped(w_near, "head", 1)
    w_far_c = flipped(w_far, "head", 1)
    w_near_cx = flipped(w_near_x, "head", 1)
    w_far_cx = flipped(w_far_x, "head", 1)
    partial = project_pair(
        a,
        got,
        (w_near, w_near_c, w_near_x, w_near_cx),
        (w_far, w_far_c, w_far_x, w_far_cx),
        members // 2,
    )
    parts = [partial[0]] + [flipped(partial[k], "head", 2 * k) for k in (3, 2, 1)]
    return [part[None] for part in parts]


def parts_in_planes(queries, new_kv, cache, w_out):
    n = lax.axis_size("head")
    local_rows, seqs, heads, width = queries.shape
    pair_heads = new_kv.shape[2]
    members = heads // pair_heads
    groups = n // members
    model = w_out.shape[2]
    side = 1 << ((n.bit_length() - 1) // 2)
    side = min(side, heads)
    planes = n // side
    planes_of_seq = heads // side
    pair_groups = [[g * members + m for m in range(members)] for g in range(groups)]
    cross_groups = [[g * members + m for g in range(groups)] for m in range(members)]
    plane_groups = [[p * side + m for m in range(side)] for p in range(planes)]
    column_groups = [[p * side + m for p in range(planes)] for m in range(side)]

    query_slots = queries.reshape(local_rows, n, width).transpose(1, 0, 2)
    q = lax.all_to_all(query_slots, "head", split_axis=0, concat_axis=0, tiled=True)
    q = q.reshape(n * local_rows, width)

    kv_slots = new_kv.reshape(local_rows, groups, 2 * width).transpose(1, 0, 2)
    kv = lax.all_to_all(
        kv_slots, "head", split_axis=0, concat_axis=0, tiled=True, axis_index_groups=cross_groups
    )
    kv = lax.all_gather(kv, "head", axis=0, axis_index_groups=pair_groups)
    pages = lax.all_gather(cache, "head", axis=0, tiled=True, axis_index_groups=pair_groups)

    share = w_out.shape[1]
    w_planes = w_out.reshape(planes_of_seq, side, share, model)
    if planes > planes_of_seq:
        w_planes = jnp.tile(w_planes, (planes // planes_of_seq, 1, 1, 1))
    w = lax.all_to_all(
        w_planes, "head", split_axis=0, concat_axis=0, tiled=True, axis_index_groups=column_groups
    )
    w = lax.all_gather(w, "head", axis=0, axis_index_groups=plane_groups)
    if share % 16:
        w = w.transpose(2, 1, 0, 3, 4).reshape(1, 1, side, width, model)
        w = w.reshape(side, width, model)

    attended = attend(q, pages.reshape(-1, 2 * width), kv)
    a = attended.reshape(planes, side, local_rows, width).transpose(1, 0, 2, 3)
    a = a.reshape(side, planes * local_rows, width)
    a = lax.all_to_all(
        a, "head", split_axis=0, concat_axis=0, tiled=True, axis_index_groups=plane_groups
    )
    if share % 16:
        partial = jnp.einsum("hri,hid->rd", a, w, preferred_element_type=F32).astype(BF16)
    else:
        partial = project(a, w)
    parts = lax.all_to_all(
        partial.reshape(planes, local_rows, model),
        "head",
        split_axis=0,
        concat_axis=0,
        tiled=True,
        axis_index_groups=column_groups,
    )
    parts = parts.reshape(seqs, planes_of_seq, local_rows, model)
    return [parts[:, k] for k in range(planes_of_seq)]


def local(queries, new_kv, cache, resid, w_out, norm_gain, expert_ids, expert_gates, w_in, w_down):
    n = lax.axis_size("head")
    local_rows, seqs, heads, width = queries.shape
    model = resid.shape[2]
    rows = local_rows * seqs
    members = heads // new_kv.shape[2]
    in_pairs = (
        lax.axis_size("grp") == 2
        and seqs == 1
        and new_kv.shape[2] == 2
        and n == heads == 2 * members
        and members == 8
        and cache.shape[0] == 1
        and w_in.shape[0] == 1
        and w_out.shape[1] % 16 == 0
    )
    plan = parts_in_pairs if in_pairs else parts_in_planes
    parts = plan(queries, new_kv, cache, w_out)

    top = expert_ids.shape[2]
    experts = w_in.shape[0] * n
    capacity = max(2, 2 * rows * top // experts)
    ids = expert_ids.transpose(1, 0, 2).reshape(rows, top)
    gates = expert_gates.transpose(1, 0, 2).reshape(rows, top)
    onehot = (ids[:, :, None] == jnp.arange(experts, dtype=jnp.int32)).astype(jnp.int32)
    named = onehot.sum(1)
    before = jnp.cumsum(named, 0) - named
    slots_of = ids * capacity + jnp.sum(onehot * before[:, None, :], 2)
    slots = experts * capacity

    stream, outgoing = route(
        parts, resid.transpose(1, 0, 2), norm_gain[None, :], slots_of.T, slots
    )
    arrived = lax.all_to_all(
        outgoing.reshape(n, slots // n, model), "head", split_axis=0, concat_axis=0, tiled=True
    )
    local_experts = w_in.shape[0]
    if local_experts == 1:
        answered = expert_pair(arrived.reshape(slots, model), w_in[0], w_down[0])
        answered = answered.reshape(n, slots // n, model)
    else:
        arrived = arrived.reshape(n, local_experts, capacity, model).transpose(1, 0, 2, 3)
        arrived = arrived.reshape(local_experts, n * capacity, model)
        answered = jnp.stack([expert(arrived[e], w_in[e], w_down[e]) for e in range(local_experts)])
        answered = answered.reshape(local_experts, n, capacity, model).transpose(1, 0, 2, 3)
        answered = answered.reshape(n, slots // n, model)
    back = lax.all_to_all(answered, "head", split_axis=0, concat_axis=0, tiled=True)
    out = combine(back.reshape(slots, model), stream, slots_of, gates, seqs)
    return out.transpose(1, 0, 2)


def solution(mesh):
    return jax.shard_map(
        local,
        mesh=mesh,
        in_specs=(
            P("head", "grp", None, None),
            P("head", "grp", None, None),
            P(("grp", "head"), None, None),
            P("head", "grp", None),
            P(None, "head", None),
            P(),
            P("head", "grp", None),
            P("head", "grp", None),
            P("head", None, None),
            P("head", None, None),
        ),
        out_specs=P("head", "grp", None),
        check_vma=False,
    )
```

```python
import functools

import jax
import jax.numpy as jnp
from jax import lax
from jax.experimental import pallas as pl
from jax.experimental.pallas import tpu as pltpu
from jax.sharding import PartitionSpec as P

eps_norm = 1e-06
F32 = jnp.float32
BF16 = jnp.bfloat16
HIGH_VMEM = 48 * 2**20
LOG2_E = 1.4426950408889634


def in_hbm():
    return pl.BlockSpec(memory_space=pltpu.HBM)


def in_vmem():
    return pl.BlockSpec(memory_space=pltpu.VMEM)


def attend_kernel(
    block, chunk, width, q_hbm, cache_hbm, kv_hbm, o_ref, q_ref, cache_ref, kv_ref, s0, s1, sems
):
    members, groups, piece, _ = kv_hbm.shape
    length = members * groups * piece
    old = cache_hbm.shape[0]
    scale = width**-0.5
    in_q = pltpu.make_async_copy(q_hbm, q_ref, sems.at[0])
    in_cache = pltpu.make_async_copy(cache_hbm, cache_ref, sems.at[1])
    in_q.start()
    in_cache.start()
    in_kv = []
    for group in range(groups):
        for member in range(members):
            place = (group * members + member) * piece
            copy = pltpu.make_async_copy(
                kv_hbm.at[member, group], kv_ref.at[pl.ds(place, piece)], sems.at[2]
            )
            copy.start()
            in_kv.append(copy)
    in_q.wait()
    in_cache.wait()
    for copy in in_kv:
        copy.wait()
    scores = [s0, s1]

    def pieces(b):
        out = [(True, k, chunk, k) for k in range(0, old, chunk)]
        last = b * block
        for k in range(0, last, chunk):
            out.append((False, k, min(chunk, last - k), old + k))
        out.append((False, last, block, old + last))
        return out

    def make_scores(b, part, running):
        of_cache, first, count, column = part
        keys = (cache_ref if of_cache else kv_ref)[pl.ds(first, count), :width]
        s = lax.dot_general(
            q_ref[pl.ds(b * block, block), :],
            keys,
            (((1,), (1,)), ((), ())),
            preferred_element_type=F32,
        )
        if not of_cache and first == b * block:
            row = lax.broadcasted_iota(jnp.int32, s.shape, 0)
            col = lax.broadcasted_iota(jnp.int32, s.shape, 1)
            s = jnp.where(col <= row, s, -jnp.inf)
        scores[b % 2][:, pl.ds(column, count)] = s
        for k in range(0, count, 128):
            piece_max = s[:, k : k + 128]
            running = piece_max if running is None else jnp.maximum(running, piece_max)
        return running

    def use_scores(b, part, top, total, acc):
        of_cache, first, count, column = part
        values = (cache_ref if of_cache else kv_ref)[pl.ds(first, count), width:]
        e = jnp.exp((scores[b % 2][:, pl.ds(column, count)] - top) * scale)
        for k in range(0, count, 128):
            total = e[:, k : k + 128] if total is None else total + e[:, k : k + 128]
        product = jnp.dot(e.astype(BF16), values, preferred_element_type=F32)
        return total, product if acc is None else acc + product

    blocks = length // block
    running = None
    for part in pieces(0):
        running = make_scores(0, part, running)
    for b in range(blocks):
        top = jnp.max(running, 1, keepdims=True)
        now, later = pieces(b), pieces(b + 1) if b + 1 < blocks else []
        running, total, acc = None, None, None
        for k in range(max(len(now), len(later))):
            if k < len(now):
                total, acc = use_scores(b, now[k], top, total, acc)
            if k < len(later):
                running = make_scores(b + 1, later[k], running)
        o_ref[pl.ds(b * block, block), :] = (acc / jnp.sum(total, 1, keepdims=True)).astype(BF16)


def attend(q, cache, kv):
    length, width = q.shape
    old = cache.shape[0]
    block = min(256, length)
    chunk = min(512, old)
    return pl.pallas_call(
        functools.partial(attend_kernel, block, chunk, width),
        out_shape=jax.ShapeDtypeStruct((length, width), BF16),
        in_specs=[in_hbm()] * 3,
        out_specs=in_vmem(),
        scratch_shapes=[
            pltpu.VMEM((length, width), BF16),
            pltpu.VMEM((old, 2 * width), BF16),
            pltpu.VMEM((length, 2 * width), BF16),
            pltpu.VMEM((block, old + length), F32),
            pltpu.VMEM((block, old + length), F32),
            pltpu.SemaphoreType.DMA((3,)),
        ],
        compiler_params=pltpu.CompilerParams(vmem_limit_bytes=HIGH_VMEM),
        cost_estimate=pl.CostEstimate(
            flops=4 * length * (old + length // 2) * width,
            bytes_accessed=4 * (2 * length + 2 * old) * width,
            transcendentals=length * (old + length // 2),
        ),
        name="attend",
    )(q, cache, kv)


def attend_pair_kernel(
    block,
    chunk,
    width,
    q_hbm,
    page_a,
    page_b,
    page_y,
    page_c,
    page_cy,
    kv_own,
    kv_y,
    kv_c,
    kv_cy,
    o_ref,
    q_ref,
    old_ref,
    kv_ref,
    s0,
    s1,
    sems,
):
    me = lax.axis_index("head")
    members, heads, piece, _ = q_hbm.shape
    length = members * piece
    planes = kv_own.shape[0]
    old = old_ref.shape[0]
    earlier_group = me // members > 0
    core = lax.rem(me, 2)
    chip = jnp.bitwise_and(me // 2, members // 2 - 1)
    copies = []

    def bring(source, target, sem):
        copy = pltpu.make_async_copy(source, target, sems.at[sem])
        copy.start()
        copies.append(copy)

    for member in range(members):
        for head in range(heads):
            bring(q_hbm.at[member, head], q_ref.at[head, pl.ds(member * piece, piece)], 0)
    place = 0
    for page in (page_a, page_b, page_y, page_c, page_cy):
        count = page.shape[0]
        bring(page, old_ref.at[pl.ds(place, count)], 1)
        place += count
    for flip, pieces_of in ((0, kv_own), (2, kv_y), (1, kv_c), (3, kv_cy)):
        for t in range(planes):
            number = jnp.bitwise_and(
                jnp.bitwise_xor(me, flip ^ (t * (members // 2))), members - 1
            )
            start = pl.multiple_of(number * piece, piece)
            area = 0 if t * (members // 2) >= members else length
            bring(pieces_of.at[t], kv_ref.at[pl.ds(area + start, piece)], 2)
    for copy in copies:
        copy.wait()
    scale = width**-0.5 * LOG2_E
    scores = [s0, s1]
    blocks = length // block
    units = [(head, b) for head in range(heads) for b in range(blocks)]

    def pieces(unit):
        _, b = units[unit]
        out = [("old", k, chunk, k) for k in range(0, old, chunk)]
        out += [("past", k, chunk, old + k) for k in range(0, length, chunk)]
        last = b * block
        for k in range(0, last, chunk):
            out.append(("new", length + k, min(chunk, last - k), old + length + k))
        out.append(("edge", length + last, block, old + length + last))
        return out

    def make_scores(unit, part, running):
        kind, first, count, column = part
        head, b = units[unit]
        keys = (old_ref if kind == "old" else kv_ref)[pl.ds(first, count), :width]
        s = lax.dot_general(
            q_ref[head, pl.ds(b * block, block), :],
            keys,
            (((1,), (1,)), ((), ())),
            preferred_element_type=F32,
        )
        if kind == "past":
            s = jnp.where(earlier_group, s, -jnp.inf)
        if kind == "edge":
            row = lax.broadcasted_iota(jnp.int32, s.shape, 0)
            col = lax.broadcasted_iota(jnp.int32, s.shape, 1)
            s = jnp.where(col <= row, s, -jnp.inf)
        scores[unit % 2][:, pl.ds(column, count)] = s
        for k in range(0, count, 128):
            piece_max = s[:, k : k + 128]
            running = piece_max if running is None else jnp.maximum(running, piece_max)
        return running

    def use_scores(unit, part, top, total, acc):
        kind, first, count, column = part
        values = (old_ref if kind == "old" else kv_ref)[pl.ds(first, count), width:]
        e = jnp.exp2((scores[unit % 2][:, pl.ds(column, count)] - top) * scale)
        for k in range(0, count, 128):
            total = e[:, k : k + 128] if total is None else total + e[:, k : k + 128]
        product = jnp.dot(e.astype(BF16), values, preferred_element_type=F32)
        return total, product if acc is None else acc + product

    running = None
    for part in pieces(0):
        running = make_scores(0, part, running)
    for unit, (head, b) in enumerate(units):
        top = jnp.max(running, 1, keepdims=True)
        now = pieces(unit)
        later = pieces(unit + 1) if unit + 1 < len(units) else []
        running, total, acc = None, None, None
        for k in range(max(len(now), len(later))):
            if k < len(now):
                total, acc = use_scores(unit, now[k], top, total, acc)
            if k < len(later):
                running = make_scores(unit + 1, later[k], running)
        done = (acc / jnp.sum(total, 1, keepdims=True)).astype(BF16)
        for k in range(0, block, piece):
            member = (b * block + k) // piece
            side = jnp.bitwise_xor(core, member % 2)
            start = pl.multiple_of(jnp.bitwise_xor(chip, member // 2) * piece, piece)
            o_ref[side, pl.ds(start, piece), pl.ds(head * width, width)] = done[k : k + piece]


def attend_pair(q, pages, kvs):
    members, heads, piece, width = q.shape
    length = members * piece
    old = sum(page.shape[0] for page in pages)
    block = 2 * piece
    chunk = min(512, old, length)
    keys = old + 2 * length
    return pl.pallas_call(
        functools.partial(attend_pair_kernel, block, chunk, width),
        out_shape=jax.ShapeDtypeStruct((2, length // 2, heads * width), BF16),
        in_specs=[in_hbm()] * (1 + len(pages) + len(kvs)),
        out_specs=in_vmem(),
        scratch_shapes=[
            pltpu.VMEM((heads, length, width), BF16),
            pltpu.VMEM((old, 2 * width), BF16),
            pltpu.VMEM((2 * length, 2 * width), BF16),
            pltpu.VMEM((block, keys), F32),
            pltpu.VMEM((block, keys), F32),
            pltpu.SemaphoreType.DMA((3,)),
        ],
        compiler_params=pltpu.CompilerParams(vmem_limit_bytes=HIGH_VMEM),
        cost_estimate=pl.CostEstimate(
            flops=4 * heads * length * (keys - length // 2) * width,
            bytes_accessed=4 * (heads * length + keys) * width,
            transcendentals=heads * length * (keys - length // 2),
        ),
        name="attend",
    )(q, *pages, *kvs)


def project_pair_kernel(a_ref, got_ref, *refs):
    given, outs, (w_ref, sems) = refs[:4], refs[4:-2], refs[-2:]
    me = lax.axis_index("head")
    half = lax.axis_index("grp")
    core = lax.rem(me, 2)
    planes, sides, heads, share, columns = given[0].shape
    width = w_ref.shape[1]
    copies = []
    for flip, x, pieces_of in zip((0, 1, 0, 1), (0, 0, 1, 1), given):
        column = pl.multiple_of(jnp.bitwise_xor(half, x) * columns, columns)
        for t in range(planes):
            for u in range(sides):
                number = jnp.bitwise_xor(me, flip ^ (2 * u) ^ (4 * t))
                row = pl.multiple_of(number * share, share)
                copy = pltpu.make_async_copy(
                    pieces_of.at[t, u],
                    w_ref.at[:, pl.ds(row, share), pl.ds(column, columns)],
                    sems.at[0],
                )
                copy.start()
                copies.append(copy)
    for copy in copies:
        copy.wait()
    acc = None
    for k in range(heads):
        mine = k < heads // 2
        at = pl.ds((k % (heads // 2)) * width, width)
        rows_of = a_ref[0, :, at] if mine else got_ref[:, at]
        head = jnp.bitwise_xor(core, 0 if mine else 1) * (heads // 2) + k % (heads // 2)
        part = jnp.dot(rows_of, w_ref[head], preferred_element_type=F32)
        acc = part if acc is None else acc + part
    rows = outs[0].shape[0]
    for k, out in enumerate(outs):
        out[...] = acc[k * rows : (k + 1) * rows].astype(BF16)


def project_pair(a, got, given, parts):
    _, _, heads, share, columns = given[0].shape
    rows = got.shape[0]
    width = 2 * got.shape[1] // heads
    model = 2 * columns
    return pl.pallas_call(
        project_pair_kernel,
        out_shape=[jax.ShapeDtypeStruct((rows // parts, model), BF16)] * parts,
        in_specs=[in_vmem(), in_vmem()] + [in_hbm()] * 4,
        out_specs=[in_vmem()] * parts,
        scratch_shapes=[
            pltpu.VMEM((heads, width, model), BF16),
            pltpu.SemaphoreType.DMA((1,)),
        ],
        compiler_params=pltpu.CompilerParams(vmem_limit_bytes=HIGH_VMEM),
        cost_estimate=pl.CostEstimate(
            flops=2 * heads * rows * width * model,
            bytes_accessed=2 * (heads * width * model + heads * rows * width + rows * model),
            transcendentals=0,
        ),
        name="project",
    )(a, got, *given)


def project_kernel(a_ref, w_ref, o_ref):
    members = a_ref.shape[0]
    planes, share = w_ref.shape[1], w_ref.shape[3]
    acc = None
    for head in range(members):
        w = jnp.concatenate(
            [w_ref[m, p, head] for p in range(planes) for m in range(members)], 0
        )
        part = jnp.dot(a_ref[head], w, preferred_element_type=F32)
        acc = part if acc is None else acc + part
    o_ref[...] = acc.astype(BF16)


def project(a, w):
    members, rows, width = a.shape
    planes, share, model = w.shape[1], w.shape[3], w.shape[4]
    tile = min(512, model)
    return pl.pallas_call(
        project_kernel,
        grid=(model // tile,),
        out_shape=jax.ShapeDtypeStruct((rows, model), BF16),
        in_specs=[
            pl.BlockSpec((members, rows, width), lambda t: (0, 0, 0)),
            pl.BlockSpec((members, planes, members, share, tile), lambda t: (0, 0, 0, 0, t)),
        ],
        out_specs=pl.BlockSpec((rows, tile), lambda t: (0, t)),
        compiler_params=pltpu.CompilerParams(vmem_limit_bytes=HIGH_VMEM),
        cost_estimate=pl.CostEstimate(
            flops=2 * members * rows * width * model,
            bytes_accessed=2 * (members * width * model + members * rows * width + rows * model),
            transcendentals=0,
        ),
        name="project",
    )(a, w)


def route_kernel(resid_ref, gain_ref, slots_ref, *refs):
    parts_refs, (stream_ref, out_ref) = refs[:-2], refs[-2:]
    seqs = resid_ref.shape[0]
    streams = []
    for seq in range(seqs):
        stream = resid_ref[seq].astype(F32)
        projected = parts_refs[0][seq].astype(F32)
        for part in parts_refs[1:]:
            projected = projected + part[seq].astype(F32)
        streams.append(stream + projected)
    stream = jnp.concatenate(streams, 0) if seqs > 1 else streams[0]
    stream_ref[...] = stream
    normed = stream * lax.rsqrt(jnp.mean(stream * stream, 1, keepdims=True) + eps_norm)
    normed = (normed * gain_ref[...]).astype(BF16)
    slots, rows = out_ref.shape[0], stream.shape[0]
    place = lax.broadcasted_iota(jnp.int32, (slots, rows), 0)
    hit = place == slots_ref[0:1, :]
    for k in range(1, slots_ref.shape[0]):
        hit = hit | (place == slots_ref[k : k + 1, :])
    out_ref[...] = jnp.dot(hit.astype(BF16), normed, preferred_element_type=F32).astype(BF16)


def route(parts, resid, gain, slots_of, slots):
    seqs, local_rows, model = resid.shape
    rows = seqs * local_rows
    return pl.pallas_call(
        route_kernel,
        out_shape=(
            jax.ShapeDtypeStruct((rows, model), F32),
            jax.ShapeDtypeStruct((slots, model), BF16),
        ),
        in_specs=[in_vmem()] * (3 + len(parts)),
        out_specs=(in_vmem(), in_vmem()),
        compiler_params=pltpu.CompilerParams(vmem_limit_bytes=HIGH_VMEM),
        cost_estimate=pl.CostEstimate(
            flops=2 * slots * rows * model,
            bytes_accessed=2 * (len(parts) + 3 + slots // rows) * rows * model,
            transcendentals=0,
        ),
        name="route",
    )(resid, gain, slots_of, *parts)


def expert_kernel(x_ref, w_in_ref, w_down_ref, o_ref):
    hidden_width = w_down_ref.shape[0]
    inner = jnp.dot(x_ref[...], w_in_ref[...], preferred_element_type=F32)
    gate = inner[:, :hidden_width]
    hidden = (gate / (1.0 + jnp.exp(-gate)) * inner[:, hidden_width:]).astype(BF16)
    o_ref[...] = jnp.dot(hidden, w_down_ref[...], preferred_element_type=F32).astype(BF16)


def expert(x, w_in, w_down):
    rows, model = x.shape
    hidden_width = w_down.shape[0]
    return pl.pallas_call(
        expert_kernel,
        out_shape=jax.ShapeDtypeStruct((rows, model), BF16),
        in_specs=[in_vmem()] * 3,
        out_specs=in_vmem(),
        compiler_params=pltpu.CompilerParams(vmem_limit_bytes=HIGH_VMEM),
        cost_estimate=pl.CostEstimate(
            flops=6 * rows * model * hidden_width,
            bytes_accessed=2 * (2 * rows * model + 3 * model * hidden_width),
            transcendentals=rows * hidden_width,
        ),
        name="expert",
    )(x, w_in, w_down)


def expert_pair(x, w_in, w_down):
    rows, model = x.shape
    hidden_width = w_down.shape[0]
    parts = 4
    depth = model // parts

    def kernel(x_hbm, in_hbm_ref, down_hbm, o_hbm, x_ref, in_ref, down_ref, o_ref, sems):
        bring_x = pltpu.make_async_copy(x_hbm, x_ref, sems.at[parts])
        bring_x.start()
        bring_in = []
        for k in range(parts):
            at = pl.ds(k * depth, depth)
            bring_in.append(pltpu.make_async_copy(in_hbm_ref.at[at], in_ref.at[at], sems.at[k]))
            bring_in[k].start()
        bring_down = pltpu.make_async_copy(down_hbm, down_ref, sems.at[parts + 1])
        bring_down.start()
        bring_x.wait()
        inner = None
        for k in range(parts):
            bring_in[k].wait()
            at = pl.ds(k * depth, depth)
            part = jnp.dot(x_ref[:, at], in_ref[at, :], preferred_element_type=F32)
            inner = part if inner is None else inner + part
        gate = inner[:, :hidden_width]
        hidden = (gate / (1.0 + jnp.exp(-gate)) * inner[:, hidden_width:]).astype(BF16)
        bring_down.wait()
        o_ref[...] = jnp.dot(hidden, down_ref[...], preferred_element_type=F32).astype(BF16)
        back = pltpu.make_async_copy(o_ref, o_hbm, sems.at[parts + 2])
        back.start()
        back.wait()

    return pl.pallas_call(
        kernel,
        out_shape=jax.ShapeDtypeStruct((rows, model), BF16),
        in_specs=[in_hbm()] * 3,
        out_specs=in_hbm(),
        scratch_shapes=[
            pltpu.VMEM((rows, model), BF16),
            pltpu.VMEM(w_in.shape, BF16),
            pltpu.VMEM(w_down.shape, BF16),
            pltpu.VMEM((rows, model), BF16),
            pltpu.SemaphoreType.DMA((parts + 3,)),
        ],
        compiler_params=pltpu.CompilerParams(vmem_limit_bytes=HIGH_VMEM),
        cost_estimate=pl.CostEstimate(
            flops=6 * rows * model * hidden_width,
            bytes_accessed=2 * (2 * rows * model + 3 * model * hidden_width),
            transcendentals=rows * hidden_width,
        ),
        name="expert",
    )(x, w_in, w_down)


def combine_kernel(seqs, back_ref, stream_ref, slots_ref, gates_ref, o_ref):
    slots = back_ref.shape[0]
    rows = stream_ref.shape[0]
    place = lax.broadcasted_iota(jnp.int32, (rows, slots), 1)
    total = stream_ref[...]
    gathered = None
    for k in range(slots_ref.shape[1]):
        pick = (place == slots_ref[:, k : k + 1]).astype(BF16)
        picked = jnp.dot(pick, back_ref[...], preferred_element_type=F32)
        part = picked * gates_ref[:, k : k + 1]
        gathered = part if gathered is None else gathered + part
    out = (total + gathered).astype(BF16)
    local_rows = rows // seqs
    for seq in range(seqs):
        o_ref[seq] = out[seq * local_rows : (seq + 1) * local_rows]


def combine(back, stream, slots_of, gates, seqs):
    slots, model = back.shape
    rows = stream.shape[0]
    top = slots_of.shape[1]
    return pl.pallas_call(
        functools.partial(combine_kernel, seqs),
        out_shape=jax.ShapeDtypeStruct((seqs, rows // seqs, model), BF16),
        in_specs=[in_vmem()] * 4,
        out_specs=in_vmem(),
        compiler_params=pltpu.CompilerParams(vmem_limit_bytes=HIGH_VMEM),
        cost_estimate=pl.CostEstimate(
            flops=2 * top * slots * rows * model,
            bytes_accessed=2 * slots * model + 6 * rows * model,
            transcendentals=0,
        ),
        name="combine",
    )(back, stream, slots_of, gates)


def slot_matrix(slots_ref, slots, rows):
    place = lax.broadcasted_iota(jnp.int32, (slots, rows), 0).astype(F32)
    hit = place == slots_ref[0:1, :]
    for k in range(1, slots_ref.shape[0]):
        hit = hit | (place == slots_ref[k : k + 1, :])
    return hit.astype(BF16)


def by_copies(body, name, inputs, outputs, flops, bytes_accessed, transcendentals=0):
    count = len(inputs)

    def kernel(*refs):
        ins, outs = refs[:count], refs[count : count + len(outputs)]
        rest = refs[count + len(outputs) :]
        in_vm, out_vm, sems = rest[:count], rest[count:-1], rest[-1]
        copies = [
            pltpu.make_async_copy(ins[k], in_vm[k], sems.at[k]) for k in range(count)
        ]
        for copy in copies:
            copy.start()
        body(lambda k: copies[k].wait(), in_vm, out_vm)
        back = [
            pltpu.make_async_copy(out_vm[k], outs[k], sems.at[count + k])
            for k in range(len(outputs))
        ]
        for copy in back:
            copy.start()
        for copy in back:
            copy.wait()

    shapes = [jax.ShapeDtypeStruct(shape, dtype) for shape, dtype in outputs]
    return pl.pallas_call(
        kernel,
        out_shape=shapes,
        in_specs=[in_hbm()] * count,
        out_specs=[in_hbm()] * len(outputs),
        scratch_shapes=[pltpu.VMEM(x.shape, x.dtype) for x in inputs]
        + [pltpu.VMEM(shape, dtype) for shape, dtype in outputs]
        + [pltpu.SemaphoreType.DMA((count + len(outputs),))],
        compiler_params=pltpu.CompilerParams(vmem_limit_bytes=HIGH_VMEM),
        cost_estimate=pl.CostEstimate(
            flops=flops, bytes_accessed=bytes_accessed, transcendentals=transcendentals
        ),
        name=name,
    )(*inputs)


def join_pair(parts, resid, gain):
    rows, model = resid.shape
    count = len(parts)

    def body(wait, ins, outs):
        wait(0)
        total = ins[0][...].astype(F32)
        for k in range(1, count):
            wait(k)
            total = total + ins[k][...].astype(F32)
        wait(count)
        stream = ins[count][...].astype(F32) + total
        outs[0][...] = stream
        normed = stream * lax.rsqrt(jnp.mean(stream * stream, 1, keepdims=True) + eps_norm)
        wait(count + 1)
        outs[1][...] = (normed * ins[count + 1][...]).astype(BF16)

    return by_copies(
        body,
        "join",
        list(parts) + [resid, gain],
        [((rows, model), F32), ((rows, model), BF16)],
        8 * rows * model,
        2 * (count + 4) * rows * model,
    )


def spread(given, slots_of, slots, which):
    rows, model = given.shape[-2:]

    def body(wait, ins, outs):
        wait(1)
        matrix = slot_matrix(ins[1], slots, rows)
        wait(0)
        chosen = ins[0][...] if which is None else ins[0][which()]
        outs[0][...] = jnp.dot(matrix, chosen, preferred_element_type=F32).astype(BF16)

    return by_copies(
        body,
        "spread",
        [given, slots_of],
        [((slots, model), BF16)],
        2 * slots * rows * model,
        2 * (rows + slots) * model,
    )[0]


def gather(back, slots_of, gates, stream, partial, which):
    slots, model = back.shape
    rows, top = slots_of.shape
    more = [] if stream is None else [stream, partial]

    def body(wait, ins, outs):
        back_ref, slots_ref, gates_ref = ins[:3]
        for k in (1, 2, 0):
            wait(k)
        place = lax.broadcasted_iota(jnp.int32, (rows, slots), 1).astype(F32)
        total = None
        for k in range(top):
            pick = (place == slots_ref[:, k : k + 1]).astype(BF16)
            picked = jnp.dot(pick, back_ref[...], preferred_element_type=F32)
            part = picked * gates_ref[:, k : k + 1]
            total = part if total is None else total + part
        if more:
            wait(3)
            wait(4)
            total = ins[3][...] + (total + ins[4][which()].astype(F32))
        outs[0][...] = total.astype(BF16)

    return by_copies(
        body,
        "gather",
        [back, slots_of, gates] + more,
        [((rows, model), BF16)],
        2 * top * slots * rows * model,
        2 * (slots + 4 * rows) * model,
    )[0]


def flipped(value, axis, mask):
    pairs = [(source, source ^ mask) for source in range(lax.axis_size(axis))]
    return lax.ppermute(value, axis, pairs)


def parts_in_pairs(queries, new_kv, cache, w_out, other):
    n = lax.axis_size("head")
    local_rows, _, heads, width = queries.shape
    pair_heads = new_kv.shape[2]
    members = heads // pair_heads
    model = w_out.shape[2]
    share = w_out.shape[1]
    me = lax.axis_index("head")
    plane_bit = members // 2
    planes = n // plane_bit
    b = (me // plane_bit) % 2
    y = (me // 2) % 2
    group_sets = [[g * members + m for m in range(members)] for g in range(n // members)]

    query_slots = queries.reshape(local_rows, heads, width).transpose(1, 0, 2)
    query_slots = query_slots.reshape(members, heads // members, local_rows, width)
    q = lax.all_to_all(
        query_slots, "head", split_axis=0, concat_axis=0, tiled=True, axis_index_groups=group_sets
    )

    def page_target(source, other):
        p, plane, rest = source // members, (source // plane_bit) % 2, source % plane_bit
        return (plane ^ other) * members + p * plane_bit + rest

    page_a, page_b = (
        lax.ppermute(cache[0], "head", [(d, page_target(d, other)) for d in range(n)])
        for other in range(2)
    )
    kv_heads = new_kv.reshape(local_rows, pair_heads, 2 * width).transpose(1, 0, 2)
    kv_same = lax.dynamic_index_in_dim(kv_heads, b, 0, keepdims=False)
    kv_other = lax.dynamic_index_in_dim(kv_heads, 1 - b, 0, keepdims=False)
    kv_own = [kv_same]
    for t in range(1, planes):
        kv_own.append(flipped(kv_other if t % 2 else kv_same, "head", t * plane_bit))

    columns = model // 2
    w = lax.dynamic_slice_in_dim(w_out, lax.axis_index("grp") * columns, columns, 2)
    w = w.reshape(2, 2, heads // 4, share, columns)
    w_keep = lax.dynamic_index_in_dim(w, y, 1, keepdims=False)
    w_give = lax.dynamic_index_in_dim(w, 1 - y, 1, keepdims=False)
    w_got = flipped(w_give, "head", 2)

    (page_a, page_b, kv_own, q), w_got = lax.optimization_barrier(
        ((page_a, page_b, kv_own, q), w_got)
    )
    own_pages = jnp.concatenate([page_a, page_b], 0)
    kv_own = jnp.stack(kv_own, 0)
    pages_y = flipped(own_pages, "head", 2)
    kv_y = flipped(kv_own, "head", 2)
    w_both = jnp.stack([w_keep, w_got], 1)
    w_same = lax.dynamic_index_in_dim(w_both, b, 0, keepdims=False)
    w_other = lax.dynamic_index_in_dim(w_both, 1 - b, 0, keepdims=False)
    w_own = [w_same]
    for t in range(1, planes):
        w_own.append(flipped(w_other if t % 2 else w_same, "head", t * plane_bit))
    pages_c = flipped(own_pages, "head", 1)
    kv_c = flipped(kv_own, "head", 1)
    (pages_y, kv_y), w_own = lax.optimization_barrier(((pages_y, kv_y), w_own))
    pages_cy = flipped(pages_y, "head", 1)
    kv_cy = flipped(kv_y, "head", 1)
    w_own = jnp.stack(w_own, 0)
    q, w_own = lax.optimization_barrier((q, w_own))
    w_x = flipped(w_own, "grp", 1)
    w_c = flipped(w_own, "head", 1)
    a = attend_pair(
        q, (page_a, page_b, pages_y, pages_c, pages_cy), (kv_own, kv_y, kv_c, kv_cy)
    )
    got = flipped(a[1], "head", 1)
    a, w_x, w_c, other = lax.optimization_barrier((a, w_x, w_c, other))
    w_cx = flipped(w_x, "head", 1)
    partial = project_pair(a, got, (w_own, w_c, w_x, w_cx), members // 2)
    parts = [partial[0]] + [flipped(partial[k], "head", 2 * k) for k in (3, 2, 1)]
    return parts, other


def parts_in_planes(queries, new_kv, cache, w_out):
    n = lax.axis_size("head")
    local_rows, seqs, heads, width = queries.shape
    pair_heads = new_kv.shape[2]
    members = heads // pair_heads
    groups = n // members
    model = w_out.shape[2]
    side = 1 << ((n.bit_length() - 1) // 2)
    side = min(side, heads)
    planes = n // side
    planes_of_seq = heads // side
    pair_groups = [[g * members + m for m in range(members)] for g in range(groups)]
    cross_groups = [[g * members + m for g in range(groups)] for m in range(members)]
    plane_groups = [[p * side + m for m in range(side)] for p in range(planes)]
    column_groups = [[p * side + m for p in range(planes)] for m in range(side)]

    query_slots = queries.reshape(local_rows, n, width).transpose(1, 0, 2)
    q = lax.all_to_all(query_slots, "head", split_axis=0, concat_axis=0, tiled=True)
    q = q.reshape(n * local_rows, width)

    kv_slots = new_kv.reshape(local_rows, groups, 2 * width).transpose(1, 0, 2)
    kv = lax.all_to_all(
        kv_slots, "head", split_axis=0, concat_axis=0, tiled=True, axis_index_groups=cross_groups
    )
    kv = lax.all_gather(kv, "head", axis=0, axis_index_groups=pair_groups)
    pages = lax.all_gather(cache, "head", axis=0, tiled=True, axis_index_groups=pair_groups)

    share = w_out.shape[1]
    w_planes = w_out.reshape(planes_of_seq, side, share, model)
    if planes > planes_of_seq:
        w_planes = jnp.tile(w_planes, (planes // planes_of_seq, 1, 1, 1))
    w = lax.all_to_all(
        w_planes, "head", split_axis=0, concat_axis=0, tiled=True, axis_index_groups=column_groups
    )
    w = lax.all_gather(w, "head", axis=0, axis_index_groups=plane_groups)
    if share % 16:
        w = w.transpose(2, 1, 0, 3, 4).reshape(1, 1, side, width, model)
        w = w.reshape(side, width, model)

    attended = attend(q, pages.reshape(-1, 2 * width), kv)
    a = attended.reshape(planes, side, local_rows, width).transpose(1, 0, 2, 3)
    a = a.reshape(side, planes * local_rows, width)
    a = lax.all_to_all(
        a, "head", split_axis=0, concat_axis=0, tiled=True, axis_index_groups=plane_groups
    )
    if share % 16:
        partial = jnp.einsum("hri,hid->rd", a, w, preferred_element_type=F32).astype(BF16)
    else:
        partial = project(a, w)
    parts = lax.all_to_all(
        partial.reshape(planes, local_rows, model),
        "head",
        split_axis=0,
        concat_axis=0,
        tiled=True,
        axis_index_groups=column_groups,
    )
    parts = parts.reshape(seqs, planes_of_seq, local_rows, model)
    return [parts[:, k] for k in range(planes_of_seq)]


def route_in_pairs(parts, resid, norm_gain, own, other, top, w_in, w_down, capacity, members):
    n = lax.axis_size("head")
    local_rows, seqs, model = resid.shape
    me = lax.axis_index("head")
    group_sets = [[g * members + m for m in range(members)] for g in range(n // members)]
    couples = [[m, m + members] for m in range(members)]
    group_slots = members * capacity

    def around(value):
        value = value.reshape(members, capacity, model)
        value = lax.all_to_all(
            value, "head", split_axis=0, concat_axis=0, tiled=True, axis_index_groups=group_sets
        )
        return value.reshape(group_slots, model)

    def across(value):
        return lax.all_gather(value, "head", axis=0, axis_index_groups=couples)

    def other_group():
        return 1 - lax.axis_index("head") // members

    first = ((me // members) * group_slots).astype(F32)
    slots_own, gates_own = own[:, :top] - first, own[:, top:]
    slots_other, gates_other = other[:, :top] - first, other[:, top:]

    stream, normed = join_pair(parts, resid.reshape(local_rows, model), norm_gain[None, :])
    both = across(normed)
    arrived_own = around(spread(normed, slots_own.T, group_slots, None))
    both, arrived_own = lax.optimization_barrier((both, arrived_own))
    answer_own = expert_pair(arrived_own, w_in, w_down)
    out_other = spread(both, slots_other.T, group_slots, other_group)
    answer_other = expert_pair(around(out_other), w_in, w_down)
    partial = gather(around(answer_other), slots_other, gates_other, None, None, None)
    partial, answer_own = lax.optimization_barrier((partial, answer_own))
    sums = across(partial)
    out = gather(around(answer_own), slots_own, gates_own, stream, sums, other_group)
    return out.reshape(local_rows, seqs, model)


def local(queries, new_kv, cache, resid, w_out, norm_gain, expert_ids, expert_gates, w_in, w_down):
    n = lax.axis_size("head")
    local_rows, seqs, heads, width = queries.shape
    model = resid.shape[2]
    rows = local_rows * seqs
    members = heads // new_kv.shape[2]
    in_pairs = (
        lax.axis_size("grp") == 2
        and seqs == 1
        and new_kv.shape[2] == 2
        and n == heads == 2 * members
        and members == 8
        and cache.shape[0] == 1
        and w_in.shape[0] == 1
        and w_out.shape[1] % 16 == 0
    )

    top = expert_ids.shape[2]
    experts = w_in.shape[0] * n
    capacity = max(2, 2 * rows * top // experts)
    ids = expert_ids.transpose(1, 0, 2).reshape(rows, top)
    gates = expert_gates.transpose(1, 0, 2).reshape(rows, top)
    onehot = (ids[:, :, None] == jnp.arange(experts, dtype=jnp.int32)).astype(jnp.int32)
    named = onehot.sum(1)
    before = jnp.cumsum(named, 0) - named
    slots_of = ids * capacity + jnp.sum(onehot * before[:, None, :], 2)
    slots = experts * capacity
    if in_pairs:
        own = jnp.concatenate([slots_of.astype(F32), gates], 1)
        other = flipped(own, "head", members)
        parts, other = parts_in_pairs(queries, new_kv, cache, w_out, other)
        return route_in_pairs(
            parts, resid, norm_gain, own, other, top, w_in[0], w_down[0], capacity, members
        )
    parts = parts_in_planes(queries, new_kv, cache, w_out)
    stream, outgoing = route(
        parts, resid.transpose(1, 0, 2), norm_gain[None, :], slots_of.T, slots
    )
    arrived = lax.all_to_all(
        outgoing.reshape(n, slots // n, model), "head", split_axis=0, concat_axis=0, tiled=True
    )
    local_experts = w_in.shape[0]
    if local_experts == 1:
        answered = expert_pair(arrived.reshape(slots, model), w_in[0], w_down[0])
        answered = answered.reshape(n, slots // n, model)
    else:
        arrived = arrived.reshape(n, local_experts, capacity, model).transpose(1, 0, 2, 3)
        arrived = arrived.reshape(local_experts, n * capacity, model)
        answered = jnp.stack([expert(arrived[e], w_in[e], w_down[e]) for e in range(local_experts)])
        answered = answered.reshape(local_experts, n, capacity, model).transpose(1, 0, 2, 3)
        answered = answered.reshape(n, slots // n, model)
    back = lax.all_to_all(answered, "head", split_axis=0, concat_axis=0, tiled=True)
    out = combine(back.reshape(slots, model), stream, slots_of, gates, seqs)
    return out.transpose(1, 0, 2)


def solution(mesh):
    return jax.shard_map(
        local,
        mesh=mesh,
        in_specs=(
            P("head", "grp", None, None),
            P("head", "grp", None, None),
            P(("grp", "head"), None, None),
            P("head", "grp", None),
            P(None, "head", None),
            P(),
            P("head", "grp", None),
            P("head", "grp", None),
            P("head", None, None),
            P("head", None, None),
        ),
        out_specs=P("head", "grp", None),
        check_vma=False,
    )
```

```python
import functools

import jax
import jax.numpy as jnp
from jax import lax
from jax.experimental import pallas as pl
from jax.experimental.pallas import tpu as pltpu
from jax.sharding import PartitionSpec as P

eps_norm = 1e-06
F32 = jnp.float32
BF16 = jnp.bfloat16
HIGH_VMEM = 48 * 2**20
LOG2_E = 1.4426950408889634


def in_hbm():
    return pl.BlockSpec(memory_space=pltpu.HBM)


def in_vmem():
    return pl.BlockSpec(memory_space=pltpu.VMEM)


def attend_kernel(
    block, chunk, width, q_hbm, cache_hbm, kv_hbm, o_ref, q_ref, cache_ref, kv_ref, s0, s1, sems
):
    members, groups, piece, _ = kv_hbm.shape
    length = members * groups * piece
    old = cache_hbm.shape[0]
    scale = width**-0.5
    in_q = pltpu.make_async_copy(q_hbm, q_ref, sems.at[0])
    in_cache = pltpu.make_async_copy(cache_hbm, cache_ref, sems.at[1])
    in_q.start()
    in_cache.start()
    in_kv = []
    for group in range(groups):
        for member in range(members):
            place = (group * members + member) * piece
            copy = pltpu.make_async_copy(
                kv_hbm.at[member, group], kv_ref.at[pl.ds(place, piece)], sems.at[2]
            )
            copy.start()
            in_kv.append(copy)
    in_q.wait()
    in_cache.wait()
    for copy in in_kv:
        copy.wait()
    scores = [s0, s1]

    def pieces(b):
        out = [(True, k, chunk, k) for k in range(0, old, chunk)]
        last = b * block
        for k in range(0, last, chunk):
            out.append((False, k, min(chunk, last - k), old + k))
        out.append((False, last, block, old + last))
        return out

    def make_scores(b, part, running):
        of_cache, first, count, column = part
        keys = (cache_ref if of_cache else kv_ref)[pl.ds(first, count), :width]
        s = lax.dot_general(
            q_ref[pl.ds(b * block, block), :],
            keys,
            (((1,), (1,)), ((), ())),
            preferred_element_type=F32,
        )
        if not of_cache and first == b * block:
            row = lax.broadcasted_iota(jnp.int32, s.shape, 0)
            col = lax.broadcasted_iota(jnp.int32, s.shape, 1)
            s = jnp.where(col <= row, s, -jnp.inf)
        scores[b % 2][:, pl.ds(column, count)] = s
        for k in range(0, count, 128):
            piece_max = s[:, k : k + 128]
            running = piece_max if running is None else jnp.maximum(running, piece_max)
        return running

    def use_scores(b, part, top, total, acc):
        of_cache, first, count, column = part
        values = (cache_ref if of_cache else kv_ref)[pl.ds(first, count), width:]
        e = jnp.exp((scores[b % 2][:, pl.ds(column, count)] - top) * scale)
        for k in range(0, count, 128):
            total = e[:, k : k + 128] if total is None else total + e[:, k : k + 128]
        product = jnp.dot(e.astype(BF16), values, preferred_element_type=F32)
        return total, product if acc is None else acc + product

    blocks = length // block
    running = None
    for part in pieces(0):
        running = make_scores(0, part, running)
    for b in range(blocks):
        top = jnp.max(running, 1, keepdims=True)
        now, later = pieces(b), pieces(b + 1) if b + 1 < blocks else []
        running, total, acc = None, None, None
        for k in range(max(len(now), len(later))):
            if k < len(now):
                total, acc = use_scores(b, now[k], top, total, acc)
            if k < len(later):
                running = make_scores(b + 1, later[k], running)
        o_ref[pl.ds(b * block, block), :] = (acc / jnp.sum(total, 1, keepdims=True)).astype(BF16)


def attend(q, cache, kv):
    length, width = q.shape
    old = cache.shape[0]
    block = min(256, length)
    chunk = min(512, old)
    return pl.pallas_call(
        functools.partial(attend_kernel, block, chunk, width),
        out_shape=jax.ShapeDtypeStruct((length, width), BF16),
        in_specs=[in_hbm()] * 3,
        out_specs=in_vmem(),
        scratch_shapes=[
            pltpu.VMEM((length, width), BF16),
            pltpu.VMEM((old, 2 * width), BF16),
            pltpu.VMEM((length, 2 * width), BF16),
            pltpu.VMEM((block, old + length), F32),
            pltpu.VMEM((block, old + length), F32),
            pltpu.SemaphoreType.DMA((3,)),
        ],
        compiler_params=pltpu.CompilerParams(vmem_limit_bytes=HIGH_VMEM),
        cost_estimate=pl.CostEstimate(
            flops=4 * length * (old + length // 2) * width,
            bytes_accessed=4 * (2 * length + 2 * old) * width,
            transcendentals=length * (old + length // 2),
        ),
        name="attend",
    )(q, cache, kv)


def attend_pair_kernel(
    block,
    chunk,
    width,
    q_hbm,
    page_own,
    page_y,
    page_c,
    page_cy,
    kv_own,
    kv_y,
    kv_c,
    kv_cy,
    o_ref,
    q_ref,
    old_ref,
    kv_ref,
    s0,
    s1,
    sems,
):
    me = lax.axis_index("head")
    members, heads, piece, _ = q_hbm.shape
    length = members * piece
    planes = kv_own.shape[0]
    old = old_ref.shape[0]
    earlier_group = me // members > 0
    core = lax.rem(me, 2)
    chip = jnp.bitwise_and(me // 2, members // 2 - 1)
    copies = []

    def bring(source, target, sem):
        copy = pltpu.make_async_copy(source, target, sems.at[sem])
        copy.start()
        copies.append(copy)

    for member in range(members):
        for head in range(heads):
            bring(q_hbm.at[member, head], q_ref.at[head, pl.ds(member * piece, piece)], 0)
    place = 0
    for page in (page_own, page_y, page_c, page_cy):
        count = page.shape[0]
        bring(page, old_ref.at[pl.ds(place, count)], 1)
        place += count
    for flip, pieces_of in ((0, kv_own), (2, kv_y), (1, kv_c), (3, kv_cy)):
        for t in range(planes):
            number = jnp.bitwise_and(
                jnp.bitwise_xor(me, flip ^ (t * (members // 2))), members - 1
            )
            start = pl.multiple_of(number * piece, piece)
            area = 0 if t * (members // 2) >= members else length
            bring(pieces_of.at[t], kv_ref.at[pl.ds(area + start, piece)], 2)
    for copy in copies:
        copy.wait()
    scale = width**-0.5 * LOG2_E
    scores = [s0, s1]
    blocks = length // block
    units = [(head, b) for head in range(heads) for b in range(blocks)]

    def pieces(unit):
        _, b = units[unit]
        out = [("old", k, chunk, k) for k in range(0, old, chunk)]
        out += [("past", k, chunk, old + k) for k in range(0, length, chunk)]
        last = b * block
        for k in range(0, last, chunk):
            out.append(("new", length + k, min(chunk, last - k), old + length + k))
        out.append(("edge", length + last, block, old + length + last))
        return out

    def make_scores(unit, part, running):
        kind, first, count, column = part
        head, b = units[unit]
        keys = (old_ref if kind == "old" else kv_ref)[pl.ds(first, count), :width]
        s = lax.dot_general(
            q_ref[head, pl.ds(b * block, block), :],
            keys,
            (((1,), (1,)), ((), ())),
            preferred_element_type=F32,
        )
        if kind == "past":
            s = jnp.where(earlier_group, s, -jnp.inf)
        if kind == "edge":
            row = lax.broadcasted_iota(jnp.int32, s.shape, 0)
            col = lax.broadcasted_iota(jnp.int32, s.shape, 1)
            s = jnp.where(col <= row, s, -jnp.inf)
        scores[unit % 2][:, pl.ds(column, count)] = s
        for k in range(0, count, 128):
            piece_max = s[:, k : k + 128]
            running = piece_max if running is None else jnp.maximum(running, piece_max)
        return running

    def use_scores(unit, part, top, total, acc):
        kind, first, count, column = part
        values = (old_ref if kind == "old" else kv_ref)[pl.ds(first, count), width:]
        e = jnp.exp2((scores[unit % 2][:, pl.ds(column, count)] - top) * scale)
        for k in range(0, count, 128):
            total = e[:, k : k + 128] if total is None else total + e[:, k : k + 128]
        product = jnp.dot(e.astype(BF16), values, preferred_element_type=F32)
        return total, product if acc is None else acc + product

    running = None
    for part in pieces(0):
        running = make_scores(0, part, running)
    for unit, (head, b) in enumerate(units):
        top = jnp.max(running, 1, keepdims=True)
        now = pieces(unit)
        later = pieces(unit + 1) if unit + 1 < len(units) else []
        running, total, acc = None, None, None
        for k in range(max(len(now), len(later))):
            if k < len(now):
                total, acc = use_scores(unit, now[k], top, total, acc)
            if k < len(later):
                running = make_scores(unit + 1, later[k], running)
        done = (acc / jnp.sum(total, 1, keepdims=True)).astype(BF16)
        for k in range(0, block, piece):
            member = (b * block + k) // piece
            side = jnp.bitwise_xor(core, member % 2)
            start = pl.multiple_of(jnp.bitwise_xor(chip, member // 2) * piece, piece)
            o_ref[side, pl.ds(start, piece), pl.ds(head * width, width)] = done[k : k + piece]


def attend_pair(q, pages, kvs):
    members, heads, piece, width = q.shape
    length = members * piece
    old = sum(page.shape[0] for page in pages)
    block = 2 * piece
    chunk = min(512, old, length)
    keys = old + 2 * length
    return pl.pallas_call(
        functools.partial(attend_pair_kernel, block, chunk, width),
        out_shape=jax.ShapeDtypeStruct((2, length // 2, heads * width), BF16),
        in_specs=[in_hbm()] * (1 + len(pages) + len(kvs)),
        out_specs=in_vmem(),
        scratch_shapes=[
            pltpu.VMEM((heads, length, width), BF16),
            pltpu.VMEM((old, 2 * width), BF16),
            pltpu.VMEM((2 * length, 2 * width), BF16),
            pltpu.VMEM((block, keys), F32),
            pltpu.VMEM((block, keys), F32),
            pltpu.SemaphoreType.DMA((3,)),
        ],
        compiler_params=pltpu.CompilerParams(vmem_limit_bytes=HIGH_VMEM),
        cost_estimate=pl.CostEstimate(
            flops=4 * heads * length * (keys - length // 2) * width,
            bytes_accessed=4 * (heads * length + keys) * width,
            transcendentals=heads * length * (keys - length // 2),
        ),
        name="attend",
    )(q, *pages, *kvs)


def project_pair_kernel(a_ref, got_ref, *refs):
    near, far, outs, (w_ref, sems) = refs[:4], refs[4:8], refs[8:-2], refs[-2:]
    me = lax.axis_index("head")
    half = lax.axis_index("grp")
    core = lax.rem(me, 2)
    steps, sides, heads, share, columns = near[0].shape
    width = w_ref.shape[1]
    copies = []
    for first, given in ((0, near), (steps, far)):
        for flip, x, pieces_of in zip((0, 1, 0, 1), (0, 0, 1, 1), given):
            column = pl.multiple_of(jnp.bitwise_xor(half, x) * columns, columns)
            for t in range(steps):
                for u in range(sides):
                    number = jnp.bitwise_xor(me, flip ^ (2 * u) ^ (4 * (first + t)))
                    row = pl.multiple_of(number * share, share)
                    copy = pltpu.make_async_copy(
                        pieces_of.at[t, u],
                        w_ref.at[:, pl.ds(row, share), pl.ds(column, columns)],
                        sems.at[0],
                    )
                    copy.start()
                    copies.append(copy)
    for copy in copies:
        copy.wait()
    acc = None
    for k in range(heads):
        mine = k < heads // 2
        at = pl.ds((k % (heads // 2)) * width, width)
        rows_of = a_ref[0, :, at] if mine else got_ref[:, at]
        head = jnp.bitwise_xor(core, 0 if mine else 1) * (heads // 2) + k % (heads // 2)
        part = jnp.dot(rows_of, w_ref[head], preferred_element_type=F32)
        acc = part if acc is None else acc + part
    rows = outs[0].shape[0]
    for k, out in enumerate(outs):
        out[...] = acc[k * rows : (k + 1) * rows].astype(BF16)


def project_pair(a, got, near, far, parts):
    _, _, heads, share, columns = near[0].shape
    rows = got.shape[0]
    width = 2 * got.shape[1] // heads
    model = 2 * columns
    return pl.pallas_call(
        project_pair_kernel,
        out_shape=[jax.ShapeDtypeStruct((rows // parts, model), BF16)] * parts,
        in_specs=[in_vmem(), in_vmem()] + [in_hbm()] * 8,
        out_specs=[in_vmem()] * parts,
        scratch_shapes=[
            pltpu.VMEM((heads, width, model), BF16),
            pltpu.SemaphoreType.DMA((1,)),
        ],
        compiler_params=pltpu.CompilerParams(vmem_limit_bytes=HIGH_VMEM),
        cost_estimate=pl.CostEstimate(
            flops=2 * heads * rows * width * model,
            bytes_accessed=2 * (heads * width * model + heads * rows * width + rows * model),
            transcendentals=0,
        ),
        name="project",
    )(a, got, *near, *far)


def project_kernel(a_ref, w_ref, o_ref):
    members = a_ref.shape[0]
    planes, share = w_ref.shape[1], w_ref.shape[3]
    acc = None
    for head in range(members):
        w = jnp.concatenate(
            [w_ref[m, p, head] for p in range(planes) for m in range(members)], 0
        )
        part = jnp.dot(a_ref[head], w, preferred_element_type=F32)
        acc = part if acc is None else acc + part
    o_ref[...] = acc.astype(BF16)


def project(a, w):
    members, rows, width = a.shape
    planes, share, model = w.shape[1], w.shape[3], w.shape[4]
    tile = min(512, model)
    return pl.pallas_call(
        project_kernel,
        grid=(model // tile,),
        out_shape=jax.ShapeDtypeStruct((rows, model), BF16),
        in_specs=[
            pl.BlockSpec((members, rows, width), lambda t: (0, 0, 0)),
            pl.BlockSpec((members, planes, members, share, tile), lambda t: (0, 0, 0, 0, t)),
        ],
        out_specs=pl.BlockSpec((rows, tile), lambda t: (0, t)),
        compiler_params=pltpu.CompilerParams(vmem_limit_bytes=HIGH_VMEM),
        cost_estimate=pl.CostEstimate(
            flops=2 * members * rows * width * model,
            bytes_accessed=2 * (members * width * model + members * rows * width + rows * model),
            transcendentals=0,
        ),
        name="project",
    )(a, w)


def route_kernel(resid_ref, gain_ref, slots_ref, *refs):
    parts_refs, (stream_ref, out_ref) = refs[:-2], refs[-2:]
    seqs = resid_ref.shape[0]
    streams = []
    for seq in range(seqs):
        stream = resid_ref[seq].astype(F32)
        projected = parts_refs[0][seq].astype(F32)
        for part in parts_refs[1:]:
            projected = projected + part[seq].astype(F32)
        streams.append(stream + projected)
    stream = jnp.concatenate(streams, 0) if seqs > 1 else streams[0]
    stream_ref[...] = stream
    normed = stream * lax.rsqrt(jnp.mean(stream * stream, 1, keepdims=True) + eps_norm)
    normed = (normed * gain_ref[...]).astype(BF16)
    slots, rows = out_ref.shape[0], stream.shape[0]
    place = lax.broadcasted_iota(jnp.int32, (slots, rows), 0)
    hit = place == slots_ref[0:1, :]
    for k in range(1, slots_ref.shape[0]):
        hit = hit | (place == slots_ref[k : k + 1, :])
    out_ref[...] = jnp.dot(hit.astype(BF16), normed, preferred_element_type=F32).astype(BF16)


def route(parts, resid, gain, slots_of, slots):
    seqs, local_rows, model = resid.shape
    rows = seqs * local_rows
    return pl.pallas_call(
        route_kernel,
        out_shape=(
            jax.ShapeDtypeStruct((rows, model), F32),
            jax.ShapeDtypeStruct((slots, model), BF16),
        ),
        in_specs=[in_vmem()] * (3 + len(parts)),
        out_specs=(in_vmem(), in_vmem()),
        compiler_params=pltpu.CompilerParams(vmem_limit_bytes=HIGH_VMEM),
        cost_estimate=pl.CostEstimate(
            flops=2 * slots * rows * model,
            bytes_accessed=2 * (len(parts) + 3 + slots // rows) * rows * model,
            transcendentals=0,
        ),
        name="route",
    )(resid, gain, slots_of, *parts)


def expert_kernel(x_ref, w_in_ref, w_down_ref, o_ref):
    hidden_width = w_down_ref.shape[0]
    inner = jnp.dot(x_ref[...], w_in_ref[...], preferred_element_type=F32)
    gate = inner[:, :hidden_width]
    hidden = (gate / (1.0 + jnp.exp(-gate)) * inner[:, hidden_width:]).astype(BF16)
    o_ref[...] = jnp.dot(hidden, w_down_ref[...], preferred_element_type=F32).astype(BF16)


def expert(x, w_in, w_down):
    rows, model = x.shape
    hidden_width = w_down.shape[0]
    return pl.pallas_call(
        expert_kernel,
        out_shape=jax.ShapeDtypeStruct((rows, model), BF16),
        in_specs=[in_vmem()] * 3,
        out_specs=in_vmem(),
        compiler_params=pltpu.CompilerParams(vmem_limit_bytes=HIGH_VMEM),
        cost_estimate=pl.CostEstimate(
            flops=6 * rows * model * hidden_width,
            bytes_accessed=2 * (2 * rows * model + 3 * model * hidden_width),
            transcendentals=rows * hidden_width,
        ),
        name="expert",
    )(x, w_in, w_down)


def expert_pair(x, w_in, w_down):
    rows, model = x.shape
    hidden_width = w_down.shape[0]
    parts = 4
    depth = model // parts

    def kernel(x_hbm, in_hbm_ref, down_hbm, o_hbm, x_ref, in_ref, down_ref, o_ref, sems):
        bring_x = pltpu.make_async_copy(x_hbm, x_ref, sems.at[parts])
        bring_x.start()
        bring_in = []
        for k in range(parts):
            at = pl.ds(k * depth, depth)
            bring_in.append(pltpu.make_async_copy(in_hbm_ref.at[at], in_ref.at[at], sems.at[k]))
            bring_in[k].start()
        bring_down = pltpu.make_async_copy(down_hbm, down_ref, sems.at[parts + 1])
        bring_down.start()
        bring_x.wait()
        inner = None
        for k in range(parts):
            bring_in[k].wait()
            at = pl.ds(k * depth, depth)
            part = jnp.dot(x_ref[:, at], in_ref[at, :], preferred_element_type=F32)
            inner = part if inner is None else inner + part
        gate = inner[:, :hidden_width]
        hidden = (gate / (1.0 + jnp.exp(-gate)) * inner[:, hidden_width:]).astype(BF16)
        bring_down.wait()
        o_ref[...] = jnp.dot(hidden, down_ref[...], preferred_element_type=F32).astype(BF16)
        back = pltpu.make_async_copy(o_ref, o_hbm, sems.at[parts + 2])
        back.start()
        back.wait()

    return pl.pallas_call(
        kernel,
        out_shape=jax.ShapeDtypeStruct((rows, model), BF16),
        in_specs=[in_hbm()] * 3,
        out_specs=in_hbm(),
        scratch_shapes=[
            pltpu.VMEM((rows, model), BF16),
            pltpu.VMEM(w_in.shape, BF16),
            pltpu.VMEM(w_down.shape, BF16),
            pltpu.VMEM((rows, model), BF16),
            pltpu.SemaphoreType.DMA((parts + 3,)),
        ],
        compiler_params=pltpu.CompilerParams(vmem_limit_bytes=HIGH_VMEM),
        cost_estimate=pl.CostEstimate(
            flops=6 * rows * model * hidden_width,
            bytes_accessed=2 * (2 * rows * model + 3 * model * hidden_width),
            transcendentals=rows * hidden_width,
        ),
        name="expert",
    )(x, w_in, w_down)


def combine_kernel(seqs, back_ref, stream_ref, slots_ref, gates_ref, o_ref):
    slots = back_ref.shape[0]
    rows = stream_ref.shape[0]
    place = lax.broadcasted_iota(jnp.int32, (rows, slots), 1)
    total = stream_ref[...]
    gathered = None
    for k in range(slots_ref.shape[1]):
        pick = (place == slots_ref[:, k : k + 1]).astype(BF16)
        picked = jnp.dot(pick, back_ref[...], preferred_element_type=F32)
        part = picked * gates_ref[:, k : k + 1]
        gathered = part if gathered is None else gathered + part
    out = (total + gathered).astype(BF16)
    local_rows = rows // seqs
    for seq in range(seqs):
        o_ref[seq] = out[seq * local_rows : (seq + 1) * local_rows]


def combine(back, stream, slots_of, gates, seqs):
    slots, model = back.shape
    rows = stream.shape[0]
    top = slots_of.shape[1]
    return pl.pallas_call(
        functools.partial(combine_kernel, seqs),
        out_shape=jax.ShapeDtypeStruct((seqs, rows // seqs, model), BF16),
        in_specs=[in_vmem()] * 4,
        out_specs=in_vmem(),
        compiler_params=pltpu.CompilerParams(vmem_limit_bytes=HIGH_VMEM),
        cost_estimate=pl.CostEstimate(
            flops=2 * top * slots * rows * model,
            bytes_accessed=2 * slots * model + 6 * rows * model,
            transcendentals=0,
        ),
        name="combine",
    )(back, stream, slots_of, gates)


def flipped(value, axis, mask):
    pairs = [(source, source ^ mask) for source in range(lax.axis_size(axis))]
    return lax.ppermute(value, axis, pairs)


def parts_in_pairs(queries, new_kv, cache, w_out):
    n = lax.axis_size("head")
    local_rows, _, heads, width = queries.shape
    pair_heads = new_kv.shape[2]
    members = heads // pair_heads
    model = w_out.shape[2]
    share = w_out.shape[1]
    me = lax.axis_index("head")
    plane_bit = members // 2
    planes = n // plane_bit
    b = (me // plane_bit) % 2
    y = (me // 2) % 2
    group_sets = [[g * members + m for m in range(members)] for g in range(n // members)]

    query_slots = queries.reshape(local_rows, heads, width).transpose(1, 0, 2)
    query_slots = query_slots.reshape(members, heads // members, local_rows, width)
    q = lax.all_to_all(
        query_slots, "head", split_axis=0, concat_axis=0, tiled=True, axis_index_groups=group_sets
    )

    def page_target(source, other):
        p, plane, rest = source // members, (source // plane_bit) % 2, source % plane_bit
        return (plane ^ other) * members + p * plane_bit + rest

    page_a, page_b = (
        lax.ppermute(cache[0], "head", [(d, page_target(d, other)) for d in range(n)])
        for other in range(2)
    )
    kv_heads = new_kv.reshape(local_rows, pair_heads, 2 * width).transpose(1, 0, 2)
    kv_same = lax.dynamic_index_in_dim(kv_heads, b, 0, keepdims=False)
    kv_other = lax.dynamic_index_in_dim(kv_heads, 1 - b, 0, keepdims=False)
    columns = model // 2
    w = lax.dynamic_slice_in_dim(w_out, lax.axis_index("grp") * columns, columns, 2)
    w = w.reshape(2, 2, heads // 4, share, columns)
    w_keep = lax.dynamic_index_in_dim(w, y, 1, keepdims=False)
    w_give = lax.dynamic_index_in_dim(w, 1 - y, 1, keepdims=False)
    kv_own = [kv_same]
    for t in range(1, planes):
        kv_own.append(flipped(kv_other if t % 2 else kv_same, "head", t * plane_bit))
    w_got = flipped(w_give, "head", 2)

    (page_a, page_b, kv_own, q), w_got = lax.optimization_barrier(
        ((page_a, page_b, kv_own, q), w_got)
    )
    own_pages = jnp.concatenate([page_a, page_b], 0)
    kv_own = jnp.stack(kv_own, 0)
    pages_y = flipped(own_pages, "head", 2)
    kv_y = flipped(kv_own, "head", 2)
    w_both = jnp.stack([w_keep, w_got], 1)
    w_same = lax.dynamic_index_in_dim(w_both, b, 0, keepdims=False)
    w_other = lax.dynamic_index_in_dim(w_both, 1 - b, 0, keepdims=False)
    w_near = jnp.stack([w_same, flipped(w_other, "head", plane_bit)], 0)
    w_near_x = flipped(w_near, "grp", 1)
    w_far = [flipped(w_same, "head", 2 * plane_bit), flipped(w_other, "head", 3 * plane_bit)]
    pages_y, kv_y, own_pages, kv_own, w_near_x = lax.optimization_barrier(
        (pages_y, kv_y, own_pages, kv_own, w_near_x)
    )
    kv_c = flipped(kv_own, "head", 1)
    kv_cy = flipped(kv_y, "head", 1)
    pages_c = flipped(own_pages, "head", 1)
    pages_cy = flipped(pages_y, "head", 1)
    w_far = jnp.stack(w_far, 0)
    q, w_far = lax.optimization_barrier((q, w_far))
    w_far_x = flipped(w_far, "grp", 1)
    a = attend_pair(q, (own_pages, pages_y, pages_c, pages_cy), (kv_own, kv_y, kv_c, kv_cy))
    got = flipped(a[1], "head", 1)
    a, w_near_x, w_far_x = lax.optimization_barrier((a, w_near_x, w_far_x))
    w_near_c = flipped(w_near, "head", 1)
    w_far_c = flipped(w_far, "head", 1)
    w_near_cx = flipped(w_near_x, "head", 1)
    w_far_cx = flipped(w_far_x, "head", 1)
    partial = project_pair(
        a,
        got,
        (w_near, w_near_c, w_near_x, w_near_cx),
        (w_far, w_far_c, w_far_x, w_far_cx),
        members // 2,
    )
    parts = [partial[0]] + [flipped(partial[k], "head", 2 * k) for k in (3, 2, 1)]
    return [part[None] for part in parts]


def parts_in_planes(queries, new_kv, cache, w_out):
    n = lax.axis_size("head")
    local_rows, seqs, heads, width = queries.shape
    pair_heads = new_kv.shape[2]
    members = heads // pair_heads
    groups = n // members
    model = w_out.shape[2]
    side = 1 << ((n.bit_length() - 1) // 2)
    side = min(side, heads)
    planes = n // side
    planes_of_seq = heads // side
    pair_groups = [[g * members + m for m in range(members)] for g in range(groups)]
    cross_groups = [[g * members + m for g in range(groups)] for m in range(members)]
    plane_groups = [[p * side + m for m in range(side)] for p in range(planes)]
    column_groups = [[p * side + m for p in range(planes)] for m in range(side)]

    query_slots = queries.reshape(local_rows, n, width).transpose(1, 0, 2)
    q = lax.all_to_all(query_slots, "head", split_axis=0, concat_axis=0, tiled=True)
    q = q.reshape(n * local_rows, width)

    kv_slots = new_kv.reshape(local_rows, groups, 2 * width).transpose(1, 0, 2)
    kv = lax.all_to_all(
        kv_slots, "head", split_axis=0, concat_axis=0, tiled=True, axis_index_groups=cross_groups
    )
    kv = lax.all_gather(kv, "head", axis=0, axis_index_groups=pair_groups)
    pages = lax.all_gather(cache, "head", axis=0, tiled=True, axis_index_groups=pair_groups)

    share = w_out.shape[1]
    w_planes = w_out.reshape(planes_of_seq, side, share, model)
    if planes > planes_of_seq:
        w_planes = jnp.tile(w_planes, (planes // planes_of_seq, 1, 1, 1))
    w = lax.all_to_all(
        w_planes, "head", split_axis=0, concat_axis=0, tiled=True, axis_index_groups=column_groups
    )
    w = lax.all_gather(w, "head", axis=0, axis_index_groups=plane_groups)
    if share % 16:
        w = w.transpose(2, 1, 0, 3, 4).reshape(1, 1, side, width, model)
        w = w.reshape(side, width, model)

    attended = attend(q, pages.reshape(-1, 2 * width), kv)
    a = attended.reshape(planes, side, local_rows, width).transpose(1, 0, 2, 3)
    a = a.reshape(side, planes * local_rows, width)
    a = lax.all_to_all(
        a, "head", split_axis=0, concat_axis=0, tiled=True, axis_index_groups=plane_groups
    )
    if share % 16:
        partial = jnp.einsum("hri,hid->rd", a, w, preferred_element_type=F32).astype(BF16)
    else:
        partial = project(a, w)
    parts = lax.all_to_all(
        partial.reshape(planes, local_rows, model),
        "head",
        split_axis=0,
        concat_axis=0,
        tiled=True,
        axis_index_groups=column_groups,
    )
    parts = parts.reshape(seqs, planes_of_seq, local_rows, model)
    return [parts[:, k] for k in range(planes_of_seq)]


def local(queries, new_kv, cache, resid, w_out, norm_gain, expert_ids, expert_gates, w_in, w_down):
    n = lax.axis_size("head")
    local_rows, seqs, heads, width = queries.shape
    model = resid.shape[2]
    rows = local_rows * seqs
    members = heads // new_kv.shape[2]
    in_pairs = (
        lax.axis_size("grp") == 2
        and seqs == 1
        and new_kv.shape[2] == 2
        and n == heads == 2 * members
        and members == 8
        and cache.shape[0] == 1
        and w_in.shape[0] == 1
        and w_out.shape[1] % 16 == 0
    )
    plan = parts_in_pairs if in_pairs else parts_in_planes
    parts = plan(queries, new_kv, cache, w_out)

    top = expert_ids.shape[2]
    experts = w_in.shape[0] * n
    capacity = max(2, 2 * rows * top // experts)
    ids = expert_ids.transpose(1, 0, 2).reshape(rows, top)
    gates = expert_gates.transpose(1, 0, 2).reshape(rows, top)
    onehot = (ids[:, :, None] == jnp.arange(experts, dtype=jnp.int32)).astype(jnp.int32)
    named = onehot.sum(1)
    before = jnp.cumsum(named, 0) - named
    slots_of = ids * capacity + jnp.sum(onehot * before[:, None, :], 2)
    slots = experts * capacity

    stream, outgoing = route(
        parts, resid.transpose(1, 0, 2), norm_gain[None, :], slots_of.T, slots
    )
    arrived = lax.all_to_all(
        outgoing.reshape(n, slots // n, model), "head", split_axis=0, concat_axis=0, tiled=True
    )
    local_experts = w_in.shape[0]
    if local_experts == 1:
        answered = expert_pair(arrived.reshape(slots, model), w_in[0], w_down[0])
        answered = answered.reshape(n, slots // n, model)
    else:
        arrived = arrived.reshape(n, local_experts, capacity, model).transpose(1, 0, 2, 3)
        arrived = arrived.reshape(local_experts, n * capacity, model)
        answered = jnp.stack([expert(arrived[e], w_in[e], w_down[e]) for e in range(local_experts)])
        answered = answered.reshape(local_experts, n, capacity, model).transpose(1, 0, 2, 3)
        answered = answered.reshape(n, slots // n, model)
    back = lax.all_to_all(answered, "head", split_axis=0, concat_axis=0, tiled=True)
    out = combine(back.reshape(slots, model), stream, slots_of, gates, seqs)
    return out.transpose(1, 0, 2)


def solution(mesh):
    return jax.shard_map(
        local,
        mesh=mesh,
        in_specs=(
            P("head", "grp", None, None),
            P("head", "grp", None, None),
            P(("grp", "head"), None, None),
            P("head", "grp", None),
            P(None, "head", None),
            P(),
            P("head", "grp", None),
            P("head", "grp", None),
            P("head", None, None),
            P("head", None, None),
        ),
        out_specs=P("head", "grp", None),
        check_vma=False,
    )
```

```python
import functools

import jax
import jax.numpy as jnp
from jax import lax
from jax.experimental import pallas as pl
from jax.experimental.pallas import tpu as pltpu
from jax.sharding import PartitionSpec as P

eps_norm = 1e-06
F32 = jnp.float32
BF16 = jnp.bfloat16
HIGH_VMEM = 48 * 2**20
LOG2_E = 1.4426950408889634


def in_hbm():
    return pl.BlockSpec(memory_space=pltpu.HBM)


def in_vmem():
    return pl.BlockSpec(memory_space=pltpu.VMEM)


def attend_kernel(
    block, chunk, width, q_hbm, cache_hbm, kv_hbm, o_ref, q_ref, cache_ref, kv_ref, s0, s1, sems
):
    members, groups, piece, _ = kv_hbm.shape
    length = members * groups * piece
    old = cache_hbm.shape[0]
    scale = width**-0.5
    in_q = pltpu.make_async_copy(q_hbm, q_ref, sems.at[0])
    in_cache = pltpu.make_async_copy(cache_hbm, cache_ref, sems.at[1])
    in_q.start()
    in_cache.start()
    in_kv = []
    for group in range(groups):
        for member in range(members):
            place = (group * members + member) * piece
            copy = pltpu.make_async_copy(
                kv_hbm.at[member, group], kv_ref.at[pl.ds(place, piece)], sems.at[2]
            )
            copy.start()
            in_kv.append(copy)
    in_q.wait()
    in_cache.wait()
    for copy in in_kv:
        copy.wait()
    scores = [s0, s1]

    def pieces(b):
        out = [(True, k, chunk, k) for k in range(0, old, chunk)]
        last = b * block
        for k in range(0, last, chunk):
            out.append((False, k, min(chunk, last - k), old + k))
        out.append((False, last, block, old + last))
        return out

    def make_scores(b, part, running):
        of_cache, first, count, column = part
        keys = (cache_ref if of_cache else kv_ref)[pl.ds(first, count), :width]
        s = lax.dot_general(
            q_ref[pl.ds(b * block, block), :],
            keys,
            (((1,), (1,)), ((), ())),
            preferred_element_type=F32,
        )
        if not of_cache and first == b * block:
            row = lax.broadcasted_iota(jnp.int32, s.shape, 0)
            col = lax.broadcasted_iota(jnp.int32, s.shape, 1)
            s = jnp.where(col <= row, s, -jnp.inf)
        scores[b % 2][:, pl.ds(column, count)] = s
        for k in range(0, count, 128):
            piece_max = s[:, k : k + 128]
            running = piece_max if running is None else jnp.maximum(running, piece_max)
        return running

    def use_scores(b, part, top, total, acc):
        of_cache, first, count, column = part
        values = (cache_ref if of_cache else kv_ref)[pl.ds(first, count), width:]
        e = jnp.exp((scores[b % 2][:, pl.ds(column, count)] - top) * scale)
        for k in range(0, count, 128):
            total = e[:, k : k + 128] if total is None else total + e[:, k : k + 128]
        product = jnp.dot(e.astype(BF16), values, preferred_element_type=F32)
        return total, product if acc is None else acc + product

    blocks = length // block
    running = None
    for part in pieces(0):
        running = make_scores(0, part, running)
    for b in range(blocks):
        top = jnp.max(running, 1, keepdims=True)
        now, later = pieces(b), pieces(b + 1) if b + 1 < blocks else []
        running, total, acc = None, None, None
        for k in range(max(len(now), len(later))):
            if k < len(now):
                total, acc = use_scores(b, now[k], top, total, acc)
            if k < len(later):
                running = make_scores(b + 1, later[k], running)
        o_ref[pl.ds(b * block, block), :] = (acc / jnp.sum(total, 1, keepdims=True)).astype(BF16)


def attend(q, cache, kv):
    length, width = q.shape
    old = cache.shape[0]
    block = min(256, length)
    chunk = min(512, old)
    return pl.pallas_call(
        functools.partial(attend_kernel, block, chunk, width),
        out_shape=jax.ShapeDtypeStruct((length, width), BF16),
        in_specs=[in_hbm()] * 3,
        out_specs=in_vmem(),
        scratch_shapes=[
            pltpu.VMEM((length, width), BF16),
            pltpu.VMEM((old, 2 * width), BF16),
            pltpu.VMEM((length, 2 * width), BF16),
            pltpu.VMEM((block, old + length), F32),
            pltpu.VMEM((block, old + length), F32),
            pltpu.SemaphoreType.DMA((3,)),
        ],
        compiler_params=pltpu.CompilerParams(vmem_limit_bytes=HIGH_VMEM),
        cost_estimate=pl.CostEstimate(
            flops=4 * length * (old + length // 2) * width,
            bytes_accessed=4 * (2 * length + 2 * old) * width,
            transcendentals=length * (old + length // 2),
        ),
        name="attend",
    )(q, cache, kv)


def attend_pair_kernel(
    block,
    chunk,
    width,
    q_hbm,
    page_own,
    page_y,
    page_c,
    page_cy,
    kv_own,
    kv_y,
    kv_c,
    kv_cy,
    o_ref,
    q_ref,
    old_ref,
    kv_ref,
    s0,
    s1,
    sems,
):
    me = lax.axis_index("head")
    members, heads, piece, _ = q_hbm.shape
    length = members * piece
    planes = kv_own.shape[0]
    old = old_ref.shape[0]
    earlier_group = me // members > 0
    core = lax.rem(me, 2)
    chip = jnp.bitwise_and(me // 2, members // 2 - 1)
    copies = [[], [], []]

    def bring(source, target, sem):
        copy = pltpu.make_async_copy(source, target, sems.at[sem])
        copy.start()
        copies[sem].append(copy)

    for member in range(members):
        for head in range(heads):
            bring(q_hbm.at[member, head], q_ref.at[head, pl.ds(member * piece, piece)], 0)
    place = 0
    for page in (page_own, page_y, page_c, page_cy):
        count = page.shape[0]
        bring(page, old_ref.at[pl.ds(place, count)], 1)
        place += count
    for flip, pieces_of in ((0, kv_own), (2, kv_y), (1, kv_c), (3, kv_cy)):
        for t in range(planes):
            number = jnp.bitwise_and(
                jnp.bitwise_xor(me, flip ^ (t * (members // 2))), members - 1
            )
            start = pl.multiple_of(number * piece, piece)
            area = 0 if t * (members // 2) >= members else length
            bring(pieces_of.at[t], kv_ref.at[pl.ds(area + start, piece)], 2)
    for copy in copies[0] + copies[1]:
        copy.wait()
    scale = width**-0.5 * LOG2_E
    scores = [s0, s1]
    blocks = length // block
    units = [(head, b) for head in range(heads) for b in range(blocks)]

    def pieces(unit):
        _, b = units[unit]
        out = [("old", k, chunk, k) for k in range(0, old, chunk)]
        out += [("past", k, chunk, old + k) for k in range(0, length, chunk)]
        last = b * block
        for k in range(0, last, chunk):
            out.append(("new", length + k, min(chunk, last - k), old + length + k))
        out.append(("edge", length + last, block, old + length + last))
        return out

    def make_scores(unit, part, running):
        kind, first, count, column = part
        head, b = units[unit]
        keys = (old_ref if kind == "old" else kv_ref)[pl.ds(first, count), :width]
        s = lax.dot_general(
            q_ref[head, pl.ds(b * block, block), :],
            keys,
            (((1,), (1,)), ((), ())),
            preferred_element_type=F32,
        )
        if kind == "past":
            s = jnp.where(earlier_group, s, -jnp.inf)
        if kind == "edge":
            row = lax.broadcasted_iota(jnp.int32, s.shape, 0)
            col = lax.broadcasted_iota(jnp.int32, s.shape, 1)
            s = jnp.where(col <= row, s, -jnp.inf)
        scores[unit % 2][:, pl.ds(column, count)] = s
        for k in range(0, count, 128):
            piece_max = s[:, k : k + 128]
            running = piece_max if running is None else jnp.maximum(running, piece_max)
        return running

    def use_scores(unit, part, top, total, acc):
        kind, first, count, column = part
        values = (old_ref if kind == "old" else kv_ref)[pl.ds(first, count), width:]
        e = jnp.exp2((scores[unit % 2][:, pl.ds(column, count)] - top) * scale)
        for k in range(0, count, 128):
            total = e[:, k : k + 128] if total is None else total + e[:, k : k + 128]
        product = jnp.dot(e.astype(BF16), values, preferred_element_type=F32)
        return total, product if acc is None else acc + product

    running = None
    for part in pieces(0):
        if part[0] == "past":
            for copy in copies[2]:
                copy.wait()
            copies[2] = []
        running = make_scores(0, part, running)
    for unit, (head, b) in enumerate(units):
        top = jnp.max(running, 1, keepdims=True)
        now = pieces(unit)
        later = pieces(unit + 1) if unit + 1 < len(units) else []
        running, total, acc = None, None, None
        for k in range(max(len(now), len(later))):
            if k < len(now):
                total, acc = use_scores(unit, now[k], top, total, acc)
            if k < len(later):
                running = make_scores(unit + 1, later[k], running)
        done = (acc / jnp.sum(total, 1, keepdims=True)).astype(BF16)
        for k in range(0, block, piece):
            member = (b * block + k) // piece
            side = jnp.bitwise_xor(core, member % 2)
            start = pl.multiple_of(jnp.bitwise_xor(chip, member // 2) * piece, piece)
            o_ref[side, pl.ds(start, piece), pl.ds(head * width, width)] = done[k : k + piece]


def attend_pair(q, pages, kvs):
    members, heads, piece, width = q.shape
    length = members * piece
    old = sum(page.shape[0] for page in pages)
    block = 2 * piece
    chunk = min(512, old, length)
    keys = old + 2 * length
    return pl.pallas_call(
        functools.partial(attend_pair_kernel, block, chunk, width),
        out_shape=jax.ShapeDtypeStruct((2, length // 2, heads * width), BF16),
        in_specs=[in_hbm()] * (1 + len(pages) + len(kvs)),
        out_specs=in_vmem(),
        scratch_shapes=[
            pltpu.VMEM((heads, length, width), BF16),
            pltpu.VMEM((old, 2 * width), BF16),
            pltpu.VMEM((2 * length, 2 * width), BF16),
            pltpu.VMEM((block, keys), F32),
            pltpu.VMEM((block, keys), F32),
            pltpu.SemaphoreType.DMA((3,)),
        ],
        compiler_params=pltpu.CompilerParams(vmem_limit_bytes=HIGH_VMEM),
        cost_estimate=pl.CostEstimate(
            flops=4 * heads * length * (keys - length // 2) * width,
            bytes_accessed=4 * (heads * length + keys) * width,
            transcendentals=heads * length * (keys - length // 2),
        ),
        name="attend",
    )(q, *pages, *kvs)


def project_pair_kernel(a_ref, got_ref, *refs):
    near, far, outs, (w_ref, all_ref, sems) = refs[:4], refs[4:8], refs[8:-3], refs[-3:]
    me = lax.axis_index("head")
    half = lax.axis_index("grp")
    core = lax.rem(me, 2)
    steps, sides, heads, share, columns = near[0].shape
    width = w_ref.shape[1]
    copies = []
    for first, given in ((0, near), (steps, far)):
        for flip, x, pieces_of in zip((0, 1, 0, 1), (0, 0, 1, 1), given):
            column = pl.multiple_of(jnp.bitwise_xor(half, x) * columns, columns)
            for t in range(steps):
                for u in range(sides):
                    number = jnp.bitwise_xor(me, flip ^ (2 * u) ^ (4 * (first + t)))
                    row = pl.multiple_of(number * share, share)
                    copy = pltpu.make_async_copy(
                        pieces_of.at[t, u],
                        w_ref.at[:, pl.ds(row, share), pl.ds(column, columns)],
                        sems.at[0],
                    )
                    copy.start()
                    copies.append(copy)
    side = got_ref.shape[1]
    for other, rows_of in enumerate((a_ref[0], got_ref[...])):
        column = pl.multiple_of(jnp.bitwise_xor(core, other) * side, side)
        all_ref[:, pl.ds(column, side)] = rows_of
    for copy in copies:
        copy.wait()
    rows, model = outs[0].shape
    tile = min(512, model)
    for column in range(0, model, tile):
        at = pl.ds(column, tile)
        w = w_ref[:, :, at].reshape(heads * width, tile)
        product = jnp.dot(all_ref[...], w, preferred_element_type=F32).astype(BF16)
        for k, out in enumerate(outs):
            out[:, at] = product[k * rows : (k + 1) * rows]


def project_pair(a, got, near, far, parts):
    _, _, heads, share, columns = near[0].shape
    rows = got.shape[0]
    width = 2 * got.shape[1] // heads
    model = 2 * columns
    return pl.pallas_call(
        project_pair_kernel,
        out_shape=[jax.ShapeDtypeStruct((rows // parts, model), BF16)] * parts,
        in_specs=[in_vmem(), in_vmem()] + [in_hbm()] * 8,
        out_specs=[in_vmem()] * parts,
        scratch_shapes=[
            pltpu.VMEM((heads, width, model), BF16),
            pltpu.VMEM((rows, heads * width), BF16),
            pltpu.SemaphoreType.DMA((1,)),
        ],
        compiler_params=pltpu.CompilerParams(vmem_limit_bytes=HIGH_VMEM),
        cost_estimate=pl.CostEstimate(
            flops=2 * heads * rows * width * model,
            bytes_accessed=2 * (heads * width * model + heads * rows * width + rows * model),
            transcendentals=0,
        ),
        name="project",
    )(a, got, *near, *far)


def project_kernel(a_ref, w_ref, o_ref):
    members = a_ref.shape[0]
    planes, share = w_ref.shape[1], w_ref.shape[3]
    acc = None
    for head in range(members):
        w = jnp.concatenate(
            [w_ref[m, p, head] for p in range(planes) for m in range(members)], 0
        )
        part = jnp.dot(a_ref[head], w, preferred_element_type=F32)
        acc = part if acc is None else acc + part
    o_ref[...] = acc.astype(BF16)


def project(a, w):
    members, rows, width = a.shape
    planes, share, model = w.shape[1], w.shape[3], w.shape[4]
    tile = min(512, model)
    return pl.pallas_call(
        project_kernel,
        grid=(model // tile,),
        out_shape=jax.ShapeDtypeStruct((rows, model), BF16),
        in_specs=[
            pl.BlockSpec((members, rows, width), lambda t: (0, 0, 0)),
            pl.BlockSpec((members, planes, members, share, tile), lambda t: (0, 0, 0, 0, t)),
        ],
        out_specs=pl.BlockSpec((rows, tile), lambda t: (0, t)),
        compiler_params=pltpu.CompilerParams(vmem_limit_bytes=HIGH_VMEM),
        cost_estimate=pl.CostEstimate(
            flops=2 * members * rows * width * model,
            bytes_accessed=2 * (members * width * model + members * rows * width + rows * model),
            transcendentals=0,
        ),
        name="project",
    )(a, w)


def route_kernel(resid_ref, gain_ref, slots_ref, *refs):
    parts_refs, (stream_ref, out_ref) = refs[:-2], refs[-2:]
    seqs = resid_ref.shape[0]
    streams = []
    for seq in range(seqs):
        stream = resid_ref[seq].astype(F32)
        projected = parts_refs[0][seq].astype(F32)
        for part in parts_refs[1:]:
            projected = projected + part[seq].astype(F32)
        streams.append(stream + projected)
    stream = jnp.concatenate(streams, 0) if seqs > 1 else streams[0]
    stream_ref[...] = stream
    normed = stream * lax.rsqrt(jnp.mean(stream * stream, 1, keepdims=True) + eps_norm)
    normed = (normed * gain_ref[...]).astype(BF16)
    slots, rows = out_ref.shape[0], stream.shape[0]
    place = lax.broadcasted_iota(jnp.int32, (slots, rows), 0)
    hit = place == slots_ref[0:1, :]
    for k in range(1, slots_ref.shape[0]):
        hit = hit | (place == slots_ref[k : k + 1, :])
    out_ref[...] = jnp.dot(hit.astype(BF16), normed, preferred_element_type=F32).astype(BF16)


def route(parts, resid, gain, slots_of, slots):
    seqs, local_rows, model = resid.shape
    rows = seqs * local_rows
    return pl.pallas_call(
        route_kernel,
        out_shape=(
            jax.ShapeDtypeStruct((rows, model), F32),
            jax.ShapeDtypeStruct((slots, model), BF16),
        ),
        in_specs=[in_vmem()] * (3 + len(parts)),
        out_specs=(in_vmem(), in_vmem()),
        compiler_params=pltpu.CompilerParams(vmem_limit_bytes=HIGH_VMEM),
        cost_estimate=pl.CostEstimate(
            flops=2 * slots * rows * model,
            bytes_accessed=2 * (len(parts) + 3 + slots // rows) * rows * model,
            transcendentals=0,
        ),
        name="route",
    )(resid, gain, slots_of, *parts)


def expert_kernel(x_ref, w_in_ref, w_down_ref, o_ref):
    hidden_width = w_down_ref.shape[0]
    inner = jnp.dot(x_ref[...], w_in_ref[...], preferred_element_type=F32)
    gate = inner[:, :hidden_width]
    hidden = (gate / (1.0 + jnp.exp(-gate)) * inner[:, hidden_width:]).astype(BF16)
    o_ref[...] = jnp.dot(hidden, w_down_ref[...], preferred_element_type=F32).astype(BF16)


def expert(x, w_in, w_down):
    rows, model = x.shape
    hidden_width = w_down.shape[0]
    return pl.pallas_call(
        expert_kernel,
        out_shape=jax.ShapeDtypeStruct((rows, model), BF16),
        in_specs=[in_vmem()] * 3,
        out_specs=in_vmem(),
        compiler_params=pltpu.CompilerParams(vmem_limit_bytes=HIGH_VMEM),
        cost_estimate=pl.CostEstimate(
            flops=6 * rows * model * hidden_width,
            bytes_accessed=2 * (2 * rows * model + 3 * model * hidden_width),
            transcendentals=rows * hidden_width,
        ),
        name="expert",
    )(x, w_in, w_down)


def expert_pair(x, w_in, w_down):
    rows, model = x.shape
    hidden_width = w_down.shape[0]
    parts = 4
    depth = model // parts

    def kernel(x_hbm, in_hbm_ref, down_hbm, o_hbm, x_ref, in_ref, down_ref, o_ref, sems):
        bring_x = pltpu.make_async_copy(x_hbm, x_ref, sems.at[parts])
        bring_x.start()
        bring_in = []
        for k in range(parts):
            at = pl.ds(k * depth, depth)
            bring_in.append(pltpu.make_async_copy(in_hbm_ref.at[at], in_ref.at[at], sems.at[k]))
            bring_in[k].start()
        bring_down = pltpu.make_async_copy(down_hbm, down_ref, sems.at[parts + 1])
        bring_down.start()
        bring_x.wait()
        inner = None
        for k in range(parts):
            bring_in[k].wait()
            at = pl.ds(k * depth, depth)
            part = jnp.dot(x_ref[:, at], in_ref[at, :], preferred_element_type=F32)
            inner = part if inner is None else inner + part
        gate = inner[:, :hidden_width]
        hidden = (gate / (1.0 + jnp.exp(-gate)) * inner[:, hidden_width:]).astype(BF16)
        bring_down.wait()
        o_ref[...] = jnp.dot(hidden, down_ref[...], preferred_element_type=F32).astype(BF16)
        back = pltpu.make_async_copy(o_ref, o_hbm, sems.at[parts + 2])
        back.start()
        back.wait()

    return pl.pallas_call(
        kernel,
        out_shape=jax.ShapeDtypeStruct((rows, model), BF16),
        in_specs=[in_hbm()] * 3,
        out_specs=in_hbm(),
        scratch_shapes=[
            pltpu.VMEM((rows, model), BF16),
            pltpu.VMEM(w_in.shape, BF16),
            pltpu.VMEM(w_down.shape, BF16),
            pltpu.VMEM((rows, model), BF16),
            pltpu.SemaphoreType.DMA((parts + 3,)),
        ],
        compiler_params=pltpu.CompilerParams(vmem_limit_bytes=HIGH_VMEM),
        cost_estimate=pl.CostEstimate(
            flops=6 * rows * model * hidden_width,
            bytes_accessed=2 * (2 * rows * model + 3 * model * hidden_width),
            transcendentals=rows * hidden_width,
        ),
        name="expert",
    )(x, w_in, w_down)


def combine_kernel(seqs, back_ref, stream_ref, slots_ref, gates_ref, o_ref):
    slots = back_ref.shape[0]
    rows = stream_ref.shape[0]
    place = lax.broadcasted_iota(jnp.int32, (rows, slots), 1)
    total = stream_ref[...]
    gathered = None
    for k in range(slots_ref.shape[1]):
        pick = (place == slots_ref[:, k : k + 1]).astype(BF16)
        picked = jnp.dot(pick, back_ref[...], preferred_element_type=F32)
        part = picked * gates_ref[:, k : k + 1]
        gathered = part if gathered is None else gathered + part
    out = (total + gathered).astype(BF16)
    local_rows = rows // seqs
    for seq in range(seqs):
        o_ref[seq] = out[seq * local_rows : (seq + 1) * local_rows]


def combine(back, stream, slots_of, gates, seqs):
    slots, model = back.shape
    rows = stream.shape[0]
    top = slots_of.shape[1]
    return pl.pallas_call(
        functools.partial(combine_kernel, seqs),
        out_shape=jax.ShapeDtypeStruct((seqs, rows // seqs, model), BF16),
        in_specs=[in_vmem()] * 4,
        out_specs=in_vmem(),
        compiler_params=pltpu.CompilerParams(vmem_limit_bytes=HIGH_VMEM),
        cost_estimate=pl.CostEstimate(
            flops=2 * top * slots * rows * model,
            bytes_accessed=2 * slots * model + 6 * rows * model,
            transcendentals=0,
        ),
        name="combine",
    )(back, stream, slots_of, gates)


def flipped(value, axis, mask):
    pairs = [(source, source ^ mask) for source in range(lax.axis_size(axis))]
    return lax.ppermute(value, axis, pairs)


def parts_in_pairs(queries, new_kv, cache, w_out):
    n = lax.axis_size("head")
    local_rows, _, heads, width = queries.shape
    pair_heads = new_kv.shape[2]
    members = heads // pair_heads
    model = w_out.shape[2]
    share = w_out.shape[1]
    me = lax.axis_index("head")
    plane_bit = members // 2
    planes = n // plane_bit
    b = (me // plane_bit) % 2
    y = (me // 2) % 2
    group_sets = [[g * members + m for m in range(members)] for g in range(n // members)]

    query_slots = queries.reshape(local_rows, heads, width).transpose(1, 0, 2)
    query_slots = query_slots.reshape(members, heads // members, local_rows, width)
    q = lax.all_to_all(
        query_slots, "head", split_axis=0, concat_axis=0, tiled=True, axis_index_groups=group_sets
    )

    def page_target(source, other):
        p, plane, rest = source // members, (source // plane_bit) % 2, source % plane_bit
        return (plane ^ other) * members + p * plane_bit + rest

    page_a, page_b = (
        lax.ppermute(cache[0], "head", [(d, page_target(d, other)) for d in range(n)])
        for other in range(2)
    )
    kv_heads = new_kv.reshape(local_rows, pair_heads, 2 * width).transpose(1, 0, 2)
    kv_same = lax.dynamic_index_in_dim(kv_heads, b, 0, keepdims=False)
    kv_other = lax.dynamic_index_in_dim(kv_heads, 1 - b, 0, keepdims=False)
    columns = model // 2
    w = lax.dynamic_slice_in_dim(w_out, lax.axis_index("grp") * columns, columns, 2)
    w = w.reshape(2, 2, heads // 4, share, columns)
    w_keep = lax.dynamic_index_in_dim(w, y, 1, keepdims=False)
    w_give = lax.dynamic_index_in_dim(w, 1 - y, 1, keepdims=False)
    kv_near = jnp.stack([kv_same, flipped(kv_other, "head", plane_bit)], 0)
    kv_far = flipped(kv_near, "head", members)
    w_got = flipped(w_give, "head", 2)

    (page_a, page_b, kv_far, q), w_got = lax.optimization_barrier(
        ((page_a, page_b, kv_far, q), w_got)
    )
    own_pages = jnp.concatenate([page_a, page_b], 0)
    kv_own = jnp.concatenate([kv_near, kv_far], 0)
    pages_y = flipped(own_pages, "head", 2)
    kv_y = flipped(kv_own, "head", 2)
    w_both = jnp.stack([w_keep, w_got], 1)
    w_same = lax.dynamic_index_in_dim(w_both, b, 0, keepdims=False)
    w_other = lax.dynamic_index_in_dim(w_both, 1 - b, 0, keepdims=False)
    w_near = jnp.stack([w_same, flipped(w_other, "head", plane_bit)], 0)
    w_near_x = flipped(w_near, "grp", 1)
    w_far = flipped(w_near, "head", members)
    pages_y, kv_y, own_pages, kv_own, w_near_x = lax.optimization_barrier(
        (pages_y, kv_y, own_pages, kv_own, w_near_x)
    )
    kv_c = flipped(kv_own, "head", 1)
    kv_cy = flipped(kv_y, "head", 1)
    pages_c = flipped(own_pages, "head", 1)
    pages_cy = flipped(pages_y, "head", 1)
    q, w_far = lax.optimization_barrier((q, w_far))
    w_far_x = flipped(w_far, "grp", 1)
    a = attend_pair(q, (own_pages, pages_y, pages_c, pages_cy), (kv_own, kv_y, kv_c, kv_cy))
    got = flipped(a[1], "head", 1)
    a, w_near_x, w_far_x = lax.optimization_barrier((a, w_near_x, w_far_x))
    w_near_c = flipped(w_near, "head", 1)
    w_far_c = flipped(w_far, "head", 1)
    w_near_cx = flipped(w_near_x, "head", 1)
    w_far_cx = flipped(w_far_x, "head", 1)
    partial = project_pair(
        a,
        got,
        (w_near, w_near_c, w_near_x, w_near_cx),
        (w_far, w_far_c, w_far_x, w_far_cx),
        members // 2,
    )
    parts = [partial[0]] + [flipped(partial[k], "head", 2 * k) for k in (3, 2, 1)]
    return [part[None] for part in parts]


def parts_in_planes(queries, new_kv, cache, w_out):
    n = lax.axis_size("head")
    local_rows, seqs, heads, width = queries.shape
    pair_heads = new_kv.shape[2]
    members = heads // pair_heads
    groups = n // members
    model = w_out.shape[2]
    side = 1 << ((n.bit_length() - 1) // 2)
    side = min(side, heads)
    planes = n // side
    planes_of_seq = heads // side
    pair_groups = [[g * members + m for m in range(members)] for g in range(groups)]
    cross_groups = [[g * members + m for g in range(groups)] for m in range(members)]
    plane_groups = [[p * side + m for m in range(side)] for p in range(planes)]
    column_groups = [[p * side + m for p in range(planes)] for m in range(side)]

    query_slots = queries.reshape(local_rows, n, width).transpose(1, 0, 2)
    q = lax.all_to_all(query_slots, "head", split_axis=0, concat_axis=0, tiled=True)
    q = q.reshape(n * local_rows, width)

    kv_slots = new_kv.reshape(local_rows, groups, 2 * width).transpose(1, 0, 2)
    kv = lax.all_to_all(
        kv_slots, "head", split_axis=0, concat_axis=0, tiled=True, axis_index_groups=cross_groups
    )
    kv = lax.all_gather(kv, "head", axis=0, axis_index_groups=pair_groups)
    pages = lax.all_gather(cache, "head", axis=0, tiled=True, axis_index_groups=pair_groups)

    share = w_out.shape[1]
    w_planes = w_out.reshape(planes_of_seq, side, share, model)
    if planes > planes_of_seq:
        w_planes = jnp.tile(w_planes, (planes // planes_of_seq, 1, 1, 1))
    w = lax.all_to_all(
        w_planes, "head", split_axis=0, concat_axis=0, tiled=True, axis_index_groups=column_groups
    )
    w = lax.all_gather(w, "head", axis=0, axis_index_groups=plane_groups)
    if share % 16:
        w = w.transpose(2, 1, 0, 3, 4).reshape(1, 1, side, width, model)
        w = w.reshape(side, width, model)

    attended = attend(q, pages.reshape(-1, 2 * width), kv)
    a = attended.reshape(planes, side, local_rows, width).transpose(1, 0, 2, 3)
    a = a.reshape(side, planes * local_rows, width)
    a = lax.all_to_all(
        a, "head", split_axis=0, concat_axis=0, tiled=True, axis_index_groups=plane_groups
    )
    if share % 16:
        partial = jnp.einsum("hri,hid->rd", a, w, preferred_element_type=F32).astype(BF16)
    else:
        partial = project(a, w)
    parts = lax.all_to_all(
        partial.reshape(planes, local_rows, model),
        "head",
        split_axis=0,
        concat_axis=0,
        tiled=True,
        axis_index_groups=column_groups,
    )
    parts = parts.reshape(seqs, planes_of_seq, local_rows, model)
    return [parts[:, k] for k in range(planes_of_seq)]


def local(queries, new_kv, cache, resid, w_out, norm_gain, expert_ids, expert_gates, w_in, w_down):
    n = lax.axis_size("head")
    local_rows, seqs, heads, width = queries.shape
    model = resid.shape[2]
    rows = local_rows * seqs
    members = heads // new_kv.shape[2]
    in_pairs = (
        lax.axis_size("grp") == 2
        and seqs == 1
        and new_kv.shape[2] == 2
        and n == heads == 2 * members
        and members == 8
        and cache.shape[0] == 1
        and w_in.shape[0] == 1
        and w_out.shape[1] % 16 == 0
    )
    plan = parts_in_pairs if in_pairs else parts_in_planes
    parts = plan(queries, new_kv, cache, w_out)

    top = expert_ids.shape[2]
    experts = w_in.shape[0] * n
    capacity = max(2, 2 * rows * top // experts)
    ids = expert_ids.transpose(1, 0, 2).reshape(rows, top)
    gates = expert_gates.transpose(1, 0, 2).reshape(rows, top)
    onehot = (ids[:, :, None] == jnp.arange(experts, dtype=jnp.int32)).astype(jnp.int32)
    named = onehot.sum(1)
    before = jnp.cumsum(named, 0) - named
    slots_of = ids * capacity + jnp.sum(onehot * before[:, None, :], 2)
    slots = experts * capacity

    stream, outgoing = route(
        parts, resid.transpose(1, 0, 2), norm_gain[None, :], slots_of.T, slots
    )
    arrived = lax.all_to_all(
        outgoing.reshape(n, slots // n, model), "head", split_axis=0, concat_axis=0, tiled=True
    )
    local_experts = w_in.shape[0]
    if local_experts == 1:
        answered = expert_pair(arrived.reshape(slots, model), w_in[0], w_down[0])
        answered = answered.reshape(n, slots // n, model)
    else:
        arrived = arrived.reshape(n, local_experts, capacity, model).transpose(1, 0, 2, 3)
        arrived = arrived.reshape(local_experts, n * capacity, model)
        answered = jnp.stack([expert(arrived[e], w_in[e], w_down[e]) for e in range(local_experts)])
        answered = answered.reshape(local_experts, n, capacity, model).transpose(1, 0, 2, 3)
        answered = answered.reshape(n, slots // n, model)
    back = lax.all_to_all(answered, "head", split_axis=0, concat_axis=0, tiled=True)
    out = combine(back.reshape(slots, model), stream, slots_of, gates, seqs)
    return out.transpose(1, 0, 2)


def solution(mesh):
    return jax.shard_map(
        local,
        mesh=mesh,
        in_specs=(
            P("head", "grp", None, None),
            P("head", "grp", None, None),
            P(("grp", "head"), None, None),
            P("head", "grp", None),
            P(None, "head", None),
            P(),
            P("head", "grp", None),
            P("head", "grp", None),
            P("head", None, None),
            P("head", None, None),
        ),
        out_specs=P("head", "grp", None),
        check_vma=False,
    )
```

```python
import functools

import jax
import jax.numpy as jnp
from jax import lax
from jax.experimental import pallas as pl
from jax.experimental.pallas import tpu as pltpu
from jax.sharding import PartitionSpec as P

eps_norm = 1e-06
F32 = jnp.float32
BF16 = jnp.bfloat16
HIGH_VMEM = 48 * 2**20
LOG2_E = 1.4426950408889634


def in_hbm():
    return pl.BlockSpec(memory_space=pltpu.HBM)


def in_vmem():
    return pl.BlockSpec(memory_space=pltpu.VMEM)


def attend_kernel(
    block, chunk, width, q_hbm, cache_hbm, kv_hbm, o_ref, q_ref, cache_ref, kv_ref, s0, s1, sems
):
    members, groups, piece, _ = kv_hbm.shape
    length = members * groups * piece
    old = cache_hbm.shape[0]
    scale = width**-0.5
    in_q = pltpu.make_async_copy(q_hbm, q_ref, sems.at[0])
    in_cache = pltpu.make_async_copy(cache_hbm, cache_ref, sems.at[1])
    in_q.start()
    in_cache.start()
    in_kv = []
    for group in range(groups):
        for member in range(members):
            place = (group * members + member) * piece
            copy = pltpu.make_async_copy(
                kv_hbm.at[member, group], kv_ref.at[pl.ds(place, piece)], sems.at[2]
            )
            copy.start()
            in_kv.append(copy)
    in_q.wait()
    in_cache.wait()
    for copy in in_kv:
        copy.wait()
    scores = [s0, s1]

    def pieces(b):
        out = [(True, k, chunk, k) for k in range(0, old, chunk)]
        last = b * block
        for k in range(0, last, chunk):
            out.append((False, k, min(chunk, last - k), old + k))
        out.append((False, last, block, old + last))
        return out

    def make_scores(b, part, running):
        of_cache, first, count, column = part
        keys = (cache_ref if of_cache else kv_ref)[pl.ds(first, count), :width]
        s = lax.dot_general(
            q_ref[pl.ds(b * block, block), :],
            keys,
            (((1,), (1,)), ((), ())),
            preferred_element_type=F32,
        )
        if not of_cache and first == b * block:
            row = lax.broadcasted_iota(jnp.int32, s.shape, 0)
            col = lax.broadcasted_iota(jnp.int32, s.shape, 1)
            s = jnp.where(col <= row, s, -jnp.inf)
        scores[b % 2][:, pl.ds(column, count)] = s
        for k in range(0, count, 128):
            piece_max = s[:, k : k + 128]
            running = piece_max if running is None else jnp.maximum(running, piece_max)
        return running

    def use_scores(b, part, top, total, acc):
        of_cache, first, count, column = part
        values = (cache_ref if of_cache else kv_ref)[pl.ds(first, count), width:]
        e = jnp.exp((scores[b % 2][:, pl.ds(column, count)] - top) * scale)
        for k in range(0, count, 128):
            total = e[:, k : k + 128] if total is None else total + e[:, k : k + 128]
        product = jnp.dot(e.astype(BF16), values, preferred_element_type=F32)
        return total, product if acc is None else acc + product

    blocks = length // block
    running = None
    for part in pieces(0):
        running = make_scores(0, part, running)
    for b in range(blocks):
        top = jnp.max(running, 1, keepdims=True)
        now, later = pieces(b), pieces(b + 1) if b + 1 < blocks else []
        running, total, acc = None, None, None
        for k in range(max(len(now), len(later))):
            if k < len(now):
                total, acc = use_scores(b, now[k], top, total, acc)
            if k < len(later):
                running = make_scores(b + 1, later[k], running)
        o_ref[pl.ds(b * block, block), :] = (acc / jnp.sum(total, 1, keepdims=True)).astype(BF16)


def attend(q, cache, kv):
    length, width = q.shape
    old = cache.shape[0]
    block = min(256, length)
    chunk = min(512, old)
    return pl.pallas_call(
        functools.partial(attend_kernel, block, chunk, width),
        out_shape=jax.ShapeDtypeStruct((length, width), BF16),
        in_specs=[in_hbm()] * 3,
        out_specs=in_vmem(),
        scratch_shapes=[
            pltpu.VMEM((length, width), BF16),
            pltpu.VMEM((old, 2 * width), BF16),
            pltpu.VMEM((length, 2 * width), BF16),
            pltpu.VMEM((block, old + length), F32),
            pltpu.VMEM((block, old + length), F32),
            pltpu.SemaphoreType.DMA((3,)),
        ],
        compiler_params=pltpu.CompilerParams(vmem_limit_bytes=HIGH_VMEM),
        cost_estimate=pl.CostEstimate(
            flops=4 * length * (old + length // 2) * width,
            bytes_accessed=4 * (2 * length + 2 * old) * width,
            transcendentals=length * (old + length // 2),
        ),
        name="attend",
    )(q, cache, kv)


def attend_pair_kernel(
    block,
    chunk,
    width,
    q_hbm,
    page_own,
    page_y,
    page_c,
    page_cy,
    kv_own,
    kv_y,
    kv_c,
    kv_cy,
    o_ref,
    q_ref,
    old_ref,
    kv_ref,
    s0,
    s1,
    sems,
):
    me = lax.axis_index("head")
    members, heads, piece, _ = q_hbm.shape
    length = members * piece
    planes = kv_own.shape[0]
    old = old_ref.shape[0]
    earlier_group = me // members > 0
    core = lax.rem(me, 2)
    chip = jnp.bitwise_and(me // 2, members // 2 - 1)
    copies = [[] for _ in range(6)]

    def bring(source, target, sem):
        copy = pltpu.make_async_copy(source, target, sems.at[sem])
        copy.start()
        copies[sem].append(copy)

    for member in range(members):
        for head in range(heads):
            bring(q_hbm.at[member, head], q_ref.at[head, pl.ds(member * piece, piece)], 0)
    place, places = 0, []
    for sem, page in enumerate((page_own, page_y, page_c, page_cy)):
        count = page.shape[0]
        bring(page, old_ref.at[pl.ds(place, count)], 1 + sem)
        places.append(place)
        place += count
    for flip, pieces_of in ((0, kv_own), (2, kv_y), (1, kv_c), (3, kv_cy)):
        for t in range(planes):
            number = jnp.bitwise_and(
                jnp.bitwise_xor(me, flip ^ (t * (members // 2))), members - 1
            )
            start = pl.multiple_of(number * piece, piece)
            area = 0 if t * (members // 2) >= members else length
            bring(pieces_of.at[t], kv_ref.at[pl.ds(area + start, piece)], 5)
    def arrive(sem):
        for copy in copies[sem]:
            copy.wait()
        copies[sem] = []

    arrive(0)
    scale = width**-0.5 * LOG2_E
    scores = [s0, s1]
    blocks = length // block
    units = [(head, b) for head in range(heads) for b in range(blocks)]

    def pieces(unit):
        _, b = units[unit]
        out = [("old", k, chunk, k) for k in range(0, old, chunk)]
        out += [("past", k, chunk, old + k) for k in range(0, length, chunk)]
        last = b * block
        for k in range(0, last, chunk):
            out.append(("new", length + k, min(chunk, last - k), old + length + k))
        out.append(("edge", length + last, block, old + length + last))
        return out

    def make_scores(unit, part, running):
        kind, first, count, column = part
        head, b = units[unit]
        keys = (old_ref if kind == "old" else kv_ref)[pl.ds(first, count), :width]
        s = lax.dot_general(
            q_ref[head, pl.ds(b * block, block), :],
            keys,
            (((1,), (1,)), ((), ())),
            preferred_element_type=F32,
        )
        if kind == "past":
            s = jnp.where(earlier_group, s, -jnp.inf)
        if kind == "edge":
            row = lax.broadcasted_iota(jnp.int32, s.shape, 0)
            col = lax.broadcasted_iota(jnp.int32, s.shape, 1)
            s = jnp.where(col <= row, s, -jnp.inf)
        scores[unit % 2][:, pl.ds(column, count)] = s
        for k in range(0, count, 128):
            piece_max = s[:, k : k + 128]
            running = piece_max if running is None else jnp.maximum(running, piece_max)
        return running

    def use_scores(unit, part, top, total, acc):
        kind, first, count, column = part
        values = (old_ref if kind == "old" else kv_ref)[pl.ds(first, count), width:]
        e = jnp.exp2((scores[unit % 2][:, pl.ds(column, count)] - top) * scale)
        for k in range(0, count, 128):
            total = e[:, k : k + 128] if total is None else total + e[:, k : k + 128]
        product = jnp.dot(e.astype(BF16), values, preferred_element_type=F32)
        return total, product if acc is None else acc + product

    running = None
    for part in pieces(0):
        if part[0] != "old":
            arrive(5)
        else:
            for sem, start in enumerate(places):
                if start < part[1] + part[2]:
                    arrive(1 + sem)
        running = make_scores(0, part, running)
    for unit, (head, b) in enumerate(units):
        top = jnp.max(running, 1, keepdims=True)
        now = pieces(unit)
        later = pieces(unit + 1) if unit + 1 < len(units) else []
        running, total, acc = None, None, None
        for k in range(max(len(now), len(later))):
            if k < len(now):
                total, acc = use_scores(unit, now[k], top, total, acc)
            if k < len(later):
                running = make_scores(unit + 1, later[k], running)
        done = (acc / jnp.sum(total, 1, keepdims=True)).astype(BF16)
        for k in range(0, block, piece):
            member = (b * block + k) // piece
            side = jnp.bitwise_xor(core, member % 2)
            start = pl.multiple_of(jnp.bitwise_xor(chip, member // 2) * piece, piece)
            o_ref[side, pl.ds(start, piece), pl.ds(head * width, width)] = done[k : k + piece]


def attend_pair(q, pages, kvs):
    members, heads, piece, width = q.shape
    length = members * piece
    old = sum(page.shape[0] for page in pages)
    block = 2 * piece
    chunk = min(512, old, length)
    keys = old + 2 * length
    return pl.pallas_call(
        functools.partial(attend_pair_kernel, block, chunk, width),
        out_shape=jax.ShapeDtypeStruct((2, length // 2, heads * width), BF16),
        in_specs=[in_hbm()] * (1 + len(pages) + len(kvs)),
        out_specs=in_vmem(),
        scratch_shapes=[
            pltpu.VMEM((heads, length, width), BF16),
            pltpu.VMEM((old, 2 * width), BF16),
            pltpu.VMEM((2 * length, 2 * width), BF16),
            pltpu.VMEM((block, keys), F32),
            pltpu.VMEM((block, keys), F32),
            pltpu.SemaphoreType.DMA((6,)),
        ],
        compiler_params=pltpu.CompilerParams(vmem_limit_bytes=HIGH_VMEM),
        cost_estimate=pl.CostEstimate(
            flops=4 * heads * length * (keys - length // 2) * width,
            bytes_accessed=4 * (heads * length + keys) * width,
            transcendentals=heads * length * (keys - length // 2),
        ),
        name="attend",
    )(q, *pages, *kvs)


def project_pair_kernel(a_hbm, got_hbm, *refs):
    near, far, outs, (w_ref, all_ref, out_ref, sems) = refs[:4], refs[4:8], refs[8:-4], refs[-4:]
    me = lax.axis_index("head")
    half = lax.axis_index("grp")
    core = lax.rem(me, 2)
    steps, sides, heads, share, columns = near[0].shape
    width = w_ref.shape[1]
    side = got_hbm.shape[1]
    bring = [[], [], []]
    for other, source in enumerate((a_hbm.at[0], got_hbm)):
        at = pl.ds(pl.multiple_of(jnp.bitwise_xor(core, other) * side, side), side)
        bring[2].append(pltpu.make_async_copy(source, all_ref.at[:, at], sems.at[2]))
    for x in range(2):
        column = pl.multiple_of(jnp.bitwise_xor(half, x) * columns, columns)
        for first, given in ((0, near), (steps, far)):
            for flip in range(2):
                for t in range(steps):
                    for u in range(sides):
                        number = jnp.bitwise_xor(me, flip ^ (2 * u) ^ (4 * (first + t)))
                        row = pl.multiple_of(number * share, share)
                        bring[x].append(
                            pltpu.make_async_copy(
                                given[2 * x + flip].at[t, u],
                                w_ref.at[:, pl.ds(row, share), pl.ds(column, columns)],
                                sems.at[x],
                            )
                        )
    for copies in (bring[2], bring[0], bring[1]):
        for copy in copies:
            copy.start()
    for copy in bring[2]:
        copy.wait()
    rows = outs[0].shape[0]
    tile = min(512, columns)
    back = []
    for x in range(2):
        for copy in bring[x]:
            copy.wait()
        for first in range(0, columns, tile):
            column = jnp.bitwise_xor(half, x) * columns + first
            at = pl.ds(pl.multiple_of(column, tile), tile)
            w = w_ref[:, :, at].reshape(heads * width, tile)
            out_ref[:, at] = jnp.dot(all_ref[...], w, preferred_element_type=F32).astype(BF16)
            for k, out in enumerate(outs):
                copy = pltpu.make_async_copy(
                    out_ref.at[pl.ds(k * rows, rows), at], out.at[:, at], sems.at[3]
                )
                copy.start()
                back.append(copy)
    for copy in back:
        copy.wait()


def project_pair(a, got, near, far, parts):
    _, _, heads, share, columns = near[0].shape
    rows = got.shape[0]
    width = 2 * got.shape[1] // heads
    model = 2 * columns
    return pl.pallas_call(
        project_pair_kernel,
        out_shape=[pltpu.HBM((rows // parts, model), BF16)] * parts,
        in_specs=[in_hbm()] * 10,
        out_specs=[in_hbm()] * parts,
        scratch_shapes=[
            pltpu.VMEM((heads, width, model), BF16),
            pltpu.VMEM((rows, heads * width), BF16),
            pltpu.VMEM((rows, model), BF16),
            pltpu.SemaphoreType.DMA((4,)),
        ],
        compiler_params=pltpu.CompilerParams(vmem_limit_bytes=HIGH_VMEM),
        cost_estimate=pl.CostEstimate(
            flops=2 * heads * rows * width * model,
            bytes_accessed=2 * (heads * width * model + heads * rows * width + rows * model),
            transcendentals=0,
        ),
        name="project",
    )(a, got, *near, *far)


def project_kernel(a_ref, w_ref, o_ref):
    members = a_ref.shape[0]
    planes, share = w_ref.shape[1], w_ref.shape[3]
    acc = None
    for head in range(members):
        w = jnp.concatenate(
            [w_ref[m, p, head] for p in range(planes) for m in range(members)], 0
        )
        part = jnp.dot(a_ref[head], w, preferred_element_type=F32)
        acc = part if acc is None else acc + part
    o_ref[...] = acc.astype(BF16)


def project(a, w):
    members, rows, width = a.shape
    planes, share, model = w.shape[1], w.shape[3], w.shape[4]
    tile = min(512, model)
    return pl.pallas_call(
        project_kernel,
        grid=(model // tile,),
        out_shape=jax.ShapeDtypeStruct((rows, model), BF16),
        in_specs=[
            pl.BlockSpec((members, rows, width), lambda t: (0, 0, 0)),
            pl.BlockSpec((members, planes, members, share, tile), lambda t: (0, 0, 0, 0, t)),
        ],
        out_specs=pl.BlockSpec((rows, tile), lambda t: (0, t)),
        compiler_params=pltpu.CompilerParams(vmem_limit_bytes=HIGH_VMEM),
        cost_estimate=pl.CostEstimate(
            flops=2 * members * rows * width * model,
            bytes_accessed=2 * (members * width * model + members * rows * width + rows * model),
            transcendentals=0,
        ),
        name="project",
    )(a, w)


def route_kernel(resid_ref, gain_ref, slots_ref, *refs):
    parts_refs, (stream_ref, out_ref) = refs[:-2], refs[-2:]
    seqs = resid_ref.shape[0]
    streams = []
    for seq in range(seqs):
        stream = resid_ref[seq].astype(F32)
        projected = parts_refs[0][seq].astype(F32)
        for part in parts_refs[1:]:
            projected = projected + part[seq].astype(F32)
        streams.append(stream + projected)
    stream = jnp.concatenate(streams, 0) if seqs > 1 else streams[0]
    stream_ref[...] = stream
    normed = stream * lax.rsqrt(jnp.mean(stream * stream, 1, keepdims=True) + eps_norm)
    normed = (normed * gain_ref[...]).astype(BF16)
    slots, rows = out_ref.shape[0], stream.shape[0]
    place = lax.broadcasted_iota(jnp.int32, (slots, rows), 0)
    hit = place == slots_ref[0:1, :]
    for k in range(1, slots_ref.shape[0]):
        hit = hit | (place == slots_ref[k : k + 1, :])
    out_ref[...] = jnp.dot(hit.astype(BF16), normed, preferred_element_type=F32).astype(BF16)


def route(parts, resid, gain, slots_of, slots):
    seqs, local_rows, model = resid.shape
    rows = seqs * local_rows
    return pl.pallas_call(
        route_kernel,
        out_shape=(
            jax.ShapeDtypeStruct((rows, model), F32),
            jax.ShapeDtypeStruct((slots, model), BF16),
        ),
        in_specs=[in_vmem()] * (3 + len(parts)),
        out_specs=(in_vmem(), in_vmem()),
        compiler_params=pltpu.CompilerParams(vmem_limit_bytes=HIGH_VMEM),
        cost_estimate=pl.CostEstimate(
            flops=2 * slots * rows * model,
            bytes_accessed=2 * (len(parts) + 3 + slots // rows) * rows * model,
            transcendentals=0,
        ),
        name="route",
    )(resid, gain, slots_of, *parts)


def expert_kernel(x_ref, w_in_ref, w_down_ref, o_ref):
    hidden_width = w_down_ref.shape[0]
    inner = jnp.dot(x_ref[...], w_in_ref[...], preferred_element_type=F32)
    gate = inner[:, :hidden_width]
    hidden = (gate / (1.0 + jnp.exp(-gate)) * inner[:, hidden_width:]).astype(BF16)
    o_ref[...] = jnp.dot(hidden, w_down_ref[...], preferred_element_type=F32).astype(BF16)


def expert(x, w_in, w_down):
    rows, model = x.shape
    hidden_width = w_down.shape[0]
    return pl.pallas_call(
        expert_kernel,
        out_shape=jax.ShapeDtypeStruct((rows, model), BF16),
        in_specs=[in_vmem()] * 3,
        out_specs=in_vmem(),
        compiler_params=pltpu.CompilerParams(vmem_limit_bytes=HIGH_VMEM),
        cost_estimate=pl.CostEstimate(
            flops=6 * rows * model * hidden_width,
            bytes_accessed=2 * (2 * rows * model + 3 * model * hidden_width),
            transcendentals=rows * hidden_width,
        ),
        name="expert",
    )(x, w_in, w_down)


def expert_pair(x, w_in, w_down):
    rows, model = x.shape
    hidden_width = w_down.shape[0]
    parts = 4
    depth = model // parts

    def kernel(x_hbm, in_hbm_ref, down_hbm, o_hbm, x_ref, in_ref, down_ref, o_ref, sems):
        bring_x = pltpu.make_async_copy(x_hbm, x_ref, sems.at[parts])
        bring_x.start()
        bring_in = []
        for k in range(parts):
            at = pl.ds(k * depth, depth)
            bring_in.append(pltpu.make_async_copy(in_hbm_ref.at[at], in_ref.at[at], sems.at[k]))
            bring_in[k].start()
        bring_down = pltpu.make_async_copy(down_hbm, down_ref, sems.at[parts + 1])
        bring_down.start()
        bring_x.wait()
        inner = None
        for k in range(parts):
            bring_in[k].wait()
            at = pl.ds(k * depth, depth)
            part = jnp.dot(x_ref[:, at], in_ref[at, :], preferred_element_type=F32)
            inner = part if inner is None else inner + part
        gate = inner[:, :hidden_width]
        hidden = (gate / (1.0 + jnp.exp(-gate)) * inner[:, hidden_width:]).astype(BF16)
        bring_down.wait()
        o_ref[...] = jnp.dot(hidden, down_ref[...], preferred_element_type=F32).astype(BF16)
        back = pltpu.make_async_copy(o_ref, o_hbm, sems.at[parts + 2])
        back.start()
        back.wait()

    return pl.pallas_call(
        kernel,
        out_shape=pltpu.HBM((rows, model), BF16),
        in_specs=[in_hbm()] * 3,
        out_specs=in_hbm(),
        scratch_shapes=[
            pltpu.VMEM((rows, model), BF16),
            pltpu.VMEM(w_in.shape, BF16),
            pltpu.VMEM(w_down.shape, BF16),
            pltpu.VMEM((rows, model), BF16),
            pltpu.SemaphoreType.DMA((parts + 3,)),
        ],
        compiler_params=pltpu.CompilerParams(vmem_limit_bytes=HIGH_VMEM),
        cost_estimate=pl.CostEstimate(
            flops=6 * rows * model * hidden_width,
            bytes_accessed=2 * (2 * rows * model + 3 * model * hidden_width),
            transcendentals=rows * hidden_width,
        ),
        name="expert",
    )(x, w_in, w_down)


def combine_kernel(
    seqs, back_ref, stream_hbm, slots_ref, gates_ref, o_ref, stream_ref, sem
):
    bring = pltpu.make_async_copy(stream_hbm, stream_ref, sem.at[0])
    bring.start()
    slots = back_ref.shape[0]
    rows = stream_ref.shape[0]
    place = lax.broadcasted_iota(jnp.int32, (rows, slots), 1)
    gathered = None
    for k in range(slots_ref.shape[1]):
        pick = (place == slots_ref[:, k : k + 1]).astype(BF16)
        picked = jnp.dot(pick, back_ref[...], preferred_element_type=F32)
        part = picked * gates_ref[:, k : k + 1]
        gathered = part if gathered is None else gathered + part
    bring.wait()
    out = (stream_ref[...] + gathered).astype(BF16)
    local_rows = rows // seqs
    for seq in range(seqs):
        o_ref[seq] = out[seq * local_rows : (seq + 1) * local_rows]


def combine(back, stream, slots_of, gates, seqs):
    slots, model = back.shape
    rows = stream.shape[0]
    top = slots_of.shape[1]
    return pl.pallas_call(
        functools.partial(combine_kernel, seqs),
        out_shape=jax.ShapeDtypeStruct((seqs, rows // seqs, model), BF16),
        in_specs=[in_vmem(), in_hbm(), in_vmem(), in_vmem()],
        out_specs=in_vmem(),
        scratch_shapes=[pltpu.VMEM((rows, model), F32), pltpu.SemaphoreType.DMA((1,))],
        compiler_params=pltpu.CompilerParams(vmem_limit_bytes=HIGH_VMEM),
        cost_estimate=pl.CostEstimate(
            flops=2 * top * slots * rows * model,
            bytes_accessed=2 * slots * model + 6 * rows * model,
            transcendentals=0,
        ),
        name="combine",
    )(back, stream, slots_of, gates)


def flipped(value, axis, mask):
    pairs = [(source, source ^ mask) for source in range(lax.axis_size(axis))]
    return lax.ppermute(value, axis, pairs)


def parts_in_pairs(queries, new_kv, cache, w_out):
    n = lax.axis_size("head")
    local_rows, _, heads, width = queries.shape
    pair_heads = new_kv.shape[2]
    members = heads // pair_heads
    model = w_out.shape[2]
    share = w_out.shape[1]
    me = lax.axis_index("head")
    plane_bit = members // 2
    planes = n // plane_bit
    b = (me // plane_bit) % 2
    y = (me // 2) % 2
    group_sets = [[g * members + m for m in range(members)] for g in range(n // members)]

    query_slots = queries.reshape(local_rows, heads, width).transpose(1, 0, 2)
    query_slots = query_slots.reshape(members, heads // members, local_rows, width)
    q = lax.all_to_all(
        query_slots, "head", split_axis=0, concat_axis=0, tiled=True, axis_index_groups=group_sets
    )

    def page_target(source, other):
        p, plane, rest = source // members, (source // plane_bit) % 2, source % plane_bit
        return (plane ^ other) * members + p * plane_bit + rest

    page_a, page_b = (
        lax.ppermute(cache[0], "head", [(d, page_target(d, other)) for d in range(n)])
        for other in range(2)
    )
    kv_heads = new_kv.reshape(local_rows, pair_heads, 2 * width).transpose(1, 0, 2)
    kv_same = lax.dynamic_index_in_dim(kv_heads, b, 0, keepdims=False)
    kv_other = lax.dynamic_index_in_dim(kv_heads, 1 - b, 0, keepdims=False)
    columns = model // 2
    w = lax.dynamic_slice_in_dim(w_out, lax.axis_index("grp") * columns, columns, 2)
    w = w.reshape(2, 2, heads // 4, share, columns)
    w_keep = lax.dynamic_index_in_dim(w, y, 1, keepdims=False)
    w_give = lax.dynamic_index_in_dim(w, 1 - y, 1, keepdims=False)
    kv_own = [kv_same]
    for t in range(1, planes):
        kv_own.append(flipped(kv_other if t % 2 else kv_same, "head", t * plane_bit))
    w_got = flipped(w_give, "head", 2)

    (page_a, page_b, kv_own, q), w_got = lax.optimization_barrier(
        ((page_a, page_b, kv_own, q), w_got)
    )
    own_pages = jnp.concatenate([page_a, page_b], 0)
    kv_own = jnp.stack(kv_own, 0)
    pages_y = flipped(own_pages, "head", 2)
    kv_y = flipped(kv_own, "head", 2)
    w_both = jnp.stack([w_keep, w_got], 1)
    w_same = lax.dynamic_index_in_dim(w_both, b, 0, keepdims=False)
    w_other = lax.dynamic_index_in_dim(w_both, 1 - b, 0, keepdims=False)
    w_near = jnp.stack([w_same, flipped(w_other, "head", plane_bit)], 0)
    w_near_x = flipped(w_near, "grp", 1)
    w_far = flipped(w_near, "head", members)
    pages_y, kv_y, own_pages, kv_own, w_near_x = lax.optimization_barrier(
        (pages_y, kv_y, own_pages, kv_own, w_near_x)
    )
    kv_c = flipped(kv_own, "head", 1)
    kv_cy = flipped(kv_y, "head", 1)
    pages_c = flipped(own_pages, "head", 1)
    pages_cy = flipped(pages_y, "head", 1)
    q, w_far = lax.optimization_barrier((q, w_far))
    w_far_x = flipped(w_far, "grp", 1)
    a = attend_pair(q, (own_pages, pages_y, pages_c, pages_cy), (kv_own, kv_y, kv_c, kv_cy))
    got = flipped(a[1], "head", 1)
    a, w_near_x, w_far_x = lax.optimization_barrier((a, w_near_x, w_far_x))
    w_near_c = flipped(w_near, "head", 1)
    w_far_c = flipped(w_far, "head", 1)
    w_near_cx = flipped(w_near_x, "head", 1)
    w_far_cx = flipped(w_far_x, "head", 1)
    partial = project_pair(
        a,
        got,
        (w_near, w_near_c, w_near_x, w_near_cx),
        (w_far, w_far_c, w_far_x, w_far_cx),
        members // 2,
    )
    parts = [partial[0]] + [flipped(partial[k], "head", 2 * k) for k in (3, 2, 1)]
    return [part[None] for part in parts]


def parts_in_planes(queries, new_kv, cache, w_out):
    n = lax.axis_size("head")
    local_rows, seqs, heads, width = queries.shape
    pair_heads = new_kv.shape[2]
    members = heads // pair_heads
    groups = n // members
    model = w_out.shape[2]
    side = 1 << ((n.bit_length() - 1) // 2)
    side = min(side, heads)
    planes = n // side
    planes_of_seq = heads // side
    pair_groups = [[g * members + m for m in range(members)] for g in range(groups)]
    cross_groups = [[g * members + m for g in range(groups)] for m in range(members)]
    plane_groups = [[p * side + m for m in range(side)] for p in range(planes)]
    column_groups = [[p * side + m for p in range(planes)] for m in range(side)]

    query_slots = queries.reshape(local_rows, n, width).transpose(1, 0, 2)
    q = lax.all_to_all(query_slots, "head", split_axis=0, concat_axis=0, tiled=True)
    q = q.reshape(n * local_rows, width)

    kv_slots = new_kv.reshape(local_rows, groups, 2 * width).transpose(1, 0, 2)
    kv = lax.all_to_all(
        kv_slots, "head", split_axis=0, concat_axis=0, tiled=True, axis_index_groups=cross_groups
    )
    kv = lax.all_gather(kv, "head", axis=0, axis_index_groups=pair_groups)
    pages = lax.all_gather(cache, "head", axis=0, tiled=True, axis_index_groups=pair_groups)

    share = w_out.shape[1]
    w_planes = w_out.reshape(planes_of_seq, side, share, model)
    if planes > planes_of_seq:
        w_planes = jnp.tile(w_planes, (planes // planes_of_seq, 1, 1, 1))
    w = lax.all_to_all(
        w_planes, "head", split_axis=0, concat_axis=0, tiled=True, axis_index_groups=column_groups
    )
    w = lax.all_gather(w, "head", axis=0, axis_index_groups=plane_groups)
    if share % 16:
        w = w.transpose(2, 1, 0, 3, 4).reshape(1, 1, side, width, model)
        w = w.reshape(side, width, model)

    attended = attend(q, pages.reshape(-1, 2 * width), kv)
    a = attended.reshape(planes, side, local_rows, width).transpose(1, 0, 2, 3)
    a = a.reshape(side, planes * local_rows, width)
    a = lax.all_to_all(
        a, "head", split_axis=0, concat_axis=0, tiled=True, axis_index_groups=plane_groups
    )
    if share % 16:
        partial = jnp.einsum("hri,hid->rd", a, w, preferred_element_type=F32).astype(BF16)
    else:
        partial = project(a, w)
    parts = lax.all_to_all(
        partial.reshape(planes, local_rows, model),
        "head",
        split_axis=0,
        concat_axis=0,
        tiled=True,
        axis_index_groups=column_groups,
    )
    parts = parts.reshape(seqs, planes_of_seq, local_rows, model)
    return [parts[:, k] for k in range(planes_of_seq)]


def local(queries, new_kv, cache, resid, w_out, norm_gain, expert_ids, expert_gates, w_in, w_down):
    n = lax.axis_size("head")
    local_rows, seqs, heads, width = queries.shape
    model = resid.shape[2]
    rows = local_rows * seqs
    members = heads // new_kv.shape[2]
    in_pairs = (
        lax.axis_size("grp") == 2
        and seqs == 1
        and new_kv.shape[2] == 2
        and n == heads == 2 * members
        and members == 8
        and cache.shape[0] == 1
        and w_in.shape[0] == 1
        and w_out.shape[1] % 16 == 0
    )
    plan = parts_in_pairs if in_pairs else parts_in_planes
    parts = plan(queries, new_kv, cache, w_out)

    top = expert_ids.shape[2]
    experts = w_in.shape[0] * n
    capacity = max(2, 2 * rows * top // experts)
    ids = expert_ids.transpose(1, 0, 2).reshape(rows, top)
    gates = expert_gates.transpose(1, 0, 2).reshape(rows, top)
    onehot = (ids[:, :, None] == jnp.arange(experts, dtype=jnp.int32)).astype(jnp.int32)
    named = onehot.sum(1)
    before = jnp.cumsum(named, 0) - named
    slots_of = ids * capacity + jnp.sum(onehot * before[:, None, :], 2)
    slots = experts * capacity

    stream, outgoing = route(
        parts, resid.transpose(1, 0, 2), norm_gain[None, :], slots_of.T, slots
    )
    arrived = lax.all_to_all(
        outgoing.reshape(n, slots // n, model), "head", split_axis=0, concat_axis=0, tiled=True
    )
    local_experts = w_in.shape[0]
    if local_experts == 1:
        answered = expert_pair(arrived.reshape(slots, model), w_in[0], w_down[0])
        answered = answered.reshape(n, slots // n, model)
    else:
        arrived = arrived.reshape(n, local_experts, capacity, model).transpose(1, 0, 2, 3)
        arrived = arrived.reshape(local_experts, n * capacity, model)
        answered = jnp.stack([expert(arrived[e], w_in[e], w_down[e]) for e in range(local_experts)])
        answered = answered.reshape(local_experts, n, capacity, model).transpose(1, 0, 2, 3)
        answered = answered.reshape(n, slots // n, model)
    back = lax.all_to_all(answered, "head", split_axis=0, concat_axis=0, tiled=True)
    out = combine(back.reshape(slots, model), stream, slots_of, gates, seqs)
    return out.transpose(1, 0, 2)


def solution(mesh):
    return jax.shard_map(
        local,
        mesh=mesh,
        in_specs=(
            P("head", "grp", None, None),
            P("head", "grp", None, None),
            P(("grp", "head"), None, None),
            P("head", "grp", None),
            P(None, "head", None),
            P(),
            P("head", "grp", None),
            P("head", "grp", None),
            P("head", None, None),
            P("head", None, None),
        ),
        out_specs=P("head", "grp", None),
        check_vma=False,
    )
```

```python
import functools

import jax
import jax.numpy as jnp
from jax import lax
from jax.experimental import pallas as pl
from jax.experimental.pallas import tpu as pltpu
from jax.sharding import PartitionSpec as P

eps_norm = 1e-06
F32 = jnp.float32
BF16 = jnp.bfloat16
HIGH_VMEM = 48 * 2**20
LOG2_E = 1.4426950408889634


def in_hbm():
    return pl.BlockSpec(memory_space=pltpu.HBM)


def in_vmem():
    return pl.BlockSpec(memory_space=pltpu.VMEM)


def attend_kernel(
    block, chunk, width, q_hbm, cache_hbm, kv_hbm, o_ref, q_ref, cache_ref, kv_ref, s0, s1, sems
):
    members, groups, piece, _ = kv_hbm.shape
    length = members * groups * piece
    old = cache_hbm.shape[0]
    scale = width**-0.5
    in_q = pltpu.make_async_copy(q_hbm, q_ref, sems.at[0])
    in_cache = pltpu.make_async_copy(cache_hbm, cache_ref, sems.at[1])
    in_q.start()
    in_cache.start()
    in_kv = []
    for group in range(groups):
        for member in range(members):
            place = (group * members + member) * piece
            copy = pltpu.make_async_copy(
                kv_hbm.at[member, group], kv_ref.at[pl.ds(place, piece)], sems.at[2]
            )
            copy.start()
            in_kv.append(copy)
    in_q.wait()
    in_cache.wait()
    for copy in in_kv:
        copy.wait()
    scores = [s0, s1]

    def pieces(b):
        out = [(True, k, chunk, k) for k in range(0, old, chunk)]
        last = b * block
        for k in range(0, last, chunk):
            out.append((False, k, min(chunk, last - k), old + k))
        out.append((False, last, block, old + last))
        return out

    def make_scores(b, part, running):
        of_cache, first, count, column = part
        keys = (cache_ref if of_cache else kv_ref)[pl.ds(first, count), :width]
        s = lax.dot_general(
            q_ref[pl.ds(b * block, block), :],
            keys,
            (((1,), (1,)), ((), ())),
            preferred_element_type=F32,
        )
        if not of_cache and first == b * block:
            row = lax.broadcasted_iota(jnp.int32, s.shape, 0)
            col = lax.broadcasted_iota(jnp.int32, s.shape, 1)
            s = jnp.where(col <= row, s, -jnp.inf)
        scores[b % 2][:, pl.ds(column, count)] = s
        for k in range(0, count, 128):
            piece_max = s[:, k : k + 128]
            running = piece_max if running is None else jnp.maximum(running, piece_max)
        return running

    def use_scores(b, part, top, total, acc):
        of_cache, first, count, column = part
        values = (cache_ref if of_cache else kv_ref)[pl.ds(first, count), width:]
        e = jnp.exp((scores[b % 2][:, pl.ds(column, count)] - top) * scale)
        for k in range(0, count, 128):
            total = e[:, k : k + 128] if total is None else total + e[:, k : k + 128]
        product = jnp.dot(e.astype(BF16), values, preferred_element_type=F32)
        return total, product if acc is None else acc + product

    blocks = length // block
    running = None
    for part in pieces(0):
        running = make_scores(0, part, running)
    for b in range(blocks):
        top = jnp.max(running, 1, keepdims=True)
        now, later = pieces(b), pieces(b + 1) if b + 1 < blocks else []
        running, total, acc = None, None, None
        for k in range(max(len(now), len(later))):
            if k < len(now):
                total, acc = use_scores(b, now[k], top, total, acc)
            if k < len(later):
                running = make_scores(b + 1, later[k], running)
        o_ref[pl.ds(b * block, block), :] = (acc / jnp.sum(total, 1, keepdims=True)).astype(BF16)


def attend(q, cache, kv):
    length, width = q.shape
    old = cache.shape[0]
    block = min(256, length)
    chunk = min(512, old)
    return pl.pallas_call(
        functools.partial(attend_kernel, block, chunk, width),
        out_shape=jax.ShapeDtypeStruct((length, width), BF16),
        in_specs=[in_hbm()] * 3,
        out_specs=in_vmem(),
        scratch_shapes=[
            pltpu.VMEM((length, width), BF16),
            pltpu.VMEM((old, 2 * width), BF16),
            pltpu.VMEM((length, 2 * width), BF16),
            pltpu.VMEM((block, old + length), F32),
            pltpu.VMEM((block, old + length), F32),
            pltpu.SemaphoreType.DMA((3,)),
        ],
        compiler_params=pltpu.CompilerParams(vmem_limit_bytes=HIGH_VMEM),
        cost_estimate=pl.CostEstimate(
            flops=4 * length * (old + length // 2) * width,
            bytes_accessed=4 * (2 * length + 2 * old) * width,
            transcendentals=length * (old + length // 2),
        ),
        name="attend",
    )(q, cache, kv)


def attend_pair_kernel(
    block,
    chunk,
    width,
    q_hbm,
    page_own,
    page_y,
    page_c,
    page_cy,
    kv_own,
    kv_y,
    kv_c,
    kv_cy,
    o_ref,
    q_ref,
    old_ref,
    kv_ref,
    s0,
    s1,
    sems,
):
    me = lax.axis_index("head")
    members, heads, piece, _ = q_hbm.shape
    length = members * piece
    planes = kv_own.shape[0]
    old = old_ref.shape[0]
    earlier_group = me // members > 0
    core = lax.rem(me, 2)
    chip = jnp.bitwise_and(me // 2, members // 2 - 1)
    copies = [[] for _ in range(6)]

    def bring(source, target, sem):
        copy = pltpu.make_async_copy(source, target, sems.at[sem])
        copy.start()
        copies[sem].append(copy)

    for member in range(members):
        for head in range(heads):
            bring(q_hbm.at[member, head], q_ref.at[head, pl.ds(member * piece, piece)], 0)
    place, places = 0, []
    for sem, page in enumerate((page_own, page_y, page_c, page_cy)):
        count = page.shape[0]
        bring(page, old_ref.at[pl.ds(place, count)], 1 + sem)
        places.append(place)
        place += count
    for flip, pieces_of in ((0, kv_own), (2, kv_y), (1, kv_c), (3, kv_cy)):
        for t in range(planes):
            number = jnp.bitwise_and(
                jnp.bitwise_xor(me, flip ^ (t * (members // 2))), members - 1
            )
            start = pl.multiple_of(number * piece, piece)
            area = 0 if t * (members // 2) >= members else length
            bring(pieces_of.at[t], kv_ref.at[pl.ds(area + start, piece)], 5)
    def arrive(sem):
        for copy in copies[sem]:
            copy.wait()
        copies[sem] = []

    arrive(0)
    scale = width**-0.5 * LOG2_E
    scores = [s0, s1]
    blocks = length // block
    units = [(head, b) for head in range(heads) for b in range(blocks)]

    def pieces(unit):
        _, b = units[unit]
        out = [("old", k, chunk, k) for k in range(0, old, chunk)]
        out += [("past", k, chunk, old + k) for k in range(0, length, chunk)]
        last = b * block
        for k in range(0, last, chunk):
            out.append(("new", length + k, min(chunk, last - k), old + length + k))
        out.append(("edge", length + last, block, old + length + last))
        return out

    def make_scores(unit, part, running):
        kind, first, count, column = part
        head, b = units[unit]
        keys = (old_ref if kind == "old" else kv_ref)[pl.ds(first, count), :width]
        s = lax.dot_general(
            q_ref[head, pl.ds(b * block, block), :],
            keys,
            (((1,), (1,)), ((), ())),
            preferred_element_type=F32,
        )
        if kind == "past":
            s = jnp.where(earlier_group, s, -jnp.inf)
        if kind == "edge":
            row = lax.broadcasted_iota(jnp.int32, s.shape, 0)
            col = lax.broadcasted_iota(jnp.int32, s.shape, 1)
            s = jnp.where(col <= row, s, -jnp.inf)
        scores[unit % 2][:, pl.ds(column, count)] = s
        for k in range(0, count, 128):
            piece_max = s[:, k : k + 128]
            running = piece_max if running is None else jnp.maximum(running, piece_max)
        return running

    def use_scores(unit, part, top, total, acc):
        kind, first, count, column = part
        values = (old_ref if kind == "old" else kv_ref)[pl.ds(first, count), width:]
        e = jnp.exp2((scores[unit % 2][:, pl.ds(column, count)] - top) * scale)
        for k in range(0, count, 128):
            total = e[:, k : k + 128] if total is None else total + e[:, k : k + 128]
        product = jnp.dot(e.astype(BF16), values, preferred_element_type=F32)
        return total, product if acc is None else acc + product

    running = None
    for part in pieces(0):
        if part[0] != "old":
            arrive(5)
        else:
            for sem, start in enumerate(places):
                if start < part[1] + part[2]:
                    arrive(1 + sem)
        running = make_scores(0, part, running)
    for unit, (head, b) in enumerate(units):
        top = jnp.max(running, 1, keepdims=True)
        now = pieces(unit)
        later = pieces(unit + 1) if unit + 1 < len(units) else []
        running, total, acc = None, None, None
        for k in range(max(len(now), len(later))):
            if k < len(now):
                total, acc = use_scores(unit, now[k], top, total, acc)
            if k < len(later):
                running = make_scores(unit + 1, later[k], running)
        done = (acc / jnp.sum(total, 1, keepdims=True)).astype(BF16)
        for k in range(0, block, piece):
            member = (b * block + k) // piece
            side = jnp.bitwise_xor(core, member % 2)
            start = pl.multiple_of(jnp.bitwise_xor(chip, member // 2) * piece, piece)
            o_ref[side, pl.ds(start, piece), pl.ds(head * width, width)] = done[k : k + piece]


def attend_pair(q, pages, kvs):
    members, heads, piece, width = q.shape
    length = members * piece
    old = sum(page.shape[0] for page in pages)
    block = 2 * piece
    chunk = min(512, old, length)
    keys = old + 2 * length
    return pl.pallas_call(
        functools.partial(attend_pair_kernel, block, chunk, width),
        out_shape=jax.ShapeDtypeStruct((2, length // 2, heads * width), BF16),
        in_specs=[in_hbm()] * (1 + len(pages) + len(kvs)),
        out_specs=in_vmem(),
        scratch_shapes=[
            pltpu.VMEM((heads, length, width), BF16),
            pltpu.VMEM((old, 2 * width), BF16),
            pltpu.VMEM((2 * length, 2 * width), BF16),
            pltpu.VMEM((block, keys), F32),
            pltpu.VMEM((block, keys), F32),
            pltpu.SemaphoreType.DMA((6,)),
        ],
        compiler_params=pltpu.CompilerParams(vmem_limit_bytes=HIGH_VMEM),
        cost_estimate=pl.CostEstimate(
            flops=4 * heads * length * (keys - length // 2) * width,
            bytes_accessed=4 * (heads * length + keys) * width,
            transcendentals=heads * length * (keys - length // 2),
        ),
        name="attend",
    )(q, *pages, *kvs)


def project_pair_kernel(a_hbm, got_hbm, *refs):
    near, far, outs, (w_ref, all_ref, out_ref, sems) = refs[:4], refs[4:8], refs[8:-4], refs[-4:]
    me = lax.axis_index("head")
    half = lax.axis_index("grp")
    core = lax.rem(me, 2)
    steps, sides, heads, share, columns = near[0].shape
    width = w_ref.shape[1]
    side = got_hbm.shape[1]
    bring = [[], [], []]
    for other, source in enumerate((a_hbm.at[0], got_hbm)):
        at = pl.ds(pl.multiple_of(jnp.bitwise_xor(core, other) * side, side), side)
        bring[2].append(pltpu.make_async_copy(source, all_ref.at[:, at], sems.at[2]))
    for x in range(2):
        column = pl.multiple_of(jnp.bitwise_xor(half, x) * columns, columns)
        for first, given in ((0, near), (steps, far)):
            for flip in range(2):
                for t in range(steps):
                    for u in range(sides):
                        number = jnp.bitwise_xor(me, flip ^ (2 * u) ^ (4 * (first + t)))
                        row = pl.multiple_of(number * share, share)
                        bring[x].append(
                            pltpu.make_async_copy(
                                given[2 * x + flip].at[t, u],
                                w_ref.at[:, pl.ds(row, share), pl.ds(column, columns)],
                                sems.at[x],
                            )
                        )
    for copies in (bring[2], bring[0], bring[1]):
        for copy in copies:
            copy.start()
    for copy in bring[2]:
        copy.wait()
    rows = outs[0].shape[0]
    tile = min(512, columns)
    back = []
    for x in range(2):
        for copy in bring[x]:
            copy.wait()
        for first in range(0, columns, tile):
            column = jnp.bitwise_xor(half, x) * columns + first
            at = pl.ds(pl.multiple_of(column, tile), tile)
            w = w_ref[:, :, at].reshape(heads * width, tile)
            out_ref[:, at] = jnp.dot(all_ref[...], w, preferred_element_type=F32).astype(BF16)
            for k, out in enumerate(outs):
                copy = pltpu.make_async_copy(
                    out_ref.at[pl.ds(k * rows, rows), at], out.at[:, at], sems.at[3]
                )
                copy.start()
                back.append(copy)
    for copy in back:
        copy.wait()


def project_pair(a, got, near, far, parts):
    _, _, heads, share, columns = near[0].shape
    rows = got.shape[0]
    width = 2 * got.shape[1] // heads
    model = 2 * columns
    return pl.pallas_call(
        project_pair_kernel,
        out_shape=[jax.ShapeDtypeStruct((rows // parts, model), BF16)]
        + [pltpu.HBM((rows // parts, model), BF16)] * (parts - 1),
        in_specs=[in_hbm()] * 10,
        out_specs=[in_hbm()] * parts,
        scratch_shapes=[
            pltpu.VMEM((heads, width, model), BF16),
            pltpu.VMEM((rows, heads * width), BF16),
            pltpu.VMEM((rows, model), BF16),
            pltpu.SemaphoreType.DMA((4,)),
        ],
        compiler_params=pltpu.CompilerParams(vmem_limit_bytes=HIGH_VMEM),
        cost_estimate=pl.CostEstimate(
            flops=2 * heads * rows * width * model,
            bytes_accessed=2 * (heads * width * model + heads * rows * width + rows * model),
            transcendentals=0,
        ),
        name="project",
    )(a, got, *near, *far)


def project_kernel(a_ref, w_ref, o_ref):
    members = a_ref.shape[0]
    planes, share = w_ref.shape[1], w_ref.shape[3]
    acc = None
    for head in range(members):
        w = jnp.concatenate(
            [w_ref[m, p, head] for p in range(planes) for m in range(members)], 0
        )
        part = jnp.dot(a_ref[head], w, preferred_element_type=F32)
        acc = part if acc is None else acc + part
    o_ref[...] = acc.astype(BF16)


def project(a, w):
    members, rows, width = a.shape
    planes, share, model = w.shape[1], w.shape[3], w.shape[4]
    tile = min(512, model)
    return pl.pallas_call(
        project_kernel,
        grid=(model // tile,),
        out_shape=jax.ShapeDtypeStruct((rows, model), BF16),
        in_specs=[
            pl.BlockSpec((members, rows, width), lambda t: (0, 0, 0)),
            pl.BlockSpec((members, planes, members, share, tile), lambda t: (0, 0, 0, 0, t)),
        ],
        out_specs=pl.BlockSpec((rows, tile), lambda t: (0, t)),
        compiler_params=pltpu.CompilerParams(vmem_limit_bytes=HIGH_VMEM),
        cost_estimate=pl.CostEstimate(
            flops=2 * members * rows * width * model,
            bytes_accessed=2 * (members * width * model + members * rows * width + rows * model),
            transcendentals=0,
        ),
        name="project",
    )(a, w)


def route_kernel(resid_ref, gain_ref, slots_ref, *refs):
    parts_refs, (stream_hbm, out_ref, stream_ref, sem) = refs[:-4], refs[-4:]
    seqs = resid_ref.shape[0]
    streams = []
    for seq in range(seqs):
        stream = resid_ref[seq].astype(F32)
        projected = parts_refs[0][seq].astype(F32)
        for part in parts_refs[1:]:
            projected = projected + part[seq].astype(F32)
        streams.append(stream + projected)
    stream = jnp.concatenate(streams, 0) if seqs > 1 else streams[0]
    stream_ref[...] = stream
    back = pltpu.make_async_copy(stream_ref, stream_hbm, sem.at[0])
    back.start()
    normed = stream * lax.rsqrt(jnp.mean(stream * stream, 1, keepdims=True) + eps_norm)
    normed = (normed * gain_ref[...]).astype(BF16)
    slots, rows = out_ref.shape[0], stream.shape[0]
    place = lax.broadcasted_iota(jnp.int32, (slots, rows), 0)
    hit = place == slots_ref[0:1, :]
    for k in range(1, slots_ref.shape[0]):
        hit = hit | (place == slots_ref[k : k + 1, :])
    out_ref[...] = jnp.dot(hit.astype(BF16), normed, preferred_element_type=F32).astype(BF16)
    back.wait()


def route(parts, resid, gain, slots_of, slots):
    seqs, local_rows, model = resid.shape
    rows = seqs * local_rows
    return pl.pallas_call(
        route_kernel,
        out_shape=(
            pltpu.HBM((rows, model), F32),
            jax.ShapeDtypeStruct((slots, model), BF16),
        ),
        in_specs=[in_vmem()] * (3 + len(parts)),
        out_specs=(in_hbm(), in_vmem()),
        scratch_shapes=[pltpu.VMEM((rows, model), F32), pltpu.SemaphoreType.DMA((1,))],
        compiler_params=pltpu.CompilerParams(vmem_limit_bytes=HIGH_VMEM),
        cost_estimate=pl.CostEstimate(
            flops=2 * slots * rows * model,
            bytes_accessed=2 * (len(parts) + 3 + slots // rows) * rows * model,
            transcendentals=0,
        ),
        name="route",
    )(resid, gain, slots_of, *parts)


def expert_kernel(x_ref, w_in_ref, w_down_ref, o_ref):
    hidden_width = w_down_ref.shape[0]
    inner = jnp.dot(x_ref[...], w_in_ref[...], preferred_element_type=F32)
    gate = inner[:, :hidden_width]
    hidden = (gate / (1.0 + jnp.exp(-gate)) * inner[:, hidden_width:]).astype(BF16)
    o_ref[...] = jnp.dot(hidden, w_down_ref[...], preferred_element_type=F32).astype(BF16)


def expert(x, w_in, w_down):
    rows, model = x.shape
    hidden_width = w_down.shape[0]
    return pl.pallas_call(
        expert_kernel,
        out_shape=jax.ShapeDtypeStruct((rows, model), BF16),
        in_specs=[in_vmem()] * 3,
        out_specs=in_vmem(),
        compiler_params=pltpu.CompilerParams(vmem_limit_bytes=HIGH_VMEM),
        cost_estimate=pl.CostEstimate(
            flops=6 * rows * model * hidden_width,
            bytes_accessed=2 * (2 * rows * model + 3 * model * hidden_width),
            transcendentals=rows * hidden_width,
        ),
        name="expert",
    )(x, w_in, w_down)


def expert_pair(x, w_in, w_down):
    rows, model = x.shape
    hidden_width = w_down.shape[0]
    parts = 2
    depth = model // parts
    tiles = 4
    tile = model // tiles

    def kernel(x_hbm, in_hbm_ref, down_hbm, o_hbm, x_ref, in_ref, down_ref, o_ref, sems):
        bring = []
        for k in range(parts):
            at = pl.ds(k * depth, depth)
            bring.append(
                [
                    pltpu.make_async_copy(x_hbm.at[:, at], x_ref.at[:, at], sems.at[2 * k]),
                    pltpu.make_async_copy(in_hbm_ref.at[at], in_ref.at[at], sems.at[2 * k + 1]),
                ]
            )
        bring.append([pltpu.make_async_copy(down_hbm, down_ref, sems.at[2 * parts])])
        for copies in bring:
            for copy in copies:
                copy.start()
        inner = None
        for k in range(parts):
            for copy in bring[k]:
                copy.wait()
            at = pl.ds(k * depth, depth)
            part = jnp.dot(x_ref[:, at], in_ref[at, :], preferred_element_type=F32)
            inner = part if inner is None else inner + part
        gate = inner[:, :hidden_width]
        hidden = (gate / (1.0 + jnp.exp(-gate)) * inner[:, hidden_width:]).astype(BF16)
        bring[parts][0].wait()
        back = []
        for k in range(tiles):
            at = pl.ds(k * tile, tile)
            product = jnp.dot(hidden, down_ref[:, at], preferred_element_type=F32)
            o_ref[:, at] = product.astype(BF16)
            back.append(
                pltpu.make_async_copy(o_ref.at[:, at], o_hbm.at[:, at], sems.at[2 * parts + 1])
            )
            back[k].start()
        for copy in back:
            copy.wait()

    return pl.pallas_call(
        kernel,
        out_shape=pltpu.HBM((rows, model), BF16),
        in_specs=[in_hbm()] * 3,
        out_specs=in_hbm(),
        scratch_shapes=[
            pltpu.VMEM((rows, model), BF16),
            pltpu.VMEM(w_in.shape, BF16),
            pltpu.VMEM(w_down.shape, BF16),
            pltpu.VMEM((rows, model), BF16),
            pltpu.SemaphoreType.DMA((2 * parts + 2,)),
        ],
        compiler_params=pltpu.CompilerParams(vmem_limit_bytes=HIGH_VMEM),
        cost_estimate=pl.CostEstimate(
            flops=6 * rows * model * hidden_width,
            bytes_accessed=2 * (2 * rows * model + 3 * model * hidden_width),
            transcendentals=rows * hidden_width,
        ),
        name="expert",
    )(x, w_in, w_down)


def combine_kernel(
    seqs, back_ref, stream_hbm, slots_ref, gates_ref, o_ref, stream_ref, sem
):
    bring = pltpu.make_async_copy(stream_hbm, stream_ref, sem.at[0])
    bring.start()
    slots = back_ref.shape[0]
    rows = stream_ref.shape[0]
    place = lax.broadcasted_iota(jnp.int32, (rows, slots), 1)
    gathered = None
    for k in range(slots_ref.shape[1]):
        pick = (place == slots_ref[:, k : k + 1]).astype(BF16)
        picked = jnp.dot(pick, back_ref[...], preferred_element_type=F32)
        part = picked * gates_ref[:, k : k + 1]
        gathered = part if gathered is None else gathered + part
    bring.wait()
    out = (stream_ref[...] + gathered).astype(BF16)
    local_rows = rows // seqs
    for seq in range(seqs):
        o_ref[seq] = out[seq * local_rows : (seq + 1) * local_rows]


def combine(back, stream, slots_of, gates, seqs):
    slots, model = back.shape
    rows = stream.shape[0]
    top = slots_of.shape[1]
    return pl.pallas_call(
        functools.partial(combine_kernel, seqs),
        out_shape=jax.ShapeDtypeStruct((seqs, rows // seqs, model), BF16),
        in_specs=[in_vmem(), in_hbm(), in_vmem(), in_vmem()],
        out_specs=in_vmem(),
        scratch_shapes=[pltpu.VMEM((rows, model), F32), pltpu.SemaphoreType.DMA((1,))],
        compiler_params=pltpu.CompilerParams(vmem_limit_bytes=HIGH_VMEM),
        cost_estimate=pl.CostEstimate(
            flops=2 * top * slots * rows * model,
            bytes_accessed=2 * slots * model + 6 * rows * model,
            transcendentals=0,
        ),
        name="combine",
    )(back, stream, slots_of, gates)


def flipped(value, axis, mask):
    pairs = [(source, source ^ mask) for source in range(lax.axis_size(axis))]
    return lax.ppermute(value, axis, pairs)


def parts_in_pairs(queries, new_kv, cache, w_out):
    n = lax.axis_size("head")
    local_rows, _, heads, width = queries.shape
    pair_heads = new_kv.shape[2]
    members = heads // pair_heads
    model = w_out.shape[2]
    share = w_out.shape[1]
    me = lax.axis_index("head")
    plane_bit = members // 2
    planes = n // plane_bit
    b = (me // plane_bit) % 2
    y = (me // 2) % 2
    group_sets = [[g * members + m for m in range(members)] for g in range(n // members)]

    query_slots = queries.reshape(local_rows, heads, width).transpose(1, 0, 2)
    query_slots = query_slots.reshape(members, heads // members, local_rows, width)

    def page_target(source, other):
        p, plane, rest = source // members, (source // plane_bit) % 2, source % plane_bit
        return (plane ^ other) * members + p * plane_bit + rest

    page_a, page_b = (
        lax.ppermute(cache[0], "head", [(d, page_target(d, other)) for d in range(n)])
        for other in range(2)
    )
    kv_heads = new_kv.reshape(local_rows, pair_heads, 2 * width).transpose(1, 0, 2)
    kv_same = lax.dynamic_index_in_dim(kv_heads, b, 0, keepdims=False)
    kv_other = lax.dynamic_index_in_dim(kv_heads, 1 - b, 0, keepdims=False)
    columns = model // 2
    w = lax.dynamic_slice_in_dim(w_out, lax.axis_index("grp") * columns, columns, 2)
    w = w.reshape(2, 2, heads // 4, share, columns)
    w_keep = lax.dynamic_index_in_dim(w, y, 1, keepdims=False)
    w_give = lax.dynamic_index_in_dim(w, 1 - y, 1, keepdims=False)
    w_got = flipped(w_give, "head", 2)
    kv_last, w_got = lax.optimization_barrier((kv_other, w_got))
    kv_own = [
        kv_same,
        flipped(kv_other, "head", plane_bit),
        flipped(kv_same, "head", 2 * plane_bit),
        flipped(kv_last, "head", 3 * plane_bit),
    ]

    page_a, page_b, kv_own, w_got, query_slots = lax.optimization_barrier(
        (page_a, page_b, kv_own, w_got, query_slots)
    )
    own_pages = jnp.concatenate([page_a, page_b], 0)
    kv_own = jnp.stack(kv_own, 0)
    pages_y = flipped(own_pages, "head", 2)
    kv_y = flipped(kv_own, "head", 2)
    q = lax.all_to_all(
        query_slots, "head", split_axis=0, concat_axis=0, tiled=True, axis_index_groups=group_sets
    )
    w_both = jnp.stack([w_keep, w_got], 1)
    w_same = lax.dynamic_index_in_dim(w_both, b, 0, keepdims=False)
    w_other = lax.dynamic_index_in_dim(w_both, 1 - b, 0, keepdims=False)
    w_near = jnp.stack([w_same, flipped(w_other, "head", plane_bit)], 0)
    w_near_x = flipped(w_near, "grp", 1)
    w_far = flipped(w_near, "head", members)
    pages_y, kv_y, own_pages, kv_own, w_near_x, q = lax.optimization_barrier(
        (pages_y, kv_y, own_pages, kv_own, w_near_x, q)
    )
    kv_c = flipped(kv_own, "head", 1)
    kv_cy = flipped(kv_y, "head", 1)
    pages_c = flipped(own_pages, "head", 1)
    pages_cy = flipped(pages_y, "head", 1)
    q, w_far = lax.optimization_barrier((q, w_far))
    w_far_x = flipped(w_far, "grp", 1)
    a = attend_pair(q, (own_pages, pages_y, pages_c, pages_cy), (kv_own, kv_y, kv_c, kv_cy))
    got = flipped(a[1], "head", 1)
    a, w_near_x, w_far_x = lax.optimization_barrier((a, w_near_x, w_far_x))
    w_near_c = flipped(w_near, "head", 1)
    w_far_c = flipped(w_far, "head", 1)
    w_near_cx = flipped(w_near_x, "head", 1)
    w_far_cx = flipped(w_far_x, "head", 1)
    partial = project_pair(
        a,
        got,
        (w_near, w_near_c, w_near_x, w_near_cx),
        (w_far, w_far_c, w_far_x, w_far_cx),
        members // 2,
    )
    parts = [partial[0]] + [flipped(partial[k], "head", 2 * k) for k in (3, 2, 1)]
    return [part[None] for part in parts]


def parts_in_planes(queries, new_kv, cache, w_out):
    n = lax.axis_size("head")
    local_rows, seqs, heads, width = queries.shape
    pair_heads = new_kv.shape[2]
    members = heads // pair_heads
    groups = n // members
    model = w_out.shape[2]
    side = 1 << ((n.bit_length() - 1) // 2)
    side = min(side, heads)
    planes = n // side
    planes_of_seq = heads // side
    pair_groups = [[g * members + m for m in range(members)] for g in range(groups)]
    cross_groups = [[g * members + m for g in range(groups)] for m in range(members)]
    plane_groups = [[p * side + m for m in range(side)] for p in range(planes)]
    column_groups = [[p * side + m for p in range(planes)] for m in range(side)]

    query_slots = queries.reshape(local_rows, n, width).transpose(1, 0, 2)
    q = lax.all_to_all(query_slots, "head", split_axis=0, concat_axis=0, tiled=True)
    q = q.reshape(n * local_rows, width)

    kv_slots = new_kv.reshape(local_rows, groups, 2 * width).transpose(1, 0, 2)
    kv = lax.all_to_all(
        kv_slots, "head", split_axis=0, concat_axis=0, tiled=True, axis_index_groups=cross_groups
    )
    kv = lax.all_gather(kv, "head", axis=0, axis_index_groups=pair_groups)
    pages = lax.all_gather(cache, "head", axis=0, tiled=True, axis_index_groups=pair_groups)

    share = w_out.shape[1]
    w_planes = w_out.reshape(planes_of_seq, side, share, model)
    if planes > planes_of_seq:
        w_planes = jnp.tile(w_planes, (planes // planes_of_seq, 1, 1, 1))
    w = lax.all_to_all(
        w_planes, "head", split_axis=0, concat_axis=0, tiled=True, axis_index_groups=column_groups
    )
    w = lax.all_gather(w, "head", axis=0, axis_index_groups=plane_groups)
    if share % 16:
        w = w.transpose(2, 1, 0, 3, 4).reshape(1, 1, side, width, model)
        w = w.reshape(side, width, model)

    attended = attend(q, pages.reshape(-1, 2 * width), kv)
    a = attended.reshape(planes, side, local_rows, width).transpose(1, 0, 2, 3)
    a = a.reshape(side, planes * local_rows, width)
    a = lax.all_to_all(
        a, "head", split_axis=0, concat_axis=0, tiled=True, axis_index_groups=plane_groups
    )
    if share % 16:
        partial = jnp.einsum("hri,hid->rd", a, w, preferred_element_type=F32).astype(BF16)
    else:
        partial = project(a, w)
    parts = lax.all_to_all(
        partial.reshape(planes, local_rows, model),
        "head",
        split_axis=0,
        concat_axis=0,
        tiled=True,
        axis_index_groups=column_groups,
    )
    parts = parts.reshape(seqs, planes_of_seq, local_rows, model)
    return [parts[:, k] for k in range(planes_of_seq)]


def local(queries, new_kv, cache, resid, w_out, norm_gain, expert_ids, expert_gates, w_in, w_down):
    n = lax.axis_size("head")
    local_rows, seqs, heads, width = queries.shape
    model = resid.shape[2]
    rows = local_rows * seqs
    members = heads // new_kv.shape[2]
    in_pairs = (
        lax.axis_size("grp") == 2
        and seqs == 1
        and new_kv.shape[2] == 2
        and n == heads == 2 * members
        and members == 8
        and cache.shape[0] == 1
        and w_in.shape[0] == 1
        and w_out.shape[1] % 16 == 0
    )
    plan = parts_in_pairs if in_pairs else parts_in_planes
    parts = plan(queries, new_kv, cache, w_out)

    top = expert_ids.shape[2]
    experts = w_in.shape[0] * n
    capacity = max(2, 2 * rows * top // experts)
    ids = expert_ids.transpose(1, 0, 2).reshape(rows, top)
    gates = expert_gates.transpose(1, 0, 2).reshape(rows, top)
    onehot = (ids[:, :, None] == jnp.arange(experts, dtype=jnp.int32)).astype(jnp.int32)
    named = onehot.sum(1)
    before = jnp.cumsum(named, 0) - named
    slots_of = ids * capacity + jnp.sum(onehot * before[:, None, :], 2)
    slots = experts * capacity

    stream, outgoing = route(
        parts, resid.transpose(1, 0, 2), norm_gain[None, :], slots_of.T, slots
    )
    arrived = lax.all_to_all(
        outgoing.reshape(n, slots // n, model), "head", split_axis=0, concat_axis=0, tiled=True
    )
    local_experts = w_in.shape[0]
    if local_experts == 1:
        answered = expert_pair(arrived.reshape(slots, model), w_in[0], w_down[0])
        answered = answered.reshape(n, slots // n, model)
    else:
        arrived = arrived.reshape(n, local_experts, capacity, model).transpose(1, 0, 2, 3)
        arrived = arrived.reshape(local_experts, n * capacity, model)
        answered = jnp.stack([expert(arrived[e], w_in[e], w_down[e]) for e in range(local_experts)])
        answered = answered.reshape(local_experts, n, capacity, model).transpose(1, 0, 2, 3)
        answered = answered.reshape(n, slots // n, model)
    back = lax.all_to_all(answered, "head", split_axis=0, concat_axis=0, tiled=True)
    out = combine(back.reshape(slots, model), stream, slots_of, gates, seqs)
    return out.transpose(1, 0, 2)


def solution(mesh):
    return jax.shard_map(
        local,
        mesh=mesh,
        in_specs=(
            P("head", "grp", None, None),
            P("head", "grp", None, None),
            P(("grp", "head"), None, None),
            P("head", "grp", None),
            P(None, "head", None),
            P(),
            P("head", "grp", None),
            P("head", "grp", None),
            P("head", None, None),
            P("head", None, None),
        ),
        out_specs=P("head", "grp", None),
        check_vma=False,
    )
```

```python
import functools

import jax
import jax.numpy as jnp
from jax import lax
from jax.experimental import pallas as pl
from jax.experimental.pallas import tpu as pltpu
from jax.sharding import PartitionSpec as P

eps_norm = 1e-06
F32 = jnp.float32
BF16 = jnp.bfloat16
HIGH_VMEM = 48 * 2**20
LOG2_E = 1.4426950408889634


def in_hbm():
    return pl.BlockSpec(memory_space=pltpu.HBM)


def in_vmem():
    return pl.BlockSpec(memory_space=pltpu.VMEM)


def attend_kernel(
    block, chunk, width, q_hbm, cache_hbm, kv_hbm, o_ref, q_ref, cache_ref, kv_ref, s0, s1, sems
):
    members, groups, piece, _ = kv_hbm.shape
    length = members * groups * piece
    old = cache_hbm.shape[0]
    scale = width**-0.5
    in_q = pltpu.make_async_copy(q_hbm, q_ref, sems.at[0])
    in_cache = pltpu.make_async_copy(cache_hbm, cache_ref, sems.at[1])
    in_q.start()
    in_cache.start()
    in_kv = []
    for group in range(groups):
        for member in range(members):
            place = (group * members + member) * piece
            copy = pltpu.make_async_copy(
                kv_hbm.at[member, group], kv_ref.at[pl.ds(place, piece)], sems.at[2]
            )
            copy.start()
            in_kv.append(copy)
    in_q.wait()
    in_cache.wait()
    for copy in in_kv:
        copy.wait()
    scores = [s0, s1]

    def pieces(b):
        out = [(True, k, chunk, k) for k in range(0, old, chunk)]
        last = b * block
        for k in range(0, last, chunk):
            out.append((False, k, min(chunk, last - k), old + k))
        out.append((False, last, block, old + last))
        return out

    def make_scores(b, part, running):
        of_cache, first, count, column = part
        keys = (cache_ref if of_cache else kv_ref)[pl.ds(first, count), :width]
        s = lax.dot_general(
            q_ref[pl.ds(b * block, block), :],
            keys,
            (((1,), (1,)), ((), ())),
            preferred_element_type=F32,
        )
        if not of_cache and first == b * block:
            row = lax.broadcasted_iota(jnp.int32, s.shape, 0)
            col = lax.broadcasted_iota(jnp.int32, s.shape, 1)
            s = jnp.where(col <= row, s, -jnp.inf)
        scores[b % 2][:, pl.ds(column, count)] = s
        for k in range(0, count, 128):
            piece_max = s[:, k : k + 128]
            running = piece_max if running is None else jnp.maximum(running, piece_max)
        return running

    def use_scores(b, part, top, total, acc):
        of_cache, first, count, column = part
        values = (cache_ref if of_cache else kv_ref)[pl.ds(first, count), width:]
        e = jnp.exp((scores[b % 2][:, pl.ds(column, count)] - top) * scale)
        for k in range(0, count, 128):
            total = e[:, k : k + 128] if total is None else total + e[:, k : k + 128]
        product = jnp.dot(e.astype(BF16), values, preferred_element_type=F32)
        return total, product if acc is None else acc + product

    blocks = length // block
    running = None
    for part in pieces(0):
        running = make_scores(0, part, running)
    for b in range(blocks):
        top = jnp.max(running, 1, keepdims=True)
        now, later = pieces(b), pieces(b + 1) if b + 1 < blocks else []
        running, total, acc = None, None, None
        for k in range(max(len(now), len(later))):
            if k < len(now):
                total, acc = use_scores(b, now[k], top, total, acc)
            if k < len(later):
                running = make_scores(b + 1, later[k], running)
        o_ref[pl.ds(b * block, block), :] = (acc / jnp.sum(total, 1, keepdims=True)).astype(BF16)


def attend(q, cache, kv):
    length, width = q.shape
    old = cache.shape[0]
    block = min(256, length)
    chunk = min(512, old)
    return pl.pallas_call(
        functools.partial(attend_kernel, block, chunk, width),
        out_shape=jax.ShapeDtypeStruct((length, width), BF16),
        in_specs=[in_hbm()] * 3,
        out_specs=in_vmem(),
        scratch_shapes=[
            pltpu.VMEM((length, width), BF16),
            pltpu.VMEM((old, 2 * width), BF16),
            pltpu.VMEM((length, 2 * width), BF16),
            pltpu.VMEM((block, old + length), F32),
            pltpu.VMEM((block, old + length), F32),
            pltpu.SemaphoreType.DMA((3,)),
        ],
        compiler_params=pltpu.CompilerParams(vmem_limit_bytes=HIGH_VMEM),
        cost_estimate=pl.CostEstimate(
            flops=4 * length * (old + length // 2) * width,
            bytes_accessed=4 * (2 * length + 2 * old) * width,
            transcendentals=length * (old + length // 2),
        ),
        name="attend",
    )(q, cache, kv)


def attend_pair_kernel(
    block,
    chunk,
    width,
    q_hbm,
    page_own,
    page_y,
    page_c,
    page_cy,
    kv_own,
    kv_y,
    kv_c,
    kv_cy,
    o_ref,
    q_ref,
    old_ref,
    kv_ref,
    s0,
    s1,
    sems,
):
    me = lax.axis_index("head")
    members, heads, piece, _ = q_hbm.shape
    length = members * piece
    planes = kv_own.shape[0]
    old = old_ref.shape[0]
    earlier_group = me // members > 0
    core = lax.rem(me, 2)
    chip = jnp.bitwise_and(me // 2, members // 2 - 1)
    copies = [[] for _ in range(6)]

    def bring(source, target, sem):
        copy = pltpu.make_async_copy(source, target, sems.at[sem])
        copy.start()
        copies[sem].append(copy)

    for member in range(members):
        for head in range(heads):
            bring(q_hbm.at[member, head], q_ref.at[head, pl.ds(member * piece, piece)], 0)
    place, places = 0, []
    for sem, page in enumerate((page_own, page_y, page_c, page_cy)):
        count = page.shape[0]
        bring(page, old_ref.at[pl.ds(place, count)], 1 + sem)
        places.append(place)
        place += count
    for flip, pieces_of in ((0, kv_own), (2, kv_y), (1, kv_c), (3, kv_cy)):
        for t in range(planes):
            number = jnp.bitwise_and(
                jnp.bitwise_xor(me, flip ^ (t * (members // 2))), members - 1
            )
            start = pl.multiple_of(number * piece, piece)
            area = 0 if t * (members // 2) >= members else length
            bring(pieces_of.at[t], kv_ref.at[pl.ds(area + start, piece)], 5)
    def arrive(sem):
        for copy in copies[sem]:
            copy.wait()
        copies[sem] = []

    arrive(0)
    scale = width**-0.5 * LOG2_E
    scores = [s0, s1]
    blocks = length // block
    units = [(head, b) for head in range(heads) for b in range(blocks)]

    def pieces(unit):
        _, b = units[unit]
        out = [("old", k, chunk, k) for k in range(0, old, chunk)]
        out += [("past", k, chunk, old + k) for k in range(0, length, chunk)]
        last = b * block
        for k in range(0, last, chunk):
            out.append(("new", length + k, min(chunk, last - k), old + length + k))
        out.append(("edge", length + last, block, old + length + last))
        return out

    def make_scores(unit, part, running):
        kind, first, count, column = part
        head, b = units[unit]
        keys = (old_ref if kind == "old" else kv_ref)[pl.ds(first, count), :width]
        s = lax.dot_general(
            q_ref[head, pl.ds(b * block, block), :],
            keys,
            (((1,), (1,)), ((), ())),
            preferred_element_type=F32,
        )
        if kind == "past":
            s = jnp.where(earlier_group, s, -jnp.inf)
        if kind == "edge":
            row = lax.broadcasted_iota(jnp.int32, s.shape, 0)
            col = lax.broadcasted_iota(jnp.int32, s.shape, 1)
            s = jnp.where(col <= row, s, -jnp.inf)
        scores[unit % 2][:, pl.ds(column, count)] = s
        for k in range(0, count, 128):
            piece_max = s[:, k : k + 128]
            running = piece_max if running is None else jnp.maximum(running, piece_max)
        return running

    def use_scores(unit, part, top, total, acc):
        kind, first, count, column = part
        values = (old_ref if kind == "old" else kv_ref)[pl.ds(first, count), width:]
        e = jnp.exp2((scores[unit % 2][:, pl.ds(column, count)] - top) * scale)
        for k in range(0, count, 128):
            total = e[:, k : k + 128] if total is None else total + e[:, k : k + 128]
        product = jnp.dot(e.astype(BF16), values, preferred_element_type=F32)
        return total, product if acc is None else acc + product

    running = None
    for part in pieces(0):
        if part[0] != "old":
            arrive(5)
        else:
            for sem, start in enumerate(places):
                if start < part[1] + part[2]:
                    arrive(1 + sem)
        running = make_scores(0, part, running)
    for unit, (head, b) in enumerate(units):
        top = jnp.max(running, 1, keepdims=True)
        now = pieces(unit)
        later = pieces(unit + 1) if unit + 1 < len(units) else []
        running, total, acc = None, None, None
        for k in range(max(len(now), len(later))):
            if k < len(now):
                total, acc = use_scores(unit, now[k], top, total, acc)
            if k < len(later):
                running = make_scores(unit + 1, later[k], running)
        done = (acc / jnp.sum(total, 1, keepdims=True)).astype(BF16)
        for k in range(0, block, piece):
            member = (b * block + k) // piece
            side = jnp.bitwise_xor(core, member % 2)
            start = pl.multiple_of(jnp.bitwise_xor(chip, member // 2) * piece, piece)
            o_ref[side, pl.ds(start, piece), pl.ds(head * width, width)] = done[k : k + piece]


def attend_pair(q, pages, kvs):
    members, heads, piece, width = q.shape
    length = members * piece
    old = sum(page.shape[0] for page in pages)
    block = 2 * piece
    chunk = min(512, old, length)
    keys = old + 2 * length
    return pl.pallas_call(
        functools.partial(attend_pair_kernel, block, chunk, width),
        out_shape=jax.ShapeDtypeStruct((2, length // 2, heads * width), BF16),
        in_specs=[in_hbm()] * (1 + len(pages) + len(kvs)),
        out_specs=in_vmem(),
        scratch_shapes=[
            pltpu.VMEM((heads, length, width), BF16),
            pltpu.VMEM((old, 2 * width), BF16),
            pltpu.VMEM((2 * length, 2 * width), BF16),
            pltpu.VMEM((block, keys), F32),
            pltpu.VMEM((block, keys), F32),
            pltpu.SemaphoreType.DMA((6,)),
        ],
        compiler_params=pltpu.CompilerParams(vmem_limit_bytes=HIGH_VMEM),
        cost_estimate=pl.CostEstimate(
            flops=4 * heads * length * (keys - length // 2) * width,
            bytes_accessed=4 * (heads * length + keys) * width,
            transcendentals=heads * length * (keys - length // 2),
        ),
        name="attend",
    )(q, *pages, *kvs)


def project_pair_kernel(a_hbm, got_hbm, *refs):
    near, far, outs, (w_ref, all_ref, out_ref, sems) = refs[:4], refs[4:8], refs[8:-4], refs[-4:]
    me = lax.axis_index("head")
    half = lax.axis_index("grp")
    core = lax.rem(me, 2)
    steps, sides, heads, share, columns = near[0].shape
    width = w_ref.shape[1]
    side = got_hbm.shape[1]
    bring = [[], [], []]
    for other, source in enumerate((a_hbm.at[0], got_hbm)):
        at = pl.ds(pl.multiple_of(jnp.bitwise_xor(core, other) * side, side), side)
        bring[2].append(pltpu.make_async_copy(source, all_ref.at[:, at], sems.at[2]))
    for x in range(2):
        column = pl.multiple_of(jnp.bitwise_xor(half, x) * columns, columns)
        for first, given in ((0, near), (steps, far)):
            for flip in range(2):
                for t in range(steps):
                    for u in range(sides):
                        number = jnp.bitwise_xor(me, flip ^ (2 * u) ^ (4 * (first + t)))
                        row = pl.multiple_of(number * share, share)
                        bring[x].append(
                            pltpu.make_async_copy(
                                given[2 * x + flip].at[t, u],
                                w_ref.at[:, pl.ds(row, share), pl.ds(column, columns)],
                                sems.at[x],
                            )
                        )
    for copies in (bring[2], bring[0], bring[1]):
        for copy in copies:
            copy.start()
    for copy in bring[2]:
        copy.wait()
    rows = outs[0].shape[0]
    tile = min(512, columns)
    back = []
    for x in range(2):
        for copy in bring[x]:
            copy.wait()
        for first in range(0, columns, tile):
            column = jnp.bitwise_xor(half, x) * columns + first
            at = pl.ds(pl.multiple_of(column, tile), tile)
            w = w_ref[:, :, at].reshape(heads * width, tile)
            out_ref[:, at] = jnp.dot(all_ref[...], w, preferred_element_type=F32).astype(BF16)
            for k, out in enumerate(outs):
                copy = pltpu.make_async_copy(
                    out_ref.at[pl.ds(k * rows, rows), at], out.at[:, at], sems.at[3]
                )
                copy.start()
                back.append(copy)
    for copy in back:
        copy.wait()


def project_pair(a, got, near, far, parts):
    _, _, heads, share, columns = near[0].shape
    rows = got.shape[0]
    width = 2 * got.shape[1] // heads
    model = 2 * columns
    return pl.pallas_call(
        project_pair_kernel,
        out_shape=[jax.ShapeDtypeStruct((rows // parts, model), BF16)]
        + [pltpu.HBM((rows // parts, model), BF16)] * (parts - 1),
        in_specs=[in_hbm()] * 10,
        out_specs=[in_hbm()] * parts,
        scratch_shapes=[
            pltpu.VMEM((heads, width, model), BF16),
            pltpu.VMEM((rows, heads * width), BF16),
            pltpu.VMEM((rows, model), BF16),
            pltpu.SemaphoreType.DMA((4,)),
        ],
        compiler_params=pltpu.CompilerParams(vmem_limit_bytes=HIGH_VMEM),
        cost_estimate=pl.CostEstimate(
            flops=2 * heads * rows * width * model,
            bytes_accessed=2 * (heads * width * model + heads * rows * width + rows * model),
            transcendentals=0,
        ),
        name="project",
    )(a, got, *near, *far)


def project_kernel(a_ref, w_ref, o_ref):
    members = a_ref.shape[0]
    planes, share = w_ref.shape[1], w_ref.shape[3]
    acc = None
    for head in range(members):
        w = jnp.concatenate(
            [w_ref[m, p, head] for p in range(planes) for m in range(members)], 0
        )
        part = jnp.dot(a_ref[head], w, preferred_element_type=F32)
        acc = part if acc is None else acc + part
    o_ref[...] = acc.astype(BF16)


def project(a, w):
    members, rows, width = a.shape
    planes, share, model = w.shape[1], w.shape[3], w.shape[4]
    tile = min(512, model)
    return pl.pallas_call(
        project_kernel,
        grid=(model // tile,),
        out_shape=jax.ShapeDtypeStruct((rows, model), BF16),
        in_specs=[
            pl.BlockSpec((members, rows, width), lambda t: (0, 0, 0)),
            pl.BlockSpec((members, planes, members, share, tile), lambda t: (0, 0, 0, 0, t)),
        ],
        out_specs=pl.BlockSpec((rows, tile), lambda t: (0, t)),
        compiler_params=pltpu.CompilerParams(vmem_limit_bytes=HIGH_VMEM),
        cost_estimate=pl.CostEstimate(
            flops=2 * members * rows * width * model,
            bytes_accessed=2 * (members * width * model + members * rows * width + rows * model),
            transcendentals=0,
        ),
        name="project",
    )(a, w)


def route_kernel(resid_ref, gain_ref, slots_ref, *refs):
    parts_refs, (stream_hbm, out_ref, stream_ref, sem) = refs[:-4], refs[-4:]
    seqs = resid_ref.shape[0]
    streams = []
    for seq in range(seqs):
        stream = resid_ref[seq].astype(F32)
        projected = parts_refs[0][seq].astype(F32)
        for part in parts_refs[1:]:
            projected = projected + part[seq].astype(F32)
        streams.append(stream + projected)
    stream = jnp.concatenate(streams, 0) if seqs > 1 else streams[0]
    stream_ref[...] = stream
    back = pltpu.make_async_copy(stream_ref, stream_hbm, sem.at[0])
    back.start()
    normed = stream * lax.rsqrt(jnp.mean(stream * stream, 1, keepdims=True) + eps_norm)
    normed = (normed * gain_ref[...]).astype(BF16)
    slots, rows = out_ref.shape[0], stream.shape[0]
    place = lax.broadcasted_iota(jnp.int32, (slots, rows), 0)
    hit = place == slots_ref[0:1, :]
    for k in range(1, slots_ref.shape[0]):
        hit = hit | (place == slots_ref[k : k + 1, :])
    out_ref[...] = jnp.dot(hit.astype(BF16), normed, preferred_element_type=F32).astype(BF16)
    back.wait()


def route(parts, resid, gain, slots_of, slots):
    seqs, local_rows, model = resid.shape
    rows = seqs * local_rows
    return pl.pallas_call(
        route_kernel,
        out_shape=(
            pltpu.HBM((rows, model), F32),
            jax.ShapeDtypeStruct((slots, model), BF16),
        ),
        in_specs=[in_vmem()] * (3 + len(parts)),
        out_specs=(in_hbm(), in_vmem()),
        scratch_shapes=[pltpu.VMEM((rows, model), F32), pltpu.SemaphoreType.DMA((1,))],
        compiler_params=pltpu.CompilerParams(vmem_limit_bytes=HIGH_VMEM),
        cost_estimate=pl.CostEstimate(
            flops=2 * slots * rows * model,
            bytes_accessed=2 * (len(parts) + 3 + slots // rows) * rows * model,
            transcendentals=0,
        ),
        name="route",
    )(resid, gain, slots_of, *parts)


def expert_kernel(x_ref, w_in_ref, w_down_ref, o_ref):
    hidden_width = w_down_ref.shape[0]
    inner = jnp.dot(x_ref[...], w_in_ref[...], preferred_element_type=F32)
    gate = inner[:, :hidden_width]
    hidden = (gate / (1.0 + jnp.exp(-gate)) * inner[:, hidden_width:]).astype(BF16)
    o_ref[...] = jnp.dot(hidden, w_down_ref[...], preferred_element_type=F32).astype(BF16)


def expert(x, w_in, w_down):
    rows, model = x.shape
    hidden_width = w_down.shape[0]
    return pl.pallas_call(
        expert_kernel,
        out_shape=jax.ShapeDtypeStruct((rows, model), BF16),
        in_specs=[in_vmem()] * 3,
        out_specs=in_vmem(),
        compiler_params=pltpu.CompilerParams(vmem_limit_bytes=HIGH_VMEM),
        cost_estimate=pl.CostEstimate(
            flops=6 * rows * model * hidden_width,
            bytes_accessed=2 * (2 * rows * model + 3 * model * hidden_width),
            transcendentals=rows * hidden_width,
        ),
        name="expert",
    )(x, w_in, w_down)


def expert_pair(x, w_in, w_down):
    rows, model = x.shape
    hidden_width = w_down.shape[0]
    parts = 4
    depth = model // parts

    def kernel(x_hbm, in_hbm_ref, down_hbm, o_hbm, x_ref, in_ref, down_ref, o_ref, sems):
        bring_x = pltpu.make_async_copy(x_hbm, x_ref, sems.at[parts])
        bring_x.start()
        bring_in = []
        for k in range(parts):
            at = pl.ds(k * depth, depth)
            bring_in.append(pltpu.make_async_copy(in_hbm_ref.at[at], in_ref.at[at], sems.at[k]))
            bring_in[k].start()
        bring_down = pltpu.make_async_copy(down_hbm, down_ref, sems.at[parts + 1])
        bring_down.start()
        bring_x.wait()
        inner = None
        for k in range(parts):
            bring_in[k].wait()
            at = pl.ds(k * depth, depth)
            part = jnp.dot(x_ref[:, at], in_ref[at, :], preferred_element_type=F32)
            inner = part if inner is None else inner + part
        gate = inner[:, :hidden_width]
        hidden = (gate / (1.0 + jnp.exp(-gate)) * inner[:, hidden_width:]).astype(BF16)
        bring_down.wait()
        o_ref[...] = jnp.dot(hidden, down_ref[...], preferred_element_type=F32).astype(BF16)
        back = pltpu.make_async_copy(o_ref, o_hbm, sems.at[parts + 2])
        back.start()
        back.wait()

    return pl.pallas_call(
        kernel,
        out_shape=pltpu.HBM((rows, model), BF16),
        in_specs=[in_hbm()] * 3,
        out_specs=in_hbm(),
        scratch_shapes=[
            pltpu.VMEM((rows, model), BF16),
            pltpu.VMEM(w_in.shape, BF16),
            pltpu.VMEM(w_down.shape, BF16),
            pltpu.VMEM((rows, model), BF16),
            pltpu.SemaphoreType.DMA((parts + 3,)),
        ],
        compiler_params=pltpu.CompilerParams(vmem_limit_bytes=HIGH_VMEM),
        cost_estimate=pl.CostEstimate(
            flops=6 * rows * model * hidden_width,
            bytes_accessed=2 * (2 * rows * model + 3 * model * hidden_width),
            transcendentals=rows * hidden_width,
        ),
        name="expert",
    )(x, w_in, w_down)


def combine_kernel(
    seqs, back_ref, stream_hbm, slots_ref, gates_ref, o_ref, stream_ref, sem
):
    bring = pltpu.make_async_copy(stream_hbm, stream_ref, sem.at[0])
    bring.start()
    slots = back_ref.shape[0]
    rows = stream_ref.shape[0]
    place = lax.broadcasted_iota(jnp.int32, (rows, slots), 1)
    gathered = None
    for k in range(slots_ref.shape[1]):
        pick = (place == slots_ref[:, k : k + 1]).astype(BF16)
        picked = jnp.dot(pick, back_ref[...], preferred_element_type=F32)
        part = picked * gates_ref[:, k : k + 1]
        gathered = part if gathered is None else gathered + part
    bring.wait()
    out = (stream_ref[...] + gathered).astype(BF16)
    local_rows = rows // seqs
    for seq in range(seqs):
        o_ref[seq] = out[seq * local_rows : (seq + 1) * local_rows]


def combine(back, stream, slots_of, gates, seqs):
    slots, model = back.shape
    rows = stream.shape[0]
    top = slots_of.shape[1]
    return pl.pallas_call(
        functools.partial(combine_kernel, seqs),
        out_shape=jax.ShapeDtypeStruct((seqs, rows // seqs, model), BF16),
        in_specs=[in_vmem(), in_hbm(), in_vmem(), in_vmem()],
        out_specs=in_vmem(),
        scratch_shapes=[pltpu.VMEM((rows, model), F32), pltpu.SemaphoreType.DMA((1,))],
        compiler_params=pltpu.CompilerParams(vmem_limit_bytes=HIGH_VMEM),
        cost_estimate=pl.CostEstimate(
            flops=2 * top * slots * rows * model,
            bytes_accessed=2 * slots * model + 6 * rows * model,
            transcendentals=0,
        ),
        name="combine",
    )(back, stream, slots_of, gates)


def flipped(value, axis, mask):
    pairs = [(source, source ^ mask) for source in range(lax.axis_size(axis))]
    return lax.ppermute(value, axis, pairs)


def parts_in_pairs(queries, new_kv, cache, w_out):
    n = lax.axis_size("head")
    local_rows, _, heads, width = queries.shape
    pair_heads = new_kv.shape[2]
    members = heads // pair_heads
    model = w_out.shape[2]
    share = w_out.shape[1]
    me = lax.axis_index("head")
    plane_bit = members // 2
    planes = n // plane_bit
    b = (me // plane_bit) % 2
    y = (me // 2) % 2
    group_sets = [[g * members + m for m in range(members)] for g in range(n // members)]

    query_slots = queries.reshape(local_rows, heads, width).transpose(1, 0, 2)
    query_slots = query_slots.reshape(members, heads // members, local_rows, width)

    def page_target(source, other):
        p, plane, rest = source // members, (source // plane_bit) % 2, source % plane_bit
        return (plane ^ other) * members + p * plane_bit + rest

    page_a, page_b = (
        lax.ppermute(cache[0], "head", [(d, page_target(d, other)) for d in range(n)])
        for other in range(2)
    )
    kv_heads = new_kv.reshape(local_rows, pair_heads, 2 * width).transpose(1, 0, 2)
    kv_same = lax.dynamic_index_in_dim(kv_heads, b, 0, keepdims=False)
    kv_other = lax.dynamic_index_in_dim(kv_heads, 1 - b, 0, keepdims=False)
    columns = model // 2
    w = lax.dynamic_slice_in_dim(w_out, lax.axis_index("grp") * columns, columns, 2)
    w = w.reshape(2, 2, heads // 4, share, columns)
    w_keep = lax.dynamic_index_in_dim(w, y, 1, keepdims=False)
    w_give = lax.dynamic_index_in_dim(w, 1 - y, 1, keepdims=False)
    w_got = flipped(w_give, "head", 2)
    kv_last, query_slots, w_got = lax.optimization_barrier((kv_other, query_slots, w_got))
    kv_own = [
        kv_same,
        flipped(kv_other, "head", plane_bit),
        flipped(kv_same, "head", 2 * plane_bit),
        flipped(kv_last, "head", 3 * plane_bit),
    ]
    q = lax.all_to_all(
        query_slots, "head", split_axis=0, concat_axis=0, tiled=True, axis_index_groups=group_sets
    )
    w_both = jnp.stack([w_keep, w_got], 1)
    w_same = lax.dynamic_index_in_dim(w_both, b, 0, keepdims=False)
    w_other = lax.dynamic_index_in_dim(w_both, 1 - b, 0, keepdims=False)
    w_first = flipped(w_other, "head", plane_bit)

    page_a, page_b, kv_own, w_first, q = lax.optimization_barrier(
        (page_a, page_b, kv_own, w_first, q)
    )
    own_pages = jnp.concatenate([page_a, page_b], 0)
    kv_own = jnp.stack(kv_own, 0)
    pages_y = flipped(own_pages, "head", 2)
    kv_y = flipped(kv_own, "head", 2)
    w_near = jnp.stack([w_same, w_first], 0)
    w_near_x = flipped(w_near, "grp", 1)
    w_far = flipped(w_near, "head", members)
    pages_y, kv_y, own_pages, kv_own, w_near_x = lax.optimization_barrier(
        (pages_y, kv_y, own_pages, kv_own, w_near_x)
    )
    kv_c = flipped(kv_own, "head", 1)
    kv_cy = flipped(kv_y, "head", 1)
    pages_c = flipped(own_pages, "head", 1)
    pages_cy = flipped(pages_y, "head", 1)
    q, w_far = lax.optimization_barrier((q, w_far))
    w_far_x = flipped(w_far, "grp", 1)
    a = attend_pair(q, (own_pages, pages_y, pages_c, pages_cy), (kv_own, kv_y, kv_c, kv_cy))
    got = flipped(a[1], "head", 1)
    a, w_near_x, w_far_x = lax.optimization_barrier((a, w_near_x, w_far_x))
    w_near_c = flipped(w_near, "head", 1)
    w_far_c = flipped(w_far, "head", 1)
    w_near_cx = flipped(w_near_x, "head", 1)
    w_far_cx = flipped(w_far_x, "head", 1)
    partial = project_pair(
        a,
        got,
        (w_near, w_near_c, w_near_x, w_near_cx),
        (w_far, w_far_c, w_far_x, w_far_cx),
        members // 2,
    )
    parts = [partial[0]] + [flipped(partial[k], "head", 2 * k) for k in (3, 2, 1)]
    return [part[None] for part in parts]


def parts_in_planes(queries, new_kv, cache, w_out):
    n = lax.axis_size("head")
    local_rows, seqs, heads, width = queries.shape
    pair_heads = new_kv.shape[2]
    members = heads // pair_heads
    groups = n // members
    model = w_out.shape[2]
    side = 1 << ((n.bit_length() - 1) // 2)
    side = min(side, heads)
    planes = n // side
    planes_of_seq = heads // side
    pair_groups = [[g * members + m for m in range(members)] for g in range(groups)]
    cross_groups = [[g * members + m for g in range(groups)] for m in range(members)]
    plane_groups = [[p * side + m for m in range(side)] for p in range(planes)]
    column_groups = [[p * side + m for p in range(planes)] for m in range(side)]

    query_slots = queries.reshape(local_rows, n, width).transpose(1, 0, 2)
    q = lax.all_to_all(query_slots, "head", split_axis=0, concat_axis=0, tiled=True)
    q = q.reshape(n * local_rows, width)

    kv_slots = new_kv.reshape(local_rows, groups, 2 * width).transpose(1, 0, 2)
    kv = lax.all_to_all(
        kv_slots, "head", split_axis=0, concat_axis=0, tiled=True, axis_index_groups=cross_groups
    )
    kv = lax.all_gather(kv, "head", axis=0, axis_index_groups=pair_groups)
    pages = lax.all_gather(cache, "head", axis=0, tiled=True, axis_index_groups=pair_groups)

    share = w_out.shape[1]
    w_planes = w_out.reshape(planes_of_seq, side, share, model)
    if planes > planes_of_seq:
        w_planes = jnp.tile(w_planes, (planes // planes_of_seq, 1, 1, 1))
    w = lax.all_to_all(
        w_planes, "head", split_axis=0, concat_axis=0, tiled=True, axis_index_groups=column_groups
    )
    w = lax.all_gather(w, "head", axis=0, axis_index_groups=plane_groups)
    if share % 16:
        w = w.transpose(2, 1, 0, 3, 4).reshape(1, 1, side, width, model)
        w = w.reshape(side, width, model)

    attended = attend(q, pages.reshape(-1, 2 * width), kv)
    a = attended.reshape(planes, side, local_rows, width).transpose(1, 0, 2, 3)
    a = a.reshape(side, planes * local_rows, width)
    a = lax.all_to_all(
        a, "head", split_axis=0, concat_axis=0, tiled=True, axis_index_groups=plane_groups
    )
    if share % 16:
        partial = jnp.einsum("hri,hid->rd", a, w, preferred_element_type=F32).astype(BF16)
    else:
        partial = project(a, w)
    parts = lax.all_to_all(
        partial.reshape(planes, local_rows, model),
        "head",
        split_axis=0,
        concat_axis=0,
        tiled=True,
        axis_index_groups=column_groups,
    )
    parts = parts.reshape(seqs, planes_of_seq, local_rows, model)
    return [parts[:, k] for k in range(planes_of_seq)]


def local(queries, new_kv, cache, resid, w_out, norm_gain, expert_ids, expert_gates, w_in, w_down):
    n = lax.axis_size("head")
    local_rows, seqs, heads, width = queries.shape
    model = resid.shape[2]
    rows = local_rows * seqs
    members = heads // new_kv.shape[2]
    in_pairs = (
        lax.axis_size("grp") == 2
        and seqs == 1
        and new_kv.shape[2] == 2
        and n == heads == 2 * members
        and members == 8
        and cache.shape[0] == 1
        and w_in.shape[0] == 1
        and w_out.shape[1] % 16 == 0
    )
    plan = parts_in_pairs if in_pairs else parts_in_planes
    parts = plan(queries, new_kv, cache, w_out)

    top = expert_ids.shape[2]
    experts = w_in.shape[0] * n
    capacity = max(2, 2 * rows * top // experts)
    ids = expert_ids.transpose(1, 0, 2).reshape(rows, top)
    gates = expert_gates.transpose(1, 0, 2).reshape(rows, top)
    onehot = (ids[:, :, None] == jnp.arange(experts, dtype=jnp.int32)).astype(jnp.int32)
    named = onehot.sum(1)
    before = jnp.cumsum(named, 0) - named
    slots_of = ids * capacity + jnp.sum(onehot * before[:, None, :], 2)
    slots = experts * capacity

    stream, outgoing = route(
        parts, resid.transpose(1, 0, 2), norm_gain[None, :], slots_of.T, slots
    )
    arrived = lax.all_to_all(
        outgoing.reshape(n, slots // n, model), "head", split_axis=0, concat_axis=0, tiled=True
    )
    local_experts = w_in.shape[0]
    if local_experts == 1:
        answered = expert_pair(arrived.reshape(slots, model), w_in[0], w_down[0])
        answered = answered.reshape(n, slots // n, model)
    else:
        arrived = arrived.reshape(n, local_experts, capacity, model).transpose(1, 0, 2, 3)
        arrived = arrived.reshape(local_experts, n * capacity, model)
        answered = jnp.stack([expert(arrived[e], w_in[e], w_down[e]) for e in range(local_experts)])
        answered = answered.reshape(local_experts, n, capacity, model).transpose(1, 0, 2, 3)
        answered = answered.reshape(n, slots // n, model)
    back = lax.all_to_all(answered, "head", split_axis=0, concat_axis=0, tiled=True)
    out = combine(back.reshape(slots, model), stream, slots_of, gates, seqs)
    return out.transpose(1, 0, 2)


def solution(mesh):
    return jax.shard_map(
        local,
        mesh=mesh,
        in_specs=(
            P("head", "grp", None, None),
            P("head", "grp", None, None),
            P(("grp", "head"), None, None),
            P("head", "grp", None),
            P(None, "head", None),
            P(),
            P("head", "grp", None),
            P("head", "grp", None),
            P("head", None, None),
            P("head", None, None),
        ),
        out_specs=P("head", "grp", None),
        check_vma=False,
    )
```

```python
import functools

import jax
import jax.numpy as jnp
from jax import lax
from jax.experimental import pallas as pl
from jax.experimental.pallas import tpu as pltpu
from jax.sharding import PartitionSpec as P

eps_norm = 1e-06
F32 = jnp.float32
BF16 = jnp.bfloat16
HIGH_VMEM = 48 * 2**20
LOG2_E = 1.4426950408889634


def in_hbm():
    return pl.BlockSpec(memory_space=pltpu.HBM)


def in_vmem():
    return pl.BlockSpec(memory_space=pltpu.VMEM)


def attend_kernel(
    block, chunk, width, q_hbm, cache_hbm, kv_hbm, o_ref, q_ref, cache_ref, kv_ref, s0, s1, sems
):
    members, groups, piece, _ = kv_hbm.shape
    length = members * groups * piece
    old = cache_hbm.shape[0]
    scale = width**-0.5
    in_q = pltpu.make_async_copy(q_hbm, q_ref, sems.at[0])
    in_cache = pltpu.make_async_copy(cache_hbm, cache_ref, sems.at[1])
    in_q.start()
    in_cache.start()
    in_kv = []
    for group in range(groups):
        for member in range(members):
            place = (group * members + member) * piece
            copy = pltpu.make_async_copy(
                kv_hbm.at[member, group], kv_ref.at[pl.ds(place, piece)], sems.at[2]
            )
            copy.start()
            in_kv.append(copy)
    in_q.wait()
    in_cache.wait()
    for copy in in_kv:
        copy.wait()
    scores = [s0, s1]

    def pieces(b):
        out = [(True, k, chunk, k) for k in range(0, old, chunk)]
        last = b * block
        for k in range(0, last, chunk):
            out.append((False, k, min(chunk, last - k), old + k))
        out.append((False, last, block, old + last))
        return out

    def make_scores(b, part, running):
        of_cache, first, count, column = part
        keys = (cache_ref if of_cache else kv_ref)[pl.ds(first, count), :width]
        s = lax.dot_general(
            q_ref[pl.ds(b * block, block), :],
            keys,
            (((1,), (1,)), ((), ())),
            preferred_element_type=F32,
        )
        if not of_cache and first == b * block:
            row = lax.broadcasted_iota(jnp.int32, s.shape, 0)
            col = lax.broadcasted_iota(jnp.int32, s.shape, 1)
            s = jnp.where(col <= row, s, -jnp.inf)
        scores[b % 2][:, pl.ds(column, count)] = s
        for k in range(0, count, 128):
            piece_max = s[:, k : k + 128]
            running = piece_max if running is None else jnp.maximum(running, piece_max)
        return running

    def use_scores(b, part, top, total, acc):
        of_cache, first, count, column = part
        values = (cache_ref if of_cache else kv_ref)[pl.ds(first, count), width:]
        e = jnp.exp((scores[b % 2][:, pl.ds(column, count)] - top) * scale)
        for k in range(0, count, 128):
            total = e[:, k : k + 128] if total is None else total + e[:, k : k + 128]
        product = jnp.dot(e.astype(BF16), values, preferred_element_type=F32)
        return total, product if acc is None else acc + product

    blocks = length // block
    running = None
    for part in pieces(0):
        running = make_scores(0, part, running)
    for b in range(blocks):
        top = jnp.max(running, 1, keepdims=True)
        now, later = pieces(b), pieces(b + 1) if b + 1 < blocks else []
        running, total, acc = None, None, None
        for k in range(max(len(now), len(later))):
            if k < len(now):
                total, acc = use_scores(b, now[k], top, total, acc)
            if k < len(later):
                running = make_scores(b + 1, later[k], running)
        o_ref[pl.ds(b * block, block), :] = (acc / jnp.sum(total, 1, keepdims=True)).astype(BF16)


def attend(q, cache, kv):
    length, width = q.shape
    old = cache.shape[0]
    block = min(256, length)
    chunk = min(512, old)
    return pl.pallas_call(
        functools.partial(attend_kernel, block, chunk, width),
        out_shape=jax.ShapeDtypeStruct((length, width), BF16),
        in_specs=[in_hbm()] * 3,
        out_specs=in_vmem(),
        scratch_shapes=[
            pltpu.VMEM((length, width), BF16),
            pltpu.VMEM((old, 2 * width), BF16),
            pltpu.VMEM((length, 2 * width), BF16),
            pltpu.VMEM((block, old + length), F32),
            pltpu.VMEM((block, old + length), F32),
            pltpu.SemaphoreType.DMA((3,)),
        ],
        compiler_params=pltpu.CompilerParams(vmem_limit_bytes=HIGH_VMEM),
        cost_estimate=pl.CostEstimate(
            flops=4 * length * (old + length // 2) * width,
            bytes_accessed=4 * (2 * length + 2 * old) * width,
            transcendentals=length * (old + length // 2),
        ),
        name="attend",
    )(q, cache, kv)


def attend_pair_kernel(
    block,
    chunk,
    width,
    q_hbm,
    page_own,
    page_y,
    page_c,
    page_cy,
    kv_own,
    kv_y,
    kv_c,
    kv_cy,
    o_ref,
    q_ref,
    old_ref,
    kv_ref,
    s0,
    s1,
    sems,
):
    me = lax.axis_index("head")
    members, heads, piece, _ = q_hbm.shape
    length = members * piece
    planes = kv_own.shape[0]
    old = old_ref.shape[0]
    earlier_group = me // members > 0
    core = lax.rem(me, 2)
    chip = jnp.bitwise_and(me // 2, members // 2 - 1)
    copies = [[] for _ in range(6)]

    def bring(source, target, sem):
        copy = pltpu.make_async_copy(source, target, sems.at[sem])
        copy.start()
        copies[sem].append(copy)

    for member in range(members):
        for head in range(heads):
            bring(q_hbm.at[member, head], q_ref.at[head, pl.ds(member * piece, piece)], 0)
    place, places = 0, []
    for sem, page in enumerate((page_own, page_y, page_c, page_cy)):
        count = page.shape[0]
        bring(page, old_ref.at[pl.ds(place, count)], 1 + sem)
        places.append(place)
        place += count
    for flip, pieces_of in ((0, kv_own), (2, kv_y), (1, kv_c), (3, kv_cy)):
        for t in range(planes):
            number = jnp.bitwise_and(
                jnp.bitwise_xor(me, flip ^ (t * (members // 2))), members - 1
            )
            start = pl.multiple_of(number * piece, piece)
            area = 0 if t * (members // 2) >= members else length
            bring(pieces_of.at[t], kv_ref.at[pl.ds(area + start, piece)], 5)
    def arrive(sem):
        for copy in copies[sem]:
            copy.wait()
        copies[sem] = []

    arrive(0)
    scale = width**-0.5 * LOG2_E
    scores = [s0, s1]
    blocks = length // block
    units = [(head, b) for head in range(heads) for b in range(blocks)]

    def pieces(unit):
        _, b = units[unit]
        out = [("old", k, chunk, k) for k in range(0, old, chunk)]
        out += [("past", k, chunk, old + k) for k in range(0, length, chunk)]
        last = b * block
        for k in range(0, last, chunk):
            out.append(("new", length + k, min(chunk, last - k), old + length + k))
        out.append(("edge", length + last, block, old + length + last))
        return out

    def make_scores(unit, part, running):
        kind, first, count, column = part
        head, b = units[unit]
        keys = (old_ref if kind == "old" else kv_ref)[pl.ds(first, count), :width]
        s = lax.dot_general(
            q_ref[head, pl.ds(b * block, block), :],
            keys,
            (((1,), (1,)), ((), ())),
            preferred_element_type=F32,
        )
        if kind == "past":
            s = jnp.where(earlier_group, s, -jnp.inf)
        if kind == "edge":
            row = lax.broadcasted_iota(jnp.int32, s.shape, 0)
            col = lax.broadcasted_iota(jnp.int32, s.shape, 1)
            s = jnp.where(col <= row, s, -jnp.inf)
        scores[unit % 2][:, pl.ds(column, count)] = s
        for k in range(0, count, 128):
            piece_max = s[:, k : k + 128]
            running = piece_max if running is None else jnp.maximum(running, piece_max)
        return running

    def use_scores(unit, part, top, total, acc):
        kind, first, count, column = part
        values = (old_ref if kind == "old" else kv_ref)[pl.ds(first, count), width:]
        e = jnp.exp2((scores[unit % 2][:, pl.ds(column, count)] - top) * scale)
        for k in range(0, count, 128):
            total = e[:, k : k + 128] if total is None else total + e[:, k : k + 128]
        product = jnp.dot(e.astype(BF16), values, preferred_element_type=F32)
        return total, product if acc is None else acc + product

    running = None
    for part in pieces(0):
        if part[0] != "old":
            arrive(5)
        else:
            for sem, start in enumerate(places):
                if start < part[1] + part[2]:
                    arrive(1 + sem)
        running = make_scores(0, part, running)
    for unit, (head, b) in enumerate(units):
        top = jnp.max(running, 1, keepdims=True)
        now = pieces(unit)
        later = pieces(unit + 1) if unit + 1 < len(units) else []
        running, total, acc = None, None, None
        for k in range(max(len(now), len(later))):
            if k < len(now):
                total, acc = use_scores(unit, now[k], top, total, acc)
            if k < len(later):
                running = make_scores(unit + 1, later[k], running)
        done = (acc / jnp.sum(total, 1, keepdims=True)).astype(BF16)
        for k in range(0, block, piece):
            member = (b * block + k) // piece
            side = jnp.bitwise_xor(core, member % 2)
            start = pl.multiple_of(jnp.bitwise_xor(chip, member // 2) * piece, piece)
            o_ref[side, pl.ds(start, piece), pl.ds(head * width, width)] = done[k : k + piece]


def attend_pair(q, pages, kvs):
    members, heads, piece, width = q.shape
    length = members * piece
    old = sum(page.shape[0] for page in pages)
    block = 2 * piece
    chunk = min(512, old, length)
    keys = old + 2 * length
    return pl.pallas_call(
        functools.partial(attend_pair_kernel, block, chunk, width),
        out_shape=jax.ShapeDtypeStruct((2, length // 2, heads * width), BF16),
        in_specs=[in_hbm()] * (1 + len(pages) + len(kvs)),
        out_specs=in_vmem(),
        scratch_shapes=[
            pltpu.VMEM((heads, length, width), BF16),
            pltpu.VMEM((old, 2 * width), BF16),
            pltpu.VMEM((2 * length, 2 * width), BF16),
            pltpu.VMEM((block, keys), F32),
            pltpu.VMEM((block, keys), F32),
            pltpu.SemaphoreType.DMA((6,)),
        ],
        compiler_params=pltpu.CompilerParams(vmem_limit_bytes=HIGH_VMEM),
        cost_estimate=pl.CostEstimate(
            flops=4 * heads * length * (keys - length // 2) * width,
            bytes_accessed=4 * (heads * length + keys) * width,
            transcendentals=heads * length * (keys - length // 2),
        ),
        name="attend",
    )(q, *pages, *kvs)


def project_pair_kernel(a_hbm, got_hbm, *refs):
    near, far, outs, (w_ref, all_ref, out_ref, sems) = refs[:4], refs[4:8], refs[8:-4], refs[-4:]
    me = lax.axis_index("head")
    half = lax.axis_index("grp")
    core = lax.rem(me, 2)
    steps, sides, heads, share, columns = near[0].shape
    width = w_ref.shape[1]
    side = got_hbm.shape[1]
    bring = [[], [], []]
    for other, source in enumerate((a_hbm.at[0], got_hbm)):
        at = pl.ds(pl.multiple_of(jnp.bitwise_xor(core, other) * side, side), side)
        bring[2].append(pltpu.make_async_copy(source, all_ref.at[:, at], sems.at[2]))
    for x in range(2):
        column = pl.multiple_of(jnp.bitwise_xor(half, x) * columns, columns)
        for first, given in ((0, near), (steps, far)):
            for flip in range(2):
                for t in range(steps):
                    for u in range(sides):
                        number = jnp.bitwise_xor(me, flip ^ (2 * u) ^ (4 * (first + t)))
                        row = pl.multiple_of(number * share, share)
                        bring[x].append(
                            pltpu.make_async_copy(
                                given[2 * x + flip].at[t, u],
                                w_ref.at[:, pl.ds(row, share), pl.ds(column, columns)],
                                sems.at[x],
                            )
                        )
    for copies in (bring[2], bring[0], bring[1]):
        for copy in copies:
            copy.start()
    for copy in bring[2]:
        copy.wait()
    rows = outs[0].shape[0]
    tile = min(512, columns)
    back = []
    for x in range(2):
        for copy in bring[x]:
            copy.wait()
        for first in range(0, columns, tile):
            column = jnp.bitwise_xor(half, x) * columns + first
            at = pl.ds(pl.multiple_of(column, tile), tile)
            w = w_ref[:, :, at].reshape(heads * width, tile)
            out_ref[:, at] = jnp.dot(all_ref[...], w, preferred_element_type=F32).astype(BF16)
            for k, out in enumerate(outs):
                copy = pltpu.make_async_copy(
                    out_ref.at[pl.ds(k * rows, rows), at], out.at[:, at], sems.at[3]
                )
                copy.start()
                back.append(copy)
    for copy in back:
        copy.wait()


def project_pair(a, got, near, far, parts):
    _, _, heads, share, columns = near[0].shape
    rows = got.shape[0]
    width = 2 * got.shape[1] // heads
    model = 2 * columns
    return pl.pallas_call(
        project_pair_kernel,
        out_shape=[jax.ShapeDtypeStruct((rows // parts, model), BF16)]
        + [pltpu.HBM((rows // parts, model), BF16)] * (parts - 1),
        in_specs=[in_hbm()] * 10,
        out_specs=[in_hbm()] * parts,
        scratch_shapes=[
            pltpu.VMEM((heads, width, model), BF16),
            pltpu.VMEM((rows, heads * width), BF16),
            pltpu.VMEM((rows, model), BF16),
            pltpu.SemaphoreType.DMA((4,)),
        ],
        compiler_params=pltpu.CompilerParams(vmem_limit_bytes=HIGH_VMEM),
        cost_estimate=pl.CostEstimate(
            flops=2 * heads * rows * width * model,
            bytes_accessed=2 * (heads * width * model + heads * rows * width + rows * model),
            transcendentals=0,
        ),
        name="project",
    )(a, got, *near, *far)


def project_kernel(a_ref, w_ref, o_ref):
    members = a_ref.shape[0]
    planes, share = w_ref.shape[1], w_ref.shape[3]
    acc = None
    for head in range(members):
        w = jnp.concatenate(
            [w_ref[m, p, head] for p in range(planes) for m in range(members)], 0
        )
        part = jnp.dot(a_ref[head], w, preferred_element_type=F32)
        acc = part if acc is None else acc + part
    o_ref[...] = acc.astype(BF16)


def project(a, w):
    members, rows, width = a.shape
    planes, share, model = w.shape[1], w.shape[3], w.shape[4]
    tile = min(512, model)
    return pl.pallas_call(
        project_kernel,
        grid=(model // tile,),
        out_shape=jax.ShapeDtypeStruct((rows, model), BF16),
        in_specs=[
            pl.BlockSpec((members, rows, width), lambda t: (0, 0, 0)),
            pl.BlockSpec((members, planes, members, share, tile), lambda t: (0, 0, 0, 0, t)),
        ],
        out_specs=pl.BlockSpec((rows, tile), lambda t: (0, t)),
        compiler_params=pltpu.CompilerParams(vmem_limit_bytes=HIGH_VMEM),
        cost_estimate=pl.CostEstimate(
            flops=2 * members * rows * width * model,
            bytes_accessed=2 * (members * width * model + members * rows * width + rows * model),
            transcendentals=0,
        ),
        name="project",
    )(a, w)


def route_kernel(resid_ref, gain_ref, slots_ref, *refs):
    parts_refs, (stream_hbm, out_ref, stream_ref, sem) = refs[:-4], refs[-4:]
    seqs = resid_ref.shape[0]
    streams = []
    for seq in range(seqs):
        stream = resid_ref[seq].astype(F32)
        projected = parts_refs[0][seq].astype(F32)
        for part in parts_refs[1:]:
            projected = projected + part[seq].astype(F32)
        streams.append(stream + projected)
    stream = jnp.concatenate(streams, 0) if seqs > 1 else streams[0]
    stream_ref[...] = stream
    back = pltpu.make_async_copy(stream_ref, stream_hbm, sem.at[0])
    back.start()
    normed = stream * lax.rsqrt(jnp.mean(stream * stream, 1, keepdims=True) + eps_norm)
    normed = (normed * gain_ref[...]).astype(BF16)
    slots, rows = out_ref.shape[0], stream.shape[0]
    place = lax.broadcasted_iota(jnp.int32, (slots, rows), 0)
    hit = place == slots_ref[0:1, :]
    for k in range(1, slots_ref.shape[0]):
        hit = hit | (place == slots_ref[k : k + 1, :])
    out_ref[...] = jnp.dot(hit.astype(BF16), normed, preferred_element_type=F32).astype(BF16)
    back.wait()


def route(parts, resid, gain, slots_of, slots):
    seqs, local_rows, model = resid.shape
    rows = seqs * local_rows
    return pl.pallas_call(
        route_kernel,
        out_shape=(
            pltpu.HBM((rows, model), F32),
            jax.ShapeDtypeStruct((slots, model), BF16),
        ),
        in_specs=[in_vmem()] * (3 + len(parts)),
        out_specs=(in_hbm(), in_vmem()),
        scratch_shapes=[pltpu.VMEM((rows, model), F32), pltpu.SemaphoreType.DMA((1,))],
        compiler_params=pltpu.CompilerParams(vmem_limit_bytes=HIGH_VMEM),
        cost_estimate=pl.CostEstimate(
            flops=2 * slots * rows * model,
            bytes_accessed=2 * (len(parts) + 3 + slots // rows) * rows * model,
            transcendentals=0,
        ),
        name="route",
    )(resid, gain, slots_of, *parts)


def expert_kernel(x_ref, w_in_ref, w_down_ref, o_ref):
    hidden_width = w_down_ref.shape[0]
    inner = jnp.dot(x_ref[...], w_in_ref[...], preferred_element_type=F32)
    gate = inner[:, :hidden_width]
    hidden = (gate / (1.0 + jnp.exp(-gate)) * inner[:, hidden_width:]).astype(BF16)
    o_ref[...] = jnp.dot(hidden, w_down_ref[...], preferred_element_type=F32).astype(BF16)


def expert(x, w_in, w_down):
    rows, model = x.shape
    hidden_width = w_down.shape[0]
    return pl.pallas_call(
        expert_kernel,
        out_shape=jax.ShapeDtypeStruct((rows, model), BF16),
        in_specs=[in_vmem()] * 3,
        out_specs=in_vmem(),
        compiler_params=pltpu.CompilerParams(vmem_limit_bytes=HIGH_VMEM),
        cost_estimate=pl.CostEstimate(
            flops=6 * rows * model * hidden_width,
            bytes_accessed=2 * (2 * rows * model + 3 * model * hidden_width),
            transcendentals=rows * hidden_width,
        ),
        name="expert",
    )(x, w_in, w_down)


def expert_pair(x, w_in, w_down):
    rows, model = x.shape
    hidden_width = w_down.shape[0]
    parts = 4
    depth = model // parts

    def kernel(x_hbm, in_hbm_ref, down_hbm, o_hbm, x_ref, in_ref, down_ref, o_ref, sems):
        bring_x = pltpu.make_async_copy(x_hbm, x_ref, sems.at[parts])
        bring_x.start()
        bring_in = []
        for k in range(parts):
            at = pl.ds(k * depth, depth)
            bring_in.append(pltpu.make_async_copy(in_hbm_ref.at[at], in_ref.at[at], sems.at[k]))
            bring_in[k].start()
        bring_down = pltpu.make_async_copy(down_hbm, down_ref, sems.at[parts + 1])
        bring_down.start()
        bring_x.wait()
        inner = None
        for k in range(parts):
            bring_in[k].wait()
            at = pl.ds(k * depth, depth)
            part = jnp.dot(x_ref[:, at], in_ref[at, :], preferred_element_type=F32)
            inner = part if inner is None else inner + part
        gate = inner[:, :hidden_width]
        hidden = (gate / (1.0 + jnp.exp(-gate)) * inner[:, hidden_width:]).astype(BF16)
        bring_down.wait()
        o_ref[...] = jnp.dot(hidden, down_ref[...], preferred_element_type=F32).astype(BF16)
        back = pltpu.make_async_copy(o_ref, o_hbm, sems.at[parts + 2])
        back.start()
        back.wait()

    return pl.pallas_call(
        kernel,
        out_shape=pltpu.HBM((rows, model), BF16),
        in_specs=[in_hbm()] * 3,
        out_specs=in_hbm(),
        scratch_shapes=[
            pltpu.VMEM((rows, model), BF16),
            pltpu.VMEM(w_in.shape, BF16),
            pltpu.VMEM(w_down.shape, BF16),
            pltpu.VMEM((rows, model), BF16),
            pltpu.SemaphoreType.DMA((parts + 3,)),
        ],
        compiler_params=pltpu.CompilerParams(vmem_limit_bytes=HIGH_VMEM),
        cost_estimate=pl.CostEstimate(
            flops=6 * rows * model * hidden_width,
            bytes_accessed=2 * (2 * rows * model + 3 * model * hidden_width),
            transcendentals=rows * hidden_width,
        ),
        name="expert",
    )(x, w_in, w_down)


def combine_kernel(
    seqs, back_ref, stream_hbm, slots_ref, gates_ref, o_ref, stream_ref, sem
):
    bring = pltpu.make_async_copy(stream_hbm, stream_ref, sem.at[0])
    bring.start()
    slots = back_ref.shape[0]
    rows = stream_ref.shape[0]
    place = lax.broadcasted_iota(jnp.int32, (rows, slots), 1)
    gathered = None
    for k in range(slots_ref.shape[1]):
        pick = (place == slots_ref[:, k : k + 1]).astype(BF16)
        picked = jnp.dot(pick, back_ref[...], preferred_element_type=F32)
        part = picked * gates_ref[:, k : k + 1]
        gathered = part if gathered is None else gathered + part
    bring.wait()
    out = (stream_ref[...] + gathered).astype(BF16)
    local_rows = rows // seqs
    for seq in range(seqs):
        o_ref[seq] = out[seq * local_rows : (seq + 1) * local_rows]


def combine(back, stream, slots_of, gates, seqs):
    slots, model = back.shape
    rows = stream.shape[0]
    top = slots_of.shape[1]
    return pl.pallas_call(
        functools.partial(combine_kernel, seqs),
        out_shape=jax.ShapeDtypeStruct((seqs, rows // seqs, model), BF16),
        in_specs=[in_vmem(), in_hbm(), in_vmem(), in_vmem()],
        out_specs=in_vmem(),
        scratch_shapes=[pltpu.VMEM((rows, model), F32), pltpu.SemaphoreType.DMA((1,))],
        compiler_params=pltpu.CompilerParams(vmem_limit_bytes=HIGH_VMEM),
        cost_estimate=pl.CostEstimate(
            flops=2 * top * slots * rows * model,
            bytes_accessed=2 * slots * model + 6 * rows * model,
            transcendentals=0,
        ),
        name="combine",
    )(back, stream, slots_of, gates)


def flipped(value, axis, mask):
    pairs = [(source, source ^ mask) for source in range(lax.axis_size(axis))]
    return lax.ppermute(value, axis, pairs)


def parts_in_pairs(queries, new_kv, cache, w_out):
    n = lax.axis_size("head")
    local_rows, _, heads, width = queries.shape
    pair_heads = new_kv.shape[2]
    members = heads // pair_heads
    model = w_out.shape[2]
    share = w_out.shape[1]
    me = lax.axis_index("head")
    plane_bit = members // 2
    planes = n // plane_bit
    b = (me // plane_bit) % 2
    y = (me // 2) % 2
    group_sets = [[g * members + m for m in range(members)] for g in range(n // members)]

    query_slots = queries.reshape(local_rows, heads, width).transpose(1, 0, 2)
    query_slots = query_slots.reshape(members, heads // members, local_rows, width)

    def page_target(source, other):
        p, plane, rest = source // members, (source // plane_bit) % 2, source % plane_bit
        return (plane ^ other) * members + p * plane_bit + rest

    page_a, page_b = (
        lax.ppermute(cache[0], "head", [(d, page_target(d, other)) for d in range(n)])
        for other in range(2)
    )
    kv_heads = new_kv.reshape(local_rows, pair_heads, 2 * width).transpose(1, 0, 2)
    kv_same = lax.dynamic_index_in_dim(kv_heads, b, 0, keepdims=False)
    kv_other = lax.dynamic_index_in_dim(kv_heads, 1 - b, 0, keepdims=False)
    columns = model // 2
    w = lax.dynamic_slice_in_dim(w_out, lax.axis_index("grp") * columns, columns, 2)
    w = w.reshape(2, 2, heads // 4, share, columns)
    w_keep = lax.dynamic_index_in_dim(w, y, 1, keepdims=False)
    w_give = lax.dynamic_index_in_dim(w, 1 - y, 1, keepdims=False)
    w_got = flipped(w_give, "head", 2)
    kv_own = [kv_same]
    for t in range(1, planes):
        kv_own.append(flipped(kv_other if t % 2 else kv_same, "head", t * plane_bit))
    q = lax.all_to_all(
        query_slots, "head", split_axis=0, concat_axis=0, tiled=True, axis_index_groups=group_sets
    )
    w_both = jnp.stack([w_keep, w_got], 1)
    w_same = lax.dynamic_index_in_dim(w_both, b, 0, keepdims=False)
    w_other = lax.dynamic_index_in_dim(w_both, 1 - b, 0, keepdims=False)
    w_first = flipped(w_other, "head", plane_bit)

    own_pages = jnp.concatenate([page_a, page_b], 0)
    own_pages, kv_own, w_first, q = lax.optimization_barrier((own_pages, kv_own, w_first, q))
    kv_own = jnp.stack(kv_own, 0)
    pages_y = flipped(own_pages, "head", 2)
    kv_y = flipped(kv_own, "head", 2)
    w_near = jnp.stack([w_same, w_first], 0)
    w_near_x = flipped(w_near, "grp", 1)
    w_far = flipped(w_near, "head", members)
    pages_y, kv_y, own_pages, kv_own, w_near_x = lax.optimization_barrier(
        (pages_y, kv_y, own_pages, kv_own, w_near_x)
    )
    kv_c = flipped(kv_own, "head", 1)
    kv_cy = flipped(kv_y, "head", 1)
    pages_c = flipped(own_pages, "head", 1)
    pages_cy = flipped(pages_y, "head", 1)
    q, w_far = lax.optimization_barrier((q, w_far))
    w_far_x = flipped(w_far, "grp", 1)
    a = attend_pair(q, (own_pages, pages_y, pages_c, pages_cy), (kv_own, kv_y, kv_c, kv_cy))
    got = flipped(a[1], "head", 1)
    a, w_near_x, w_far_x = lax.optimization_barrier((a, w_near_x, w_far_x))
    w_near_c = flipped(w_near, "head", 1)
    w_far_c = flipped(w_far, "head", 1)
    w_near_cx = flipped(w_near_x, "head", 1)
    w_far_cx = flipped(w_far_x, "head", 1)
    partial = project_pair(
        a,
        got,
        (w_near, w_near_c, w_near_x, w_near_cx),
        (w_far, w_far_c, w_far_x, w_far_cx),
        members // 2,
    )
    parts = [partial[0]] + [flipped(partial[k], "head", 2 * k) for k in (3, 2, 1)]
    return [part[None] for part in parts]


def parts_in_planes(queries, new_kv, cache, w_out):
    n = lax.axis_size("head")
    local_rows, seqs, heads, width = queries.shape
    pair_heads = new_kv.shape[2]
    members = heads // pair_heads
    groups = n // members
    model = w_out.shape[2]
    side = 1 << ((n.bit_length() - 1) // 2)
    side = min(side, heads)
    planes = n // side
    planes_of_seq = heads // side
    pair_groups = [[g * members + m for m in range(members)] for g in range(groups)]
    cross_groups = [[g * members + m for g in range(groups)] for m in range(members)]
    plane_groups = [[p * side + m for m in range(side)] for p in range(planes)]
    column_groups = [[p * side + m for p in range(planes)] for m in range(side)]

    query_slots = queries.reshape(local_rows, n, width).transpose(1, 0, 2)
    q = lax.all_to_all(query_slots, "head", split_axis=0, concat_axis=0, tiled=True)
    q = q.reshape(n * local_rows, width)

    kv_slots = new_kv.reshape(local_rows, groups, 2 * width).transpose(1, 0, 2)
    kv = lax.all_to_all(
        kv_slots, "head", split_axis=0, concat_axis=0, tiled=True, axis_index_groups=cross_groups
    )
    kv = lax.all_gather(kv, "head", axis=0, axis_index_groups=pair_groups)
    pages = lax.all_gather(cache, "head", axis=0, tiled=True, axis_index_groups=pair_groups)

    share = w_out.shape[1]
    w_planes = w_out.reshape(planes_of_seq, side, share, model)
    if planes > planes_of_seq:
        w_planes = jnp.tile(w_planes, (planes // planes_of_seq, 1, 1, 1))
    w = lax.all_to_all(
        w_planes, "head", split_axis=0, concat_axis=0, tiled=True, axis_index_groups=column_groups
    )
    w = lax.all_gather(w, "head", axis=0, axis_index_groups=plane_groups)
    if share % 16:
        w = w.transpose(2, 1, 0, 3, 4).reshape(1, 1, side, width, model)
        w = w.reshape(side, width, model)

    attended = attend(q, pages.reshape(-1, 2 * width), kv)
    a = attended.reshape(planes, side, local_rows, width).transpose(1, 0, 2, 3)
    a = a.reshape(side, planes * local_rows, width)
    a = lax.all_to_all(
        a, "head", split_axis=0, concat_axis=0, tiled=True, axis_index_groups=plane_groups
    )
    if share % 16:
        partial = jnp.einsum("hri,hid->rd", a, w, preferred_element_type=F32).astype(BF16)
    else:
        partial = project(a, w)
    parts = lax.all_to_all(
        partial.reshape(planes, local_rows, model),
        "head",
        split_axis=0,
        concat_axis=0,
        tiled=True,
        axis_index_groups=column_groups,
    )
    parts = parts.reshape(seqs, planes_of_seq, local_rows, model)
    return [parts[:, k] for k in range(planes_of_seq)]


def local(queries, new_kv, cache, resid, w_out, norm_gain, expert_ids, expert_gates, w_in, w_down):
    n = lax.axis_size("head")
    local_rows, seqs, heads, width = queries.shape
    model = resid.shape[2]
    rows = local_rows * seqs
    members = heads // new_kv.shape[2]
    in_pairs = (
        lax.axis_size("grp") == 2
        and seqs == 1
        and new_kv.shape[2] == 2
        and n == heads == 2 * members
        and members == 8
        and cache.shape[0] == 1
        and w_in.shape[0] == 1
        and w_out.shape[1] % 16 == 0
    )
    plan = parts_in_pairs if in_pairs else parts_in_planes
    parts = plan(queries, new_kv, cache, w_out)

    top = expert_ids.shape[2]
    experts = w_in.shape[0] * n
    capacity = max(2, 2 * rows * top // experts)
    ids = expert_ids.transpose(1, 0, 2).reshape(rows, top)
    gates = expert_gates.transpose(1, 0, 2).reshape(rows, top)
    onehot = (ids[:, :, None] == jnp.arange(experts, dtype=jnp.int32)).astype(jnp.int32)
    named = onehot.sum(1)
    before = jnp.cumsum(named, 0) - named
    slots_of = ids * capacity + jnp.sum(onehot * before[:, None, :], 2)
    slots = experts * capacity

    stream, outgoing = route(
        parts, resid.transpose(1, 0, 2), norm_gain[None, :], slots_of.T, slots
    )
    arrived = lax.all_to_all(
        outgoing.reshape(n, slots // n, model), "head", split_axis=0, concat_axis=0, tiled=True
    )
    local_experts = w_in.shape[0]
    if local_experts == 1:
        answered = expert_pair(arrived.reshape(slots, model), w_in[0], w_down[0])
        answered = answered.reshape(n, slots // n, model)
    else:
        arrived = arrived.reshape(n, local_experts, capacity, model).transpose(1, 0, 2, 3)
        arrived = arrived.reshape(local_experts, n * capacity, model)
        answered = jnp.stack([expert(arrived[e], w_in[e], w_down[e]) for e in range(local_experts)])
        answered = answered.reshape(local_experts, n, capacity, model).transpose(1, 0, 2, 3)
        answered = answered.reshape(n, slots // n, model)
    back = lax.all_to_all(answered, "head", split_axis=0, concat_axis=0, tiled=True)
    out = combine(back.reshape(slots, model), stream, slots_of, gates, seqs)
    return out.transpose(1, 0, 2)


def solution(mesh):
    return jax.shard_map(
        local,
        mesh=mesh,
        in_specs=(
            P("head", "grp", None, None),
            P("head", "grp", None, None),
            P(("grp", "head"), None, None),
            P("head", "grp", None),
            P(None, "head", None),
            P(),
            P("head", "grp", None),
            P("head", "grp", None),
            P("head", None, None),
            P("head", None, None),
        ),
        out_specs=P("head", "grp", None),
        check_vma=False,
    )
```

```python
import functools

import jax
import jax.numpy as jnp
from jax import lax
from jax.experimental import pallas as pl
from jax.experimental.pallas import tpu as pltpu
from jax.sharding import PartitionSpec as P

eps_norm = 1e-06
F32 = jnp.float32
BF16 = jnp.bfloat16
HIGH_VMEM = 48 * 2**20
LOG2_E = 1.4426950408889634


def in_hbm():
    return pl.BlockSpec(memory_space=pltpu.HBM)


def in_vmem():
    return pl.BlockSpec(memory_space=pltpu.VMEM)


def attend_kernel(
    block, chunk, width, q_hbm, cache_hbm, kv_hbm, o_ref, q_ref, cache_ref, kv_ref, s0, s1, sems
):
    members, groups, piece, _ = kv_hbm.shape
    length = members * groups * piece
    old = cache_hbm.shape[0]
    scale = width**-0.5
    in_q = pltpu.make_async_copy(q_hbm, q_ref, sems.at[0])
    in_cache = pltpu.make_async_copy(cache_hbm, cache_ref, sems.at[1])
    in_q.start()
    in_cache.start()
    in_kv = []
    for group in range(groups):
        for member in range(members):
            place = (group * members + member) * piece
            copy = pltpu.make_async_copy(
                kv_hbm.at[member, group], kv_ref.at[pl.ds(place, piece)], sems.at[2]
            )
            copy.start()
            in_kv.append(copy)
    in_q.wait()
    in_cache.wait()
    for copy in in_kv:
        copy.wait()
    scores = [s0, s1]

    def pieces(b):
        out = [(True, k, chunk, k) for k in range(0, old, chunk)]
        last = b * block
        for k in range(0, last, chunk):
            out.append((False, k, min(chunk, last - k), old + k))
        out.append((False, last, block, old + last))
        return out

    def make_scores(b, part, running):
        of_cache, first, count, column = part
        keys = (cache_ref if of_cache else kv_ref)[pl.ds(first, count), :width]
        s = lax.dot_general(
            q_ref[pl.ds(b * block, block), :],
            keys,
            (((1,), (1,)), ((), ())),
            preferred_element_type=F32,
        )
        if not of_cache and first == b * block:
            row = lax.broadcasted_iota(jnp.int32, s.shape, 0)
            col = lax.broadcasted_iota(jnp.int32, s.shape, 1)
            s = jnp.where(col <= row, s, -jnp.inf)
        scores[b % 2][:, pl.ds(column, count)] = s
        for k in range(0, count, 128):
            piece_max = s[:, k : k + 128]
            running = piece_max if running is None else jnp.maximum(running, piece_max)
        return running

    def use_scores(b, part, top, total, acc):
        of_cache, first, count, column = part
        values = (cache_ref if of_cache else kv_ref)[pl.ds(first, count), width:]
        e = jnp.exp((scores[b % 2][:, pl.ds(column, count)] - top) * scale)
        for k in range(0, count, 128):
            total = e[:, k : k + 128] if total is None else total + e[:, k : k + 128]
        product = jnp.dot(e.astype(BF16), values, preferred_element_type=F32)
        return total, product if acc is None else acc + product

    blocks = length // block
    running = None
    for part in pieces(0):
        running = make_scores(0, part, running)
    for b in range(blocks):
        top = jnp.max(running, 1, keepdims=True)
        now, later = pieces(b), pieces(b + 1) if b + 1 < blocks else []
        running, total, acc = None, None, None
        for k in range(max(len(now), len(later))):
            if k < len(now):
                total, acc = use_scores(b, now[k], top, total, acc)
            if k < len(later):
                running = make_scores(b + 1, later[k], running)
        o_ref[pl.ds(b * block, block), :] = (acc / jnp.sum(total, 1, keepdims=True)).astype(BF16)


def attend(q, cache, kv):
    length, width = q.shape
    old = cache.shape[0]
    block = min(256, length)
    chunk = min(512, old)
    return pl.pallas_call(
        functools.partial(attend_kernel, block, chunk, width),
        out_shape=jax.ShapeDtypeStruct((length, width), BF16),
        in_specs=[in_hbm()] * 3,
        out_specs=in_vmem(),
        scratch_shapes=[
            pltpu.VMEM((length, width), BF16),
            pltpu.VMEM((old, 2 * width), BF16),
            pltpu.VMEM((length, 2 * width), BF16),
            pltpu.VMEM((block, old + length), F32),
            pltpu.VMEM((block, old + length), F32),
            pltpu.SemaphoreType.DMA((3,)),
        ],
        compiler_params=pltpu.CompilerParams(vmem_limit_bytes=HIGH_VMEM),
        cost_estimate=pl.CostEstimate(
            flops=4 * length * (old + length // 2) * width,
            bytes_accessed=4 * (2 * length + 2 * old) * width,
            transcendentals=length * (old + length // 2),
        ),
        name="attend",
    )(q, cache, kv)


def attend_pair_kernel(
    block,
    chunk,
    width,
    q_hbm,
    page_own,
    page_y,
    page_c,
    page_cy,
    kv_own,
    kv_y,
    kv_c,
    kv_cy,
    o_ref,
    q_ref,
    old_ref,
    kv_ref,
    s0,
    s1,
    sems,
):
    me = lax.axis_index("head")
    members, heads, piece, _ = q_hbm.shape
    length = members * piece
    planes = kv_own.shape[0]
    old = old_ref.shape[0]
    earlier_group = me // members > 0
    core = lax.rem(me, 2)
    chip = jnp.bitwise_and(me // 2, members // 2 - 1)
    copies = [[] for _ in range(6)]

    def bring(source, target, sem):
        copy = pltpu.make_async_copy(source, target, sems.at[sem])
        copy.start()
        copies[sem].append(copy)

    for member in range(members):
        for head in range(heads):
            bring(q_hbm.at[member, head], q_ref.at[head, pl.ds(member * piece, piece)], 0)
    place, places = 0, []
    for sem, page in enumerate((page_own, page_y, page_c, page_cy)):
        count = page.shape[0]
        bring(page, old_ref.at[pl.ds(place, count)], 1 + sem)
        places.append(place)
        place += count
    for flip, pieces_of in ((0, kv_own), (2, kv_y), (1, kv_c), (3, kv_cy)):
        for t in range(planes):
            number = jnp.bitwise_and(
                jnp.bitwise_xor(me, flip ^ (t * (members // 2))), members - 1
            )
            start = pl.multiple_of(number * piece, piece)
            area = 0 if t * (members // 2) >= members else length
            bring(pieces_of.at[t], kv_ref.at[pl.ds(area + start, piece)], 5)
    def arrive(sem):
        for copy in copies[sem]:
            copy.wait()
        copies[sem] = []

    arrive(0)
    scale = width**-0.5 * LOG2_E
    scores = [s0, s1]
    blocks = length // block
    units = [(head, b) for head in range(heads) for b in range(blocks)]

    def pieces(unit):
        _, b = units[unit]
        out = [("old", k, chunk, k) for k in range(0, old, chunk)]
        out += [("past", k, chunk, old + k) for k in range(0, length, chunk)]
        last = b * block
        for k in range(0, last, chunk):
            out.append(("new", length + k, min(chunk, last - k), old + length + k))
        out.append(("edge", length + last, block, old + length + last))
        return out

    def make_scores(unit, part, running):
        kind, first, count, column = part
        head, b = units[unit]
        keys = (old_ref if kind == "old" else kv_ref)[pl.ds(first, count), :width]
        s = lax.dot_general(
            q_ref[head, pl.ds(b * block, block), :],
            keys,
            (((1,), (1,)), ((), ())),
            preferred_element_type=F32,
        )
        if kind == "past":
            s = jnp.where(earlier_group, s, -jnp.inf)
        if kind == "edge":
            row = lax.broadcasted_iota(jnp.int32, s.shape, 0)
            col = lax.broadcasted_iota(jnp.int32, s.shape, 1)
            s = jnp.where(col <= row, s, -jnp.inf)
        scores[unit % 2][:, pl.ds(column, count)] = s
        for k in range(0, count, 128):
            piece_max = s[:, k : k + 128]
            running = piece_max if running is None else jnp.maximum(running, piece_max)
        return running

    def use_scores(unit, part, top, total, acc):
        kind, first, count, column = part
        values = (old_ref if kind == "old" else kv_ref)[pl.ds(first, count), width:]
        e = jnp.exp2((scores[unit % 2][:, pl.ds(column, count)] - top) * scale)
        for k in range(0, count, 128):
            total = e[:, k : k + 128] if total is None else total + e[:, k : k + 128]
        product = jnp.dot(e.astype(BF16), values, preferred_element_type=F32)
        return total, product if acc is None else acc + product

    running = None
    for part in pieces(0):
        if part[0] != "old":
            arrive(5)
        else:
            for sem, start in enumerate(places):
                if start < part[1] + part[2]:
                    arrive(1 + sem)
        running = make_scores(0, part, running)
    for unit, (head, b) in enumerate(units):
        top = jnp.max(running, 1, keepdims=True)
        now = pieces(unit)
        later = pieces(unit + 1) if unit + 1 < len(units) else []
        running, total, acc = None, None, None
        for k in range(max(len(now), len(later))):
            if k < len(now):
                total, acc = use_scores(unit, now[k], top, total, acc)
            if k < len(later):
                running = make_scores(unit + 1, later[k], running)
        done = (acc / jnp.sum(total, 1, keepdims=True)).astype(BF16)
        for k in range(0, block, piece):
            member = (b * block + k) // piece
            side = jnp.bitwise_xor(core, member % 2)
            start = pl.multiple_of(jnp.bitwise_xor(chip, member // 2) * piece, piece)
            o_ref[side, pl.ds(start, piece), pl.ds(head * width, width)] = done[k : k + piece]


def attend_pair(q, pages, kvs):
    members, heads, piece, width = q.shape
    length = members * piece
    old = sum(page.shape[0] for page in pages)
    block = 2 * piece
    chunk = min(512, old, length)
    keys = old + 2 * length
    return pl.pallas_call(
        functools.partial(attend_pair_kernel, block, chunk, width),
        out_shape=jax.ShapeDtypeStruct((2, length // 2, heads * width), BF16),
        in_specs=[in_hbm()] * (1 + len(pages) + len(kvs)),
        out_specs=in_vmem(),
        scratch_shapes=[
            pltpu.VMEM((heads, length, width), BF16),
            pltpu.VMEM((old, 2 * width), BF16),
            pltpu.VMEM((2 * length, 2 * width), BF16),
            pltpu.VMEM((block, keys), F32),
            pltpu.VMEM((block, keys), F32),
            pltpu.SemaphoreType.DMA((6,)),
        ],
        compiler_params=pltpu.CompilerParams(vmem_limit_bytes=HIGH_VMEM),
        cost_estimate=pl.CostEstimate(
            flops=4 * heads * length * (keys - length // 2) * width,
            bytes_accessed=4 * (heads * length + keys) * width,
            transcendentals=heads * length * (keys - length // 2),
        ),
        name="attend",
    )(q, *pages, *kvs)


def project_pair_kernel(a_hbm, got_hbm, *refs):
    near, far, outs, (w_ref, all_ref, out_ref, sems) = refs[:4], refs[4:8], refs[8:-4], refs[-4:]
    me = lax.axis_index("head")
    half = lax.axis_index("grp")
    core = lax.rem(me, 2)
    steps, sides, heads, share, columns = near[0].shape
    width = w_ref.shape[1]
    side = got_hbm.shape[1]
    bring = [[], [], []]
    for other, source in enumerate((a_hbm.at[0], got_hbm)):
        at = pl.ds(pl.multiple_of(jnp.bitwise_xor(core, other) * side, side), side)
        bring[2].append(pltpu.make_async_copy(source, all_ref.at[:, at], sems.at[2]))
    for x in range(2):
        column = pl.multiple_of(jnp.bitwise_xor(half, x) * columns, columns)
        for first, given in ((0, near), (steps, far)):
            for flip in range(2):
                for t in range(steps):
                    for u in range(sides):
                        number = jnp.bitwise_xor(me, flip ^ (2 * u) ^ (4 * (first + t)))
                        row = pl.multiple_of(number * share, share)
                        bring[x].append(
                            pltpu.make_async_copy(
                                given[2 * x + flip].at[t, u],
                                w_ref.at[:, pl.ds(row, share), pl.ds(column, columns)],
                                sems.at[x],
                            )
                        )
    for copies in (bring[2], bring[0], bring[1]):
        for copy in copies:
            copy.start()
    for copy in bring[2]:
        copy.wait()
    rows = outs[0].shape[0]
    tile = min(512, columns)
    back = []
    for x in range(2):
        for copy in bring[x]:
            copy.wait()
        for first in range(0, columns, tile):
            column = jnp.bitwise_xor(half, x) * columns + first
            at = pl.ds(pl.multiple_of(column, tile), tile)
            w = w_ref[:, :, at].reshape(heads * width, tile)
            out_ref[:, at] = jnp.dot(all_ref[...], w, preferred_element_type=F32).astype(BF16)
            for k, out in enumerate(outs):
                copy = pltpu.make_async_copy(
                    out_ref.at[pl.ds(k * rows, rows), at], out.at[:, at], sems.at[3]
                )
                copy.start()
                back.append(copy)
    for copy in back:
        copy.wait()


def project_pair(a, got, near, far, parts):
    _, _, heads, share, columns = near[0].shape
    rows = got.shape[0]
    width = 2 * got.shape[1] // heads
    model = 2 * columns
    return pl.pallas_call(
        project_pair_kernel,
        out_shape=[pltpu.HBM((rows // parts, model), BF16)] * parts,
        in_specs=[in_hbm()] * 10,
        out_specs=[in_hbm()] * parts,
        scratch_shapes=[
            pltpu.VMEM((heads, width, model), BF16),
            pltpu.VMEM((rows, heads * width), BF16),
            pltpu.VMEM((rows, model), BF16),
            pltpu.SemaphoreType.DMA((4,)),
        ],
        compiler_params=pltpu.CompilerParams(vmem_limit_bytes=HIGH_VMEM),
        cost_estimate=pl.CostEstimate(
            flops=2 * heads * rows * width * model,
            bytes_accessed=2 * (heads * width * model + heads * rows * width + rows * model),
            transcendentals=0,
        ),
        name="project",
    )(a, got, *near, *far)


def project_kernel(a_ref, w_ref, o_ref):
    members = a_ref.shape[0]
    planes, share = w_ref.shape[1], w_ref.shape[3]
    acc = None
    for head in range(members):
        w = jnp.concatenate(
            [w_ref[m, p, head] for p in range(planes) for m in range(members)], 0
        )
        part = jnp.dot(a_ref[head], w, preferred_element_type=F32)
        acc = part if acc is None else acc + part
    o_ref[...] = acc.astype(BF16)


def project(a, w):
    members, rows, width = a.shape
    planes, share, model = w.shape[1], w.shape[3], w.shape[4]
    tile = min(512, model)
    return pl.pallas_call(
        project_kernel,
        grid=(model // tile,),
        out_shape=jax.ShapeDtypeStruct((rows, model), BF16),
        in_specs=[
            pl.BlockSpec((members, rows, width), lambda t: (0, 0, 0)),
            pl.BlockSpec((members, planes, members, share, tile), lambda t: (0, 0, 0, 0, t)),
        ],
        out_specs=pl.BlockSpec((rows, tile), lambda t: (0, t)),
        compiler_params=pltpu.CompilerParams(vmem_limit_bytes=HIGH_VMEM),
        cost_estimate=pl.CostEstimate(
            flops=2 * members * rows * width * model,
            bytes_accessed=2 * (members * width * model + members * rows * width + rows * model),
            transcendentals=0,
        ),
        name="project",
    )(a, w)


def route_kernel(resid_ref, gain_ref, slots_ref, *refs):
    parts_refs, (stream_ref, out_ref) = refs[:-2], refs[-2:]
    seqs = resid_ref.shape[0]
    streams = []
    for seq in range(seqs):
        stream = resid_ref[seq].astype(F32)
        projected = parts_refs[0][seq].astype(F32)
        for part in parts_refs[1:]:
            projected = projected + part[seq].astype(F32)
        streams.append(stream + projected)
    stream = jnp.concatenate(streams, 0) if seqs > 1 else streams[0]
    stream_ref[...] = stream
    normed = stream * lax.rsqrt(jnp.mean(stream * stream, 1, keepdims=True) + eps_norm)
    normed = (normed * gain_ref[...]).astype(BF16)
    slots, rows = out_ref.shape[0], stream.shape[0]
    place = lax.broadcasted_iota(jnp.int32, (slots, rows), 0)
    hit = place == slots_ref[0:1, :]
    for k in range(1, slots_ref.shape[0]):
        hit = hit | (place == slots_ref[k : k + 1, :])
    out_ref[...] = jnp.dot(hit.astype(BF16), normed, preferred_element_type=F32).astype(BF16)


def route(parts, resid, gain, slots_of, slots):
    seqs, local_rows, model = resid.shape
    rows = seqs * local_rows
    return pl.pallas_call(
        route_kernel,
        out_shape=(
            jax.ShapeDtypeStruct((rows, model), F32),
            jax.ShapeDtypeStruct((slots, model), BF16),
        ),
        in_specs=[in_vmem()] * (3 + len(parts)),
        out_specs=(in_vmem(), in_vmem()),
        compiler_params=pltpu.CompilerParams(vmem_limit_bytes=HIGH_VMEM),
        cost_estimate=pl.CostEstimate(
            flops=2 * slots * rows * model,
            bytes_accessed=2 * (len(parts) + 3 + slots // rows) * rows * model,
            transcendentals=0,
        ),
        name="route",
    )(resid, gain, slots_of, *parts)


def expert_kernel(x_ref, w_in_ref, w_down_ref, o_ref):
    hidden_width = w_down_ref.shape[0]
    inner = jnp.dot(x_ref[...], w_in_ref[...], preferred_element_type=F32)
    gate = inner[:, :hidden_width]
    hidden = (gate / (1.0 + jnp.exp(-gate)) * inner[:, hidden_width:]).astype(BF16)
    o_ref[...] = jnp.dot(hidden, w_down_ref[...], preferred_element_type=F32).astype(BF16)


def expert(x, w_in, w_down):
    rows, model = x.shape
    hidden_width = w_down.shape[0]
    return pl.pallas_call(
        expert_kernel,
        out_shape=jax.ShapeDtypeStruct((rows, model), BF16),
        in_specs=[in_vmem()] * 3,
        out_specs=in_vmem(),
        compiler_params=pltpu.CompilerParams(vmem_limit_bytes=HIGH_VMEM),
        cost_estimate=pl.CostEstimate(
            flops=6 * rows * model * hidden_width,
            bytes_accessed=2 * (2 * rows * model + 3 * model * hidden_width),
            transcendentals=rows * hidden_width,
        ),
        name="expert",
    )(x, w_in, w_down)


def expert_pair(x, w_in, w_down):
    rows, model = x.shape
    hidden_width = w_down.shape[0]
    parts = 4
    depth = model // parts

    def kernel(x_hbm, in_hbm_ref, down_hbm, o_hbm, x_ref, in_ref, down_ref, o_ref, sems):
        bring_x = pltpu.make_async_copy(x_hbm, x_ref, sems.at[parts])
        bring_x.start()
        bring_in = []
        for k in range(parts):
            at = pl.ds(k * depth, depth)
            bring_in.append(pltpu.make_async_copy(in_hbm_ref.at[at], in_ref.at[at], sems.at[k]))
            bring_in[k].start()
        bring_down = pltpu.make_async_copy(down_hbm, down_ref, sems.at[parts + 1])
        bring_down.start()
        bring_x.wait()
        inner = None
        for k in range(parts):
            bring_in[k].wait()
            at = pl.ds(k * depth, depth)
            part = jnp.dot(x_ref[:, at], in_ref[at, :], preferred_element_type=F32)
            inner = part if inner is None else inner + part
        gate = inner[:, :hidden_width]
        hidden = (gate / (1.0 + jnp.exp(-gate)) * inner[:, hidden_width:]).astype(BF16)
        bring_down.wait()
        o_ref[...] = jnp.dot(hidden, down_ref[...], preferred_element_type=F32).astype(BF16)
        back = pltpu.make_async_copy(o_ref, o_hbm, sems.at[parts + 2])
        back.start()
        back.wait()

    return pl.pallas_call(
        kernel,
        out_shape=pltpu.HBM((rows, model), BF16),
        in_specs=[in_hbm()] * 3,
        out_specs=in_hbm(),
        scratch_shapes=[
            pltpu.VMEM((rows, model), BF16),
            pltpu.VMEM(w_in.shape, BF16),
            pltpu.VMEM(w_down.shape, BF16),
            pltpu.VMEM((rows, model), BF16),
            pltpu.SemaphoreType.DMA((parts + 3,)),
        ],
        compiler_params=pltpu.CompilerParams(vmem_limit_bytes=HIGH_VMEM),
        cost_estimate=pl.CostEstimate(
            flops=6 * rows * model * hidden_width,
            bytes_accessed=2 * (2 * rows * model + 3 * model * hidden_width),
            transcendentals=rows * hidden_width,
        ),
        name="expert",
    )(x, w_in, w_down)


def combine_kernel(
    seqs, back_ref, stream_hbm, slots_ref, gates_ref, o_ref, stream_ref, sem
):
    bring = pltpu.make_async_copy(stream_hbm, stream_ref, sem.at[0])
    bring.start()
    slots = back_ref.shape[0]
    rows = stream_ref.shape[0]
    place = lax.broadcasted_iota(jnp.int32, (rows, slots), 1)
    gathered = None
    for k in range(slots_ref.shape[1]):
        pick = (place == slots_ref[:, k : k + 1]).astype(BF16)
        picked = jnp.dot(pick, back_ref[...], preferred_element_type=F32)
        part = picked * gates_ref[:, k : k + 1]
        gathered = part if gathered is None else gathered + part
    bring.wait()
    out = (stream_ref[...] + gathered).astype(BF16)
    local_rows = rows // seqs
    for seq in range(seqs):
        o_ref[seq] = out[seq * local_rows : (seq + 1) * local_rows]


def combine(back, stream, slots_of, gates, seqs):
    slots, model = back.shape
    rows = stream.shape[0]
    top = slots_of.shape[1]
    return pl.pallas_call(
        functools.partial(combine_kernel, seqs),
        out_shape=jax.ShapeDtypeStruct((seqs, rows // seqs, model), BF16),
        in_specs=[in_vmem(), in_hbm(), in_vmem(), in_vmem()],
        out_specs=in_vmem(),
        scratch_shapes=[pltpu.VMEM((rows, model), F32), pltpu.SemaphoreType.DMA((1,))],
        compiler_params=pltpu.CompilerParams(vmem_limit_bytes=HIGH_VMEM),
        cost_estimate=pl.CostEstimate(
            flops=2 * top * slots * rows * model,
            bytes_accessed=2 * slots * model + 6 * rows * model,
            transcendentals=0,
        ),
        name="combine",
    )(back, stream, slots_of, gates)


def flipped(value, axis, mask):
    pairs = [(source, source ^ mask) for source in range(lax.axis_size(axis))]
    return lax.ppermute(value, axis, pairs)


def parts_in_pairs(queries, new_kv, cache, w_out):
    n = lax.axis_size("head")
    local_rows, _, heads, width = queries.shape
    pair_heads = new_kv.shape[2]
    members = heads // pair_heads
    model = w_out.shape[2]
    share = w_out.shape[1]
    me = lax.axis_index("head")
    plane_bit = members // 2
    planes = n // plane_bit
    b = (me // plane_bit) % 2
    y = (me // 2) % 2
    group_sets = [[g * members + m for m in range(members)] for g in range(n // members)]

    query_slots = queries.reshape(local_rows, heads, width).transpose(1, 0, 2)
    query_slots = query_slots.reshape(members, heads // members, local_rows, width)
    q = lax.all_to_all(
        query_slots, "head", split_axis=0, concat_axis=0, tiled=True, axis_index_groups=group_sets
    )

    def page_target(source, other):
        p, plane, rest = source // members, (source // plane_bit) % 2, source % plane_bit
        return (plane ^ other) * members + p * plane_bit + rest

    page_a, page_b = (
        lax.ppermute(cache[0], "head", [(d, page_target(d, other)) for d in range(n)])
        for other in range(2)
    )
    kv_heads = new_kv.reshape(local_rows, pair_heads, 2 * width).transpose(1, 0, 2)
    kv_same = lax.dynamic_index_in_dim(kv_heads, b, 0, keepdims=False)
    kv_other = lax.dynamic_index_in_dim(kv_heads, 1 - b, 0, keepdims=False)
    columns = model // 2
    w = lax.dynamic_slice_in_dim(w_out, lax.axis_index("grp") * columns, columns, 2)
    w = w.reshape(2, 2, heads // 4, share, columns)
    w_keep = lax.dynamic_index_in_dim(w, y, 1, keepdims=False)
    w_give = lax.dynamic_index_in_dim(w, 1 - y, 1, keepdims=False)
    kv_own = [kv_same]
    for t in range(1, planes):
        kv_own.append(flipped(kv_other if t % 2 else kv_same, "head", t * plane_bit))
    w_got = flipped(w_give, "head", 2)

    kv_own[1], kv_own[2], w_got = lax.optimization_barrier((kv_own[1], kv_own[2], w_got))
    w_both = jnp.stack([w_keep, w_got], 1)
    w_same = lax.dynamic_index_in_dim(w_both, b, 0, keepdims=False)
    w_other = lax.dynamic_index_in_dim(w_both, 1 - b, 0, keepdims=False)
    w_first = flipped(w_other, "head", plane_bit)

    own_pages = jnp.concatenate([page_a, page_b], 0)
    own_pages, kv_own, w_first, q = lax.optimization_barrier((own_pages, kv_own, w_first, q))
    kv_own = jnp.stack(kv_own, 0)
    pages_y = flipped(own_pages, "head", 2)
    kv_y = flipped(kv_own, "head", 2)
    w_near = jnp.stack([w_same, w_first], 0)
    w_near_x = flipped(w_near, "grp", 1)
    w_far = flipped(w_near, "head", members)
    pages_y, kv_y, own_pages, kv_own, w_near_x = lax.optimization_barrier(
        (pages_y, kv_y, own_pages, kv_own, w_near_x)
    )
    kv_c = flipped(kv_own, "head", 1)
    kv_cy = flipped(kv_y, "head", 1)
    pages_c = flipped(own_pages, "head", 1)
    pages_cy = flipped(pages_y, "head", 1)
    q, w_far = lax.optimization_barrier((q, w_far))
    w_far_x = flipped(w_far, "grp", 1)
    a = attend_pair(q, (own_pages, pages_y, pages_c, pages_cy), (kv_own, kv_y, kv_c, kv_cy))
    got = flipped(a[1], "head", 1)
    a, w_near_x, w_far_x = lax.optimization_barrier((a, w_near_x, w_far_x))
    w_near_c = flipped(w_near, "head", 1)
    w_far_c = flipped(w_far, "head", 1)
    w_near_cx = flipped(w_near_x, "head", 1)
    w_far_cx = flipped(w_far_x, "head", 1)
    partial = project_pair(
        a,
        got,
        (w_near, w_near_c, w_near_x, w_near_cx),
        (w_far, w_far_c, w_far_x, w_far_cx),
        members // 2,
    )
    parts = [partial[0]] + [flipped(partial[k], "head", 2 * k) for k in (3, 2, 1)]
    return [part[None] for part in parts]


def parts_in_planes(queries, new_kv, cache, w_out):
    n = lax.axis_size("head")
    local_rows, seqs, heads, width = queries.shape
    pair_heads = new_kv.shape[2]
    members = heads // pair_heads
    groups = n // members
    model = w_out.shape[2]
    side = 1 << ((n.bit_length() - 1) // 2)
    side = min(side, heads)
    planes = n // side
    planes_of_seq = heads // side
    pair_groups = [[g * members + m for m in range(members)] for g in range(groups)]
    cross_groups = [[g * members + m for g in range(groups)] for m in range(members)]
    plane_groups = [[p * side + m for m in range(side)] for p in range(planes)]
    column_groups = [[p * side + m for p in range(planes)] for m in range(side)]

    query_slots = queries.reshape(local_rows, n, width).transpose(1, 0, 2)
    q = lax.all_to_all(query_slots, "head", split_axis=0, concat_axis=0, tiled=True)
    q = q.reshape(n * local_rows, width)

    kv_slots = new_kv.reshape(local_rows, groups, 2 * width).transpose(1, 0, 2)
    kv = lax.all_to_all(
        kv_slots, "head", split_axis=0, concat_axis=0, tiled=True, axis_index_groups=cross_groups
    )
    kv = lax.all_gather(kv, "head", axis=0, axis_index_groups=pair_groups)
    pages = lax.all_gather(cache, "head", axis=0, tiled=True, axis_index_groups=pair_groups)

    share = w_out.shape[1]
    w_planes = w_out.reshape(planes_of_seq, side, share, model)
    if planes > planes_of_seq:
        w_planes = jnp.tile(w_planes, (planes // planes_of_seq, 1, 1, 1))
    w = lax.all_to_all(
        w_planes, "head", split_axis=0, concat_axis=0, tiled=True, axis_index_groups=column_groups
    )
    w = lax.all_gather(w, "head", axis=0, axis_index_groups=plane_groups)
    if share % 16:
        w = w.transpose(2, 1, 0, 3, 4).reshape(1, 1, side, width, model)
        w = w.reshape(side, width, model)

    attended = attend(q, pages.reshape(-1, 2 * width), kv)
    a = attended.reshape(planes, side, local_rows, width).transpose(1, 0, 2, 3)
    a = a.reshape(side, planes * local_rows, width)
    a = lax.all_to_all(
        a, "head", split_axis=0, concat_axis=0, tiled=True, axis_index_groups=plane_groups
    )
    if share % 16:
        partial = jnp.einsum("hri,hid->rd", a, w, preferred_element_type=F32).astype(BF16)
    else:
        partial = project(a, w)
    parts = lax.all_to_all(
        partial.reshape(planes, local_rows, model),
        "head",
        split_axis=0,
        concat_axis=0,
        tiled=True,
        axis_index_groups=column_groups,
    )
    parts = parts.reshape(seqs, planes_of_seq, local_rows, model)
    return [parts[:, k] for k in range(planes_of_seq)]


def local(queries, new_kv, cache, resid, w_out, norm_gain, expert_ids, expert_gates, w_in, w_down):
    n = lax.axis_size("head")
    local_rows, seqs, heads, width = queries.shape
    model = resid.shape[2]
    rows = local_rows * seqs
    members = heads // new_kv.shape[2]
    in_pairs = (
        lax.axis_size("grp") == 2
        and seqs == 1
        and new_kv.shape[2] == 2
        and n == heads == 2 * members
        and members == 8
        and cache.shape[0] == 1
        and w_in.shape[0] == 1
        and w_out.shape[1] % 16 == 0
    )
    plan = parts_in_pairs if in_pairs else parts_in_planes
    parts = plan(queries, new_kv, cache, w_out)

    top = expert_ids.shape[2]
    experts = w_in.shape[0] * n
    capacity = max(2, 2 * rows * top // experts)
    ids = expert_ids.transpose(1, 0, 2).reshape(rows, top)
    gates = expert_gates.transpose(1, 0, 2).reshape(rows, top)
    onehot = (ids[:, :, None] == jnp.arange(experts, dtype=jnp.int32)).astype(jnp.int32)
    named = onehot.sum(1)
    before = jnp.cumsum(named, 0) - named
    slots_of = ids * capacity + jnp.sum(onehot * before[:, None, :], 2)
    slots = experts * capacity

    stream, outgoing = route(
        parts, resid.transpose(1, 0, 2), norm_gain[None, :], slots_of.T, slots
    )
    arrived = lax.all_to_all(
        outgoing.reshape(n, slots // n, model), "head", split_axis=0, concat_axis=0, tiled=True
    )
    local_experts = w_in.shape[0]
    if local_experts == 1:
        answered = expert_pair(arrived.reshape(slots, model), w_in[0], w_down[0])
        answered = answered.reshape(n, slots // n, model)
    else:
        arrived = arrived.reshape(n, local_experts, capacity, model).transpose(1, 0, 2, 3)
        arrived = arrived.reshape(local_experts, n * capacity, model)
        answered = jnp.stack([expert(arrived[e], w_in[e], w_down[e]) for e in range(local_experts)])
        answered = answered.reshape(local_experts, n, capacity, model).transpose(1, 0, 2, 3)
        answered = answered.reshape(n, slots // n, model)
    back = lax.all_to_all(answered, "head", split_axis=0, concat_axis=0, tiled=True)
    out = combine(back.reshape(slots, model), stream, slots_of, gates, seqs)
    return out.transpose(1, 0, 2)


def solution(mesh):
    return jax.shard_map(
        local,
        mesh=mesh,
        in_specs=(
            P("head", "grp", None, None),
            P("head", "grp", None, None),
            P(("grp", "head"), None, None),
            P("head", "grp", None),
            P(None, "head", None),
            P(),
            P("head", "grp", None),
            P("head", "grp", None),
            P("head", None, None),
            P("head", None, None),
        ),
        out_specs=P("head", "grp", None),
        check_vma=False,
    )
```

```python
import functools

import jax
import jax.numpy as jnp
from jax import lax
from jax.experimental import pallas as pl
from jax.experimental.pallas import tpu as pltpu
from jax.sharding import PartitionSpec as P

eps_norm = 1e-06
F32 = jnp.float32
BF16 = jnp.bfloat16
HIGH_VMEM = 48 * 2**20
LOG2_E = 1.4426950408889634


def in_hbm():
    return pl.BlockSpec(memory_space=pltpu.HBM)


def in_vmem():
    return pl.BlockSpec(memory_space=pltpu.VMEM)


def attend_kernel(
    block, chunk, width, q_hbm, cache_hbm, kv_hbm, o_ref, q_ref, cache_ref, kv_ref, s0, s1, sems
):
    members, groups, piece, _ = kv_hbm.shape
    length = members * groups * piece
    old = cache_hbm.shape[0]
    scale = width**-0.5
    in_q = pltpu.make_async_copy(q_hbm, q_ref, sems.at[0])
    in_cache = pltpu.make_async_copy(cache_hbm, cache_ref, sems.at[1])
    in_q.start()
    in_cache.start()
    in_kv = []
    for group in range(groups):
        for member in range(members):
            place = (group * members + member) * piece
            copy = pltpu.make_async_copy(
                kv_hbm.at[member, group], kv_ref.at[pl.ds(place, piece)], sems.at[2]
            )
            copy.start()
            in_kv.append(copy)
    in_q.wait()
    in_cache.wait()
    for copy in in_kv:
        copy.wait()
    scores = [s0, s1]

    def pieces(b):
        out = [(True, k, chunk, k) for k in range(0, old, chunk)]
        last = b * block
        for k in range(0, last, chunk):
            out.append((False, k, min(chunk, last - k), old + k))
        out.append((False, last, block, old + last))
        return out

    def make_scores(b, part, running):
        of_cache, first, count, column = part
        keys = (cache_ref if of_cache else kv_ref)[pl.ds(first, count), :width]
        s = lax.dot_general(
            q_ref[pl.ds(b * block, block), :],
            keys,
            (((1,), (1,)), ((), ())),
            preferred_element_type=F32,
        )
        if not of_cache and first == b * block:
            row = lax.broadcasted_iota(jnp.int32, s.shape, 0)
            col = lax.broadcasted_iota(jnp.int32, s.shape, 1)
            s = jnp.where(col <= row, s, -jnp.inf)
        scores[b % 2][:, pl.ds(column, count)] = s
        for k in range(0, count, 128):
            piece_max = s[:, k : k + 128]
            running = piece_max if running is None else jnp.maximum(running, piece_max)
        return running

    def use_scores(b, part, top, total, acc):
        of_cache, first, count, column = part
        values = (cache_ref if of_cache else kv_ref)[pl.ds(first, count), width:]
        e = jnp.exp((scores[b % 2][:, pl.ds(column, count)] - top) * scale)
        for k in range(0, count, 128):
            total = e[:, k : k + 128] if total is None else total + e[:, k : k + 128]
        product = jnp.dot(e.astype(BF16), values, preferred_element_type=F32)
        return total, product if acc is None else acc + product

    blocks = length // block
    running = None
    for part in pieces(0):
        running = make_scores(0, part, running)
    for b in range(blocks):
        top = jnp.max(running, 1, keepdims=True)
        now, later = pieces(b), pieces(b + 1) if b + 1 < blocks else []
        running, total, acc = None, None, None
        for k in range(max(len(now), len(later))):
            if k < len(now):
                total, acc = use_scores(b, now[k], top, total, acc)
            if k < len(later):
                running = make_scores(b + 1, later[k], running)
        o_ref[pl.ds(b * block, block), :] = (acc / jnp.sum(total, 1, keepdims=True)).astype(BF16)


def attend(q, cache, kv):
    length, width = q.shape
    old = cache.shape[0]
    block = min(256, length)
    chunk = min(512, old)
    return pl.pallas_call(
        functools.partial(attend_kernel, block, chunk, width),
        out_shape=jax.ShapeDtypeStruct((length, width), BF16),
        in_specs=[in_hbm()] * 3,
        out_specs=in_vmem(),
        scratch_shapes=[
            pltpu.VMEM((length, width), BF16),
            pltpu.VMEM((old, 2 * width), BF16),
            pltpu.VMEM((length, 2 * width), BF16),
            pltpu.VMEM((block, old + length), F32),
            pltpu.VMEM((block, old + length), F32),
            pltpu.SemaphoreType.DMA((3,)),
        ],
        compiler_params=pltpu.CompilerParams(vmem_limit_bytes=HIGH_VMEM),
        cost_estimate=pl.CostEstimate(
            flops=4 * length * (old + length // 2) * width,
            bytes_accessed=4 * (2 * length + 2 * old) * width,
            transcendentals=length * (old + length // 2),
        ),
        name="attend",
    )(q, cache, kv)


def attend_pair_kernel(
    block,
    chunk,
    width,
    q_hbm,
    page_own,
    page_y,
    page_c,
    page_cy,
    kv_own,
    kv_y,
    kv_c,
    kv_cy,
    o_ref,
    q_ref,
    old_ref,
    kv_ref,
    s0,
    s1,
    sems,
):
    me = lax.axis_index("head")
    members, heads, piece, _ = q_hbm.shape
    length = members * piece
    planes = kv_own.shape[0]
    old = old_ref.shape[0]
    earlier_group = me // members > 0
    core = lax.rem(me, 2)
    chip = jnp.bitwise_and(me // 2, members // 2 - 1)
    copies = []

    def bring(source, target, sem):
        copy = pltpu.make_async_copy(source, target, sems.at[sem])
        copy.start()
        copies.append(copy)

    for member in range(members):
        for head in range(heads):
            bring(q_hbm.at[member, head], q_ref.at[head, pl.ds(member * piece, piece)], 0)
    place = 0
    for page in (page_own, page_y, page_c, page_cy):
        count = page.shape[0]
        bring(page, old_ref.at[pl.ds(place, count)], 1)
        place += count
    for flip, pieces_of in ((0, kv_own), (2, kv_y), (1, kv_c), (3, kv_cy)):
        for t in range(planes):
            number = jnp.bitwise_and(
                jnp.bitwise_xor(me, flip ^ (t * (members // 2))), members - 1
            )
            start = pl.multiple_of(number * piece, piece)
            area = 0 if t * (members // 2) >= members else length
            bring(pieces_of.at[t], kv_ref.at[pl.ds(area + start, piece)], 2)
    for copy in copies:
        copy.wait()
    scale = width**-0.5 * LOG2_E
    scores = [s0, s1]
    blocks = length // block
    units = [(head, b) for head in range(heads) for b in range(blocks)]

    def pieces(unit):
        _, b = units[unit]
        out = [("old", k, chunk, k) for k in range(0, old, chunk)]
        out += [("past", k, chunk, old + k) for k in range(0, length, chunk)]
        last = b * block
        for k in range(0, last, chunk):
            out.append(("new", length + k, min(chunk, last - k), old + length + k))
        out.append(("edge", length + last, block, old + length + last))
        return out

    def make_scores(unit, part, running):
        kind, first, count, column = part
        head, b = units[unit]
        keys = (old_ref if kind == "old" else kv_ref)[pl.ds(first, count), :width]
        s = lax.dot_general(
            q_ref[head, pl.ds(b * block, block), :],
            keys,
            (((1,), (1,)), ((), ())),
            preferred_element_type=F32,
        )
        if kind == "past":
            s = jnp.where(earlier_group, s, -jnp.inf)
        if kind == "edge":
            row = lax.broadcasted_iota(jnp.int32, s.shape, 0)
            col = lax.broadcasted_iota(jnp.int32, s.shape, 1)
            s = jnp.where(col <= row, s, -jnp.inf)
        scores[unit % 2][:, pl.ds(column, count)] = s
        for k in range(0, count, 128):
            piece_max = s[:, k : k + 128]
            running = piece_max if running is None else jnp.maximum(running, piece_max)
        return running

    def use_scores(unit, part, top, total, acc):
        kind, first, count, column = part
        values = (old_ref if kind == "old" else kv_ref)[pl.ds(first, count), width:]
        e = jnp.exp2((scores[unit % 2][:, pl.ds(column, count)] - top) * scale)
        for k in range(0, count, 128):
            total = e[:, k : k + 128] if total is None else total + e[:, k : k + 128]
        product = jnp.dot(e.astype(BF16), values, preferred_element_type=F32)
        return total, product if acc is None else acc + product

    running = None
    for part in pieces(0):
        running = make_scores(0, part, running)
    for unit, (head, b) in enumerate(units):
        top = jnp.max(running, 1, keepdims=True)
        now = pieces(unit)
        later = pieces(unit + 1) if unit + 1 < len(units) else []
        running, total, acc = None, None, None
        for k in range(max(len(now), len(later))):
            if k < len(now):
                total, acc = use_scores(unit, now[k], top, total, acc)
            if k < len(later):
                running = make_scores(unit + 1, later[k], running)
        done = (acc / jnp.sum(total, 1, keepdims=True)).astype(BF16)
        for k in range(0, block, piece):
            member = (b * block + k) // piece
            side = jnp.bitwise_xor(core, member % 2)
            start = pl.multiple_of(jnp.bitwise_xor(chip, member // 2) * piece, piece)
            o_ref[side, pl.ds(start, piece), pl.ds(head * width, width)] = done[k : k + piece]


def attend_pair(q, pages, kvs):
    members, heads, piece, width = q.shape
    length = members * piece
    old = sum(page.shape[0] for page in pages)
    block = 2 * piece
    chunk = min(512, old, length)
    keys = old + 2 * length
    return pl.pallas_call(
        functools.partial(attend_pair_kernel, block, chunk, width),
        out_shape=jax.ShapeDtypeStruct((2, length // 2, heads * width), BF16),
        in_specs=[in_hbm()] * (1 + len(pages) + len(kvs)),
        out_specs=in_vmem(),
        scratch_shapes=[
            pltpu.VMEM((heads, length, width), BF16),
            pltpu.VMEM((old, 2 * width), BF16),
            pltpu.VMEM((2 * length, 2 * width), BF16),
            pltpu.VMEM((block, keys), F32),
            pltpu.VMEM((block, keys), F32),
            pltpu.SemaphoreType.DMA((3,)),
        ],
        compiler_params=pltpu.CompilerParams(vmem_limit_bytes=HIGH_VMEM),
        cost_estimate=pl.CostEstimate(
            flops=4 * heads * length * (keys - length // 2) * width,
            bytes_accessed=4 * (heads * length + keys) * width,
            transcendentals=heads * length * (keys - length // 2),
        ),
        name="attend",
    )(q, *pages, *kvs)


def project_pair_kernel(a_hbm, got_hbm, *refs):
    near, far, outs, (w_ref, all_ref, out_ref, sems) = refs[:4], refs[4:8], refs[8:-4], refs[-4:]
    me = lax.axis_index("head")
    half = lax.axis_index("grp")
    core = lax.rem(me, 2)
    steps, sides, heads, share, columns = near[0].shape
    width = w_ref.shape[1]
    side = got_hbm.shape[1]
    bring = [[], [], []]
    for other, source in enumerate((a_hbm.at[0], got_hbm)):
        at = pl.ds(pl.multiple_of(jnp.bitwise_xor(core, other) * side, side), side)
        bring[2].append(pltpu.make_async_copy(source, all_ref.at[:, at], sems.at[2]))
    for x in range(2):
        column = pl.multiple_of(jnp.bitwise_xor(half, x) * columns, columns)
        for first, given in ((0, near), (steps, far)):
            for flip in range(2):
                for t in range(steps):
                    for u in range(sides):
                        number = jnp.bitwise_xor(me, flip ^ (2 * u) ^ (4 * (first + t)))
                        row = pl.multiple_of(number * share, share)
                        bring[x].append(
                            pltpu.make_async_copy(
                                given[2 * x + flip].at[t, u],
                                w_ref.at[:, pl.ds(row, share), pl.ds(column, columns)],
                                sems.at[x],
                            )
                        )
    for copies in (bring[2], bring[0], bring[1]):
        for copy in copies:
            copy.start()
    for copy in bring[2]:
        copy.wait()
    rows = outs[0].shape[0]
    tile = min(512, columns)
    back = []
    for x in range(2):
        for copy in bring[x]:
            copy.wait()
        for first in range(0, columns, tile):
            column = jnp.bitwise_xor(half, x) * columns + first
            at = pl.ds(pl.multiple_of(column, tile), tile)
            w = w_ref[:, :, at].reshape(heads * width, tile)
            out_ref[:, at] = jnp.dot(all_ref[...], w, preferred_element_type=F32).astype(BF16)
            for k, out in enumerate(outs):
                copy = pltpu.make_async_copy(
                    out_ref.at[pl.ds(k * rows, rows), at], out.at[:, at], sems.at[3]
                )
                copy.start()
                back.append(copy)
    for copy in back:
        copy.wait()


def project_pair(a, got, near, far, parts):
    _, _, heads, share, columns = near[0].shape
    rows = got.shape[0]
    width = 2 * got.shape[1] // heads
    model = 2 * columns
    return pl.pallas_call(
        project_pair_kernel,
        out_shape=[pltpu.HBM((rows // parts, model), BF16)] * parts,
        in_specs=[in_hbm()] * 10,
        out_specs=[in_hbm()] * parts,
        scratch_shapes=[
            pltpu.VMEM((heads, width, model), BF16),
            pltpu.VMEM((rows, heads * width), BF16),
            pltpu.VMEM((rows, model), BF16),
            pltpu.SemaphoreType.DMA((4,)),
        ],
        compiler_params=pltpu.CompilerParams(vmem_limit_bytes=HIGH_VMEM),
        cost_estimate=pl.CostEstimate(
            flops=2 * heads * rows * width * model,
            bytes_accessed=2 * (heads * width * model + heads * rows * width + rows * model),
            transcendentals=0,
        ),
        name="project",
    )(a, got, *near, *far)


def project_kernel(a_ref, w_ref, o_ref):
    members = a_ref.shape[0]
    planes, share = w_ref.shape[1], w_ref.shape[3]
    acc = None
    for head in range(members):
        w = jnp.concatenate(
            [w_ref[m, p, head] for p in range(planes) for m in range(members)], 0
        )
        part = jnp.dot(a_ref[head], w, preferred_element_type=F32)
        acc = part if acc is None else acc + part
    o_ref[...] = acc.astype(BF16)


def project(a, w):
    members, rows, width = a.shape
    planes, share, model = w.shape[1], w.shape[3], w.shape[4]
    tile = min(512, model)
    return pl.pallas_call(
        project_kernel,
        grid=(model // tile,),
        out_shape=jax.ShapeDtypeStruct((rows, model), BF16),
        in_specs=[
            pl.BlockSpec((members, rows, width), lambda t: (0, 0, 0)),
            pl.BlockSpec((members, planes, members, share, tile), lambda t: (0, 0, 0, 0, t)),
        ],
        out_specs=pl.BlockSpec((rows, tile), lambda t: (0, t)),
        compiler_params=pltpu.CompilerParams(vmem_limit_bytes=HIGH_VMEM),
        cost_estimate=pl.CostEstimate(
            flops=2 * members * rows * width * model,
            bytes_accessed=2 * (members * width * model + members * rows * width + rows * model),
            transcendentals=0,
        ),
        name="project",
    )(a, w)


def route_kernel(resid_ref, gain_ref, slots_ref, *refs):
    parts_refs, (stream_ref, out_ref) = refs[:-2], refs[-2:]
    seqs = resid_ref.shape[0]
    streams = []
    for seq in range(seqs):
        stream = resid_ref[seq].astype(F32)
        projected = parts_refs[0][seq].astype(F32)
        for part in parts_refs[1:]:
            projected = projected + part[seq].astype(F32)
        streams.append(stream + projected)
    stream = jnp.concatenate(streams, 0) if seqs > 1 else streams[0]
    stream_ref[...] = stream
    normed = stream * lax.rsqrt(jnp.mean(stream * stream, 1, keepdims=True) + eps_norm)
    normed = (normed * gain_ref[...]).astype(BF16)
    slots, rows = out_ref.shape[0], stream.shape[0]
    place = lax.broadcasted_iota(jnp.int32, (slots, rows), 0)
    hit = place == slots_ref[0:1, :]
    for k in range(1, slots_ref.shape[0]):
        hit = hit | (place == slots_ref[k : k + 1, :])
    out_ref[...] = jnp.dot(hit.astype(BF16), normed, preferred_element_type=F32).astype(BF16)


def route(parts, resid, gain, slots_of, slots):
    seqs, local_rows, model = resid.shape
    rows = seqs * local_rows
    return pl.pallas_call(
        route_kernel,
        out_shape=(
            jax.ShapeDtypeStruct((rows, model), F32),
            jax.ShapeDtypeStruct((slots, model), BF16),
        ),
        in_specs=[in_vmem()] * (3 + len(parts)),
        out_specs=(in_vmem(), in_vmem()),
        compiler_params=pltpu.CompilerParams(vmem_limit_bytes=HIGH_VMEM),
        cost_estimate=pl.CostEstimate(
            flops=2 * slots * rows * model,
            bytes_accessed=2 * (len(parts) + 3 + slots // rows) * rows * model,
            transcendentals=0,
        ),
        name="route",
    )(resid, gain, slots_of, *parts)


def expert_kernel(x_ref, w_in_ref, w_down_ref, o_ref):
    hidden_width = w_down_ref.shape[0]
    inner = jnp.dot(x_ref[...], w_in_ref[...], preferred_element_type=F32)
    gate = inner[:, :hidden_width]
    hidden = (gate / (1.0 + jnp.exp(-gate)) * inner[:, hidden_width:]).astype(BF16)
    o_ref[...] = jnp.dot(hidden, w_down_ref[...], preferred_element_type=F32).astype(BF16)


def expert(x, w_in, w_down):
    rows, model = x.shape
    hidden_width = w_down.shape[0]
    return pl.pallas_call(
        expert_kernel,
        out_shape=jax.ShapeDtypeStruct((rows, model), BF16),
        in_specs=[in_vmem()] * 3,
        out_specs=in_vmem(),
        compiler_params=pltpu.CompilerParams(vmem_limit_bytes=HIGH_VMEM),
        cost_estimate=pl.CostEstimate(
            flops=6 * rows * model * hidden_width,
            bytes_accessed=2 * (2 * rows * model + 3 * model * hidden_width),
            transcendentals=rows * hidden_width,
        ),
        name="expert",
    )(x, w_in, w_down)


def expert_pair(x, w_in, w_down):
    rows, model = x.shape
    hidden_width = w_down.shape[0]
    parts = 4
    depth = model // parts

    def kernel(x_hbm, in_hbm_ref, down_hbm, o_hbm, x_ref, in_ref, down_ref, o_ref, sems):
        bring_x = pltpu.make_async_copy(x_hbm, x_ref, sems.at[parts])
        bring_x.start()
        bring_in = []
        for k in range(parts):
            at = pl.ds(k * depth, depth)
            bring_in.append(pltpu.make_async_copy(in_hbm_ref.at[at], in_ref.at[at], sems.at[k]))
            bring_in[k].start()
        bring_down = pltpu.make_async_copy(down_hbm, down_ref, sems.at[parts + 1])
        bring_down.start()
        bring_x.wait()
        inner = None
        for k in range(parts):
            bring_in[k].wait()
            at = pl.ds(k * depth, depth)
            part = jnp.dot(x_ref[:, at], in_ref[at, :], preferred_element_type=F32)
            inner = part if inner is None else inner + part
        gate = inner[:, :hidden_width]
        hidden = (gate / (1.0 + jnp.exp(-gate)) * inner[:, hidden_width:]).astype(BF16)
        bring_down.wait()
        o_ref[...] = jnp.dot(hidden, down_ref[...], preferred_element_type=F32).astype(BF16)
        back = pltpu.make_async_copy(o_ref, o_hbm, sems.at[parts + 2])
        back.start()
        back.wait()

    return pl.pallas_call(
        kernel,
        out_shape=pltpu.HBM((rows, model), BF16),
        in_specs=[in_hbm()] * 3,
        out_specs=in_hbm(),
        scratch_shapes=[
            pltpu.VMEM((rows, model), BF16),
            pltpu.VMEM(w_in.shape, BF16),
            pltpu.VMEM(w_down.shape, BF16),
            pltpu.VMEM((rows, model), BF16),
            pltpu.SemaphoreType.DMA((parts + 3,)),
        ],
        compiler_params=pltpu.CompilerParams(vmem_limit_bytes=HIGH_VMEM),
        cost_estimate=pl.CostEstimate(
            flops=6 * rows * model * hidden_width,
            bytes_accessed=2 * (2 * rows * model + 3 * model * hidden_width),
            transcendentals=rows * hidden_width,
        ),
        name="expert",
    )(x, w_in, w_down)


def combine_kernel(
    seqs, back_ref, stream_hbm, slots_ref, gates_ref, o_ref, stream_ref, sem
):
    bring = pltpu.make_async_copy(stream_hbm, stream_ref, sem.at[0])
    bring.start()
    slots = back_ref.shape[0]
    rows = stream_ref.shape[0]
    place = lax.broadcasted_iota(jnp.int32, (rows, slots), 1)
    gathered = None
    for k in range(slots_ref.shape[1]):
        pick = (place == slots_ref[:, k : k + 1]).astype(BF16)
        picked = jnp.dot(pick, back_ref[...], preferred_element_type=F32)
        part = picked * gates_ref[:, k : k + 1]
        gathered = part if gathered is None else gathered + part
    bring.wait()
    out = (stream_ref[...] + gathered).astype(BF16)
    local_rows = rows // seqs
    for seq in range(seqs):
        o_ref[seq] = out[seq * local_rows : (seq + 1) * local_rows]


def combine(back, stream, slots_of, gates, seqs):
    slots, model = back.shape
    rows = stream.shape[0]
    top = slots_of.shape[1]
    return pl.pallas_call(
        functools.partial(combine_kernel, seqs),
        out_shape=jax.ShapeDtypeStruct((seqs, rows // seqs, model), BF16),
        in_specs=[in_vmem(), in_hbm(), in_vmem(), in_vmem()],
        out_specs=in_vmem(),
        scratch_shapes=[pltpu.VMEM((rows, model), F32), pltpu.SemaphoreType.DMA((1,))],
        compiler_params=pltpu.CompilerParams(vmem_limit_bytes=HIGH_VMEM),
        cost_estimate=pl.CostEstimate(
            flops=2 * top * slots * rows * model,
            bytes_accessed=2 * slots * model + 6 * rows * model,
            transcendentals=0,
        ),
        name="combine",
    )(back, stream, slots_of, gates)


def flipped(value, axis, mask):
    pairs = [(source, source ^ mask) for source in range(lax.axis_size(axis))]
    return lax.ppermute(value, axis, pairs)


def parts_in_pairs(queries, new_kv, cache, w_out):
    n = lax.axis_size("head")
    local_rows, _, heads, width = queries.shape
    pair_heads = new_kv.shape[2]
    members = heads // pair_heads
    model = w_out.shape[2]
    share = w_out.shape[1]
    me = lax.axis_index("head")
    plane_bit = members // 2
    planes = n // plane_bit
    b = (me // plane_bit) % 2
    y = (me // 2) % 2
    group_sets = [[g * members + m for m in range(members)] for g in range(n // members)]

    query_slots = queries.reshape(local_rows, heads, width).transpose(1, 0, 2)
    query_slots = query_slots.reshape(members, heads // members, local_rows, width)
    q = lax.all_to_all(
        query_slots, "head", split_axis=0, concat_axis=0, tiled=True, axis_index_groups=group_sets
    )

    def page_target(source, other):
        p, plane, rest = source // members, (source // plane_bit) % 2, source % plane_bit
        return (plane ^ other) * members + p * plane_bit + rest

    page_a, page_b = (
        lax.ppermute(cache[0], "head", [(d, page_target(d, other)) for d in range(n)])
        for other in range(2)
    )
    kv_heads = new_kv.reshape(local_rows, pair_heads, 2 * width).transpose(1, 0, 2)
    kv_same = lax.dynamic_index_in_dim(kv_heads, b, 0, keepdims=False)
    kv_other = lax.dynamic_index_in_dim(kv_heads, 1 - b, 0, keepdims=False)
    columns = model // 2
    w = lax.dynamic_slice_in_dim(w_out, lax.axis_index("grp") * columns, columns, 2)
    w = w.reshape(2, 2, heads // 4, share, columns)
    w_keep = lax.dynamic_index_in_dim(w, y, 1, keepdims=False)
    w_give = lax.dynamic_index_in_dim(w, 1 - y, 1, keepdims=False)
    kv_own = [kv_same]
    for t in range(1, planes):
        kv_own.append(flipped(kv_other if t % 2 else kv_same, "head", t * plane_bit))
    w_got = flipped(w_give, "head", 2)

    kv_own[1], kv_own[2], w_got = lax.optimization_barrier((kv_own[1], kv_own[2], w_got))
    w_both = jnp.stack([w_keep, w_got], 1)
    w_same = lax.dynamic_index_in_dim(w_both, b, 0, keepdims=False)
    w_other = lax.dynamic_index_in_dim(w_both, 1 - b, 0, keepdims=False)
    w_first = flipped(w_other, "head", plane_bit)

    own_pages = jnp.concatenate([page_a, page_b], 0)
    own_pages, kv_own, w_first, q = lax.optimization_barrier((own_pages, kv_own, w_first, q))
    kv_own = jnp.stack(kv_own, 0)
    pages_y = flipped(own_pages, "head", 2)
    kv_y = flipped(kv_own, "head", 2)
    w_near = jnp.stack([w_same, w_first], 0)
    w_near_x = flipped(w_near, "grp", 1)
    w_far = flipped(w_near, "head", members)
    pages_y, kv_y, own_pages, kv_own, w_near_x = lax.optimization_barrier(
        (pages_y, kv_y, own_pages, kv_own, w_near_x)
    )
    kv_c = flipped(kv_own, "head", 1)
    kv_cy = flipped(kv_y, "head", 1)
    pages_c = flipped(own_pages, "head", 1)
    pages_cy = flipped(pages_y, "head", 1)
    q, w_far = lax.optimization_barrier((q, w_far))
    w_far_x = flipped(w_far, "grp", 1)
    a = attend_pair(q, (own_pages, pages_y, pages_c, pages_cy), (kv_own, kv_y, kv_c, kv_cy))
    got = flipped(a[1], "head", 1)
    a, w_near_x, w_far_x = lax.optimization_barrier((a, w_near_x, w_far_x))
    w_near_c = flipped(w_near, "head", 1)
    w_far_c = flipped(w_far, "head", 1)
    w_near_cx = flipped(w_near_x, "head", 1)
    w_far_cx = flipped(w_far_x, "head", 1)
    partial = project_pair(
        a,
        got,
        (w_near, w_near_c, w_near_x, w_near_cx),
        (w_far, w_far_c, w_far_x, w_far_cx),
        members // 2,
    )
    parts = [partial[0]] + [flipped(partial[k], "head", 2 * k) for k in (3, 2, 1)]
    return [part[None] for part in parts]


def parts_in_planes(queries, new_kv, cache, w_out):
    n = lax.axis_size("head")
    local_rows, seqs, heads, width = queries.shape
    pair_heads = new_kv.shape[2]
    members = heads // pair_heads
    groups = n // members
    model = w_out.shape[2]
    side = 1 << ((n.bit_length() - 1) // 2)
    side = min(side, heads)
    planes = n // side
    planes_of_seq = heads // side
    pair_groups = [[g * members + m for m in range(members)] for g in range(groups)]
    cross_groups = [[g * members + m for g in range(groups)] for m in range(members)]
    plane_groups = [[p * side + m for m in range(side)] for p in range(planes)]
    column_groups = [[p * side + m for p in range(planes)] for m in range(side)]

    query_slots = queries.reshape(local_rows, n, width).transpose(1, 0, 2)
    q = lax.all_to_all(query_slots, "head", split_axis=0, concat_axis=0, tiled=True)
    q = q.reshape(n * local_rows, width)

    kv_slots = new_kv.reshape(local_rows, groups, 2 * width).transpose(1, 0, 2)
    kv = lax.all_to_all(
        kv_slots, "head", split_axis=0, concat_axis=0, tiled=True, axis_index_groups=cross_groups
    )
    kv = lax.all_gather(kv, "head", axis=0, axis_index_groups=pair_groups)
    pages = lax.all_gather(cache, "head", axis=0, tiled=True, axis_index_groups=pair_groups)

    share = w_out.shape[1]
    w_planes = w_out.reshape(planes_of_seq, side, share, model)
    if planes > planes_of_seq:
        w_planes = jnp.tile(w_planes, (planes // planes_of_seq, 1, 1, 1))
    w = lax.all_to_all(
        w_planes, "head", split_axis=0, concat_axis=0, tiled=True, axis_index_groups=column_groups
    )
    w = lax.all_gather(w, "head", axis=0, axis_index_groups=plane_groups)
    if share % 16:
        w = w.transpose(2, 1, 0, 3, 4).reshape(1, 1, side, width, model)
        w = w.reshape(side, width, model)

    attended = attend(q, pages.reshape(-1, 2 * width), kv)
    a = attended.reshape(planes, side, local_rows, width).transpose(1, 0, 2, 3)
    a = a.reshape(side, planes * local_rows, width)
    a = lax.all_to_all(
        a, "head", split_axis=0, concat_axis=0, tiled=True, axis_index_groups=plane_groups
    )
    if share % 16:
        partial = jnp.einsum("hri,hid->rd", a, w, preferred_element_type=F32).astype(BF16)
    else:
        partial = project(a, w)
    parts = lax.all_to_all(
        partial.reshape(planes, local_rows, model),
        "head",
        split_axis=0,
        concat_axis=0,
        tiled=True,
        axis_index_groups=column_groups,
    )
    parts = parts.reshape(seqs, planes_of_seq, local_rows, model)
    return [parts[:, k] for k in range(planes_of_seq)]


def local(queries, new_kv, cache, resid, w_out, norm_gain, expert_ids, expert_gates, w_in, w_down):
    n = lax.axis_size("head")
    local_rows, seqs, heads, width = queries.shape
    model = resid.shape[2]
    rows = local_rows * seqs
    members = heads // new_kv.shape[2]
    in_pairs = (
        lax.axis_size("grp") == 2
        and seqs == 1
        and new_kv.shape[2] == 2
        and n == heads == 2 * members
        and members == 8
        and cache.shape[0] == 1
        and w_in.shape[0] == 1
        and w_out.shape[1] % 16 == 0
    )
    plan = parts_in_pairs if in_pairs else parts_in_planes
    parts = plan(queries, new_kv, cache, w_out)

    top = expert_ids.shape[2]
    experts = w_in.shape[0] * n
    capacity = max(2, 2 * rows * top // experts)
    ids = expert_ids.transpose(1, 0, 2).reshape(rows, top)
    gates = expert_gates.transpose(1, 0, 2).reshape(rows, top)
    onehot = (ids[:, :, None] == jnp.arange(experts, dtype=jnp.int32)).astype(jnp.int32)
    named = onehot.sum(1)
    before = jnp.cumsum(named, 0) - named
    slots_of = ids * capacity + jnp.sum(onehot * before[:, None, :], 2)
    slots = experts * capacity

    stream, outgoing = route(
        parts, resid.transpose(1, 0, 2), norm_gain[None, :], slots_of.T, slots
    )
    arrived = lax.all_to_all(
        outgoing.reshape(n, slots // n, model), "head", split_axis=0, concat_axis=0, tiled=True
    )
    local_experts = w_in.shape[0]
    if local_experts == 1:
        answered = expert_pair(arrived.reshape(slots, model), w_in[0], w_down[0])
        answered = answered.reshape(n, slots // n, model)
    else:
        arrived = arrived.reshape(n, local_experts, capacity, model).transpose(1, 0, 2, 3)
        arrived = arrived.reshape(local_experts, n * capacity, model)
        answered = jnp.stack([expert(arrived[e], w_in[e], w_down[e]) for e in range(local_experts)])
        answered = answered.reshape(local_experts, n, capacity, model).transpose(1, 0, 2, 3)
        answered = answered.reshape(n, slots // n, model)
    back = lax.all_to_all(answered, "head", split_axis=0, concat_axis=0, tiled=True)
    out = combine(back.reshape(slots, model), stream, slots_of, gates, seqs)
    return out.transpose(1, 0, 2)


def solution(mesh):
    return jax.shard_map(
        local,
        mesh=mesh,
        in_specs=(
            P("head", "grp", None, None),
            P("head", "grp", None, None),
            P(("grp", "head"), None, None),
            P("head", "grp", None),
            P(None, "head", None),
            P(),
            P("head", "grp", None),
            P("head", "grp", None),
            P("head", None, None),
            P("head", None, None),
        ),
        out_specs=P("head", "grp", None),
        check_vma=False,
    )
```

```python
import functools

import jax
import jax.numpy as jnp
from jax import lax
from jax.experimental import pallas as pl
from jax.experimental.pallas import tpu as pltpu
from jax.sharding import PartitionSpec as P

eps_norm = 1e-06
F32 = jnp.float32
BF16 = jnp.bfloat16
HIGH_VMEM = 48 * 2**20
LOG2_E = 1.4426950408889634


def in_hbm():
    return pl.BlockSpec(memory_space=pltpu.HBM)


def in_vmem():
    return pl.BlockSpec(memory_space=pltpu.VMEM)


def attend_kernel(
    block, chunk, width, q_hbm, cache_hbm, kv_hbm, o_ref, q_ref, cache_ref, kv_ref, s0, s1, sems
):
    members, groups, piece, _ = kv_hbm.shape
    length = members * groups * piece
    old = cache_hbm.shape[0]
    scale = width**-0.5
    in_q = pltpu.make_async_copy(q_hbm, q_ref, sems.at[0])
    in_cache = pltpu.make_async_copy(cache_hbm, cache_ref, sems.at[1])
    in_q.start()
    in_cache.start()
    in_kv = []
    for group in range(groups):
        for member in range(members):
            place = (group * members + member) * piece
            copy = pltpu.make_async_copy(
                kv_hbm.at[member, group], kv_ref.at[pl.ds(place, piece)], sems.at[2]
            )
            copy.start()
            in_kv.append(copy)
    in_q.wait()
    in_cache.wait()
    for copy in in_kv:
        copy.wait()
    scores = [s0, s1]

    def pieces(b):
        out = [(True, k, chunk, k) for k in range(0, old, chunk)]
        last = b * block
        for k in range(0, last, chunk):
            out.append((False, k, min(chunk, last - k), old + k))
        out.append((False, last, block, old + last))
        return out

    def make_scores(b, part, running):
        of_cache, first, count, column = part
        keys = (cache_ref if of_cache else kv_ref)[pl.ds(first, count), :width]
        s = lax.dot_general(
            q_ref[pl.ds(b * block, block), :],
            keys,
            (((1,), (1,)), ((), ())),
            preferred_element_type=F32,
        )
        if not of_cache and first == b * block:
            row = lax.broadcasted_iota(jnp.int32, s.shape, 0)
            col = lax.broadcasted_iota(jnp.int32, s.shape, 1)
            s = jnp.where(col <= row, s, -jnp.inf)
        scores[b % 2][:, pl.ds(column, count)] = s
        for k in range(0, count, 128):
            piece_max = s[:, k : k + 128]
            running = piece_max if running is None else jnp.maximum(running, piece_max)
        return running

    def use_scores(b, part, top, total, acc):
        of_cache, first, count, column = part
        values = (cache_ref if of_cache else kv_ref)[pl.ds(first, count), width:]
        e = jnp.exp((scores[b % 2][:, pl.ds(column, count)] - top) * scale)
        for k in range(0, count, 128):
            total = e[:, k : k + 128] if total is None else total + e[:, k : k + 128]
        product = jnp.dot(e.astype(BF16), values, preferred_element_type=F32)
        return total, product if acc is None else acc + product

    blocks = length // block
    running = None
    for part in pieces(0):
        running = make_scores(0, part, running)
    for b in range(blocks):
        top = jnp.max(running, 1, keepdims=True)
        now, later = pieces(b), pieces(b + 1) if b + 1 < blocks else []
        running, total, acc = None, None, None
        for k in range(max(len(now), len(later))):
            if k < len(now):
                total, acc = use_scores(b, now[k], top, total, acc)
            if k < len(later):
                running = make_scores(b + 1, later[k], running)
        o_ref[pl.ds(b * block, block), :] = (acc / jnp.sum(total, 1, keepdims=True)).astype(BF16)


def attend(q, cache, kv):
    length, width = q.shape
    old = cache.shape[0]
    block = min(256, length)
    chunk = min(512, old)
    return pl.pallas_call(
        functools.partial(attend_kernel, block, chunk, width),
        out_shape=jax.ShapeDtypeStruct((length, width), BF16),
        in_specs=[in_hbm()] * 3,
        out_specs=in_vmem(),
        scratch_shapes=[
            pltpu.VMEM((length, width), BF16),
            pltpu.VMEM((old, 2 * width), BF16),
            pltpu.VMEM((length, 2 * width), BF16),
            pltpu.VMEM((block, old + length), F32),
            pltpu.VMEM((block, old + length), F32),
            pltpu.SemaphoreType.DMA((3,)),
        ],
        compiler_params=pltpu.CompilerParams(vmem_limit_bytes=HIGH_VMEM),
        cost_estimate=pl.CostEstimate(
            flops=4 * length * (old + length // 2) * width,
            bytes_accessed=4 * (2 * length + 2 * old) * width,
            transcendentals=length * (old + length // 2),
        ),
        name="attend",
    )(q, cache, kv)


def attend_pair_kernel(
    block,
    chunk,
    width,
    q_hbm,
    page_own,
    page_y,
    page_c,
    page_cy,
    kv_own,
    kv_y,
    kv_c,
    kv_cy,
    o_ref,
    q_ref,
    old_ref,
    kv_ref,
    s0,
    s1,
    sems,
):
    me = lax.axis_index("head")
    members, heads, piece, _ = q_hbm.shape
    length = members * piece
    planes = kv_own.shape[0]
    old = old_ref.shape[0]
    earlier_group = me // members > 0
    core = lax.rem(me, 2)
    chip = jnp.bitwise_and(me // 2, members // 2 - 1)
    copies = []

    def bring(source, target, sem):
        copy = pltpu.make_async_copy(source, target, sems.at[sem])
        copy.start()
        copies.append(copy)

    for member in range(members):
        for head in range(heads):
            bring(q_hbm.at[member, head], q_ref.at[head, pl.ds(member * piece, piece)], 0)
    place = 0
    for page in (page_own, page_y, page_c, page_cy):
        count = page.shape[0]
        bring(page, old_ref.at[pl.ds(place, count)], 1)
        place += count
    for flip, pieces_of in ((0, kv_own), (2, kv_y), (1, kv_c), (3, kv_cy)):
        for t in range(planes):
            number = jnp.bitwise_and(
                jnp.bitwise_xor(me, flip ^ (t * (members // 2))), members - 1
            )
            start = pl.multiple_of(number * piece, piece)
            area = 0 if t * (members // 2) >= members else length
            bring(pieces_of.at[t], kv_ref.at[pl.ds(area + start, piece)], 2)
    for copy in copies:
        copy.wait()
    scale = width**-0.5 * LOG2_E
    scores = [s0, s1]
    blocks = length // block
    units = [(head, b) for head in range(heads) for b in range(blocks)]

    def pieces(unit):
        _, b = units[unit]
        out = [("old", k, chunk, k) for k in range(0, old, chunk)]
        out += [("past", k, chunk, old + k) for k in range(0, length, chunk)]
        last = b * block
        for k in range(0, last, chunk):
            out.append(("new", length + k, min(chunk, last - k), old + length + k))
        out.append(("edge", length + last, block, old + length + last))
        return out

    def make_scores(unit, part, running):
        kind, first, count, column = part
        head, b = units[unit]
        keys = (old_ref if kind == "old" else kv_ref)[pl.ds(first, count), :width]
        s = lax.dot_general(
            q_ref[head, pl.ds(b * block, block), :],
            keys,
            (((1,), (1,)), ((), ())),
            preferred_element_type=F32,
        )
        if kind == "past":
            s = jnp.where(earlier_group, s, -jnp.inf)
        if kind == "edge":
            row = lax.broadcasted_iota(jnp.int32, s.shape, 0)
            col = lax.broadcasted_iota(jnp.int32, s.shape, 1)
            s = jnp.where(col <= row, s, -jnp.inf)
        scores[unit % 2][:, pl.ds(column, count)] = s
        for k in range(0, count, 128):
            piece_max = s[:, k : k + 128]
            running = piece_max if running is None else jnp.maximum(running, piece_max)
        return running

    def use_scores(unit, part, top, total, acc):
        kind, first, count, column = part
        values = (old_ref if kind == "old" else kv_ref)[pl.ds(first, count), width:]
        e = jnp.exp2((scores[unit % 2][:, pl.ds(column, count)] - top) * scale)
        for k in range(0, count, 128):
            total = e[:, k : k + 128] if total is None else total + e[:, k : k + 128]
        product = jnp.dot(e.astype(BF16), values, preferred_element_type=F32)
        return total, product if acc is None else acc + product

    running = None
    for part in pieces(0):
        running = make_scores(0, part, running)
    for unit, (head, b) in enumerate(units):
        top = jnp.max(running, 1, keepdims=True)
        now = pieces(unit)
        later = pieces(unit + 1) if unit + 1 < len(units) else []
        running, total, acc = None, None, None
        for k in range(max(len(now), len(later))):
            if k < len(now):
                total, acc = use_scores(unit, now[k], top, total, acc)
            if k < len(later):
                running = make_scores(unit + 1, later[k], running)
        done = (acc / jnp.sum(total, 1, keepdims=True)).astype(BF16)
        for k in range(0, block, piece):
            member = (b * block + k) // piece
            side = jnp.bitwise_xor(core, member % 2)
            start = pl.multiple_of(jnp.bitwise_xor(chip, member // 2) * piece, piece)
            o_ref[side, pl.ds(start, piece), pl.ds(head * width, width)] = done[k : k + piece]


def attend_pair(q, pages, kvs):
    members, heads, piece, width = q.shape
    length = members * piece
    old = sum(page.shape[0] for page in pages)
    block = 2 * piece
    chunk = min(512, old, length)
    keys = old + 2 * length
    return pl.pallas_call(
        functools.partial(attend_pair_kernel, block, chunk, width),
        out_shape=jax.ShapeDtypeStruct((2, length // 2, heads * width), BF16),
        in_specs=[in_hbm()] * (1 + len(pages) + len(kvs)),
        out_specs=in_vmem(),
        scratch_shapes=[
            pltpu.VMEM((heads, length, width), BF16),
            pltpu.VMEM((old, 2 * width), BF16),
            pltpu.VMEM((2 * length, 2 * width), BF16),
            pltpu.VMEM((block, keys), F32),
            pltpu.VMEM((block, keys), F32),
            pltpu.SemaphoreType.DMA((3,)),
        ],
        compiler_params=pltpu.CompilerParams(vmem_limit_bytes=HIGH_VMEM),
        cost_estimate=pl.CostEstimate(
            flops=4 * heads * length * (keys - length // 2) * width,
            bytes_accessed=4 * (heads * length + keys) * width,
            transcendentals=heads * length * (keys - length // 2),
        ),
        name="attend",
    )(q, *pages, *kvs)


def project_pair_kernel(a_hbm, got_hbm, *refs):
    near, far, outs, (w_ref, all_ref, out_ref, sems) = refs[:4], refs[4:8], refs[8:-4], refs[-4:]
    me = lax.axis_index("head")
    half = lax.axis_index("grp")
    core = lax.rem(me, 2)
    steps, sides, heads, share, columns = near[0].shape
    width = w_ref.shape[1]
    side = got_hbm.shape[1]
    bring = [[], [], []]
    for other, source in enumerate((a_hbm.at[0], got_hbm)):
        at = pl.ds(pl.multiple_of(jnp.bitwise_xor(core, other) * side, side), side)
        bring[2].append(pltpu.make_async_copy(source, all_ref.at[:, at], sems.at[2]))
    for x in range(2):
        column = pl.multiple_of(jnp.bitwise_xor(half, x) * columns, columns)
        for first, given in ((0, near), (steps, far)):
            for flip in range(2):
                for t in range(steps):
                    for u in range(sides):
                        number = jnp.bitwise_xor(me, flip ^ (2 * u) ^ (4 * (first + t)))
                        row = pl.multiple_of(number * share, share)
                        bring[x].append(
                            pltpu.make_async_copy(
                                given[2 * x + flip].at[t, u],
                                w_ref.at[:, pl.ds(row, share), pl.ds(column, columns)],
                                sems.at[x],
                            )
                        )
    for copies in (bring[2], bring[0], bring[1]):
        for copy in copies:
            copy.start()
    for copy in bring[2]:
        copy.wait()
    rows = outs[0].shape[0]
    tile = min(512, columns)
    back = []
    for x in range(2):
        for copy in bring[x]:
            copy.wait()
        for first in range(0, columns, tile):
            column = jnp.bitwise_xor(half, x) * columns + first
            at = pl.ds(pl.multiple_of(column, tile), tile)
            w = w_ref[:, :, at].reshape(heads * width, tile)
            out_ref[:, at] = jnp.dot(all_ref[...], w, preferred_element_type=F32).astype(BF16)
            for k, out in enumerate(outs):
                copy = pltpu.make_async_copy(
                    out_ref.at[pl.ds(k * rows, rows), at], out.at[:, at], sems.at[3]
                )
                copy.start()
                back.append(copy)
    for copy in back:
        copy.wait()


def project_pair(a, got, near, far, parts):
    _, _, heads, share, columns = near[0].shape
    rows = got.shape[0]
    width = 2 * got.shape[1] // heads
    model = 2 * columns
    return pl.pallas_call(
        project_pair_kernel,
        out_shape=[pltpu.HBM((rows // parts, model), BF16)] * parts,
        in_specs=[in_hbm()] * 10,
        out_specs=[in_hbm()] * parts,
        scratch_shapes=[
            pltpu.VMEM((heads, width, model), BF16),
            pltpu.VMEM((rows, heads * width), BF16),
            pltpu.VMEM((rows, model), BF16),
            pltpu.SemaphoreType.DMA((4,)),
        ],
        compiler_params=pltpu.CompilerParams(vmem_limit_bytes=HIGH_VMEM),
        cost_estimate=pl.CostEstimate(
            flops=2 * heads * rows * width * model,
            bytes_accessed=2 * (heads * width * model + heads * rows * width + rows * model),
            transcendentals=0,
        ),
        name="project",
    )(a, got, *near, *far)


def project_kernel(a_ref, w_ref, o_ref):
    members = a_ref.shape[0]
    planes, share = w_ref.shape[1], w_ref.shape[3]
    acc = None
    for head in range(members):
        w = jnp.concatenate(
            [w_ref[m, p, head] for p in range(planes) for m in range(members)], 0
        )
        part = jnp.dot(a_ref[head], w, preferred_element_type=F32)
        acc = part if acc is None else acc + part
    o_ref[...] = acc.astype(BF16)


def project(a, w):
    members, rows, width = a.shape
    planes, share, model = w.shape[1], w.shape[3], w.shape[4]
    tile = min(512, model)
    return pl.pallas_call(
        project_kernel,
        grid=(model // tile,),
        out_shape=jax.ShapeDtypeStruct((rows, model), BF16),
        in_specs=[
            pl.BlockSpec((members, rows, width), lambda t: (0, 0, 0)),
            pl.BlockSpec((members, planes, members, share, tile), lambda t: (0, 0, 0, 0, t)),
        ],
        out_specs=pl.BlockSpec((rows, tile), lambda t: (0, t)),
        compiler_params=pltpu.CompilerParams(vmem_limit_bytes=HIGH_VMEM),
        cost_estimate=pl.CostEstimate(
            flops=2 * members * rows * width * model,
            bytes_accessed=2 * (members * width * model + members * rows * width + rows * model),
            transcendentals=0,
        ),
        name="project",
    )(a, w)


def route_kernel(resid_ref, gain_ref, slots_ref, *refs):
    parts_refs, (stream_ref, out_ref) = refs[:-2], refs[-2:]
    seqs = resid_ref.shape[0]
    streams = []
    for seq in range(seqs):
        stream = resid_ref[seq].astype(F32)
        projected = parts_refs[0][seq].astype(F32)
        for part in parts_refs[1:]:
            projected = projected + part[seq].astype(F32)
        streams.append(stream + projected)
    stream = jnp.concatenate(streams, 0) if seqs > 1 else streams[0]
    stream_ref[...] = stream
    normed = stream * lax.rsqrt(jnp.mean(stream * stream, 1, keepdims=True) + eps_norm)
    normed = (normed * gain_ref[...]).astype(BF16)
    slots, rows = out_ref.shape[0], stream.shape[0]
    place = lax.broadcasted_iota(jnp.int32, (slots, rows), 0)
    hit = place == slots_ref[0:1, :]
    for k in range(1, slots_ref.shape[0]):
        hit = hit | (place == slots_ref[k : k + 1, :])
    out_ref[...] = jnp.dot(hit.astype(BF16), normed, preferred_element_type=F32).astype(BF16)


def route(parts, resid, gain, slots_of, slots):
    seqs, local_rows, model = resid.shape
    rows = seqs * local_rows
    return pl.pallas_call(
        route_kernel,
        out_shape=(
            jax.ShapeDtypeStruct((rows, model), F32),
            jax.ShapeDtypeStruct((slots, model), BF16),
        ),
        in_specs=[in_vmem()] * (3 + len(parts)),
        out_specs=(in_vmem(), in_vmem()),
        compiler_params=pltpu.CompilerParams(vmem_limit_bytes=HIGH_VMEM),
        cost_estimate=pl.CostEstimate(
            flops=2 * slots * rows * model,
            bytes_accessed=2 * (len(parts) + 3 + slots // rows) * rows * model,
            transcendentals=0,
        ),
        name="route",
    )(resid, gain, slots_of, *parts)


def expert_kernel(x_ref, w_in_ref, w_down_ref, o_ref):
    hidden_width = w_down_ref.shape[0]
    inner = jnp.dot(x_ref[...], w_in_ref[...], preferred_element_type=F32)
    gate = inner[:, :hidden_width]
    hidden = (gate / (1.0 + jnp.exp(-gate)) * inner[:, hidden_width:]).astype(BF16)
    o_ref[...] = jnp.dot(hidden, w_down_ref[...], preferred_element_type=F32).astype(BF16)


def expert(x, w_in, w_down):
    rows, model = x.shape
    hidden_width = w_down.shape[0]
    return pl.pallas_call(
        expert_kernel,
        out_shape=jax.ShapeDtypeStruct((rows, model), BF16),
        in_specs=[in_vmem()] * 3,
        out_specs=in_vmem(),
        compiler_params=pltpu.CompilerParams(vmem_limit_bytes=HIGH_VMEM),
        cost_estimate=pl.CostEstimate(
            flops=6 * rows * model * hidden_width,
            bytes_accessed=2 * (2 * rows * model + 3 * model * hidden_width),
            transcendentals=rows * hidden_width,
        ),
        name="expert",
    )(x, w_in, w_down)


def expert_pair(x, w_in, w_down):
    rows, model = x.shape
    hidden_width = w_down.shape[0]
    parts = 4
    depth = model // parts

    def kernel(x_hbm, in_hbm_ref, down_hbm, o_hbm, x_ref, in_ref, down_ref, o_ref, sems):
        bring_x = pltpu.make_async_copy(x_hbm, x_ref, sems.at[parts])
        bring_x.start()
        bring_in = []
        for k in range(parts):
            at = pl.ds(k * depth, depth)
            bring_in.append(pltpu.make_async_copy(in_hbm_ref.at[at], in_ref.at[at], sems.at[k]))
            bring_in[k].start()
        bring_down = pltpu.make_async_copy(down_hbm, down_ref, sems.at[parts + 1])
        bring_down.start()
        bring_x.wait()
        inner = None
        for k in range(parts):
            bring_in[k].wait()
            at = pl.ds(k * depth, depth)
            part = jnp.dot(x_ref[:, at], in_ref[at, :], preferred_element_type=F32)
            inner = part if inner is None else inner + part
        gate = inner[:, :hidden_width]
        hidden = (gate / (1.0 + jnp.exp(-gate)) * inner[:, hidden_width:]).astype(BF16)
        bring_down.wait()
        o_ref[...] = jnp.dot(hidden, down_ref[...], preferred_element_type=F32).astype(BF16)
        back = pltpu.make_async_copy(o_ref, o_hbm, sems.at[parts + 2])
        back.start()
        back.wait()

    return pl.pallas_call(
        kernel,
        out_shape=pltpu.HBM((rows, model), BF16),
        in_specs=[in_hbm()] * 3,
        out_specs=in_hbm(),
        scratch_shapes=[
            pltpu.VMEM((rows, model), BF16),
            pltpu.VMEM(w_in.shape, BF16),
            pltpu.VMEM(w_down.shape, BF16),
            pltpu.VMEM((rows, model), BF16),
            pltpu.SemaphoreType.DMA((parts + 3,)),
        ],
        compiler_params=pltpu.CompilerParams(vmem_limit_bytes=HIGH_VMEM),
        cost_estimate=pl.CostEstimate(
            flops=6 * rows * model * hidden_width,
            bytes_accessed=2 * (2 * rows * model + 3 * model * hidden_width),
            transcendentals=rows * hidden_width,
        ),
        name="expert",
    )(x, w_in, w_down)


def combine_kernel(
    seqs, back_ref, stream_hbm, slots_ref, gates_ref, o_ref, stream_ref, sem
):
    bring = pltpu.make_async_copy(stream_hbm, stream_ref, sem.at[0])
    bring.start()
    slots = back_ref.shape[0]
    rows = stream_ref.shape[0]
    place = lax.broadcasted_iota(jnp.int32, (rows, slots), 1)
    gathered = None
    for k in range(slots_ref.shape[1]):
        pick = (place == slots_ref[:, k : k + 1]).astype(BF16)
        picked = jnp.dot(pick, back_ref[...], preferred_element_type=F32)
        part = picked * gates_ref[:, k : k + 1]
        gathered = part if gathered is None else gathered + part
    bring.wait()
    out = (stream_ref[...] + gathered).astype(BF16)
    local_rows = rows // seqs
    for seq in range(seqs):
        o_ref[seq] = out[seq * local_rows : (seq + 1) * local_rows]


def combine(back, stream, slots_of, gates, seqs):
    slots, model = back.shape
    rows = stream.shape[0]
    top = slots_of.shape[1]
    return pl.pallas_call(
        functools.partial(combine_kernel, seqs),
        out_shape=jax.ShapeDtypeStruct((seqs, rows // seqs, model), BF16),
        in_specs=[in_vmem(), in_hbm(), in_vmem(), in_vmem()],
        out_specs=in_vmem(),
        scratch_shapes=[pltpu.VMEM((rows, model), F32), pltpu.SemaphoreType.DMA((1,))],
        compiler_params=pltpu.CompilerParams(vmem_limit_bytes=HIGH_VMEM),
        cost_estimate=pl.CostEstimate(
            flops=2 * top * slots * rows * model,
            bytes_accessed=2 * slots * model + 6 * rows * model,
            transcendentals=0,
        ),
        name="combine",
    )(back, stream, slots_of, gates)


def flipped(value, axis, mask):
    pairs = [(source, source ^ mask) for source in range(lax.axis_size(axis))]
    return lax.ppermute(value, axis, pairs)


def parts_in_pairs(queries, new_kv, cache, w_out):
    n = lax.axis_size("head")
    local_rows, _, heads, width = queries.shape
    pair_heads = new_kv.shape[2]
    members = heads // pair_heads
    model = w_out.shape[2]
    share = w_out.shape[1]
    me = lax.axis_index("head")
    plane_bit = members // 2
    planes = n // plane_bit
    b = (me // plane_bit) % 2
    y = (me // 2) % 2
    group_sets = [[g * members + m for m in range(members)] for g in range(n // members)]

    query_slots = queries.reshape(local_rows, heads, width).transpose(1, 0, 2)
    query_slots = query_slots.reshape(members, heads // members, local_rows, width)

    def page_target(source, other):
        p, plane, rest = source // members, (source // plane_bit) % 2, source % plane_bit
        return (plane ^ other) * members + p * plane_bit + rest

    page_a, page_b = (
        lax.ppermute(cache[0], "head", [(d, page_target(d, other)) for d in range(n)])
        for other in range(2)
    )
    kv_heads = new_kv.reshape(local_rows, pair_heads, 2 * width).transpose(1, 0, 2)
    kv_same = lax.dynamic_index_in_dim(kv_heads, b, 0, keepdims=False)
    kv_other = lax.dynamic_index_in_dim(kv_heads, 1 - b, 0, keepdims=False)
    columns = model // 2
    w = lax.dynamic_slice_in_dim(w_out, lax.axis_index("grp") * columns, columns, 2)
    w = w.reshape(2, 2, heads // 4, share, columns)
    w_keep = lax.dynamic_index_in_dim(w, y, 1, keepdims=False)
    w_give = lax.dynamic_index_in_dim(w, 1 - y, 1, keepdims=False)
    kv_own = [kv_same]
    for t in range(1, planes):
        kv_own.append(flipped(kv_other if t % 2 else kv_same, "head", t * plane_bit))
    w_got = flipped(w_give, "head", 2)

    kv_own[1], kv_own[2], w_got, query_slots = lax.optimization_barrier(
        (kv_own[1], kv_own[2], w_got, query_slots)
    )
    q = lax.all_to_all(
        query_slots, "head", split_axis=0, concat_axis=0, tiled=True, axis_index_groups=group_sets
    )
    w_both = jnp.stack([w_keep, w_got], 1)
    w_same = lax.dynamic_index_in_dim(w_both, b, 0, keepdims=False)
    w_other = lax.dynamic_index_in_dim(w_both, 1 - b, 0, keepdims=False)
    w_first = flipped(w_other, "head", plane_bit)

    own_pages = jnp.concatenate([page_a, page_b], 0)
    own_pages, kv_own, w_first = lax.optimization_barrier((own_pages, kv_own, w_first))
    kv_own = jnp.stack(kv_own, 0)
    pages_y = flipped(own_pages, "head", 2)
    kv_y = flipped(kv_own, "head", 2)
    w_near = jnp.stack([w_same, w_first], 0)
    w_near_x = flipped(w_near, "grp", 1)
    w_far = flipped(w_near, "head", members)
    pages_y, kv_y, own_pages, kv_own, w_near_x = lax.optimization_barrier(
        (pages_y, kv_y, own_pages, kv_own, w_near_x)
    )
    kv_c = flipped(kv_own, "head", 1)
    kv_cy = flipped(kv_y, "head", 1)
    pages_c = flipped(own_pages, "head", 1)
    pages_cy = flipped(pages_y, "head", 1)
    q, w_far = lax.optimization_barrier((q, w_far))
    w_far_x = flipped(w_far, "grp", 1)
    a = attend_pair(q, (own_pages, pages_y, pages_c, pages_cy), (kv_own, kv_y, kv_c, kv_cy))
    got = flipped(a[1], "head", 1)
    a, w_near_x, w_far_x = lax.optimization_barrier((a, w_near_x, w_far_x))
    w_near_c = flipped(w_near, "head", 1)
    w_far_c = flipped(w_far, "head", 1)
    w_near_cx = flipped(w_near_x, "head", 1)
    w_far_cx = flipped(w_far_x, "head", 1)
    partial = project_pair(
        a,
        got,
        (w_near, w_near_c, w_near_x, w_near_cx),
        (w_far, w_far_c, w_far_x, w_far_cx),
        members // 2,
    )
    parts = [partial[0]] + [flipped(partial[k], "head", 2 * k) for k in (3, 2, 1)]
    return [part[None] for part in parts]


def parts_in_planes(queries, new_kv, cache, w_out):
    n = lax.axis_size("head")
    local_rows, seqs, heads, width = queries.shape
    pair_heads = new_kv.shape[2]
    members = heads // pair_heads
    groups = n // members
    model = w_out.shape[2]
    side = 1 << ((n.bit_length() - 1) // 2)
    side = min(side, heads)
    planes = n // side
    planes_of_seq = heads // side
    pair_groups = [[g * members + m for m in range(members)] for g in range(groups)]
    cross_groups = [[g * members + m for g in range(groups)] for m in range(members)]
    plane_groups = [[p * side + m for m in range(side)] for p in range(planes)]
    column_groups = [[p * side + m for p in range(planes)] for m in range(side)]

    query_slots = queries.reshape(local_rows, n, width).transpose(1, 0, 2)
    q = lax.all_to_all(query_slots, "head", split_axis=0, concat_axis=0, tiled=True)
    q = q.reshape(n * local_rows, width)

    kv_slots = new_kv.reshape(local_rows, groups, 2 * width).transpose(1, 0, 2)
    kv = lax.all_to_all(
        kv_slots, "head", split_axis=0, concat_axis=0, tiled=True, axis_index_groups=cross_groups
    )
    kv = lax.all_gather(kv, "head", axis=0, axis_index_groups=pair_groups)
    pages = lax.all_gather(cache, "head", axis=0, tiled=True, axis_index_groups=pair_groups)

    share = w_out.shape[1]
    w_planes = w_out.reshape(planes_of_seq, side, share, model)
    if planes > planes_of_seq:
        w_planes = jnp.tile(w_planes, (planes // planes_of_seq, 1, 1, 1))
    w = lax.all_to_all(
        w_planes, "head", split_axis=0, concat_axis=0, tiled=True, axis_index_groups=column_groups
    )
    w = lax.all_gather(w, "head", axis=0, axis_index_groups=plane_groups)
    if share % 16:
        w = w.transpose(2, 1, 0, 3, 4).reshape(1, 1, side, width, model)
        w = w.reshape(side, width, model)

    attended = attend(q, pages.reshape(-1, 2 * width), kv)
    a = attended.reshape(planes, side, local_rows, width).transpose(1, 0, 2, 3)
    a = a.reshape(side, planes * local_rows, width)
    a = lax.all_to_all(
        a, "head", split_axis=0, concat_axis=0, tiled=True, axis_index_groups=plane_groups
    )
    if share % 16:
        partial = jnp.einsum("hri,hid->rd", a, w, preferred_element_type=F32).astype(BF16)
    else:
        partial = project(a, w)
    parts = lax.all_to_all(
        partial.reshape(planes, local_rows, model),
        "head",
        split_axis=0,
        concat_axis=0,
        tiled=True,
        axis_index_groups=column_groups,
    )
    parts = parts.reshape(seqs, planes_of_seq, local_rows, model)
    return [parts[:, k] for k in range(planes_of_seq)]


def local(queries, new_kv, cache, resid, w_out, norm_gain, expert_ids, expert_gates, w_in, w_down):
    n = lax.axis_size("head")
    local_rows, seqs, heads, width = queries.shape
    model = resid.shape[2]
    rows = local_rows * seqs
    members = heads // new_kv.shape[2]
    in_pairs = (
        lax.axis_size("grp") == 2
        and seqs == 1
        and new_kv.shape[2] == 2
        and n == heads == 2 * members
        and members == 8
        and cache.shape[0] == 1
        and w_in.shape[0] == 1
        and w_out.shape[1] % 16 == 0
    )
    plan = parts_in_pairs if in_pairs else parts_in_planes
    parts = plan(queries, new_kv, cache, w_out)

    top = expert_ids.shape[2]
    experts = w_in.shape[0] * n
    capacity = max(2, 2 * rows * top // experts)
    ids = expert_ids.transpose(1, 0, 2).reshape(rows, top)
    gates = expert_gates.transpose(1, 0, 2).reshape(rows, top)
    onehot = (ids[:, :, None] == jnp.arange(experts, dtype=jnp.int32)).astype(jnp.int32)
    named = onehot.sum(1)
    before = jnp.cumsum(named, 0) - named
    slots_of = ids * capacity + jnp.sum(onehot * before[:, None, :], 2)
    slots = experts * capacity

    stream, outgoing = route(
        parts, resid.transpose(1, 0, 2), norm_gain[None, :], slots_of.T, slots
    )
    arrived = lax.all_to_all(
        outgoing.reshape(n, slots // n, model), "head", split_axis=0, concat_axis=0, tiled=True
    )
    local_experts = w_in.shape[0]
    if local_experts == 1:
        answered = expert_pair(arrived.reshape(slots, model), w_in[0], w_down[0])
        answered = answered.reshape(n, slots // n, model)
    else:
        arrived = arrived.reshape(n, local_experts, capacity, model).transpose(1, 0, 2, 3)
        arrived = arrived.reshape(local_experts, n * capacity, model)
        answered = jnp.stack([expert(arrived[e], w_in[e], w_down[e]) for e in range(local_experts)])
        answered = answered.reshape(local_experts, n, capacity, model).transpose(1, 0, 2, 3)
        answered = answered.reshape(n, slots // n, model)
    back = lax.all_to_all(answered, "head", split_axis=0, concat_axis=0, tiled=True)
    out = combine(back.reshape(slots, model), stream, slots_of, gates, seqs)
    return out.transpose(1, 0, 2)


def solution(mesh):
    return jax.shard_map(
        local,
        mesh=mesh,
        in_specs=(
            P("head", "grp", None, None),
            P("head", "grp", None, None),
            P(("grp", "head"), None, None),
            P("head", "grp", None),
            P(None, "head", None),
            P(),
            P("head", "grp", None),
            P("head", "grp", None),
            P("head", None, None),
            P("head", None, None),
        ),
        out_specs=P("head", "grp", None),
        check_vma=False,
    )
```
